32 devices in a mesh: gx: 2 (over y), gy: 16 (over z, x, core).
Axes of the slice: x: 2, y: 2, z: 4, core: 2. Of those that a mesh axis runs over, the one named last changes fastest.
Arguments:
- duals: float32 [16, 4, 64, 128], P(None, 'gx', 'gy'), may hold values from -6 to 6
- residual: float32 [16, 4, 64, 128], P(None, 'gx', 'gy')
- direction: float32 [16, 4, 64, 128], P(None, 'gx', 'gy'), may hold values from -6 to 6
- prev_rho: float32 [16], replicated, may hold values from 16384 to 65536
- dual_schur: float32 [4, 64, 256, 256], P('gx', 'gy'), as said below
- coupling: float32 [4, 64, 8, 256], P('gx', 'gy'), may hold values from -0.75 to 0.75
- coarse_inverse: float32 [2, 384, 384], P('gx'), as said below
- edge_map: int32 [4, 64, 256], P('gx', 'gy'), may hold values from 0 to 255, each once within a row
- corner_slot: int32 [4, 64, 8], P('gx', 'gy'), may hold values from 0 to 384, as said below
- active: int32 [4, 64, 128], P('gx', 'gy'), may hold values 0 or 1
- scaling: float32 [4, 64, 128], P('gx', 'gy'), may hold values from 0.25 to 1
Outputs:
- new_duals: float32 [16, 4, 64, 128], P(None, 'gx', 'gy')
- new_residual: float32 [16, 4, 64, 128], P(None, 'gx', 'gy')
- new_direction: float32 [16, 4, 64, 128], P(None, 'gx', 'gy')
The draws below stay inside these ranges and needn't reach their ends.
Inputs may be any that keep to these rules, and one draw needn't show every extreme that they name: Each subdomain's block of dual_schur and each region's block of coarse_inverse is symmetric positive definite. `coarse_inverse`: each region's block is symmetric positive definite. `corner_slot`: slots number the corner dofs of a region; a corner shared by subdomains of one region has one slot; 384 marks corners on the clamped bottom edge, which have no dof.
All inputs are finite; a program needn't handle non-finite values. No bound on the sum of `active` on one device may be relied on, other than what follows from the above.
Results may differ from the reference program's by a relative error of at most 0.00014.
Values sent between devices are 32-bit elements; how exact they have to be, the bound alone decides.
No kernel may reach another device: no remote copies, remote signals or barrier semaphores. Data moves between devices by JAX's collectives and lax.ppermute only.
A program may use at most 64 MiB of HBM per device.

```python
import math
import jax
import jax.numpy as jnp
from jax import lax

NI = 256
NE = 64
NC = 8
K = 16
SX = 2
ITERS = 6
SUBX = 4
SUBY = 64
REGIONS = 2
NCR = 384


def spd_blocks(key, lead, order, scale_lo, scale_hi):
    first, second = jax.random.split(key)
    limit = 0.9 / math.sqrt(order)
    noise = jax.random.uniform(first, lead + (order, order), jnp.float32, -limit, limit)
    sym = 0.5 * (noise + jnp.swapaxes(noise, -1, -2))
    ident = jnp.eye(order, dtype=jnp.float32)
    scales = jnp.exp(jax.random.uniform(second, lead + (order,), jnp.float32, math.log(scale_lo), math.log(scale_hi)))
    return scales[..., :, None] * scales[..., None, :] * (ident + sym)


def draw_dual_schur(key, part):
    return spd_blocks(key, (SUBX, SUBY), NI, 0.4, 1.6)


def draw_coarse_inverse(key, part):
    return spd_blocks(key, (REGIONS,), NCR, 0.45, 0.65)


def draw_residual(key, part):
    cols = jnp.arange(SUBX, dtype=jnp.float32)[None, :, None, None]
    rows = jnp.arange(SUBY, dtype=jnp.float32)[None, None, :, None]
    place = (cols * SUBY + rows) / (SUBX * SUBY)
    shape = (K, SUBX, SUBY, 2 * NE)
    values = jnp.clip(jax.random.normal(key, shape, jnp.float32), -6.0, 6.0)
    return values * jnp.sqrt(1.0 + 2.0 * place)


def draw_corner_slot(key, part):
    cols = jnp.arange(SUBX, dtype=jnp.int32)[:, None, None]
    rows = jnp.arange(SUBY, dtype=jnp.int32)[None, :, None]
    which = jnp.arange(NC, dtype=jnp.int32)[None, None, :]
    corner = which // 2
    dof_id = which % 2
    along = cols % SX + corner % 2
    height = rows + corner // 2
    region = jnp.broadcast_to(cols // SX, (SUBX, SUBY, NC))
    ident = (along * SUBY + (height - 1)) * 2 + dof_id
    ident = jnp.clip(ident, 0, NCR - 1)
    orders = jax.vmap(lambda idx: jax.random.permutation(jax.random.fold_in(key, idx), NCR))(jnp.arange(REGIONS, dtype=jnp.int32))
    slot = orders[region, jnp.broadcast_to(ident, (SUBX, SUBY, NC))].astype(jnp.int32)
    return jnp.where(jnp.broadcast_to(height, (SUBX, SUBY, NC)) == 0, NCR, slot).astype(jnp.int32)


def touch_ends(entries, own_key, smallest, top_value):
    shape = entries.shape
    spot = [jax.random.randint(jax.random.fold_in(own_key, axis), (), 0, shape[axis]) for axis in range(len(shape))]
    entries = entries.at[tuple(spot)].set(smallest)
    longest = shape.index(max(shape))
    spot[longest] = (spot[longest] + 1) % shape[longest]
    return entries.at[tuple(spot)].set(top_value)


def level_of(own_key, extent, pieces, least, largest):
    def one(position, shards_of):
        draws = jax.random.uniform(jax.random.fold_in(jax.random.fold_in(own_key, 6), position), (shards_of,), jnp.float32, least / len(pieces), largest / len(pieces))
        return jnp.repeat(jnp.exp(draws), extent[position] // shards_of).reshape((-1,) + (1,) * (len(extent) - position - 1))

    loudness = one(*pieces[0])
    for cut in pieces[1:]:
        loudness = loudness * one(*cut)
    return loudness


def centred(stream_key, dims, spread, reach, cuts=(), kind=jnp.bfloat16):
    drawn = jax.random.normal(stream_key, dims, jnp.float32) * spread
    if len(cuts) > 0:
        drawn = level_of(stream_key, dims, cuts, -0.22, 0.18) * drawn
    return jnp.clip(drawn, min=-reach, max=reach).astype(kind)


def setup_inputs(seed: int = 0) -> dict:
    key_list = jax.random.split(jax.random.key(seed), 12)
    return {
        "duals": centred(key_list[0], (K, SUBX, SUBY, 2 * NE), 1.0, 6.0, ((1, 2), (2, 16)), jnp.float32),
        "residual": draw_residual(jax.random.fold_in(key_list[11], 71), 0),
        "direction": centred(key_list[2], (K, SUBX, SUBY, 2 * NE), 1.0, 6.0, ((1, 2), (2, 16)), jnp.float32),
        "prev_rho": jnp.clip(jnp.exp(jax.random.uniform(key_list[3], (K,), jnp.float32, math.log(16384.0), math.log(65536.0))), 16384.0, 65536.0),
        "dual_schur": draw_dual_schur(jax.random.fold_in(key_list[11], 71), 0),
        "coupling": centred(key_list[5], (SUBX, SUBY, NC, NI), (8 * NC) ** -0.5, 0.75, ((0, 2), (1, 16)), jnp.float32),
        "coarse_inverse": draw_coarse_inverse(jax.random.fold_in(key_list[11], 71), 0),
        "edge_map": jax.vmap(lambda own: jax.random.permutation(own, NI))(jax.random.split(key_list[7], SUBX * SUBY)).reshape((SUBX, SUBY, NI)).astype(jnp.int32),
        "corner_slot": draw_corner_slot(jax.random.fold_in(key_list[11], 71), 0),
        "active": touch_ends((jax.random.randint(key_list[9], (SUBX, SUBY, 2 * NE), 0, 8) < 7).astype(jnp.int32), jax.random.fold_in(key_list[9], 1), 0, 1),
        "scaling": jnp.clip(jnp.exp(math.log(1.0) - 1.3862944 * jax.random.uniform(key_list[10], (SUBX, SUBY, 2 * NE), jnp.float32) ** level_of(key_list[10], (SUBX, SUBY, 2 * NE), ((0, 2), (1, 16)), -0.2, 0.2)), 0.25, 1.0),
    }


def make_keep(active):
    east = (jnp.arange(SUBX) < SUBX - 1)[:, None, None]
    north = (jnp.arange(SUBY) < SUBY - 1)[None, :, None]
    east = jnp.broadcast_to(east, (SUBX, SUBY, NE))
    north = jnp.broadcast_to(north, (SUBX, SUBY, NE))
    return active.astype(jnp.float32) * jnp.concatenate([east, north], -1).astype(jnp.float32)


def apply_dual(field, keep, dual_schur, coupling, coarse_inverse, edge_map, inverse, onehot):
    high = lax.Precision.HIGHEST
    part_e = field[..., :NE]
    part_n = field[..., NE:]
    west = -jnp.pad(part_e, ((0, 0), (1, 0), (0, 0), (0, 0)))[:, :-1]
    south = -jnp.pad(part_n, ((0, 0), (0, 0), (1, 0), (0, 0)))[:, :, :-1]
    edge_vec = jnp.concatenate([west, part_e, south, part_n], -1)
    local = jnp.take_along_axis(edge_vec, edge_map[None], -1)
    work = jnp.einsum('xyij,kxyj->kxyi', dual_schur, local, precision=high)
    corner_val = jnp.einsum('xycj,kxyj->kxyc', coupling, local, precision=high)
    grouped = corner_val.reshape(K, REGIONS, SX, SUBY, NC)
    table = onehot.reshape(REGIONS, SX, SUBY, NC, NCR)
    total = jnp.einsum('krayc,raycn->krn', grouped, table, precision=high)
    solved = jnp.einsum('rnm,krm->krn', coarse_inverse, total, precision=high)
    back = jnp.einsum('raycn,krn->krayc', table, solved, precision=high).reshape(K, SUBX, SUBY, NC)
    work = work + jnp.einsum('xycj,kxyc->kxyj', coupling, back, precision=high)
    work_edge = jnp.take_along_axis(work, inverse[None], -1)
    west_w = work_edge[..., :NE]
    east_w = work_edge[..., NE:2 * NE]
    south_w = work_edge[..., 2 * NE:3 * NE]
    north_w = work_edge[..., 3 * NE:]
    from_east = jnp.pad(west_w, ((0, 0), (0, 1), (0, 0), (0, 0)))[:, 1:]
    from_north = jnp.pad(south_w, ((0, 0), (0, 0), (0, 1), (0, 0)))[:, :, 1:]
    return jnp.concatenate([east_w - from_east, north_w - from_north], -1) * keep


def reference(duals, residual, direction, prev_rho, dual_schur, coupling, coarse_inverse, edge_map, corner_slot, active, scaling):
    keep = make_keep(active)
    inverse = jnp.argsort(edge_map, axis=-1).astype(jnp.int32)
    onehot = (corner_slot[..., None] == jnp.arange(NCR, dtype=jnp.int32)).astype(jnp.float32)
    lam = duals
    res = residual
    pprev = keep * direction
    rho_old = prev_rho
    for step in range(ITERS):
        zvec = keep * scaling * res
        rho = jnp.sum(res * zvec, axis=(1, 2, 3))
        beta = rho / rho_old
        pvec = zvec + beta[:, None, None, None] * pprev
        qvec = apply_dual(pvec, keep, dual_schur, coupling, coarse_inverse, edge_map, inverse, onehot)
        alpha = rho / jnp.sum(pvec * qvec, axis=(1, 2, 3))
        lam = lam + alpha[:, None, None, None] * pvec
        res = res - alpha[:, None, None, None] * qvec
        rho_old = rho
        pprev = pvec
    return lam, res, pprev
```

```python
import jax
import jax.numpy as jnp
from jax import lax
from jax.sharding import PartitionSpec as P

ITERS = 6
HIGH = lax.Precision.HIGH
EXACT = lax.Precision.HIGHEST
BOTH = ("gx", "gy")


def pairs_from(first, peers):
    return [(i, i + 1) for i in range(first, peers - 1, 2)]


def both_ways(pairs):
    return pairs + [(b, a) for a, b in pairs]


def up_gy(value, peers):
    even = lax.ppermute(value, "gy", pairs_from(0, peers))
    odd = lax.ppermute(value, "gy", pairs_from(1, peers))
    return jnp.where(lax.axis_index("gy") % 2 == 1, even, odd)


def swap_gy(low, high, peers):
    is_even = lax.axis_index("gy") % 2 == 0
    first = lax.ppermute(jnp.where(is_even, high, low), "gy", both_ways(pairs_from(0, peers)))
    second = lax.ppermute(jnp.where(is_even, low, high), "gy", both_ways(pairs_from(1, peers)))
    return jnp.where(is_even, second, first), jnp.where(is_even, first, second)


def swap_gx(low, high, peers):
    if peers == 2:
        is_first = lax.axis_index("gx") == 0
        got = lax.ppermute(jnp.where(is_first, high, low), "gx", [(0, 1), (1, 0)])
        zero = jnp.zeros_like(got)
        return jnp.where(is_first, zero, got), jnp.where(is_first, got, zero)
    below = lax.ppermute(high, "gx", [(i, i + 1) for i in range(peers - 1)])
    above = lax.ppermute(low, "gx", [(i + 1, i) for i in range(peers - 1)])
    return below, above


def everywhere(block, axes):
    sent = jnp.broadcast_to(block[None], (lax.axis_size(axes),) + block.shape)
    return lax.all_to_all(sent, axes, 0, 0, tiled=False)


def shards(
    duals, residual, direction, prev_rho, dual_schur, coupling, coarse_inverse, edge_map, corner_slot, active, scaling
):
    cases, span_x, span_y, owned = duals.shape
    half = owned // 2
    full = 2 * owned
    corners = coupling.shape[2]
    width_c = coarse_inverse.shape[-1]
    peers_x, peers_y = lax.axis_size("gx"), lax.axis_size("gy")
    whole = peers_x == 2
    axes = BOTH if whole else "gy"
    regions = peers_x if whole else 1
    peers = regions * peers_y
    here_x, here_y = lax.axis_index("gx"), lax.axis_index("gy")
    used = 2 * (span_x + 1) * (span_y + 1)
    slots = used + 2

    columns = here_x * span_x + jnp.arange(span_x)
    rowset = here_y * span_y + jnp.arange(span_y)
    east_ok = jnp.broadcast_to((columns < span_x * peers_x - 1)[:, None, None], (span_x, span_y, half))
    north_ok = jnp.broadcast_to((rowset < span_y * peers_y - 1)[None, :, None], (span_x, span_y, half))
    keep_own = active.astype(jnp.float32) * jnp.concatenate([east_ok, north_ok], -1).astype(jnp.float32)
    scale_own = keep_own * scaling

    by_place = lambda v: jnp.transpose(v, (1, 2, 0, 3))
    lam = by_place(duals)
    p = keep_own[:, :, None] * by_place(direction)
    stacked = jnp.concatenate([by_place(residual), p, scale_own[:, :, None], keep_own[:, :, None]], 2)
    part_e, part_n = stacked[..., :half], stacked[..., half:]
    from_west = lax.ppermute(part_e[-1], "gx", [(i, i + 1) for i in range(peers_x - 1)])
    from_south = up_gy(part_n[:, -1], peers_y)
    west = jnp.concatenate([from_west[None], part_e[:-1]], 0)
    south = jnp.concatenate([from_south[:, None], part_n[:, :-1]], 1)
    stacked = jnp.concatenate([west, part_e, south, part_n], -1)
    r = stacked[:, :, :cases]
    p_all = stacked[:, :, cases : 2 * cases]
    scale = stacked[:, :, 2 * cases : 2 * cases + 1]
    keep = stacked[:, :, 2 * cases + 1 :]

    sign = jnp.concatenate([-jnp.ones(half), jnp.ones(half), -jnp.ones(half), jnp.ones(half)]).astype(jnp.float32)
    place = (edge_map[..., None] == jnp.arange(full, dtype=jnp.int32)).astype(jnp.float32) * sign
    schur = jnp.einsum("xyij,xyjf->xyif", dual_schur, place, precision=EXACT)
    schur = jnp.einsum("xyie,xyif->xyef", place, schur, precision=EXACT)
    couple = jnp.einsum("xycj,xyjf->xycf", coupling, place, precision=EXACT)

    flat = corner_slot.reshape(-1)
    count = flat.shape[0]
    order = jnp.arange(count)
    same = flat[:, None] == flat[None, :]
    first = ~jnp.any(same & (order[None, :] < order[:, None]), 1) & (flat != width_c)
    rank = jnp.sum((flat[None, :] < flat[:, None]) & first[None, :], 1)
    local_slot = jnp.arange(slots)
    compact = ((rank[:, None] == local_slot) & (flat != width_c)[:, None]).astype(jnp.float32)
    named = jnp.where(
        jnp.any(compact > 0, 0), jnp.max(compact * flat[:, None].astype(jnp.float32), 0), float(width_c)
    )
    compact = compact.reshape(span_x, span_y, corners, slots)
    gather_c = jnp.einsum("xycs,xycf->xysf", compact, couple, precision=EXACT)

    blocks = lambda a: (a[..., :half], a[..., half : 2 * half], a[..., 2 * half : 3 * half], a[..., 3 * half :])

    def jump(y, from_w, from_e, from_s, from_n):
        w, e, s, n = blocks(y)
        w_nb = jnp.concatenate([from_w[None], e[:-1]], 0)
        e_nb = jnp.concatenate([w[1:], from_e[None]], 0)
        s_nb = jnp.concatenate([from_s[:, None], n[:, :-1]], 1)
        n_nb = jnp.concatenate([s[:, 1:], from_n[:, None]], 1)
        return jnp.concatenate([w + w_nb, e + e_nb, s + s_nb, n + n_nb], -1)

    def rims(y):
        w, e, s, n = blocks(y)
        return w[0], e[-1], s[:, 0], n[:, -1]

    def exchange(y):
        w, e, s, n = rims(y)
        from_w, from_e = swap_gx(w, e, peers_x)
        from_s, from_n = swap_gy(s, n, peers_y)
        return from_w, from_e, from_s, from_n

    def put(rim, name):
        zero = jnp.zeros((span_x, span_y, rim.shape[-2], half), jnp.float32)
        parts = [zero, zero, zero, zero]
        if name == 0:
            parts[0] = zero.at[0].set(rim)
        elif name == 1:
            parts[1] = zero.at[-1].set(rim)
        elif name == 2:
            parts[2] = zero.at[:, 0].set(rim)
        else:
            parts[3] = zero.at[:, -1].set(rim)
        return jnp.concatenate(parts, -1)

    nb = exchange(gather_c)
    none = [jnp.zeros_like(v) for v in nb]
    spread = jnp.concatenate([jump(gather_c, *none)] + [put(v, i) for i, v in enumerate(nb)], 2)
    spread = spread * keep

    region_inv = coarse_inverse[0]

    def local_part(v):
        y = jnp.einsum("xykj,xyji->xyki", v, schur, precision=HIGH)
        c = jnp.einsum("xykj,xysj->ks", v, gather_c[:, :, :used], precision=HIGH)
        return y, c

    def over_cases(a, b):
        return jnp.sum(a * b, axis=(0, 1, 3))

    def pack(c, one, two):
        return jnp.concatenate([c, one[:, None], two[:, None]], 1).reshape(-1, 128)

    def unpack(got):
        got = got.reshape(peers, cases, slots)
        sums = jnp.sum(got[:, :, used:], 0)
        return jnp.transpose(got, (1, 0, 2)).reshape(cases, regions, peers_y, slots), sums[:, 0], sums[:, 1]

    def own_part(a):
        return jnp.concatenate([a[..., half : 2 * half], a[..., 3 * half :]], -1)

    u = scale * r
    both = jnp.concatenate([u, p_all], 2)
    y, c = local_part(both)
    yu, yp = y[:, :, :cases], y[:, :, cases:]
    rho_part = over_cases(own_part(r), own_part(u))
    names = jnp.concatenate([named, jnp.zeros(4 * 128 - slots, jnp.float32)]).reshape(4, 128)
    block = jnp.concatenate(
        [pack(c[:cases], rho_part, over_cases(u, yu)), pack(c[cases:], over_cases(p_all, yu), over_cases(p_all, yp)), names]
    )
    got = everywhere(block, axes)
    from_all = exchange(y)

    rows = cases * slots // 128
    slot_of = got[:, 2 * rows :].reshape(peers, -1)[:, :slots].reshape(regions, peers_y * slots)

    if whole:
        other = lax.ppermute(region_inv, "gx", [(0, 1), (1, 0)])
        inverses = jnp.where(here_x == 0, jnp.stack([region_inv, other]), jnp.stack([other, region_inv]))
    else:
        inverses = region_inv[None]
    pick = (slot_of[..., None] == jnp.arange(width_c, dtype=jnp.float32)).astype(jnp.float32)
    dense = jnp.einsum("ran,rnm->ram", pick, inverses, precision=EXACT)
    dense = jnp.einsum("ram,rbm->rab", dense, pick, precision=EXACT)

    def solve(c_all):
        flat_c = c_all.reshape(cases, regions, peers_y * slots)
        sol = jnp.einsum("kra,rab->krb", flat_c, dense, precision=HIGH)
        return flat_c, sol

    def total(a, b):
        return jnp.sum(a * b, (1, 2))

    def over_gx(*sums):
        return sums if whole else tuple(lax.psum(jnp.stack(sums), "gx"))

    def at(sol, ix, dy):
        sol = sol.reshape(cases, regions, peers_y, slots)
        iy = jnp.clip(here_y + dy, 0, peers_y - 1)
        return lax.dynamic_slice(sol, (0, ix, iy, 0), (cases, 1, 1, slots))[:, 0, 0]

    def beside(sol):
        if whole:
            return at(sol, 0, 0), at(sol, 1, 0)
        mine = at(sol, 0, 0)
        return swap_gx(mine, mine, peers_x)

    def coarse_part(sol):
        mine = here_x if whole else 0
        near = jnp.concatenate([at(sol, mine, 0), *beside(sol), at(sol, mine, -1), at(sol, mine, 1)], 1)
        return jnp.einsum("kn,xynj->xykj", near, spread, precision=HIGH)

    cu, rho, delta = unpack(got[:, :rows])
    cp, cross, eta = unpack(got[:, rows : 2 * rows])
    cu, su = solve(cu)
    cp, sp = solve(cp)
    delta, cross, eta = delta + total(cu, su), cross + total(cu, sp), eta + total(cp, sp)
    rho, delta, cross, eta = over_gx(rho, delta, cross, eta)
    f_both = keep * jump(y, *from_all)
    w = f_both[:, :, :cases] + coarse_part(su)
    s = f_both[:, :, cases:] + coarse_part(sp)

    wide = lambda a: a[None, None, :, None]
    beta = rho / prev_rho
    skew = cross + beta * eta
    pi = delta + 2.0 * beta * skew - beta * beta * eta
    for step in range(ITERS):
        if step > 0:
            u = scale * r
            y, c = local_part(u)
            block = pack(c, over_cases(own_part(r), own_part(u)), over_cases(u, y))
            got = everywhere(block, axes)
            from_all = exchange(y)
            rho_old = rho
            c_all, rho, delta = unpack(got)
            c_all, sol = solve(c_all)
            rho, delta = over_gx(rho, delta + total(c_all, sol))
            w = keep * jump(y, *from_all) + coarse_part(sol)
            skew = beta * skew
            beta = rho / rho_old
            pi = delta + 2.0 * beta * skew - beta * beta * pi
        alpha = rho / pi
        p = own_part(u) + wide(beta) * p
        s = w + wide(beta) * s
        lam = lam + wide(alpha) * p
        r = r - wide(alpha) * s
    back = lambda v: jnp.transpose(v, (2, 0, 1, 3))
    return back(lam), back(own_part(r)), back(p)


def solution(mesh):
    placed = (
        P(None, "gx", "gy", None),
        P(None, "gx", "gy", None),
        P(None, "gx", "gy", None),
        P(),
        P("gx", "gy", None, None),
        P("gx", "gy", None, None),
        P("gx", None, None),
        P("gx", "gy", None),
        P("gx", "gy", None),
        P("gx", "gy", None),
        P("gx", "gy", None),
    )
    return jax.shard_map(
        shards,
        mesh=mesh,
        in_specs=placed,
        out_specs=(P(None, "gx", "gy", None), P(None, "gx", "gy", None), P(None, "gx", "gy", None)),
        check_vma=False,
    )
```

```python
import jax
import jax.numpy as jnp
from jax import lax
from jax.experimental import pallas as pl
from jax.experimental.pallas import tpu as pltpu
from jax.sharding import PartitionSpec as P

ITERS = 6
HIGH = lax.Precision.HIGH
EXACT = lax.Precision.HIGHEST
BOTH = ("gx", "gy")


def pairs_from(first, peers):
    return [(i, i + 1) for i in range(first, peers - 1, 2)]


def both_ways(pairs):
    return pairs + [(b, a) for a, b in pairs]


def up_gy(value, peers):
    even = lax.ppermute(value, "gy", pairs_from(0, peers))
    odd = lax.ppermute(value, "gy", pairs_from(1, peers))
    return jnp.where(lax.axis_index("gy") % 2 == 1, even, odd)


def swap_gy(low, high, peers):
    is_even = lax.axis_index("gy") % 2 == 0
    first = lax.ppermute(jnp.where(is_even, high, low), "gy", both_ways(pairs_from(0, peers)))
    second = lax.ppermute(jnp.where(is_even, low, high), "gy", both_ways(pairs_from(1, peers)))
    return jnp.where(is_even, second, first), jnp.where(is_even, first, second)


def swap_gx(low, high, peers):
    if peers == 2:
        is_first = lax.axis_index("gx") == 0
        got = lax.ppermute(jnp.where(is_first, high, low), "gx", [(0, 1), (1, 0)])
        zero = jnp.zeros_like(got)
        return jnp.where(is_first, zero, got), jnp.where(is_first, got, zero)
    below = lax.ppermute(high, "gx", [(i, i + 1) for i in range(peers - 1)])
    above = lax.ppermute(low, "gx", [(i + 1, i) for i in range(peers - 1)])
    return below, above


def everywhere(block, axes):
    sent = jnp.broadcast_to(block[None], (lax.axis_size(axes),) + block.shape)
    return lax.all_to_all(sent, axes, 0, 0, tiled=False)


def general(
    duals, residual, direction, prev_rho, dual_schur, coupling, coarse_inverse, edge_map, corner_slot, active, scaling
):
    cases, span_x, span_y, owned = duals.shape
    half = owned // 2
    full = 2 * owned
    corners = coupling.shape[2]
    width_c = coarse_inverse.shape[-1]
    peers_x, peers_y = lax.axis_size("gx"), lax.axis_size("gy")
    whole = peers_x == 2
    axes = BOTH if whole else "gy"
    regions = peers_x if whole else 1
    peers = regions * peers_y
    here_x, here_y = lax.axis_index("gx"), lax.axis_index("gy")
    used = 2 * (span_x + 1) * (span_y + 1)
    slots = used + 2

    columns = here_x * span_x + jnp.arange(span_x)
    rowset = here_y * span_y + jnp.arange(span_y)
    east_ok = jnp.broadcast_to((columns < span_x * peers_x - 1)[:, None, None], (span_x, span_y, half))
    north_ok = jnp.broadcast_to((rowset < span_y * peers_y - 1)[None, :, None], (span_x, span_y, half))
    keep_own = active.astype(jnp.float32) * jnp.concatenate([east_ok, north_ok], -1).astype(jnp.float32)
    scale_own = keep_own * scaling

    by_place = lambda v: jnp.transpose(v, (1, 2, 0, 3))
    lam = by_place(duals)
    p = keep_own[:, :, None] * by_place(direction)
    stacked = jnp.concatenate([by_place(residual), p, scale_own[:, :, None], keep_own[:, :, None]], 2)
    part_e, part_n = stacked[..., :half], stacked[..., half:]
    from_west = lax.ppermute(part_e[-1], "gx", [(i, i + 1) for i in range(peers_x - 1)])
    from_south = up_gy(part_n[:, -1], peers_y)
    west = jnp.concatenate([from_west[None], part_e[:-1]], 0)
    south = jnp.concatenate([from_south[:, None], part_n[:, :-1]], 1)
    stacked = jnp.concatenate([west, part_e, south, part_n], -1)
    r = stacked[:, :, :cases]
    p_all = stacked[:, :, cases : 2 * cases]
    scale = stacked[:, :, 2 * cases : 2 * cases + 1]
    keep = stacked[:, :, 2 * cases + 1 :]

    sign = jnp.concatenate([-jnp.ones(half), jnp.ones(half), -jnp.ones(half), jnp.ones(half)]).astype(jnp.float32)
    place = (edge_map[..., None] == jnp.arange(full, dtype=jnp.int32)).astype(jnp.float32) * sign
    schur = jnp.einsum("xyij,xyjf->xyif", dual_schur, place, precision=EXACT)
    schur = jnp.einsum("xyie,xyif->xyef", place, schur, precision=EXACT)
    couple = jnp.einsum("xycj,xyjf->xycf", coupling, place, precision=EXACT)

    flat = corner_slot.reshape(-1)
    count = flat.shape[0]
    order = jnp.arange(count)
    same = flat[:, None] == flat[None, :]
    first = ~jnp.any(same & (order[None, :] < order[:, None]), 1) & (flat != width_c)
    rank = jnp.sum((flat[None, :] < flat[:, None]) & first[None, :], 1)
    local_slot = jnp.arange(slots)
    compact = ((rank[:, None] == local_slot) & (flat != width_c)[:, None]).astype(jnp.float32)
    named = jnp.where(
        jnp.any(compact > 0, 0), jnp.max(compact * flat[:, None].astype(jnp.float32), 0), float(width_c)
    )
    compact = compact.reshape(span_x, span_y, corners, slots)
    gather_c = jnp.einsum("xycs,xycf->xysf", compact, couple, precision=EXACT)

    blocks = lambda a: (a[..., :half], a[..., half : 2 * half], a[..., 2 * half : 3 * half], a[..., 3 * half :])

    def jump(y, from_w, from_e, from_s, from_n):
        w, e, s, n = blocks(y)
        w_nb = jnp.concatenate([from_w[None], e[:-1]], 0)
        e_nb = jnp.concatenate([w[1:], from_e[None]], 0)
        s_nb = jnp.concatenate([from_s[:, None], n[:, :-1]], 1)
        n_nb = jnp.concatenate([s[:, 1:], from_n[:, None]], 1)
        return jnp.concatenate([w + w_nb, e + e_nb, s + s_nb, n + n_nb], -1)

    def rims(y):
        w, e, s, n = blocks(y)
        return w[0], e[-1], s[:, 0], n[:, -1]

    def exchange(y):
        w, e, s, n = rims(y)
        from_w, from_e = swap_gx(w, e, peers_x)
        from_s, from_n = swap_gy(s, n, peers_y)
        return from_w, from_e, from_s, from_n

    def put(rim, name):
        zero = jnp.zeros((span_x, span_y, rim.shape[-2], half), jnp.float32)
        parts = [zero, zero, zero, zero]
        if name == 0:
            parts[0] = zero.at[0].set(rim)
        elif name == 1:
            parts[1] = zero.at[-1].set(rim)
        elif name == 2:
            parts[2] = zero.at[:, 0].set(rim)
        else:
            parts[3] = zero.at[:, -1].set(rim)
        return jnp.concatenate(parts, -1)

    nb = exchange(gather_c)
    none = [jnp.zeros_like(v) for v in nb]
    spread = jnp.concatenate([jump(gather_c, *none)] + [put(v, i) for i, v in enumerate(nb)], 2)
    spread = spread * keep

    region_inv = coarse_inverse[0]

    def local_part(v):
        y = jnp.einsum("xykj,xyji->xyki", v, schur, precision=HIGH)
        c = jnp.einsum("xykj,xysj->ks", v, gather_c[:, :, :used], precision=HIGH)
        return y, c

    def over_cases(a, b):
        return jnp.sum(a * b, axis=(0, 1, 3))

    def pack(c, one, two):
        return jnp.concatenate([c, one[:, None], two[:, None]], 1).reshape(-1, 128)

    def unpack(got):
        got = got.reshape(peers, cases, slots)
        sums = jnp.sum(got[:, :, used:], 0)
        return jnp.transpose(got, (1, 0, 2)).reshape(cases, regions, peers_y, slots), sums[:, 0], sums[:, 1]

    def own_part(a):
        return jnp.concatenate([a[..., half : 2 * half], a[..., 3 * half :]], -1)

    u = scale * r
    both = jnp.concatenate([u, p_all], 2)
    y, c = local_part(both)
    yu, yp = y[:, :, :cases], y[:, :, cases:]
    rho_part = over_cases(own_part(r), own_part(u))
    names = jnp.concatenate([named, jnp.zeros(4 * 128 - slots, jnp.float32)]).reshape(4, 128)
    block = jnp.concatenate(
        [pack(c[:cases], rho_part, over_cases(u, yu)), pack(c[cases:], over_cases(p_all, yu), over_cases(p_all, yp)), names]
    )
    got = everywhere(block, axes)
    from_all = exchange(y)

    rows = cases * slots // 128
    slot_of = got[:, 2 * rows :].reshape(peers, -1)[:, :slots].reshape(regions, peers_y * slots)

    if whole:
        other = lax.ppermute(region_inv, "gx", [(0, 1), (1, 0)])
        inverses = jnp.where(here_x == 0, jnp.stack([region_inv, other]), jnp.stack([other, region_inv]))
    else:
        inverses = region_inv[None]
    pick = (slot_of[..., None] == jnp.arange(width_c, dtype=jnp.float32)).astype(jnp.float32)
    dense = jnp.einsum("ran,rnm->ram", pick, inverses, precision=EXACT)
    dense = jnp.einsum("ram,rbm->rab", dense, pick, precision=EXACT)

    def solve(c_all):
        flat_c = c_all.reshape(cases, regions, peers_y * slots)
        sol = jnp.einsum("kra,rab->krb", flat_c, dense, precision=HIGH)
        return flat_c, sol

    def total(a, b):
        return jnp.sum(a * b, (1, 2))

    def over_gx(*sums):
        return sums if whole else tuple(lax.psum(jnp.stack(sums), "gx"))

    def at(sol, ix, dy):
        sol = sol.reshape(cases, regions, peers_y, slots)
        iy = jnp.clip(here_y + dy, 0, peers_y - 1)
        return lax.dynamic_slice(sol, (0, ix, iy, 0), (cases, 1, 1, slots))[:, 0, 0]

    def beside(sol):
        if whole:
            return at(sol, 0, 0), at(sol, 1, 0)
        mine = at(sol, 0, 0)
        return swap_gx(mine, mine, peers_x)

    def coarse_part(sol):
        mine = here_x if whole else 0
        near = jnp.concatenate([at(sol, mine, 0), *beside(sol), at(sol, mine, -1), at(sol, mine, 1)], 1)
        return jnp.einsum("kn,xynj->xykj", near, spread, precision=HIGH)

    cu, rho, delta = unpack(got[:, :rows])
    cp, cross, eta = unpack(got[:, rows : 2 * rows])
    cu, su = solve(cu)
    cp, sp = solve(cp)
    delta, cross, eta = delta + total(cu, su), cross + total(cu, sp), eta + total(cp, sp)
    rho, delta, cross, eta = over_gx(rho, delta, cross, eta)
    f_both = keep * jump(y, *from_all)
    w = f_both[:, :, :cases] + coarse_part(su)
    s = f_both[:, :, cases:] + coarse_part(sp)

    wide = lambda a: a[None, None, :, None]
    beta = rho / prev_rho
    skew = cross + beta * eta
    pi = delta + 2.0 * beta * skew - beta * beta * eta
    for step in range(ITERS):
        if step > 0:
            u = scale * r
            y, c = local_part(u)
            block = pack(c, over_cases(own_part(r), own_part(u)), over_cases(u, y))
            got = everywhere(block, axes)
            from_all = exchange(y)
            rho_old = rho
            c_all, rho, delta = unpack(got)
            c_all, sol = solve(c_all)
            rho, delta = over_gx(rho, delta + total(c_all, sol))
            w = keep * jump(y, *from_all) + coarse_part(sol)
            skew = beta * skew
            beta = rho / rho_old
            pi = delta + 2.0 * beta * skew - beta * beta * pi
        alpha = rho / pi
        p = own_part(u) + wide(beta) * p
        s = w + wide(beta) * s
        lam = lam + wide(alpha) * p
        r = r - wide(alpha) * s
    back = lambda v: jnp.transpose(v, (2, 0, 1, 3))
    return back(lam), back(own_part(r)), back(p)


F32, BF16 = jnp.float32, jnp.bfloat16
SPAN_X, SPAN_Y = 2, 4
SUBS = SPAN_X * SPAN_Y
CASES = 16
SLOTS = 32
USED = 2 * (SPAN_X + 1) * (SPAN_Y + 1)
CAST = 40
LIMIT = 16 * 1024 * 1024


def iota(shape, dim):
    return lax.broadcasted_iota(jnp.int32, shape, dim)


def split(v):
    high = v.astype(BF16)
    return high, (v - high.astype(F32)).astype(BF16)


def dot(a, b):
    return jnp.dot(a, b, preferred_element_type=F32)


def dot_split(v, high, low):
    n = v.shape[0]
    vh, vl = split(v)
    wide = dot(jnp.concatenate([vh, vl], 0), high)
    return wide[:n] + wide[n:] + dot(vh, low)


def dot_exact(v, ones):
    n = v.shape[0]
    vh, vl = split(v)
    wide = dot(jnp.concatenate([vh, vl], 0), ones)
    return wide[:n] + wide[n:]


def odd(i):
    return (i // SPAN_Y + i % SPAN_Y) % 2


def lower(rows):
    return iota((rows, 128), 1) < 64


def packs(ys):
    rows = ys[0].shape[0]
    low = lower(rows)
    column = lambda x: [
        jnp.where(low, ys[x * SPAN_Y + t][:, :128], ys[x * SPAN_Y + t + 1][:, :128]) for t in range(0, SPAN_Y, 2)
    ]
    row = lambda y: jnp.where(low, ys[y][:, 128:], ys[SPAN_Y + y][:, 128:])
    return column(0), column(SPAN_X - 1), row(0), row(SPAN_Y - 1)


def send(ys, x_ref, a_ref, b_ref, at):
    rows = pl.ds(at, ys[0].shape[0])
    west, east, south, north = packs(ys)
    first = lax.axis_index("gx") == 0
    even = lax.axis_index("gy") % 2 == 0
    for t in range(SPAN_Y // 2):
        x_ref[t, rows, :] = jnp.where(first, east[t], west[t])
    a_ref[rows, :] = jnp.where(even, north, south)
    b_ref[rows, :] = jnp.where(even, south, north)


def received(x_ref, a_ref, b_ref, at, n):
    rows = pl.ds(at, n)
    first = lax.axis_index("gx") == 0
    even = lax.axis_index("gy") % 2 == 0
    xs = [x_ref[t, rows, :] for t in range(SPAN_Y // 2)]
    a, b = a_ref[rows, :], b_ref[rows, :]
    zero = jnp.zeros_like(a)
    return (
        [jnp.where(first, zero, v) for v in xs],
        [jnp.where(first, v, zero) for v in xs],
        jnp.where(even, b, a),
        jnp.where(even, a, b),
    )


def across(ys, nb, rows):
    low = lower(rows)
    zero = jnp.zeros((rows, 128), F32)
    inside = lambda x, y, part: zero if ys is None else ys[x * SPAN_Y + y][:, part * 128 : part * 128 + 128]
    out = []
    for x in range(SPAN_X):
        for y in range(SPAN_Y):
            beyond = lambda v: zero if nb is None else v()
            west = inside(x - 1, y, 0) if x else beyond(lambda: nb[0][y // 2])
            east = inside(x + 1, y, 0) if x < SPAN_X - 1 else beyond(lambda: nb[1][y // 2])
            south = inside(x, y - 1, 1) if y else beyond(lambda: nb[2])
            north = inside(x, y + 1, 1) if y < SPAN_Y - 1 else beyond(lambda: nb[3])
            if (x + y) % 2:
                west, east, south, north = east, west, north, south
            out.append(jnp.concatenate([jnp.where(low, west, east), jnp.where(low, south, north)], 1))
    return out


def owned_lanes(i, rows):
    lane = iota((rows, 256), 1) % 128
    return lane < 64 if odd(i) else lane >= 64


def spread_owned(v, i):
    zero = jnp.zeros_like(v)
    low = lower(v.shape[0])
    turned = pltpu.roll(v, 64, 1)
    if odd(i):
        return jnp.concatenate([jnp.where(low, v, zero), jnp.where(low, turned, zero)], 1)
    return jnp.concatenate([jnp.where(low, zero, turned), jnp.where(low, zero, v)], 1)


def take_owned(v, i):
    low = lower(v.shape[0])
    if odd(i):
        return jnp.where(low, v[:, :128], pltpu.roll(v[:, 128:], 64, 1))
    return jnp.where(low, pltpu.roll(v[:, :128], 64, 1), v[:, 128:])


def start_kernel(res_ref, dir_ref, act_ref, scale_ref, own_ref, x_ref, a_ref, b_ref):
    gx, gy = lax.axis_index("gx"), lax.axis_index("gy")
    last_x = gx * SPAN_X + SPAN_X - 1 == lax.axis_size("gx") * SPAN_X - 1
    last_y = gy * SPAN_Y + SPAN_Y - 1 == lax.axis_size("gy") * SPAN_Y - 1
    east = iota((1, 128), 1) < 64
    ys = []
    for i in range(SUBS):
        x, y = i // SPAN_Y, i % SPAN_Y
        keep = act_ref[i : i + 1, :].astype(F32)
        if x == SPAN_X - 1:
            keep = jnp.where(jnp.logical_and(last_x, east), 0.0, keep)
        if y == SPAN_Y - 1:
            keep = jnp.where(jnp.logical_and(last_y, jnp.logical_not(east)), 0.0, keep)
        mine = pl.ds(i, CASES, stride=SUBS)
        v = jnp.concatenate(
            [
                res_ref[mine, :],
                dir_ref[mine, :] * keep,
                scale_ref[i : i + 1, :] * keep,
                keep,
                jnp.zeros((CAST - 2 * CASES - 2, 128), F32),
            ],
            0,
        )
        v = spread_owned(v, i)
        own_ref[i] = v
        ys.append(v)
    send(ys, x_ref, a_ref, b_ref, 0)


def operator_kernel(schur_ref, couple_ref, map_ref, slot_ref, high_ref, low_ref, cc_ref, wh_ref, wl_ref, name_ref):
    none = 384
    slot = slot_ref[...].astype(F32)
    eye = iota((8, 8), 0) == iota((8, 8), 1)
    column = jnp.concatenate(
        [jnp.sum(jnp.where(eye, jnp.broadcast_to(slot[i : i + 1, :], (8, 8)), 0.0), 1, keepdims=True) for i in range(SUBS)], 0
    )
    row = jnp.concatenate([slot[i : i + 1, :] for i in range(SUBS)], 1)
    count = SUBS * 8
    earlier = iota((count, count), 1) < iota((count, count), 0)
    again = jnp.sum(jnp.where(jnp.logical_and(column == row, earlier), 1.0, 0.0), 1, keepdims=True)
    first = jnp.where(jnp.logical_and(again == 0.0, column != float(none)), 1.0, 0.0)
    first_row = jnp.sum(
        jnp.where(jnp.logical_and(column == row, iota((count, count), 0) < iota((count, count), 1)), 1.0, 0.0), 0, keepdims=True
    )
    first_row = jnp.where(jnp.logical_and(first_row == 0.0, row != float(none)), 1.0, 0.0)
    rank = jnp.sum(jnp.where(row < column, first_row, 0.0), 1, keepdims=True)
    hit = jnp.where(rank == iota((count, 128), 1).astype(F32), first, 0.0)
    name_ref[...] = jnp.broadcast_to(
        jnp.where(jnp.sum(hit, 0, keepdims=True) > 0.0, jnp.sum(hit * column, 0, keepdims=True), float(none)), (8, 128)
    )
    sub = iota((256, 256), 0)
    west = (sub // 64) % 2 == 0
    all_cc = []
    for i in range(SUBS):
        spots = map_ref[i : i + 1, :]
        if odd(i):
            spots = jnp.where((spots // 64) % 2 == 0, spots + 64, spots - 64)
        sign = jnp.where(west, 1.0, -1.0) if odd(i) else jnp.where(west, -1.0, 1.0)
        place = jnp.where(sub == spots, sign, 0.0).astype(BF16)
        mine = slot[i : i + 1, :]
        number = jnp.sum(jnp.where(column < mine, first, 0.0), 0, keepdims=True)
        compact = jnp.where(
            jnp.logical_and(number == iota((SLOTS, 8), 0).astype(F32), mine != float(none)), 1.0, 0.0
        )
        cc = jnp.dot(compact, couple_ref[i], precision=EXACT, preferred_element_type=F32)
        c1, rest = split(cc)
        c2, c3 = split(cc - c1.astype(F32))
        s1, s2 = split(schur_ref[i])
        tall = lax.dot_general(
            jnp.concatenate([s1, s2, c1, c2, c3], 0), place, (((1,), (1,)), ((), ())), preferred_element_type=F32
        )
        high_ref[i] = dot(place, tall[:256].astype(BF16)).astype(BF16)
        low_ref[i] = dot(place, tall[256:512].astype(BF16)).astype(BF16)
        cc = tall[512 : 512 + SLOTS] + tall[512 + SLOTS : 512 + 2 * SLOTS] + tall[512 + 2 * SLOTS :]
        cc_ref[i] = cc
        all_cc.append(cc)
    wh_ref[...], wl_ref[...] = split(jnp.transpose(jnp.concatenate(all_cc, 0)))


def inverse_kernel(mine_ref, other_ref, high_ref, low_ref):
    first = lax.axis_index("gx") == 0
    mine, other = mine_ref[...], other_ref[...]
    high_ref[0], low_ref[0] = split(jnp.where(first, mine, other))
    high_ref[1], low_ref[1] = split(jnp.where(first, other, mine))


def spread_kernel(cc_ref, name_ref, mk_ref, x_ref, a_ref, b_ref, high_ref, low_ref, near_ref):
    at = 2 * CASES
    cc = [cc_ref[i] for i in range(SUBS)]
    inside = across(cc, None, SLOTS)
    nb = received(x_ref, a_ref, b_ref, at, SLOTS)
    blank = jnp.zeros((SLOTS, 128), F32)
    blanks = [blank] * (SPAN_Y // 2)
    even = lax.axis_index("gy") % 2 == 0
    by_x = across(None, (nb[0], nb[1], blank, blank), SLOTS)
    a_low, a_high = jnp.where(even, 0.0, 1.0), jnp.where(even, 1.0, 0.0)
    by_a = across(None, (blanks, blanks, nb[2] * a_low, nb[3] * a_high), SLOTS)
    by_b = across(None, (blanks, blanks, nb[2] * a_high, nb[3] * a_low), SLOTS)
    for i in range(SUBS):
        keep = mk_ref[i, 1:2, :]
        whole = jnp.concatenate([cc[i] + inside[i], by_a[i], by_b[i], by_x[i]], 0) * keep
        high_ref[i], low_ref[i] = split(whole)
    named = pl.ds(at + SLOTS, 1)
    group = iota((1, 128), 1) // SLOTS
    turn = lambda v, g: pltpu.roll(jnp.broadcast_to(v, (8, 128)), g * SLOTS, 1)[0:1]
    names = [turn(name_ref[0:1, :], 0), turn(a_ref[named, :], 1), turn(b_ref[named, :], 2), turn(x_ref[0, named, :], 3)]
    wanted = jnp.where(group == 0, names[0], jnp.where(group == 1, names[1], jnp.where(group == 2, names[2], names[3])))
    found = iota((384, 128), 0).astype(F32) == wanted
    mine = jnp.where(iota((384, 128), 1) < 3 * SLOTS, 1.0, 0.0)
    gx = lax.axis_index("gx")
    for region in range(2):
        near_ref[region] = jnp.where(found, jnp.where(gx == region, mine, 1.0 - mine), 0.0).astype(BF16)


def local_part(us, rs, high_ref, low_ref, wh_ref, wl_ref):
    ys = [dot_split(us[i], high_ref[i], low_ref[i]) for i in range(SUBS)]
    n = us[0].shape[0]
    corner = dot_split(jnp.concatenate(us, 0), wh_ref[...], wl_ref[...])
    group = iota((n, 128), 1) // SLOTS
    total = jnp.zeros((n, 128), F32)
    for i in range(SUBS):
        part = corner[n * i : n * i + n, 128 * (i // 4) : 128 * (i // 4) + 128]
        total = total + jnp.where(group == i % 4, part, 0.0)
    total = total + pltpu.roll(total, 64, 1)
    total = total + pltpu.roll(total, 32, 1)
    return ys, total


def over_lanes(terms):
    total = terms[0]
    for t in terms[1:]:
        total = total + t
    return jnp.sum(total[:, :128] + total[:, 128:], 1, keepdims=True)


def packed(corner, one, two):
    slot = iota((CASES, 128), 1) % SLOTS
    full = jnp.where(slot == USED, one, jnp.where(slot == USED + 1, two, corner))
    group = iota((4, 128), 1) // SLOTS
    out = jnp.zeros((4, 128), F32)
    for b in range(4):
        out = jnp.where(group == b, full[4 * b : 4 * b + 4], out)
    return out


def by_slot(vs):
    group = iota((8, 128), 1) // SLOTS
    out = []
    for region in range(2):
        rows = []
        for b in range(4):
            halves = []
            for h in range(2):
                acc = None
                for q in range(4):
                    v = vs[8 * region + 4 * h + q]
                    turned = v if q == b else pltpu.roll(v, (SLOTS * (q - b)) % 128, 1)
                    acc = turned if acc is None else jnp.where(group == q, turned, acc)
                halves.append(acc)
            rows.append(jnp.concatenate(halves, 1))
        out.append(jnp.concatenate(rows, 0))
    return out


def inner(vs):
    total = vs[0]
    for v in vs[1:]:
        total = total + v
    total = total[:4] + total[4:]
    tall = jnp.concatenate([total] * 4, 0)
    lane, row = iota((CASES, 128), 1), iota((CASES, 128), 0)
    column = lambda s: jnp.sum(jnp.where(lane == SLOTS * (row // 4) + s, tall, 0.0), 1, keepdims=True)
    return column(USED), column(USED + 1)


def first_of_pairs(v):
    return jnp.concatenate([v[8 * b : 8 * b + 4] for b in range(v.shape[0] // 8)], 0)


def solve(spots, pick_ref, gh_ref, gl_ref, near_ref):
    totals, sols, near = [], [], None
    for region in range(2):
        v = spots[region]
        n = v.shape[0]
        even = dot_exact(v, pick_ref[region, 0])
        odds = dot_exact(v, pick_ref[region, 1])
        z = jnp.where((iota((n, 384), 0) // 4) % 2 == 0, even, odds).reshape(n // 8, 8, 384)
        total = (z + pltpu.roll(z, 4, 1)).reshape(n, 384)
        sol = dot_split(total, gh_ref[region], gl_ref[region])
        part = dot_exact(sol, near_ref[region])
        near = part if near is None else near + part
        totals.append(total)
        sols.append(sol)
    return totals, sols, near


def energy(totals, sols):
    both = totals[0] * sols[0] + totals[1] * sols[1]
    return first_of_pairs(jnp.sum(both, 1, keepdims=True))


def emit(rs, mk_ref, high_ref, low_ref, wh_ref, wl_ref, block_ref, y_ref, x_ref, a_ref, b_ref):
    us = [mk_ref[i, 0:1, :] * rs[i] for i in range(SUBS)]
    ys, corner = local_part(us, rs, high_ref, low_ref, wh_ref, wl_ref)
    send(ys, x_ref, a_ref, b_ref, 0)
    rho = over_lanes([jnp.where(owned_lanes(i, CASES), rs[i] * us[i], 0.0) for i in range(SUBS)])
    delta = over_lanes([us[i] * ys[i] for i in range(SUBS)])
    block = packed(corner, rho, delta)
    twice = jnp.concatenate([block, block], 0)
    for j in range(16):
        block_ref[j] = twice
    for i in range(SUBS):
        y_ref[i] = ys[i]


def first_kernel(
    own_ref, x_ref, a_ref, b_ref, high_ref, low_ref, cc_ref, wh_ref, wl_ref, name_ref,
    r_ref, p_ref, mk_ref, y_ref, block_ref, sx_ref, sa_ref, sb_ref,
):
    own = [own_ref[i] for i in range(SUBS)]
    other = across(own, received(x_ref, a_ref, b_ref, 0, CAST), CAST)
    rs, vs = [], []
    for i in range(SUBS):
        full = own[i] + other[i]
        rs.append(full[:CASES])
        r_ref[i] = full[:CASES]
        p_ref[i] = full[CASES : 2 * CASES]
        mk_ref[i] = full[2 * CASES : 2 * CASES + 8]
        vs.append(jnp.concatenate([full[2 * CASES : 2 * CASES + 1] * full[:CASES], full[CASES : 2 * CASES]], 0))
    ys, corner = local_part(vs, rs, high_ref, low_ref, wh_ref, wl_ref)
    names = name_ref[...]
    send([jnp.concatenate([ys[i], cc_ref[i]], 0) for i in range(SUBS)], sx_ref, sa_ref, sb_ref, 0)
    at = pl.ds(2 * CASES + SLOTS, 8)
    for t in range(SPAN_Y // 2):
        sx_ref[t, at, :] = names
    sa_ref[at, :] = names
    sb_ref[at, :] = names
    us = [v[:CASES] for v in vs]
    ps = [v[CASES:] for v in vs]
    rho = over_lanes([jnp.where(owned_lanes(i, CASES), rs[i] * us[i], 0.0) for i in range(SUBS)])
    delta = over_lanes([us[i] * ys[i][:CASES] for i in range(SUBS)])
    cross = over_lanes([ps[i] * ys[i][:CASES] for i in range(SUBS)])
    eta = over_lanes([ps[i] * ys[i][CASES:] for i in range(SUBS)])
    one, two = packed(corner[:CASES], rho, delta), packed(corner[CASES:], cross, eta)
    blocks = [
        jnp.concatenate([one, two], 0),
        jnp.concatenate([names[:4], one], 0),
        jnp.concatenate([two, names[:4]], 0),
    ]
    for j in range(16):
        for t in range(3):
            block_ref[3 * j + t] = blocks[t]
    for i in range(SUBS):
        y_ref[i] = ys[i]


def column_of(row):
    eye = iota((CASES, CASES), 0) == iota((CASES, CASES), 1)
    return jnp.sum(jnp.where(eye, jnp.broadcast_to(row, (CASES, CASES)), 0.0), 1, keepdims=True)


def keep_scalars(scal_ref, values):
    for t, v in enumerate(values):
        scal_ref[t] = jnp.broadcast_to(v, (CASES, 128))


def second_kernel(
    got_ref, x_ref, a_ref, b_ref, y_ref, r_ref, p_ref, mk_ref, dual_ref, rho_ref, gh_ref, gl_ref, near_ref, dh_ref, dl_ref,
    high_ref, low_ref, wh_ref, wl_ref,
    pick_ref, ro_ref, so_ref, po_ref, lo_ref, scal_ref, block_ref, yo_ref, sx_ref, sa_ref, sb_ref,
):
    top = iota((8, 128), 0) < 4
    us, ps, names = [], [], []
    for j in range(16):
        v = [got_ref[3 * j + t] for t in range(3)]
        us.append(jnp.where(top, v[0], v[1]))
        ps.append(pltpu.roll(jnp.where(top, v[2], v[0]), 4, 0))
        names.append((v[1], pltpu.roll(v[2], 4, 0)))
    group = iota((8, 128), 1) // SLOTS
    for region in range(2):
        for par in range(2):
            halves = []
            for h in range(2):
                acc = None
                for q in range(4):
                    v = names[8 * region + 4 * h + q][par]
                    turned = pltpu.roll(v, SLOTS * q, 1) if q else v
                    acc = turned if acc is None else jnp.where(group == q, turned, acc)
                halves.append(acc[0:1])
            wanted = jnp.concatenate(halves, 1)
            hit = jnp.where(iota((384, 256), 0).astype(F32) == wanted, 1.0, 0.0)
            pick_ref[region, par] = jnp.transpose(hit).astype(BF16)
    lhs_u, lhs_p = by_slot(us), by_slot(ps)
    n = lhs_u[0].shape[0]
    totals, sols, near = solve(
        [jnp.concatenate([lhs_u[t], lhs_p[t]], 0) for t in range(2)], pick_ref, gh_ref, gl_ref, near_ref
    )
    of_u, of_p = lambda vs: [v[:n] for v in vs], lambda vs: [v[n:] for v in vs]
    rho, delta = inner(us)
    cross, eta = inner(ps)
    delta = delta + energy(of_u(totals), of_u(sols))
    cross = cross + energy(of_p(totals), of_u(sols))
    eta = eta + energy(of_p(totals), of_p(sols))
    near = first_of_pairs(near)
    beta = rho / column_of(rho_ref[...])
    skew = cross + beta * eta
    pi = delta + 2.0 * beta * skew - beta * beta * eta
    alpha = rho / pi
    ys = [y_ref[i] for i in range(SUBS)]
    other = across(ys, received(x_ref, a_ref, b_ref, 0, 2 * CASES), 2 * CASES)
    rs = []
    for i in range(SUBS):
        f = mk_ref[i, 1:2, :] * (ys[i] + other[i]) + dot_split(near, dh_ref[i], dl_ref[i])
        r = r_ref[i]
        p = mk_ref[i, 0:1, :] * r + beta * p_ref[i]
        s = f[:CASES] + beta * f[CASES:]
        r = r - alpha * s
        rs.append(r)
        ro_ref[i], so_ref[i], po_ref[i] = r, s, p
        lo_ref[i] = spread_owned(dual_ref[pl.ds(i, CASES, stride=SUBS), :], i) + alpha * p
    keep_scalars(scal_ref, (rho, pi, beta, skew))
    emit(rs, mk_ref, high_ref, low_ref, wh_ref, wl_ref, block_ref, yo_ref, sx_ref, sa_ref, sb_ref)


def absorb(got_ref, x_ref, a_ref, b_ref, y_ref, r_ref, s_ref, p_ref, l_ref, scal_ref, mk_ref, pick_ref, gh_ref, gl_ref, near_ref, dh_ref, dl_ref):
    vs = [got_ref[j] for j in range(16)]
    totals, sols, near = solve(by_slot(vs), pick_ref, gh_ref, gl_ref, near_ref)
    rho, delta = inner(vs)
    delta = delta + energy(totals, sols)
    near = first_of_pairs(near)
    rho_old, pi, beta, skew = (scal_ref[t][:, 0:1] for t in range(4))
    skew = beta * skew
    beta = rho / rho_old
    pi = delta + 2.0 * beta * skew - beta * beta * pi
    alpha = rho / pi
    ys = [y_ref[i] for i in range(SUBS)]
    other = across(ys, received(x_ref, a_ref, b_ref, 0, CASES), CASES)
    out = []
    for i in range(SUBS):
        f = mk_ref[i, 1:2, :] * (ys[i] + other[i]) + dot_split(near, dh_ref[i], dl_ref[i])
        r = r_ref[i]
        p = mk_ref[i, 0:1, :] * r + beta * p_ref[i]
        s = f + beta * s_ref[i]
        out.append((r - alpha * s, s, p, l_ref[i] + alpha * p))
    return out, (rho, pi, beta, skew)


def round_kernel(
    got_ref, x_ref, a_ref, b_ref, y_ref, r_ref, s_ref, p_ref, l_ref, scal_ref, mk_ref, pick_ref, gh_ref, gl_ref, near_ref,
    dh_ref, dl_ref, high_ref, low_ref, wh_ref, wl_ref,
    ro_ref, so_ref, po_ref, lo_ref, scalo_ref, block_ref, yo_ref, sx_ref, sa_ref, sb_ref,
):
    out, scalars = absorb(
        got_ref, x_ref, a_ref, b_ref, y_ref, r_ref, s_ref, p_ref, l_ref, scal_ref, mk_ref, pick_ref, gh_ref, gl_ref, near_ref,
        dh_ref, dl_ref,
    )
    for i, (r, s, p, lam) in enumerate(out):
        ro_ref[i], so_ref[i], po_ref[i], lo_ref[i] = r, s, p, lam
    keep_scalars(scalo_ref, scalars)
    emit([v[0] for v in out], mk_ref, high_ref, low_ref, wh_ref, wl_ref, block_ref, yo_ref, sx_ref, sa_ref, sb_ref)


def last_kernel(
    got_ref, x_ref, a_ref, b_ref, y_ref, r_ref, s_ref, p_ref, l_ref, scal_ref, mk_ref, pick_ref, gh_ref, gl_ref, near_ref,
    dh_ref, dl_ref, lo_ref, ro_ref, po_ref,
):
    out, _ = absorb(
        got_ref, x_ref, a_ref, b_ref, y_ref, r_ref, s_ref, p_ref, l_ref, scal_ref, mk_ref, pick_ref, gh_ref, gl_ref, near_ref,
        dh_ref, dl_ref,
    )
    for i, (r, _, p, lam) in enumerate(out):
        mine = pl.ds(i, CASES, stride=SUBS)
        lo_ref[mine, :] = take_owned(lam, i)
        ro_ref[mine, :] = take_owned(r, i)
        po_ref[mine, :] = take_owned(p, i)


def call(kernel, args, outs):
    vmem = pl.BlockSpec(memory_space=pltpu.VMEM)
    return pl.pallas_call(
        kernel,
        out_shape=[jax.ShapeDtypeStruct(shape, kind) for shape, kind in outs],
        in_specs=[vmem] * len(args),
        out_specs=[vmem] * len(outs),
        compiler_params=pltpu.CompilerParams(vmem_limit_bytes=LIMIT),
    )(*args)


def trade(x, a, b):
    peers = lax.axis_size("gy")
    return (
        lax.ppermute(x, "gx", [(0, 1), (1, 0)]),
        lax.ppermute(a, "gy", both_ways(pairs_from(0, peers))),
        lax.ppermute(b, "gy", both_ways(pairs_from(1, peers))),
    )


def two_regions(
    duals, residual, direction, prev_rho, dual_schur, coupling, coarse_inverse, edge_map, corner_slot, active, scaling
):
    native = lambda v: v.reshape(CASES * SUBS, 128)
    by_sub = lambda v: v.reshape((SUBS,) + v.shape[2:])
    width = coarse_inverse.shape[-1]
    sends = lambda rows: [((SPAN_Y // 2, rows, 128), F32), ((rows, 128), F32), ((rows, 128), F32)]
    state = ((SUBS, CASES, 256), F32)

    other = lax.ppermute(coarse_inverse[0], "gx", [(0, 1), (1, 0)])
    own, *out = call(
        start_kernel,
        [native(residual), native(direction), by_sub(active), by_sub(scaling)],
        [((SUBS, CAST, 256), F32)] + sends(CAST),
    )
    come = trade(*out)
    matrix = ((SUBS, 256, 256), BF16)
    high, low, cc, wh, wl, names = call(
        operator_kernel,
        [by_sub(dual_schur), by_sub(coupling), by_sub(edge_map), by_sub(corner_slot)],
        [matrix, matrix, ((SUBS, SLOTS, 256), F32), ((256, 256), BF16), ((256, 256), BF16), ((8, 128), F32)],
    )
    square = ((2, width, width), BF16)
    gh, gl = call(inverse_kernel, [coarse_inverse[0], other], [square, square])
    rows = 2 * CASES + SLOTS + 8
    r, p, mk, y, block, *out = call(
        first_kernel,
        [own, *come, high, low, cc, wh, wl, names],
        [state, state, ((SUBS, 8, 256), F32), ((SUBS, 2 * CASES, 256), F32), ((48, 8, 128), F32)] + sends(rows),
    )
    got = lax.all_to_all(block.reshape(32, 12, 128), BOTH, 0, 0, tiled=False).reshape(48, 8, 128)
    come = trade(*out)
    wide = ((SUBS, 128, 256), BF16)
    dh, dl, near = call(spread_kernel, [cc, names, mk, *come], [wide, wide, ((2, width, 128), BF16)])
    weights = [high, low, wh, wl]
    onward = [state, state, state, state, ((4, CASES, 128), F32), ((16, 8, 128), F32), state] + sends(CASES)
    pick, r, s, p, lam, scal, block, y, *out = call(
        second_kernel,
        [got, *come, y, r, p, mk, native(duals), prev_rho.reshape(1, CASES), gh, gl, near, dh, dl, *weights],
        [((2, 2, 256, width), BF16)] + onward,
    )
    for step in range(1, ITERS):
        got = lax.all_to_all(block.reshape(32, 4, 128), BOTH, 0, 0, tiled=False).reshape(16, 8, 128)
        come = trade(*out)
        args = [got, *come, y, r, s, p, lam, scal, mk, pick, gh, gl, near, dh, dl]
        if step < ITERS - 1:
            r, s, p, lam, scal, block, y, *out = call(round_kernel, args + weights, onward)
        else:
            plain = ((CASES * SUBS, 128), F32)
            results = call(last_kernel, args, [plain, plain, plain])
    return tuple(v.reshape(duals.shape) for v in results)


def shards(*args):
    cases, span_x, span_y, owned = args[0].shape
    fits = (cases, span_x, span_y, owned, args[6].shape[-1]) == (CASES, SPAN_X, SPAN_Y, 128, 384)
    if fits and lax.axis_size("gx") == 2 and lax.axis_size("gy") == 16:
        return two_regions(*args)
    return general(*args)


def solution(mesh):
    placed = (
        P(None, "gx", "gy", None),
        P(None, "gx", "gy", None),
        P(None, "gx", "gy", None),
        P(),
        P("gx", "gy", None, None),
        P("gx", "gy", None, None),
        P("gx", None, None),
        P("gx", "gy", None),
        P("gx", "gy", None),
        P("gx", "gy", None),
        P("gx", "gy", None),
    )
    return jax.shard_map(
        shards,
        mesh=mesh,
        in_specs=placed,
        out_specs=(P(None, "gx", "gy", None), P(None, "gx", "gy", None), P(None, "gx", "gy", None)),
        check_vma=False,
    )
```

```python
import jax
import jax.numpy as jnp
from jax import lax
from jax.experimental import pallas as pl
from jax.experimental.pallas import tpu as pltpu
from jax.sharding import PartitionSpec as P

ITERS = 6
HIGH = lax.Precision.HIGH
EXACT = lax.Precision.HIGHEST
BOTH = ("gx", "gy")


def pairs_from(first, peers):
    return [(i, i + 1) for i in range(first, peers - 1, 2)]


def both_ways(pairs):
    return pairs + [(b, a) for a, b in pairs]


def up_gy(value, peers):
    even = lax.ppermute(value, "gy", pairs_from(0, peers))
    odd = lax.ppermute(value, "gy", pairs_from(1, peers))
    return jnp.where(lax.axis_index("gy") % 2 == 1, even, odd)


def swap_gy(low, high, peers):
    is_even = lax.axis_index("gy") % 2 == 0
    first = lax.ppermute(jnp.where(is_even, high, low), "gy", both_ways(pairs_from(0, peers)))
    second = lax.ppermute(jnp.where(is_even, low, high), "gy", both_ways(pairs_from(1, peers)))
    return jnp.where(is_even, second, first), jnp.where(is_even, first, second)


def swap_gx(low, high, peers):
    if peers == 2:
        is_first = lax.axis_index("gx") == 0
        got = lax.ppermute(jnp.where(is_first, high, low), "gx", [(0, 1), (1, 0)])
        zero = jnp.zeros_like(got)
        return jnp.where(is_first, zero, got), jnp.where(is_first, got, zero)
    below = lax.ppermute(high, "gx", [(i, i + 1) for i in range(peers - 1)])
    above = lax.ppermute(low, "gx", [(i + 1, i) for i in range(peers - 1)])
    return below, above


def everywhere(block, axes):
    sent = jnp.broadcast_to(block[None], (lax.axis_size(axes),) + block.shape)
    return lax.all_to_all(sent, axes, 0, 0, tiled=False)


def general(
    duals, residual, direction, prev_rho, dual_schur, coupling, coarse_inverse, edge_map, corner_slot, active, scaling
):
    cases, span_x, span_y, owned = duals.shape
    half = owned // 2
    full = 2 * owned
    corners = coupling.shape[2]
    width_c = coarse_inverse.shape[-1]
    peers_x, peers_y = lax.axis_size("gx"), lax.axis_size("gy")
    whole = peers_x == 2
    axes = BOTH if whole else "gy"
    regions = peers_x if whole else 1
    peers = regions * peers_y
    here_x, here_y = lax.axis_index("gx"), lax.axis_index("gy")
    used = 2 * (span_x + 1) * (span_y + 1)
    slots = used + 2

    columns = here_x * span_x + jnp.arange(span_x)
    rowset = here_y * span_y + jnp.arange(span_y)
    east_ok = jnp.broadcast_to((columns < span_x * peers_x - 1)[:, None, None], (span_x, span_y, half))
    north_ok = jnp.broadcast_to((rowset < span_y * peers_y - 1)[None, :, None], (span_x, span_y, half))
    keep_own = active.astype(jnp.float32) * jnp.concatenate([east_ok, north_ok], -1).astype(jnp.float32)
    scale_own = keep_own * scaling

    by_place = lambda v: jnp.transpose(v, (1, 2, 0, 3))
    lam = by_place(duals)
    p = keep_own[:, :, None] * by_place(direction)
    stacked = jnp.concatenate([by_place(residual), p, scale_own[:, :, None], keep_own[:, :, None]], 2)
    part_e, part_n = stacked[..., :half], stacked[..., half:]
    from_west = lax.ppermute(part_e[-1], "gx", [(i, i + 1) for i in range(peers_x - 1)])
    from_south = up_gy(part_n[:, -1], peers_y)
    west = jnp.concatenate([from_west[None], part_e[:-1]], 0)
    south = jnp.concatenate([from_south[:, None], part_n[:, :-1]], 1)
    stacked = jnp.concatenate([west, part_e, south, part_n], -1)
    r = stacked[:, :, :cases]
    p_all = stacked[:, :, cases : 2 * cases]
    scale = stacked[:, :, 2 * cases : 2 * cases + 1]
    keep = stacked[:, :, 2 * cases + 1 :]

    sign = jnp.concatenate([-jnp.ones(half), jnp.ones(half), -jnp.ones(half), jnp.ones(half)]).astype(jnp.float32)
    place = (edge_map[..., None] == jnp.arange(full, dtype=jnp.int32)).astype(jnp.float32) * sign
    schur = jnp.einsum("xyij,xyjf->xyif", dual_schur, place, precision=EXACT)
    schur = jnp.einsum("xyie,xyif->xyef", place, schur, precision=EXACT)
    couple = jnp.einsum("xycj,xyjf->xycf", coupling, place, precision=EXACT)

    flat = corner_slot.reshape(-1)
    count = flat.shape[0]
    order = jnp.arange(count)
    same = flat[:, None] == flat[None, :]
    first = ~jnp.any(same & (order[None, :] < order[:, None]), 1) & (flat != width_c)
    rank = jnp.sum((flat[None, :] < flat[:, None]) & first[None, :], 1)
    local_slot = jnp.arange(slots)
    compact = ((rank[:, None] == local_slot) & (flat != width_c)[:, None]).astype(jnp.float32)
    named = jnp.where(
        jnp.any(compact > 0, 0), jnp.max(compact * flat[:, None].astype(jnp.float32), 0), float(width_c)
    )
    compact = compact.reshape(span_x, span_y, corners, slots)
    gather_c = jnp.einsum("xycs,xycf->xysf", compact, couple, precision=EXACT)

    blocks = lambda a: (a[..., :half], a[..., half : 2 * half], a[..., 2 * half : 3 * half], a[..., 3 * half :])

    def jump(y, from_w, from_e, from_s, from_n):
        w, e, s, n = blocks(y)
        w_nb = jnp.concatenate([from_w[None], e[:-1]], 0)
        e_nb = jnp.concatenate([w[1:], from_e[None]], 0)
        s_nb = jnp.concatenate([from_s[:, None], n[:, :-1]], 1)
        n_nb = jnp.concatenate([s[:, 1:], from_n[:, None]], 1)
        return jnp.concatenate([w + w_nb, e + e_nb, s + s_nb, n + n_nb], -1)

    def rims(y):
        w, e, s, n = blocks(y)
        return w[0], e[-1], s[:, 0], n[:, -1]

    def exchange(y):
        w, e, s, n = rims(y)
        from_w, from_e = swap_gx(w, e, peers_x)
        from_s, from_n = swap_gy(s, n, peers_y)
        return from_w, from_e, from_s, from_n

    def put(rim, name):
        zero = jnp.zeros((span_x, span_y, rim.shape[-2], half), jnp.float32)
        parts = [zero, zero, zero, zero]
        if name == 0:
            parts[0] = zero.at[0].set(rim)
        elif name == 1:
            parts[1] = zero.at[-1].set(rim)
        elif name == 2:
            parts[2] = zero.at[:, 0].set(rim)
        else:
            parts[3] = zero.at[:, -1].set(rim)
        return jnp.concatenate(parts, -1)

    nb = exchange(gather_c)
    none = [jnp.zeros_like(v) for v in nb]
    spread = jnp.concatenate([jump(gather_c, *none)] + [put(v, i) for i, v in enumerate(nb)], 2)
    spread = spread * keep

    region_inv = coarse_inverse[0]

    def local_part(v):
        y = jnp.einsum("xykj,xyji->xyki", v, schur, precision=HIGH)
        c = jnp.einsum("xykj,xysj->ks", v, gather_c[:, :, :used], precision=HIGH)
        return y, c

    def over_cases(a, b):
        return jnp.sum(a * b, axis=(0, 1, 3))

    def pack(c, one, two):
        return jnp.concatenate([c, one[:, None], two[:, None]], 1).reshape(-1, 128)

    def unpack(got):
        got = got.reshape(peers, cases, slots)
        sums = jnp.sum(got[:, :, used:], 0)
        return jnp.transpose(got, (1, 0, 2)).reshape(cases, regions, peers_y, slots), sums[:, 0], sums[:, 1]

    def own_part(a):
        return jnp.concatenate([a[..., half : 2 * half], a[..., 3 * half :]], -1)

    u = scale * r
    both = jnp.concatenate([u, p_all], 2)
    y, c = local_part(both)
    yu, yp = y[:, :, :cases], y[:, :, cases:]
    rho_part = over_cases(own_part(r), own_part(u))
    names = jnp.concatenate([named, jnp.zeros(4 * 128 - slots, jnp.float32)]).reshape(4, 128)
    block = jnp.concatenate(
        [pack(c[:cases], rho_part, over_cases(u, yu)), pack(c[cases:], over_cases(p_all, yu), over_cases(p_all, yp)), names]
    )
    got = everywhere(block, axes)
    from_all = exchange(y)

    rows = cases * slots // 128
    slot_of = got[:, 2 * rows :].reshape(peers, -1)[:, :slots].reshape(regions, peers_y * slots)

    if whole:
        other = lax.ppermute(region_inv, "gx", [(0, 1), (1, 0)])
        inverses = jnp.where(here_x == 0, jnp.stack([region_inv, other]), jnp.stack([other, region_inv]))
    else:
        inverses = region_inv[None]
    pick = (slot_of[..., None] == jnp.arange(width_c, dtype=jnp.float32)).astype(jnp.float32)
    dense = jnp.einsum("ran,rnm->ram", pick, inverses, precision=EXACT)
    dense = jnp.einsum("ram,rbm->rab", dense, pick, precision=EXACT)

    def solve(c_all):
        flat_c = c_all.reshape(cases, regions, peers_y * slots)
        sol = jnp.einsum("kra,rab->krb", flat_c, dense, precision=HIGH)
        return flat_c, sol

    def total(a, b):
        return jnp.sum(a * b, (1, 2))

    def over_gx(*sums):
        return sums if whole else tuple(lax.psum(jnp.stack(sums), "gx"))

    def at(sol, ix, dy):
        sol = sol.reshape(cases, regions, peers_y, slots)
        iy = jnp.clip(here_y + dy, 0, peers_y - 1)
        return lax.dynamic_slice(sol, (0, ix, iy, 0), (cases, 1, 1, slots))[:, 0, 0]

    def beside(sol):
        if whole:
            return at(sol, 0, 0), at(sol, 1, 0)
        mine = at(sol, 0, 0)
        return swap_gx(mine, mine, peers_x)

    def coarse_part(sol):
        mine = here_x if whole else 0
        near = jnp.concatenate([at(sol, mine, 0), *beside(sol), at(sol, mine, -1), at(sol, mine, 1)], 1)
        return jnp.einsum("kn,xynj->xykj", near, spread, precision=HIGH)

    cu, rho, delta = unpack(got[:, :rows])
    cp, cross, eta = unpack(got[:, rows : 2 * rows])
    cu, su = solve(cu)
    cp, sp = solve(cp)
    delta, cross, eta = delta + total(cu, su), cross + total(cu, sp), eta + total(cp, sp)
    rho, delta, cross, eta = over_gx(rho, delta, cross, eta)
    f_both = keep * jump(y, *from_all)
    w = f_both[:, :, :cases] + coarse_part(su)
    s = f_both[:, :, cases:] + coarse_part(sp)

    wide = lambda a: a[None, None, :, None]
    beta = rho / prev_rho
    skew = cross + beta * eta
    pi = delta + 2.0 * beta * skew - beta * beta * eta
    for step in range(ITERS):
        if step > 0:
            u = scale * r
            y, c = local_part(u)
            block = pack(c, over_cases(own_part(r), own_part(u)), over_cases(u, y))
            got = everywhere(block, axes)
            from_all = exchange(y)
            rho_old = rho
            c_all, rho, delta = unpack(got)
            c_all, sol = solve(c_all)
            rho, delta = over_gx(rho, delta + total(c_all, sol))
            w = keep * jump(y, *from_all) + coarse_part(sol)
            skew = beta * skew
            beta = rho / rho_old
            pi = delta + 2.0 * beta * skew - beta * beta * pi
        alpha = rho / pi
        p = own_part(u) + wide(beta) * p
        s = w + wide(beta) * s
        lam = lam + wide(alpha) * p
        r = r - wide(alpha) * s
    back = lambda v: jnp.transpose(v, (2, 0, 1, 3))
    return back(lam), back(own_part(r)), back(p)


F32, BF16 = jnp.float32, jnp.bfloat16
SPAN_X, SPAN_Y = 2, 4
SUBS = SPAN_X * SPAN_Y
CASES = 16
SLOTS = 32
USED = 2 * (SPAN_X + 1) * (SPAN_Y + 1)
CAST = 40
LIMIT = 16 * 1024 * 1024


def iota(shape, dim):
    return lax.broadcasted_iota(jnp.int32, shape, dim)


def split(v):
    high = v.astype(BF16)
    return high, (v - high.astype(F32)).astype(BF16)


def dot(a, b):
    return jnp.dot(a, b, preferred_element_type=F32)


def dot_turned(a, b):
    return lax.dot_general(a, b, (((1,), (1,)), ((), ())), preferred_element_type=F32)


def dot_split(v, high, low, dot=dot):
    n = v.shape[0]
    vh, vl = split(v)
    wide = dot(jnp.concatenate([vh, vl], 0), high)
    return wide[:n] + wide[n:] + dot(vh, low)


def dot_exact(v, ones):
    n = v.shape[0]
    vh, vl = split(v)
    wide = dot(jnp.concatenate([vh, vl], 0), ones)
    return wide[:n] + wide[n:]


def odd(i):
    return (i // SPAN_Y + i % SPAN_Y) % 2


def lower(rows):
    return iota((rows, 128), 1) < 64


def packs(ys):
    rows = ys[0].shape[0]
    low = lower(rows)
    column = lambda x: [
        jnp.where(low, ys[x * SPAN_Y + t][:, :128], ys[x * SPAN_Y + t + 1][:, :128]) for t in range(0, SPAN_Y, 2)
    ]
    row = lambda y: jnp.where(low, ys[y][:, 128:], ys[SPAN_Y + y][:, 128:])
    return column(0), column(SPAN_X - 1), row(0), row(SPAN_Y - 1)


def send(ys, x_ref, a_ref, b_ref, at):
    rows = pl.ds(at, ys[0].shape[0])
    west, east, south, north = packs(ys)
    first = lax.axis_index("gx") == 0
    even = lax.axis_index("gy") % 2 == 0
    for t in range(SPAN_Y // 2):
        x_ref[t, rows, :] = jnp.where(first, east[t], west[t])
    a_ref[rows, :] = jnp.where(even, north, south)
    b_ref[rows, :] = jnp.where(even, south, north)


def received(x_ref, a_ref, b_ref, at, n, side=None):
    rows = pl.ds(at, n)
    first = lax.axis_index("gx") == 0
    even = lax.axis_index("gy") % 2 == 0
    xs = [x_ref[t, rows, :] for t in range(SPAN_Y // 2)]
    a, b = a_ref[rows, :], b_ref[rows, :]
    if side is not None:
        a, b = a + side[:, :128], b + side[:, 128:256]
        xs = [xs[t] + side[:, 256 + 128 * t : 384 + 128 * t] for t in range(SPAN_Y // 2)]
    zero = jnp.zeros_like(a)
    return (
        [jnp.where(first, zero, v) for v in xs],
        [jnp.where(first, v, zero) for v in xs],
        jnp.where(even, b, a),
        jnp.where(even, a, b),
    )


def across(ys, nb, rows):
    low = lower(rows)
    zero = jnp.zeros((rows, 128), F32)
    inside = lambda x, y, part: zero if ys is None else ys[x * SPAN_Y + y][:, part * 128 : part * 128 + 128]
    out = []
    for x in range(SPAN_X):
        for y in range(SPAN_Y):
            beyond = lambda v: zero if nb is None else v()
            west = inside(x - 1, y, 0) if x else beyond(lambda: nb[0][y // 2])
            east = inside(x + 1, y, 0) if x < SPAN_X - 1 else beyond(lambda: nb[1][y // 2])
            south = inside(x, y - 1, 1) if y else beyond(lambda: nb[2])
            north = inside(x, y + 1, 1) if y < SPAN_Y - 1 else beyond(lambda: nb[3])
            if (x + y) % 2:
                west, east, south, north = east, west, north, south
            out.append(jnp.concatenate([jnp.where(low, west, east), jnp.where(low, south, north)], 1))
    return out


def owned_lanes(i, rows):
    lane = iota((rows, 256), 1) % 128
    return lane < 64 if odd(i) else lane >= 64


def spread_owned(v, i):
    zero = jnp.zeros_like(v)
    low = lower(v.shape[0])
    turned = pltpu.roll(v, 64, 1)
    if odd(i):
        return jnp.concatenate([jnp.where(low, v, zero), jnp.where(low, turned, zero)], 1)
    return jnp.concatenate([jnp.where(low, zero, turned), jnp.where(low, zero, v)], 1)


def take_owned(v, i):
    low = lower(v.shape[0])
    if odd(i):
        return jnp.where(low, v[:, :128], pltpu.roll(v[:, 128:], 64, 1))
    return jnp.where(low, pltpu.roll(v[:, :128], 64, 1), v[:, 128:])


def start_kernel(res_ref, dir_ref, act_ref, scale_ref, own_ref, x_ref, a_ref, b_ref):
    gx, gy = lax.axis_index("gx"), lax.axis_index("gy")
    last_x = gx * SPAN_X + SPAN_X - 1 == lax.axis_size("gx") * SPAN_X - 1
    last_y = gy * SPAN_Y + SPAN_Y - 1 == lax.axis_size("gy") * SPAN_Y - 1
    east = iota((1, 128), 1) < 64
    ys = []
    for i in range(SUBS):
        x, y = i // SPAN_Y, i % SPAN_Y
        keep = act_ref[i : i + 1, :].astype(F32)
        if x == SPAN_X - 1:
            keep = jnp.where(jnp.logical_and(last_x, east), 0.0, keep)
        if y == SPAN_Y - 1:
            keep = jnp.where(jnp.logical_and(last_y, jnp.logical_not(east)), 0.0, keep)
        mine = pl.ds(i, CASES, stride=SUBS)
        v = jnp.concatenate(
            [
                res_ref[mine, :],
                dir_ref[mine, :] * keep,
                scale_ref[i : i + 1, :] * keep,
                keep,
                jnp.zeros((CAST - 2 * CASES - 2, 128), F32),
            ],
            0,
        )
        v = spread_owned(v, i)
        own_ref[i] = v
        ys.append(v)
    send(ys, x_ref, a_ref, b_ref, 0)


def operator_kernel(schur_ref, couple_ref, map_ref, slot_ref, high_ref, low_ref, cc_ref, ch_ref, cl_ref, name_ref):
    none = 384
    slot = slot_ref[...].astype(F32)
    eye = iota((8, 8), 0) == iota((8, 8), 1)
    column = jnp.concatenate(
        [jnp.sum(jnp.where(eye, jnp.broadcast_to(slot[i : i + 1, :], (8, 8)), 0.0), 1, keepdims=True) for i in range(SUBS)], 0
    )
    row = jnp.concatenate([slot[i : i + 1, :] for i in range(SUBS)], 1)
    count = SUBS * 8
    earlier = iota((count, count), 1) < iota((count, count), 0)
    again = jnp.sum(jnp.where(jnp.logical_and(column == row, earlier), 1.0, 0.0), 1, keepdims=True)
    first = jnp.where(jnp.logical_and(again == 0.0, column != float(none)), 1.0, 0.0)
    first_row = jnp.sum(
        jnp.where(jnp.logical_and(column == row, iota((count, count), 0) < iota((count, count), 1)), 1.0, 0.0), 0, keepdims=True
    )
    first_row = jnp.where(jnp.logical_and(first_row == 0.0, row != float(none)), 1.0, 0.0)
    rank = jnp.sum(jnp.where(row < column, first_row, 0.0), 1, keepdims=True)
    hit = jnp.where(rank == iota((count, 128), 1).astype(F32), first, 0.0)
    name_ref[...] = jnp.broadcast_to(
        jnp.where(jnp.sum(hit, 0, keepdims=True) > 0.0, jnp.sum(hit * column, 0, keepdims=True), float(none)), (8, 128)
    )
    sub = iota((256, 256), 0)
    west = (sub // 64) % 2 == 0
    for i in range(SUBS):
        spots = map_ref[i // SPAN_Y, i % SPAN_Y : i % SPAN_Y + 1, :]
        if odd(i):
            spots = jnp.where((spots // 64) % 2 == 0, spots + 64, spots - 64)
        sign = jnp.where(west, 1.0, -1.0) if odd(i) else jnp.where(west, -1.0, 1.0)
        place = jnp.where(sub == spots, sign, 0.0).astype(BF16)
        mine = slot[i : i + 1, :]
        number = jnp.sum(jnp.where(column < mine, first, 0.0), 0, keepdims=True)
        compact = jnp.where(
            jnp.logical_and(number == iota((SLOTS, 8), 0).astype(F32), mine != float(none)), 1.0, 0.0
        )
        cc = jnp.dot(compact, couple_ref[i], precision=EXACT, preferred_element_type=F32)
        c1, rest = split(cc)
        c2, c3 = split(cc - c1.astype(F32))
        s1, s2 = split(schur_ref[i])
        tall = dot_turned(jnp.concatenate([s1, s2, c1, c2, c3], 0), place)
        high_ref[i] = dot(place, tall[:256].astype(BF16)).astype(BF16)
        low_ref[i] = dot(place, tall[256:512].astype(BF16)).astype(BF16)
        cc = tall[512 : 512 + SLOTS] + tall[512 + SLOTS : 512 + 2 * SLOTS] + tall[512 + 2 * SLOTS :]
        cc_ref[i] = cc
        ch_ref[i], cl_ref[i] = split(cc)


def inverse_kernel(mine_ref, other_ref, high_ref, low_ref):
    first = lax.axis_index("gx") == 0
    mine, other = mine_ref[...], other_ref[...]
    high_ref[0], low_ref[0] = split(jnp.where(first, mine, other))
    high_ref[1], low_ref[1] = split(jnp.where(first, other, mine))


def near_names(name_ref, x_ref, a_ref, b_ref, near_ref):
    named = pl.ds(2 * CASES + SLOTS, 8)
    group = iota((8, 128), 1) // SLOTS
    turn = lambda v, g: jnp.where(group == g, pltpu.roll(v, g * SLOTS, 1), 0.0)
    wanted = name_ref[...] + 0.0
    wanted = jnp.where(group == 0, wanted, turn(a_ref[named, :], 1) + turn(b_ref[named, :], 2) + turn(x_ref[0, named, :], 3))
    found = iota((384, 128), 0).astype(F32) == wanted[0:1]
    mine = jnp.where(iota((384, 128), 1) < 3 * SLOTS, 1.0, 0.0)
    gx = lax.axis_index("gx")
    for region in range(2):
        near_ref[region] = jnp.where(found, jnp.where(gx == region, mine, 1.0 - mine), 0.0).astype(BF16)


def near_spread(x_ref, a_ref, b_ref, nh_ref, nl_ref):
    rows = pl.ds(2 * CASES, SLOTS)
    blank = jnp.zeros((SLOTS, 128), F32)
    parts = [
        [blank] * 4,
        [a_ref[rows, :], blank, blank, blank],
        [blank, b_ref[rows, :], blank, blank],
        [blank, blank, x_ref[0, rows, :], x_ref[1, rows, :]],
    ]
    nh_ref[...], nl_ref[...] = split(jnp.concatenate([jnp.concatenate(row, 1) for row in parts], 0))


def operator(ys, x_ref, a_ref, b_ref, near, mk_ref, ch_ref, cl_ref, nh_ref, nl_ref):
    n = ys[0].shape[0]
    side = dot_split(near, nh_ref[...], nl_ref[...])
    west, east, south, north = received(x_ref, a_ref, b_ref, 0, n, side)
    mine = near[:, :SLOTS]
    ys = [ys[i] + dot_split(mine, ch_ref[i], cl_ref[i]) for i in range(SUBS)]
    other = across(ys, (west, east, south, north), n)
    return [mk_ref[i, 1:2, :] * (ys[i] + other[i]) for i in range(SUBS)]


def local_part(us, high_ref, low_ref, ch_ref, cl_ref):
    ys = [dot_split(us[i], high_ref[i], low_ref[i]) for i in range(SUBS)]
    n = us[0].shape[0]
    couple = lambda ref: jnp.concatenate([ref[i] for i in range(SUBS)], 0)
    corner = dot_split(jnp.concatenate(us, 0), couple(ch_ref), couple(cl_ref), dot_turned)
    group = iota((n, 128), 1) // SLOTS
    total = jnp.zeros((n, 128), F32)
    for i in range(SUBS):
        part = corner[n * i : n * i + n, 128 * (i // 4) : 128 * (i // 4) + 128]
        total = total + jnp.where(group == i % 4, part, 0.0)
    total = total + pltpu.roll(total, 64, 1)
    total = total + pltpu.roll(total, 32, 1)
    return ys, total


def over_lanes(terms):
    total = terms[0]
    for t in terms[1:]:
        total = total + t
    return jnp.sum(total[:, :128] + total[:, 128:], 1, keepdims=True)


def packed(corner, one, two):
    slot = iota((CASES, 128), 1) % SLOTS
    full = jnp.where(slot == USED, one, jnp.where(slot == USED + 1, two, corner))
    group = iota((4, 128), 1) // SLOTS
    out = jnp.zeros((4, 128), F32)
    for b in range(4):
        out = jnp.where(group == b, full[4 * b : 4 * b + 4], out)
    return out


def by_slot(vs):
    group = iota((8, 128), 1) // SLOTS
    out = []
    for region in range(2):
        rows = []
        for b in range(4):
            halves = []
            for h in range(2):
                acc = None
                for q in range(4):
                    v = vs[8 * region + 4 * h + q]
                    turned = v if q == b else pltpu.roll(v, (SLOTS * (q - b)) % 128, 1)
                    acc = turned if acc is None else jnp.where(group == q, turned, acc)
                halves.append(acc)
            rows.append(jnp.concatenate(halves, 1))
        out.append(jnp.concatenate(rows, 0))
    return out


def inner(vs):
    total = vs[0]
    for v in vs[1:]:
        total = total + v
    total = total[:4] + total[4:]
    tall = jnp.concatenate([total] * 4, 0)
    lane, row = iota((CASES, 128), 1), iota((CASES, 128), 0)
    column = lambda s: jnp.sum(jnp.where(lane == SLOTS * (row // 4) + s, tall, 0.0), 1, keepdims=True)
    return column(USED), column(USED + 1)


def first_of_pairs(v):
    return jnp.concatenate([v[8 * b : 8 * b + 4] for b in range(v.shape[0] // 8)], 0)


def solve(spots, pick_ref, gh_ref, gl_ref, near_ref):
    totals, sols, near = [], [], None
    for region in range(2):
        v = spots[region]
        n = v.shape[0]
        even = dot_exact(v, pick_ref[region, 0])
        odds = dot_exact(v, pick_ref[region, 1])
        z = jnp.where((iota((n, 384), 0) // 4) % 2 == 0, even, odds).reshape(n // 8, 8, 384)
        total = (z + pltpu.roll(z, 4, 1)).reshape(n, 384)
        sol = dot_split(total, gh_ref[region], gl_ref[region])
        part = dot_exact(sol, near_ref[region])
        near = part if near is None else near + part
        totals.append(total)
        sols.append(sol)
    return totals, sols, near


def energy(totals, sols):
    both = totals[0] * sols[0] + totals[1] * sols[1]
    return first_of_pairs(jnp.sum(both, 1, keepdims=True))


def emit(rs, mk_ref, high_ref, low_ref, ch_ref, cl_ref, block_ref, y_ref, x_ref, a_ref, b_ref):
    us = [mk_ref[i, 0:1, :] * rs[i] for i in range(SUBS)]
    ys, corner = local_part(us, high_ref, low_ref, ch_ref, cl_ref)
    send(ys, x_ref, a_ref, b_ref, 0)
    for i in range(SUBS):
        y_ref[i] = ys[i]
    for ref in (x_ref, a_ref, b_ref, y_ref):
        ref.flush()
    rho = over_lanes([jnp.where(owned_lanes(i, CASES), rs[i] * us[i], 0.0) for i in range(SUBS)])
    delta = over_lanes([us[i] * ys[i] for i in range(SUBS)])
    block = packed(corner, rho, delta)
    twice = jnp.concatenate([block, block], 0)
    for j in range(16):
        block_ref[j] = twice


def first_kernel(
    own_ref, x_ref, a_ref, b_ref, high_ref, low_ref, cc_ref, ch_ref, cl_ref, name_ref,
    r_ref, p_ref, mk_ref, y_ref, block_ref, sx_ref, sa_ref, sb_ref,
):
    own = [own_ref[i] for i in range(SUBS)]
    other = across(own, received(x_ref, a_ref, b_ref, 0, CAST), CAST)
    rs, vs = [], []
    for i in range(SUBS):
        full = own[i] + other[i]
        rs.append(full[:CASES])
        r_ref[i] = full[:CASES]
        p_ref[i] = full[CASES : 2 * CASES]
        mk_ref[i] = full[2 * CASES : 2 * CASES + 8]
        vs.append(jnp.concatenate([full[2 * CASES : 2 * CASES + 1] * full[:CASES], full[CASES : 2 * CASES]], 0))
    ys, corner = local_part(vs, high_ref, low_ref, ch_ref, cl_ref)
    names = name_ref[...]
    send([jnp.concatenate([ys[i], cc_ref[i]], 0) for i in range(SUBS)], sx_ref, sa_ref, sb_ref, 0)
    at = pl.ds(2 * CASES + SLOTS, 8)
    for t in range(SPAN_Y // 2):
        sx_ref[t, at, :] = names
    sa_ref[at, :] = names
    sb_ref[at, :] = names
    us = [v[:CASES] for v in vs]
    ps = [v[CASES:] for v in vs]
    rho = over_lanes([jnp.where(owned_lanes(i, CASES), rs[i] * us[i], 0.0) for i in range(SUBS)])
    delta = over_lanes([us[i] * ys[i][:CASES] for i in range(SUBS)])
    cross = over_lanes([ps[i] * ys[i][:CASES] for i in range(SUBS)])
    eta = over_lanes([ps[i] * ys[i][CASES:] for i in range(SUBS)])
    one, two = packed(corner[:CASES], rho, delta), packed(corner[CASES:], cross, eta)
    blocks = [
        jnp.concatenate([one, two], 0),
        jnp.concatenate([names[:4], one], 0),
        jnp.concatenate([two, names[:4]], 0),
    ]
    for j in range(16):
        for t in range(3):
            block_ref[3 * j + t] = blocks[t]
    for i in range(SUBS):
        y_ref[i] = ys[i]


def column_of(row):
    eye = iota((CASES, CASES), 0) == iota((CASES, CASES), 1)
    return jnp.sum(jnp.where(eye, jnp.broadcast_to(row, (CASES, CASES)), 0.0), 1, keepdims=True)


def keep_scalars(scal_ref, values):
    for t, v in enumerate(values):
        scal_ref[t] = jnp.broadcast_to(v, (CASES, 128))


def second_kernel(
    got_ref, x_ref, a_ref, b_ref, y_ref, r_ref, p_ref, mk_ref, dual_ref, rho_ref, gh_ref, gl_ref, name_ref,
    high_ref, low_ref, ch_ref, cl_ref,
    pick_ref, near_ref, nh_ref, nl_ref, ro_ref, so_ref, po_ref, lo_ref, scal_ref, block_ref, yo_ref, sx_ref, sa_ref, sb_ref,
):
    near_names(name_ref, x_ref, a_ref, b_ref, near_ref)
    near_spread(x_ref, a_ref, b_ref, nh_ref, nl_ref)
    top = iota((8, 128), 0) < 4
    us, ps, names = [], [], []
    for j in range(16):
        v = [got_ref[3 * j + t] for t in range(3)]
        us.append(jnp.where(top, v[0], v[1]))
        ps.append(pltpu.roll(jnp.where(top, v[2], v[0]), 4, 0))
        names.append((v[1], pltpu.roll(v[2], 4, 0)))
    group = iota((8, 128), 1) // SLOTS
    for region in range(2):
        for par in range(2):
            halves = []
            for h in range(2):
                acc = None
                for q in range(4):
                    v = names[8 * region + 4 * h + q][par]
                    turned = pltpu.roll(v, SLOTS * q, 1) if q else v
                    acc = turned if acc is None else jnp.where(group == q, turned, acc)
                halves.append(acc[0:1])
            wanted = jnp.concatenate(halves, 1)
            hit = jnp.where(iota((384, 256), 0).astype(F32) == wanted, 1.0, 0.0)
            pick_ref[region, par] = jnp.transpose(hit).astype(BF16)
    lhs_u, lhs_p = by_slot(us), by_slot(ps)
    n = lhs_u[0].shape[0]
    totals, sols, near = solve(
        [jnp.concatenate([lhs_u[t], lhs_p[t]], 0) for t in range(2)], pick_ref, gh_ref, gl_ref, near_ref
    )
    of_u, of_p = lambda vs: [v[:n] for v in vs], lambda vs: [v[n:] for v in vs]
    rho, delta = inner(us)
    cross, eta = inner(ps)
    delta = delta + energy(of_u(totals), of_u(sols))
    cross = cross + energy(of_p(totals), of_u(sols))
    eta = eta + energy(of_p(totals), of_p(sols))
    near = first_of_pairs(near)
    beta = rho / column_of(rho_ref[...])
    skew = cross + beta * eta
    pi = delta + 2.0 * beta * skew - beta * beta * eta
    alpha = rho / pi
    fs = operator([y_ref[i] for i in range(SUBS)], x_ref, a_ref, b_ref, near, mk_ref, ch_ref, cl_ref, nh_ref, nl_ref)
    rs = []
    for i in range(SUBS):
        f, r = fs[i], r_ref[i]
        p = mk_ref[i, 0:1, :] * r + beta * p_ref[i]
        s = f[:CASES] + beta * f[CASES:]
        r = r - alpha * s
        rs.append(r)
        ro_ref[i], so_ref[i], po_ref[i] = r, s, p
        lo_ref[i] = spread_owned(dual_ref[pl.ds(i, CASES, stride=SUBS), :], i) + alpha * p
    keep_scalars(scal_ref, (rho, pi, beta, skew))
    for ref in (pick_ref, near_ref, nh_ref, nl_ref, ro_ref, so_ref, po_ref, lo_ref, scal_ref):
        ref.flush()
    emit(rs, mk_ref, high_ref, low_ref, ch_ref, cl_ref, block_ref, yo_ref, sx_ref, sa_ref, sb_ref)


def absorb(got_ref, x_ref, a_ref, b_ref, y_ref, r_ref, s_ref, p_ref, l_ref, scal_ref, mk_ref, pick_ref, gh_ref, gl_ref, near_ref, nh_ref, nl_ref, ch_ref, cl_ref):
    vs = [got_ref[j] for j in range(16)]
    totals, sols, near = solve(by_slot(vs), pick_ref, gh_ref, gl_ref, near_ref)
    rho, delta = inner(vs)
    delta = delta + energy(totals, sols)
    near = first_of_pairs(near)
    rho_old, pi, beta, skew = (scal_ref[t][:, 0:1] for t in range(4))
    skew = beta * skew
    beta = rho / rho_old
    pi = delta + 2.0 * beta * skew - beta * beta * pi
    alpha = rho / pi
    fs = operator([y_ref[i] for i in range(SUBS)], x_ref, a_ref, b_ref, near, mk_ref, ch_ref, cl_ref, nh_ref, nl_ref)
    out = []
    for i in range(SUBS):
        r = r_ref[i]
        p = mk_ref[i, 0:1, :] * r + beta * p_ref[i]
        s = fs[i] + beta * s_ref[i]
        out.append((r - alpha * s, s, p, l_ref[i] + alpha * p))
    return out, (rho, pi, beta, skew)


def round_kernel(
    got_ref, x_ref, a_ref, b_ref, y_ref, r_ref, s_ref, p_ref, l_ref, scal_ref, mk_ref, pick_ref, gh_ref, gl_ref, near_ref,
    nh_ref, nl_ref, ch_ref, cl_ref, high_ref, low_ref,
    ro_ref, so_ref, po_ref, lo_ref, scalo_ref, block_ref, yo_ref, sx_ref, sa_ref, sb_ref,
):
    out, scalars = absorb(
        got_ref, x_ref, a_ref, b_ref, y_ref, r_ref, s_ref, p_ref, l_ref, scal_ref, mk_ref, pick_ref, gh_ref, gl_ref, near_ref,
        nh_ref, nl_ref, ch_ref, cl_ref,
    )
    for i, (r, s, p, lam) in enumerate(out):
        ro_ref[i], so_ref[i], po_ref[i], lo_ref[i] = r, s, p, lam
    keep_scalars(scalo_ref, scalars)
    for ref in (ro_ref, so_ref, po_ref, lo_ref, scalo_ref):
        ref.flush()
    emit([v[0] for v in out], mk_ref, high_ref, low_ref, ch_ref, cl_ref, block_ref, yo_ref, sx_ref, sa_ref, sb_ref)


def last_kernel(
    got_ref, x_ref, a_ref, b_ref, y_ref, r_ref, s_ref, p_ref, l_ref, scal_ref, mk_ref, pick_ref, gh_ref, gl_ref, near_ref,
    nh_ref, nl_ref, ch_ref, cl_ref, lo_ref, ro_ref, po_ref,
):
    out, _ = absorb(
        got_ref, x_ref, a_ref, b_ref, y_ref, r_ref, s_ref, p_ref, l_ref, scal_ref, mk_ref, pick_ref, gh_ref, gl_ref, near_ref,
        nh_ref, nl_ref, ch_ref, cl_ref,
    )
    for i, (r, _, p, lam) in enumerate(out):
        mine = pl.ds(i, CASES, stride=SUBS)
        lo_ref[mine, :] = take_owned(lam, i)
        ro_ref[mine, :] = take_owned(r, i)
        po_ref[mine, :] = take_owned(p, i)


class Fetched:
    def __init__(self, source, buffer, semaphore):
        self.buffer = buffer
        self.copy = pltpu.make_async_copy(source, buffer, semaphore)
        self.copy.start()
        self.here = False

    def __getitem__(self, index):
        if not self.here:
            self.copy.wait()
            self.here = True
        return self.buffer[index]


class Stored:
    def __init__(self, target, buffer, semaphore):
        self.buffer = buffer
        self.copy = pltpu.make_async_copy(buffer, target, semaphore)
        self.sent = False

    def __setitem__(self, index, value):
        self.buffer[index] = value

    def __getitem__(self, index):
        return self.buffer[index]

    def flush(self):
        if not self.sent:
            self.copy.start()
            self.sent = True


class Kept:
    def __init__(self, ref):
        self.ref = ref

    def __setitem__(self, index, value):
        self.ref[index] = value

    def flush(self):
        pass


def call(kernel, args, outs, kept=(), kept_out=()):
    moved = [i for i in range(len(args)) if i not in kept]
    written = [i for i in range(len(outs)) if i not in kept_out]

    def body(*refs):
        ins, results = refs[: len(args)], refs[len(args) : len(args) + len(outs)]
        buffers, (in_sem, out_sem) = refs[len(args) + len(outs) : -2], refs[-2:]
        fetched, stored = list(ins), [Kept(ref) for ref in results]
        for t, i in enumerate(moved):
            fetched[i] = Fetched(ins[i], buffers[t], in_sem.at[t])
        for t, i in enumerate(written):
            stored[i] = Stored(results[i], buffers[len(moved) + t], out_sem.at[t])
        kernel(*fetched, *stored)
        for i in written:
            stored[i].flush()
        for i in moved:
            if not fetched[i].here:
                fetched[i].copy.wait()
        for i in written:
            stored[i].copy.wait()

    place = lambda held: pl.BlockSpec(memory_space=pltpu.VMEM if held else pltpu.HBM)
    args = [a if i in kept else pltpu.with_memory_space_constraint(a, pltpu.HBM) for i, a in enumerate(args)]
    return pl.pallas_call(
        body,
        out_shape=[
            jax.ShapeDtypeStruct(*out) if i in kept_out else pltpu.HBM(*out) for i, out in enumerate(outs)
        ],
        in_specs=[place(i in kept) for i in range(len(args))],
        out_specs=[place(i in kept_out) for i in range(len(outs))],
        scratch_shapes=[pltpu.VMEM(args[i].shape, args[i].dtype) for i in moved]
        + [pltpu.VMEM(*outs[i]) for i in written]
        + [pltpu.SemaphoreType.DMA((max(len(moved), 1),)), pltpu.SemaphoreType.DMA((max(len(written), 1),))],
        compiler_params=pltpu.CompilerParams(vmem_limit_bytes=LIMIT),
    )(*args)


def trade(x, a, b):
    peers = lax.axis_size("gy")
    return (
        lax.ppermute(x, "gx", [(0, 1), (1, 0)]),
        lax.ppermute(a, "gy", both_ways(pairs_from(0, peers))),
        lax.ppermute(b, "gy", both_ways(pairs_from(1, peers))),
    )


def two_regions(
    duals, residual, direction, prev_rho, dual_schur, coupling, coarse_inverse, edge_map, corner_slot, active, scaling
):
    native = lambda v: v.reshape(CASES * SUBS, 128)
    by_sub = lambda v: v.reshape((SUBS,) + v.shape[2:])
    width = coarse_inverse.shape[-1]
    sends = lambda rows: [((SPAN_Y // 2, rows, 128), F32), ((rows, 128), F32), ((rows, 128), F32)]
    state = ((SUBS, CASES, 256), F32)

    other = lax.ppermute(coarse_inverse[0], "gx", [(0, 1), (1, 0)])
    own, *out = call(
        start_kernel,
        [native(residual), native(direction), by_sub(active), by_sub(scaling)],
        [((SUBS, CAST, 256), F32)] + sends(CAST),
    )
    come = trade(*out)
    matrix = ((SUBS, 256, 256), BF16)
    couple = ((SUBS, SLOTS, 256), BF16)
    high, low, cc, ch, cl, names = call(
        operator_kernel,
        [by_sub(dual_schur), by_sub(coupling), edge_map, by_sub(corner_slot)],
        [matrix, matrix, ((SUBS, SLOTS, 256), F32), couple, couple, ((8, 128), F32)],
        kept_out=(0, 1),
    )
    square = ((2, width, width), BF16)
    gh, gl = call(inverse_kernel, [coarse_inverse[0], other], [square, square], kept_out=(0, 1))
    rows = 2 * CASES + SLOTS + 8
    r, p, mk, y, block, *out = call(
        first_kernel,
        [own, *come, high, low, cc, ch, cl, names],
        [state, state, ((SUBS, 8, 256), F32), ((SUBS, 2 * CASES, 256), F32), ((48, 8, 128), F32)] + sends(rows),
        kept=(4, 5),
    )
    got = lax.all_to_all(block.reshape(32, 12, 128), BOTH, 0, 0, tiled=False).reshape(48, 8, 128)
    come = trade(*out)
    side = ((128, 512), BF16)
    weights = [ch, cl, high, low]
    onward = [state, state, state, state, ((4, CASES, 128), F32), ((16, 8, 128), F32), state] + sends(CASES)
    pick, near, nh, nl, r, s, p, lam, scal, block, y, *out = call(
        second_kernel,
        [got, *come, y, r, p, mk, native(duals), prev_rho.reshape(1, CASES), gh, gl, names, high, low, ch, cl],
        [((2, 2, 256, width), BF16), ((2, width, 128), BF16), side, side] + onward,
        kept=(10, 11, 13, 14),
    )
    for step in range(1, ITERS):
        got = lax.all_to_all(block.reshape(32, 4, 128), BOTH, 0, 0, tiled=False).reshape(16, 8, 128)
        come = trade(*out)
        args = [got, *come, y, r, s, p, lam, scal, mk, pick, gh, gl, near, nh, nl, ch, cl]
        if step < ITERS - 1:
            r, s, p, lam, scal, block, y, *out = call(round_kernel, args + [high, low], onward, kept=(12, 13, 19, 20))
        else:
            plain = ((CASES * SUBS, 128), F32)
            results = call(last_kernel, args, [plain, plain, plain], kept=(12, 13))
    return tuple(v.reshape(duals.shape) for v in results)


def shards(*args):
    cases, span_x, span_y, owned = args[0].shape
    fits = (cases, span_x, span_y, owned, args[6].shape[-1]) == (CASES, SPAN_X, SPAN_Y, 128, 384)
    if fits and lax.axis_size("gx") == 2 and lax.axis_size("gy") == 16:
        return two_regions(*args)
    return general(*args)


def solution(mesh):
    placed = (
        P(None, "gx", "gy", None),
        P(None, "gx", "gy", None),
        P(None, "gx", "gy", None),
        P(),
        P("gx", "gy", None, None),
        P("gx", "gy", None, None),
        P("gx", None, None),
        P("gx", "gy", None),
        P("gx", "gy", None),
        P("gx", "gy", None),
        P("gx", "gy", None),
    )
    return jax.shard_map(
        shards,
        mesh=mesh,
        in_specs=placed,
        out_specs=(P(None, "gx", "gy", None), P(None, "gx", "gy", None), P(None, "gx", "gy", None)),
        check_vma=False,
    )
```

```python
import jax
import jax.numpy as jnp
from jax import lax
from jax.experimental import pallas as pl
from jax.experimental.pallas import tpu as pltpu
from jax.sharding import PartitionSpec as P

ITERS = 6
HIGH = lax.Precision.HIGH
EXACT = lax.Precision.HIGHEST
BOTH = ("gx", "gy")


def pairs_from(first, peers):
    return [(i, i + 1) for i in range(first, peers - 1, 2)]


def both_ways(pairs):
    return pairs + [(b, a) for a, b in pairs]


def up_gy(value, peers):
    even = lax.ppermute(value, "gy", pairs_from(0, peers))
    odd = lax.ppermute(value, "gy", pairs_from(1, peers))
    return jnp.where(lax.axis_index("gy") % 2 == 1, even, odd)


def swap_gy(low, high, peers):
    is_even = lax.axis_index("gy") % 2 == 0
    first = lax.ppermute(jnp.where(is_even, high, low), "gy", both_ways(pairs_from(0, peers)))
    second = lax.ppermute(jnp.where(is_even, low, high), "gy", both_ways(pairs_from(1, peers)))
    return jnp.where(is_even, second, first), jnp.where(is_even, first, second)


def swap_gx(low, high, peers):
    if peers == 2:
        is_first = lax.axis_index("gx") == 0
        got = lax.ppermute(jnp.where(is_first, high, low), "gx", [(0, 1), (1, 0)])
        zero = jnp.zeros_like(got)
        return jnp.where(is_first, zero, got), jnp.where(is_first, got, zero)
    below = lax.ppermute(high, "gx", [(i, i + 1) for i in range(peers - 1)])
    above = lax.ppermute(low, "gx", [(i + 1, i) for i in range(peers - 1)])
    return below, above


def everywhere(block, axes):
    sent = jnp.broadcast_to(block[None], (lax.axis_size(axes),) + block.shape)
    return lax.all_to_all(sent, axes, 0, 0, tiled=False)


def general(
    duals, residual, direction, prev_rho, dual_schur, coupling, coarse_inverse, edge_map, corner_slot, active, scaling
):
    cases, span_x, span_y, owned = duals.shape
    half = owned // 2
    full = 2 * owned
    corners = coupling.shape[2]
    width_c = coarse_inverse.shape[-1]
    peers_x, peers_y = lax.axis_size("gx"), lax.axis_size("gy")
    whole = peers_x == 2
    axes = BOTH if whole else "gy"
    regions = peers_x if whole else 1
    peers = regions * peers_y
    here_x, here_y = lax.axis_index("gx"), lax.axis_index("gy")
    used = 2 * (span_x + 1) * (span_y + 1)
    slots = used + 2

    columns = here_x * span_x + jnp.arange(span_x)
    rowset = here_y * span_y + jnp.arange(span_y)
    east_ok = jnp.broadcast_to((columns < span_x * peers_x - 1)[:, None, None], (span_x, span_y, half))
    north_ok = jnp.broadcast_to((rowset < span_y * peers_y - 1)[None, :, None], (span_x, span_y, half))
    keep_own = active.astype(jnp.float32) * jnp.concatenate([east_ok, north_ok], -1).astype(jnp.float32)
    scale_own = keep_own * scaling

    by_place = lambda v: jnp.transpose(v, (1, 2, 0, 3))
    lam = by_place(duals)
    p = keep_own[:, :, None] * by_place(direction)
    stacked = jnp.concatenate([by_place(residual), p, scale_own[:, :, None], keep_own[:, :, None]], 2)
    part_e, part_n = stacked[..., :half], stacked[..., half:]
    from_west = lax.ppermute(part_e[-1], "gx", [(i, i + 1) for i in range(peers_x - 1)])
    from_south = up_gy(part_n[:, -1], peers_y)
    west = jnp.concatenate([from_west[None], part_e[:-1]], 0)
    south = jnp.concatenate([from_south[:, None], part_n[:, :-1]], 1)
    stacked = jnp.concatenate([west, part_e, south, part_n], -1)
    r = stacked[:, :, :cases]
    p_all = stacked[:, :, cases : 2 * cases]
    scale = stacked[:, :, 2 * cases : 2 * cases + 1]
    keep = stacked[:, :, 2 * cases + 1 :]

    sign = jnp.concatenate([-jnp.ones(half), jnp.ones(half), -jnp.ones(half), jnp.ones(half)]).astype(jnp.float32)
    place = (edge_map[..., None] == jnp.arange(full, dtype=jnp.int32)).astype(jnp.float32) * sign
    schur = jnp.einsum("xyij,xyjf->xyif", dual_schur, place, precision=EXACT)
    schur = jnp.einsum("xyie,xyif->xyef", place, schur, precision=EXACT)
    couple = jnp.einsum("xycj,xyjf->xycf", coupling, place, precision=EXACT)

    flat = corner_slot.reshape(-1)
    count = flat.shape[0]
    order = jnp.arange(count)
    same = flat[:, None] == flat[None, :]
    first = ~jnp.any(same & (order[None, :] < order[:, None]), 1) & (flat != width_c)
    rank = jnp.sum((flat[None, :] < flat[:, None]) & first[None, :], 1)
    local_slot = jnp.arange(slots)
    compact = ((rank[:, None] == local_slot) & (flat != width_c)[:, None]).astype(jnp.float32)
    named = jnp.where(
        jnp.any(compact > 0, 0), jnp.max(compact * flat[:, None].astype(jnp.float32), 0), float(width_c)
    )
    compact = compact.reshape(span_x, span_y, corners, slots)
    gather_c = jnp.einsum("xycs,xycf->xysf", compact, couple, precision=EXACT)

    blocks = lambda a: (a[..., :half], a[..., half : 2 * half], a[..., 2 * half : 3 * half], a[..., 3 * half :])

    def jump(y, from_w, from_e, from_s, from_n):
        w, e, s, n = blocks(y)
        w_nb = jnp.concatenate([from_w[None], e[:-1]], 0)
        e_nb = jnp.concatenate([w[1:], from_e[None]], 0)
        s_nb = jnp.concatenate([from_s[:, None], n[:, :-1]], 1)
        n_nb = jnp.concatenate([s[:, 1:], from_n[:, None]], 1)
        return jnp.concatenate([w + w_nb, e + e_nb, s + s_nb, n + n_nb], -1)

    def rims(y):
        w, e, s, n = blocks(y)
        return w[0], e[-1], s[:, 0], n[:, -1]

    def exchange(y):
        w, e, s, n = rims(y)
        from_w, from_e = swap_gx(w, e, peers_x)
        from_s, from_n = swap_gy(s, n, peers_y)
        return from_w, from_e, from_s, from_n

    def put(rim, name):
        zero = jnp.zeros((span_x, span_y, rim.shape[-2], half), jnp.float32)
        parts = [zero, zero, zero, zero]
        if name == 0:
            parts[0] = zero.at[0].set(rim)
        elif name == 1:
            parts[1] = zero.at[-1].set(rim)
        elif name == 2:
            parts[2] = zero.at[:, 0].set(rim)
        else:
            parts[3] = zero.at[:, -1].set(rim)
        return jnp.concatenate(parts, -1)

    nb = exchange(gather_c)
    none = [jnp.zeros_like(v) for v in nb]
    spread = jnp.concatenate([jump(gather_c, *none)] + [put(v, i) for i, v in enumerate(nb)], 2)
    spread = spread * keep

    region_inv = coarse_inverse[0]

    def local_part(v):
        y = jnp.einsum("xykj,xyji->xyki", v, schur, precision=HIGH)
        c = jnp.einsum("xykj,xysj->ks", v, gather_c[:, :, :used], precision=HIGH)
        return y, c

    def over_cases(a, b):
        return jnp.sum(a * b, axis=(0, 1, 3))

    def pack(c, one, two):
        return jnp.concatenate([c, one[:, None], two[:, None]], 1).reshape(-1, 128)

    def unpack(got):
        got = got.reshape(peers, cases, slots)
        sums = jnp.sum(got[:, :, used:], 0)
        return jnp.transpose(got, (1, 0, 2)).reshape(cases, regions, peers_y, slots), sums[:, 0], sums[:, 1]

    def own_part(a):
        return jnp.concatenate([a[..., half : 2 * half], a[..., 3 * half :]], -1)

    u = scale * r
    both = jnp.concatenate([u, p_all], 2)
    y, c = local_part(both)
    yu, yp = y[:, :, :cases], y[:, :, cases:]
    rho_part = over_cases(own_part(r), own_part(u))
    names = jnp.concatenate([named, jnp.zeros(4 * 128 - slots, jnp.float32)]).reshape(4, 128)
    block = jnp.concatenate(
        [pack(c[:cases], rho_part, over_cases(u, yu)), pack(c[cases:], over_cases(p_all, yu), over_cases(p_all, yp)), names]
    )
    got = everywhere(block, axes)
    from_all = exchange(y)

    rows = cases * slots // 128
    slot_of = got[:, 2 * rows :].reshape(peers, -1)[:, :slots].reshape(regions, peers_y * slots)

    if whole:
        other = lax.ppermute(region_inv, "gx", [(0, 1), (1, 0)])
        inverses = jnp.where(here_x == 0, jnp.stack([region_inv, other]), jnp.stack([other, region_inv]))
    else:
        inverses = region_inv[None]
    pick = (slot_of[..., None] == jnp.arange(width_c, dtype=jnp.float32)).astype(jnp.float32)
    dense = jnp.einsum("ran,rnm->ram", pick, inverses, precision=EXACT)
    dense = jnp.einsum("ram,rbm->rab", dense, pick, precision=EXACT)

    def solve(c_all):
        flat_c = c_all.reshape(cases, regions, peers_y * slots)
        sol = jnp.einsum("kra,rab->krb", flat_c, dense, precision=HIGH)
        return flat_c, sol

    def total(a, b):
        return jnp.sum(a * b, (1, 2))

    def over_gx(*sums):
        return sums if whole else tuple(lax.psum(jnp.stack(sums), "gx"))

    def at(sol, ix, dy):
        sol = sol.reshape(cases, regions, peers_y, slots)
        iy = jnp.clip(here_y + dy, 0, peers_y - 1)
        return lax.dynamic_slice(sol, (0, ix, iy, 0), (cases, 1, 1, slots))[:, 0, 0]

    def beside(sol):
        if whole:
            return at(sol, 0, 0), at(sol, 1, 0)
        mine = at(sol, 0, 0)
        return swap_gx(mine, mine, peers_x)

    def coarse_part(sol):
        mine = here_x if whole else 0
        near = jnp.concatenate([at(sol, mine, 0), *beside(sol), at(sol, mine, -1), at(sol, mine, 1)], 1)
        return jnp.einsum("kn,xynj->xykj", near, spread, precision=HIGH)

    cu, rho, delta = unpack(got[:, :rows])
    cp, cross, eta = unpack(got[:, rows : 2 * rows])
    cu, su = solve(cu)
    cp, sp = solve(cp)
    delta, cross, eta = delta + total(cu, su), cross + total(cu, sp), eta + total(cp, sp)
    rho, delta, cross, eta = over_gx(rho, delta, cross, eta)
    f_both = keep * jump(y, *from_all)
    w = f_both[:, :, :cases] + coarse_part(su)
    s = f_both[:, :, cases:] + coarse_part(sp)

    wide = lambda a: a[None, None, :, None]
    beta = rho / prev_rho
    skew = cross + beta * eta
    pi = delta + 2.0 * beta * skew - beta * beta * eta
    for step in range(ITERS):
        if step > 0:
            u = scale * r
            y, c = local_part(u)
            block = pack(c, over_cases(own_part(r), own_part(u)), over_cases(u, y))
            got = everywhere(block, axes)
            from_all = exchange(y)
            rho_old = rho
            c_all, rho, delta = unpack(got)
            c_all, sol = solve(c_all)
            rho, delta = over_gx(rho, delta + total(c_all, sol))
            w = keep * jump(y, *from_all) + coarse_part(sol)
            skew = beta * skew
            beta = rho / rho_old
            pi = delta + 2.0 * beta * skew - beta * beta * pi
        alpha = rho / pi
        p = own_part(u) + wide(beta) * p
        s = w + wide(beta) * s
        lam = lam + wide(alpha) * p
        r = r - wide(alpha) * s
    back = lambda v: jnp.transpose(v, (2, 0, 1, 3))
    return back(lam), back(own_part(r)), back(p)


F32, BF16 = jnp.float32, jnp.bfloat16
SPAN_X, SPAN_Y = 2, 4
SUBS = SPAN_X * SPAN_Y
CASES = 16
SLOTS = 32
USED = 2 * (SPAN_X + 1) * (SPAN_Y + 1)
CAST = 40
LIMIT = 16 * 1024 * 1024
UPPER = [(i, j) for i in range(3) for j in range(i, 3)]


def iota(shape, dim):
    return lax.broadcasted_iota(jnp.int32, shape, dim)


def split(v):
    high = v.astype(BF16)
    return high, (v - high.astype(F32)).astype(BF16)


def dot(a, b):
    return jnp.dot(a, b, preferred_element_type=F32)


def dot_turned(a, b):
    return lax.dot_general(a, b, (((1,), (1,)), ((), ())), preferred_element_type=F32)


def dot_split(v, high, low, dot=dot):
    n = v.shape[0]
    vh, vl = split(v)
    wide = dot(jnp.concatenate([vh, vl], 0), high)
    return wide[:n] + wide[n:] + dot(vh, low)


def dot_exact(v, ones):
    n = v.shape[0]
    vh, vl = split(v)
    wide = dot(jnp.concatenate([vh, vl], 0), ones)
    return wide[:n] + wide[n:]


def odd(i):
    return (i // SPAN_Y + i % SPAN_Y) % 2


def lower(rows):
    return iota((rows, 128), 1) < 64


def packs(ys):
    rows = ys[0].shape[0]
    low = lower(rows)
    column = lambda x: [
        jnp.where(low, ys[x * SPAN_Y + t][:, :128], ys[x * SPAN_Y + t + 1][:, :128]) for t in range(0, SPAN_Y, 2)
    ]
    row = lambda y: jnp.where(low, ys[y][:, 128:], ys[SPAN_Y + y][:, 128:])
    return column(0), column(SPAN_X - 1), row(0), row(SPAN_Y - 1)


def send(ys, x_ref, a_ref, b_ref, at):
    rows = pl.ds(at, ys[0].shape[0])
    west, east, south, north = packs(ys)
    first = lax.axis_index("gx") == 0
    even = lax.axis_index("gy") % 2 == 0
    for t in range(SPAN_Y // 2):
        x_ref[t, rows, :] = jnp.where(first, east[t], west[t])
    a_ref[rows, :] = jnp.where(even, north, south)
    b_ref[rows, :] = jnp.where(even, south, north)


def received(x_ref, a_ref, b_ref, at, n, side=None):
    rows = pl.ds(at, n)
    first = lax.axis_index("gx") == 0
    even = lax.axis_index("gy") % 2 == 0
    xs = [x_ref[t, rows, :] for t in range(SPAN_Y // 2)]
    a, b = a_ref[rows, :], b_ref[rows, :]
    if side is not None:
        a, b = a + side[:, :128], b + side[:, 128:256]
        xs = [xs[t] + side[:, 256 + 128 * t : 384 + 128 * t] for t in range(SPAN_Y // 2)]
    zero = jnp.zeros_like(a)
    return (
        [jnp.where(first, zero, v) for v in xs],
        [jnp.where(first, v, zero) for v in xs],
        jnp.where(even, b, a),
        jnp.where(even, a, b),
    )


def across(ys, nb, rows):
    low = lower(rows)
    zero = jnp.zeros((rows, 128), F32)
    inside = lambda x, y, part: zero if ys is None else ys[x * SPAN_Y + y][:, part * 128 : part * 128 + 128]
    out = []
    for x in range(SPAN_X):
        for y in range(SPAN_Y):
            beyond = lambda v: zero if nb is None else v()
            west = inside(x - 1, y, 0) if x else beyond(lambda: nb[0][y // 2])
            east = inside(x + 1, y, 0) if x < SPAN_X - 1 else beyond(lambda: nb[1][y // 2])
            south = inside(x, y - 1, 1) if y else beyond(lambda: nb[2])
            north = inside(x, y + 1, 1) if y < SPAN_Y - 1 else beyond(lambda: nb[3])
            if (x + y) % 2:
                west, east, south, north = east, west, north, south
            out.append(jnp.concatenate([jnp.where(low, west, east), jnp.where(low, south, north)], 1))
    return out


def owned_lanes(i, rows):
    lane = iota((rows, 256), 1) % 128
    return lane < 64 if odd(i) else lane >= 64


def spread_owned(v, i):
    zero = jnp.zeros_like(v)
    low = lower(v.shape[0])
    turned = pltpu.roll(v, 64, 1)
    if odd(i):
        return jnp.concatenate([jnp.where(low, v, zero), jnp.where(low, turned, zero)], 1)
    return jnp.concatenate([jnp.where(low, zero, turned), jnp.where(low, zero, v)], 1)


def take_owned(v, i):
    low = lower(v.shape[0])
    if odd(i):
        return jnp.where(low, v[:, :128], pltpu.roll(v[:, 128:], 64, 1))
    return jnp.where(low, pltpu.roll(v[:, :128], 64, 1), v[:, 128:])


def start_kernel(res_ref, dir_ref, act_ref, scale_ref, *refs):
    inverse_ref, own_ref, x_ref, a_ref, b_ref = refs[4:9]
    upper_ref = refs[13]
    gx, gy = lax.axis_index("gx"), lax.axis_index("gy")
    last_x = gx * SPAN_X + SPAN_X - 1 == lax.axis_size("gx") * SPAN_X - 1
    last_y = gy * SPAN_Y + SPAN_Y - 1 == lax.axis_size("gy") * SPAN_Y - 1
    east = iota((1, 128), 1) < 64
    ys = []
    for i in range(SUBS):
        x, y = i // SPAN_Y, i % SPAN_Y
        keep = act_ref[i : i + 1, :].astype(F32)
        if x == SPAN_X - 1:
            keep = jnp.where(jnp.logical_and(last_x, east), 0.0, keep)
        if y == SPAN_Y - 1:
            keep = jnp.where(jnp.logical_and(last_y, jnp.logical_not(east)), 0.0, keep)
        mine = pl.ds(i, CASES, stride=SUBS)
        v = jnp.concatenate(
            [
                res_ref[mine, :],
                dir_ref[mine, :] * keep,
                scale_ref[i : i + 1, :] * keep,
                keep,
                jnp.zeros((CAST - 2 * CASES - 2, 128), F32),
            ],
            0,
        )
        v = spread_owned(v, i)
        own_ref[i] = v
        ys.append(v)
    send(ys, x_ref, a_ref, b_ref, 0)
    for ref in (x_ref, a_ref, b_ref):
        ref.flush()
    for t, (i, j) in enumerate(UPPER):
        upper_ref[t] = inverse_ref[128 * i : 128 * i + 128, 128 * j : 128 * j + 128]


def operator_kernel(
    schur_ref, couple_ref, map_ref, slot_ref, high_ref, low_ref, cc_ref, ch_ref, cl_ref, name_ref,
):
    none = 384
    slot = slot_ref[...].astype(F32)
    eye = iota((8, 8), 0) == iota((8, 8), 1)
    column = jnp.concatenate(
        [jnp.sum(jnp.where(eye, jnp.broadcast_to(slot[i : i + 1, :], (8, 8)), 0.0), 1, keepdims=True) for i in range(SUBS)], 0
    )
    row = jnp.concatenate([slot[i : i + 1, :] for i in range(SUBS)], 1)
    count = SUBS * 8
    earlier = iota((count, count), 1) < iota((count, count), 0)
    again = jnp.sum(jnp.where(jnp.logical_and(column == row, earlier), 1.0, 0.0), 1, keepdims=True)
    first = jnp.where(jnp.logical_and(again == 0.0, column != float(none)), 1.0, 0.0)
    first_row = jnp.sum(
        jnp.where(jnp.logical_and(column == row, iota((count, count), 0) < iota((count, count), 1)), 1.0, 0.0), 0, keepdims=True
    )
    first_row = jnp.where(jnp.logical_and(first_row == 0.0, row != float(none)), 1.0, 0.0)
    rank = jnp.sum(jnp.where(row < column, first_row, 0.0), 1, keepdims=True)
    hit = jnp.where(rank == iota((count, 128), 1).astype(F32), first, 0.0)
    name_ref[...] = jnp.broadcast_to(
        jnp.where(jnp.sum(hit, 0, keepdims=True) > 0.0, jnp.sum(hit * column, 0, keepdims=True), float(none)), (8, 128)
    )
    sub = iota((256, 256), 0)
    west = (sub // 64) % 2 == 0
    for i in range(SUBS):
        spots = map_ref[i // SPAN_Y, i % SPAN_Y : i % SPAN_Y + 1, :]
        if odd(i):
            spots = jnp.where((spots // 64) % 2 == 0, spots + 64, spots - 64)
        sign = jnp.where(west, 1.0, -1.0) if odd(i) else jnp.where(west, -1.0, 1.0)
        place = jnp.where(sub == spots, sign, 0.0).astype(BF16)
        mine = slot[i : i + 1, :]
        number = jnp.sum(jnp.where(column < mine, first, 0.0), 0, keepdims=True)
        compact = jnp.where(
            jnp.logical_and(number == iota((SLOTS, 8), 0).astype(F32), mine != float(none)), 1.0, 0.0
        )
        cc = jnp.dot(compact, couple_ref[i], precision=EXACT, preferred_element_type=F32)
        c1, rest = split(cc)
        c2, c3 = split(cc - c1.astype(F32))
        s1, s2 = split(schur_ref[i])
        tall = dot_turned(jnp.concatenate([s1, s2, c1, c2, c3], 0), place)
        high, low = (dot(place, tall[t : t + 256].astype(BF16)).astype(BF16) for t in (0, 256))
        high_ref[i], low_ref[i] = high, low
        cc = tall[512 : 512 + SLOTS] + tall[512 + SLOTS : 512 + 2 * SLOTS] + tall[512 + 2 * SLOTS :]
        cc_ref[i] = cc
        ch_ref[i], cl_ref[i] = split(cc)


def inverse_kernel(mine_ref, upper_ref, high_ref, low_ref):
    first = lax.axis_index("gx") == 0
    mine = mine_ref[...]
    blocks = {spot: upper_ref[t] for t, spot in enumerate(UPPER)}
    side = lambda i, j: blocks[i, j] if i <= j else jnp.transpose(blocks[j, i])
    other = jnp.concatenate([jnp.concatenate([side(i, j) for j in range(3)], 1) for i in range(3)], 0)
    high_ref[0], low_ref[0] = split(jnp.where(first, mine, other))
    high_ref[1], low_ref[1] = split(jnp.where(first, other, mine))


def near_names(name_ref, x_ref, a_ref, b_ref, near_ref):
    named = pl.ds(2 * CASES + SLOTS, 8)
    group = iota((8, 128), 1) // SLOTS
    turn = lambda v, g: jnp.where(group == g, pltpu.roll(v, g * SLOTS, 1), 0.0)
    wanted = name_ref[...] + 0.0
    wanted = jnp.where(group == 0, wanted, turn(a_ref[named, :], 1) + turn(b_ref[named, :], 2) + turn(x_ref[0, named, :], 3))
    found = iota((384, 128), 0).astype(F32) == wanted[0:1]
    mine = jnp.where(iota((384, 128), 1) < 3 * SLOTS, 1.0, 0.0)
    gx = lax.axis_index("gx")
    for region in range(2):
        near_ref[region] = jnp.where(found, jnp.where(gx == region, mine, 1.0 - mine), 0.0).astype(BF16)


def near_spread(x_ref, a_ref, b_ref, nh_ref, nl_ref):
    rows = pl.ds(2 * CASES, SLOTS)
    blank = jnp.zeros((SLOTS, 128), F32)
    parts = [
        [blank] * 4,
        [a_ref[rows, :], blank, blank, blank],
        [blank, b_ref[rows, :], blank, blank],
        [blank, blank, x_ref[0, rows, :], x_ref[1, rows, :]],
    ]
    nh_ref[...], nl_ref[...] = split(jnp.concatenate([jnp.concatenate(row, 1) for row in parts], 0))


def operator(ys, x_ref, a_ref, b_ref, near, mk_ref, ch_ref, cl_ref, nh_ref, nl_ref):
    n = ys[0].shape[0]
    side = dot_split(near, nh_ref[...], nl_ref[...])
    west, east, south, north = received(x_ref, a_ref, b_ref, 0, n, side)
    mine = near[:, :SLOTS]
    ys = [ys[i] + dot_split(mine, ch_ref[i], cl_ref[i]) for i in range(SUBS)]
    other = across(ys, (west, east, south, north), n)
    return [mk_ref[i, 1:2, :] * (ys[i] + other[i]) for i in range(SUBS)]


def local_part(us, high_ref, low_ref, ch_ref, cl_ref):
    ys = [dot_split(us[i], high_ref[i], low_ref[i]) for i in range(SUBS)]
    n = us[0].shape[0]
    couple = lambda ref: jnp.concatenate([ref[i] for i in range(SUBS)], 0)
    corner = dot_split(jnp.concatenate(us, 0), couple(ch_ref), couple(cl_ref), dot_turned)
    group = iota((n, 128), 1) // SLOTS
    total = jnp.zeros((n, 128), F32)
    for i in range(SUBS):
        part = corner[n * i : n * i + n, 128 * (i // 4) : 128 * (i // 4) + 128]
        total = total + jnp.where(group == i % 4, part, 0.0)
    total = total + pltpu.roll(total, 64, 1)
    total = total + pltpu.roll(total, 32, 1)
    return ys, total


def over_lanes(terms):
    total = terms[0]
    for t in terms[1:]:
        total = total + t
    return jnp.sum(total[:, :128] + total[:, 128:], 1, keepdims=True)


def packed(corner, one, two):
    slot = iota((CASES, 128), 1) % SLOTS
    full = jnp.where(slot == USED, one, jnp.where(slot == USED + 1, two, corner))
    group = iota((4, 128), 1) // SLOTS
    out = jnp.zeros((4, 128), F32)
    for b in range(4):
        out = jnp.where(group == b, full[4 * b : 4 * b + 4], out)
    return out


def by_slot(vs):
    group = iota((8, 128), 1) // SLOTS
    out = []
    for region in range(2):
        rows = []
        for b in range(4):
            halves = []
            for h in range(2):
                acc = None
                for q in range(4):
                    v = vs[8 * region + 4 * h + q]
                    turned = v if q == b else pltpu.roll(v, (SLOTS * (q - b)) % 128, 1)
                    acc = turned if acc is None else jnp.where(group == q, turned, acc)
                halves.append(acc)
            rows.append(jnp.concatenate(halves, 1))
        out.append(jnp.concatenate(rows, 0))
    return out


def inner(vs):
    total = vs[0]
    for v in vs[1:]:
        total = total + v
    total = total[:4] + total[4:]
    tall = jnp.concatenate([total] * 4, 0)
    lane, row = iota((CASES, 128), 1), iota((CASES, 128), 0)
    column = lambda s: jnp.sum(jnp.where(lane == SLOTS * (row // 4) + s, tall, 0.0), 1, keepdims=True)
    return column(USED), column(USED + 1)


def first_of_pairs(v):
    return jnp.concatenate([v[8 * b : 8 * b + 4] for b in range(v.shape[0] // 8)], 0)


def solve(spots, pick_ref, gh_ref, gl_ref, near_ref):
    totals, sols, near = [], [], None
    for region in range(2):
        v = spots[region]
        n = v.shape[0]
        even = dot_exact(v, pick_ref[region, 0])
        odds = dot_exact(v, pick_ref[region, 1])
        z = jnp.where((iota((n, 384), 0) // 4) % 2 == 0, even, odds).reshape(n // 8, 8, 384)
        total = (z + pltpu.roll(z, 4, 1)).reshape(n, 384)
        sol = dot_split(total, gh_ref[region], gl_ref[region])
        part = dot_exact(sol, near_ref[region])
        near = part if near is None else near + part
        totals.append(total)
        sols.append(sol)
    return totals, sols, near


def energy(totals, sols):
    both = totals[0] * sols[0] + totals[1] * sols[1]
    return first_of_pairs(jnp.sum(both, 1, keepdims=True))


def emit(rs, mk_ref, high_ref, low_ref, ch_ref, cl_ref, block_ref, y_ref, x_ref, a_ref, b_ref):
    us = [mk_ref[i, 0:1, :] * rs[i] for i in range(SUBS)]
    ys, corner = local_part(us, high_ref, low_ref, ch_ref, cl_ref)
    send(ys, x_ref, a_ref, b_ref, 0)
    for i in range(SUBS):
        y_ref[i] = ys[i]
    for ref in (x_ref, a_ref, b_ref, y_ref):
        ref.flush()
    rho = over_lanes([jnp.where(owned_lanes(i, CASES), rs[i] * us[i], 0.0) for i in range(SUBS)])
    delta = over_lanes([us[i] * ys[i] for i in range(SUBS)])
    block = packed(corner, rho, delta)
    twice = jnp.concatenate([block, block], 0)
    for j in range(16):
        block_ref[j] = twice


def first_kernel(
    own_ref, x_ref, a_ref, b_ref, high_ref, low_ref, cc_ref, ch_ref, cl_ref, name_ref,
    r_ref, p_ref, mk_ref, y_ref, block_ref, sx_ref, sa_ref, sb_ref, high_out_ref, low_out_ref,
):
    own = [own_ref[i] for i in range(SUBS)]
    other = across(own, received(x_ref, a_ref, b_ref, 0, CAST), CAST)
    rs, vs = [], []
    for i in range(SUBS):
        full = own[i] + other[i]
        rs.append(full[:CASES])
        r_ref[i] = full[:CASES]
        p_ref[i] = full[CASES : 2 * CASES]
        mk_ref[i] = full[2 * CASES : 2 * CASES + 8]
        vs.append(jnp.concatenate([full[2 * CASES : 2 * CASES + 1] * full[:CASES], full[CASES : 2 * CASES]], 0))
    ys, corner = local_part(vs, high_ref, low_ref, ch_ref, cl_ref)
    names = name_ref[...]
    send([jnp.concatenate([ys[i], cc_ref[i]], 0) for i in range(SUBS)], sx_ref, sa_ref, sb_ref, 0)
    at = pl.ds(2 * CASES + SLOTS, 8)
    for t in range(SPAN_Y // 2):
        sx_ref[t, at, :] = names
    sa_ref[at, :] = names
    sb_ref[at, :] = names
    us = [v[:CASES] for v in vs]
    ps = [v[CASES:] for v in vs]
    rho = over_lanes([jnp.where(owned_lanes(i, CASES), rs[i] * us[i], 0.0) for i in range(SUBS)])
    delta = over_lanes([us[i] * ys[i][:CASES] for i in range(SUBS)])
    cross = over_lanes([ps[i] * ys[i][:CASES] for i in range(SUBS)])
    eta = over_lanes([ps[i] * ys[i][CASES:] for i in range(SUBS)])
    one, two = packed(corner[:CASES], rho, delta), packed(corner[CASES:], cross, eta)
    blocks = [
        jnp.concatenate([one, two], 0),
        jnp.concatenate([names[:4], one], 0),
        jnp.concatenate([two, names[:4]], 0),
    ]
    for j in range(16):
        for t in range(3):
            block_ref[3 * j + t] = blocks[t]
    for i in range(SUBS):
        y_ref[i] = ys[i]


def column_of(row):
    eye = iota((CASES, CASES), 0) == iota((CASES, CASES), 1)
    return jnp.sum(jnp.where(eye, jnp.broadcast_to(row, (CASES, CASES)), 0.0), 1, keepdims=True)


def keep_scalars(scal_ref, values):
    for t, v in enumerate(values):
        scal_ref[t] = jnp.broadcast_to(v, (CASES, 128))


def second_kernel(
    got_ref, x_ref, a_ref, b_ref, y_ref, r_ref, p_ref, mk_ref, dual_ref, rho_ref, gh_ref, gl_ref, name_ref,
    high_ref, low_ref, ch_ref, cl_ref,
    pick_ref, near_ref, nh_ref, nl_ref, ro_ref, so_ref, po_ref, lo_ref, scal_ref, block_ref, yo_ref, sx_ref, sa_ref, sb_ref,
):
    near_names(name_ref, x_ref, a_ref, b_ref, near_ref)
    near_spread(x_ref, a_ref, b_ref, nh_ref, nl_ref)
    top = iota((8, 128), 0) < 4
    us, ps, names = [], [], []
    for j in range(16):
        v = [got_ref[3 * j + t] for t in range(3)]
        us.append(jnp.where(top, v[0], v[1]))
        ps.append(pltpu.roll(jnp.where(top, v[2], v[0]), 4, 0))
        names.append((v[1], pltpu.roll(v[2], 4, 0)))
    group = iota((8, 128), 1) // SLOTS
    for region in range(2):
        for par in range(2):
            halves = []
            for h in range(2):
                acc = None
                for q in range(4):
                    v = names[8 * region + 4 * h + q][par]
                    turned = pltpu.roll(v, SLOTS * q, 1) if q else v
                    acc = turned if acc is None else jnp.where(group == q, turned, acc)
                halves.append(acc[0:1])
            wanted = jnp.concatenate(halves, 1)
            hit = jnp.where(iota((384, 256), 0).astype(F32) == wanted, 1.0, 0.0)
            pick_ref[region, par] = jnp.transpose(hit).astype(BF16)
    lhs_u, lhs_p = by_slot(us), by_slot(ps)
    n = lhs_u[0].shape[0]
    totals, sols, near = solve(
        [jnp.concatenate([lhs_u[t], lhs_p[t]], 0) for t in range(2)], pick_ref, gh_ref, gl_ref, near_ref
    )
    of_u, of_p = lambda vs: [v[:n] for v in vs], lambda vs: [v[n:] for v in vs]
    rho, delta = inner(us)
    cross, eta = inner(ps)
    delta = delta + energy(of_u(totals), of_u(sols))
    cross = cross + energy(of_p(totals), of_u(sols))
    eta = eta + energy(of_p(totals), of_p(sols))
    near = first_of_pairs(near)
    beta = rho / column_of(rho_ref[...])
    skew = cross + beta * eta
    pi = delta + 2.0 * beta * skew - beta * beta * eta
    alpha = rho / pi
    fs = operator([y_ref[i] for i in range(SUBS)], x_ref, a_ref, b_ref, near, mk_ref, ch_ref, cl_ref, nh_ref, nl_ref)
    rs = []
    for i in range(SUBS):
        f, r = fs[i], r_ref[i]
        p = mk_ref[i, 0:1, :] * r + beta * p_ref[i]
        s = f[:CASES] + beta * f[CASES:]
        r = r - alpha * s
        rs.append(r)
        ro_ref[i], so_ref[i], po_ref[i] = r, s, p
        lo_ref[i] = spread_owned(dual_ref[pl.ds(i, CASES, stride=SUBS), :], i) + alpha * p
    keep_scalars(scal_ref, (rho, pi, beta, skew))
    for ref in (pick_ref, near_ref, nh_ref, nl_ref, ro_ref, so_ref, po_ref, lo_ref, scal_ref):
        ref.flush()
    emit(rs, mk_ref, high_ref, low_ref, ch_ref, cl_ref, block_ref, yo_ref, sx_ref, sa_ref, sb_ref)


def absorb(got_ref, x_ref, a_ref, b_ref, y_ref, r_ref, s_ref, p_ref, l_ref, scal_ref, mk_ref, pick_ref, gh_ref, gl_ref, near_ref, nh_ref, nl_ref, ch_ref, cl_ref):
    vs = [got_ref[j] for j in range(16)]
    totals, sols, near = solve(by_slot(vs), pick_ref, gh_ref, gl_ref, near_ref)
    rho, delta = inner(vs)
    delta = delta + energy(totals, sols)
    near = first_of_pairs(near)
    rho_old, pi, beta, skew = (scal_ref[t][:, 0:1] for t in range(4))
    skew = beta * skew
    beta = rho / rho_old
    pi = delta + 2.0 * beta * skew - beta * beta * pi
    alpha = rho / pi
    fs = operator([y_ref[i] for i in range(SUBS)], x_ref, a_ref, b_ref, near, mk_ref, ch_ref, cl_ref, nh_ref, nl_ref)
    out = []
    for i in range(SUBS):
        r = r_ref[i]
        p = mk_ref[i, 0:1, :] * r + beta * p_ref[i]
        s = fs[i] + beta * s_ref[i]
        out.append((r - alpha * s, s, p, l_ref[i] + alpha * p))
    return out, (rho, pi, beta, skew)


def round_kernel(
    got_ref, x_ref, a_ref, b_ref, y_ref, r_ref, s_ref, p_ref, l_ref, scal_ref, mk_ref, pick_ref, gh_ref, gl_ref, near_ref,
    nh_ref, nl_ref, ch_ref, cl_ref, high_ref, low_ref,
    ro_ref, so_ref, po_ref, lo_ref, scalo_ref, block_ref, yo_ref, sx_ref, sa_ref, sb_ref,
):
    out, scalars = absorb(
        got_ref, x_ref, a_ref, b_ref, y_ref, r_ref, s_ref, p_ref, l_ref, scal_ref, mk_ref, pick_ref, gh_ref, gl_ref, near_ref,
        nh_ref, nl_ref, ch_ref, cl_ref,
    )
    for i, (r, s, p, lam) in enumerate(out):
        ro_ref[i], so_ref[i], po_ref[i], lo_ref[i] = r, s, p, lam
    keep_scalars(scalo_ref, scalars)
    for ref in (ro_ref, so_ref, po_ref, lo_ref, scalo_ref):
        ref.flush()
    emit([v[0] for v in out], mk_ref, high_ref, low_ref, ch_ref, cl_ref, block_ref, yo_ref, sx_ref, sa_ref, sb_ref)


def last_kernel(
    got_ref, x_ref, a_ref, b_ref, y_ref, r_ref, s_ref, p_ref, l_ref, scal_ref, mk_ref, pick_ref, gh_ref, gl_ref, near_ref,
    nh_ref, nl_ref, ch_ref, cl_ref, lo_ref, ro_ref, po_ref,
):
    out, _ = absorb(
        got_ref, x_ref, a_ref, b_ref, y_ref, r_ref, s_ref, p_ref, l_ref, scal_ref, mk_ref, pick_ref, gh_ref, gl_ref, near_ref,
        nh_ref, nl_ref, ch_ref, cl_ref,
    )
    for i, (r, _, p, lam) in enumerate(out):
        mine = pl.ds(i, CASES, stride=SUBS)
        lo_ref[mine, :] = take_owned(lam, i)
        ro_ref[mine, :] = take_owned(r, i)
        po_ref[mine, :] = take_owned(p, i)


class Fetched:
    def __init__(self, source, buffer, semaphore):
        self.buffer = buffer
        self.copy = pltpu.make_async_copy(source, buffer, semaphore)
        self.copy.start()
        self.here = False

    def __getitem__(self, index):
        if not self.here:
            self.copy.wait()
            self.here = True
        return self.buffer[index]


class Stored:
    def __init__(self, target, buffer, semaphore):
        self.buffer = buffer
        self.copy = pltpu.make_async_copy(buffer, target, semaphore)
        self.sent = False

    def __setitem__(self, index, value):
        self.buffer[index] = value

    def __getitem__(self, index):
        return self.buffer[index]

    def flush(self):
        if not self.sent:
            self.copy.start()
            self.sent = True


class Kept:
    def __init__(self, ref):
        self.ref = ref

    def __setitem__(self, index, value):
        self.ref[index] = value

    def __getitem__(self, index):
        return self.ref[index]

    def flush(self):
        pass


def call(kernel, args, outs, kept=(), kept_out=(), raw=(), through=None, flops=None):
    through = through or {}
    moved = [i for i in range(len(args)) if i not in kept and i not in raw]
    written = [i for i in range(len(outs)) if i not in kept_out and i not in through]

    def body(*refs):
        ins, results = refs[: len(args)], refs[len(args) : len(args) + len(outs)]
        buffers, (in_sem, out_sem, through_sem) = refs[len(args) + len(outs) : -3], refs[-3:]
        fetched, stored = list(ins), [Kept(ref) for ref in results]
        for t, i in enumerate(moved):
            fetched[i] = Fetched(ins[i], buffers[t], in_sem.at[t])
        for t, i in enumerate(written):
            stored[i] = Stored(results[i], buffers[len(moved) + t], out_sem.at[t])
        passing = [
            pltpu.make_async_copy(source(ins), results[i], through_sem.at[t]) for t, (i, source) in enumerate(through.items())
        ]
        for copy in passing:
            copy.start()
        kernel(*fetched, *stored)
        for i in written:
            stored[i].flush()
        for i in moved:
            if not fetched[i].here:
                fetched[i].copy.wait()
        for copy in passing:
            copy.wait()
        for i in written:
            stored[i].copy.wait()

    place = lambda held: pl.BlockSpec(memory_space=pltpu.VMEM if held else pltpu.HBM)
    semaphores = lambda n: pltpu.SemaphoreType.DMA((max(n, 1),))
    args = [a if i in kept else pltpu.with_memory_space_constraint(a, pltpu.HBM) for i, a in enumerate(args)]
    return pl.pallas_call(
        body,
        out_shape=[
            jax.ShapeDtypeStruct(*out) if i in kept_out else pltpu.HBM(*out) for i, out in enumerate(outs)
        ],
        in_specs=[place(i in kept) for i in range(len(args))],
        out_specs=[place(i in kept_out) for i in range(len(outs))],
        scratch_shapes=[pltpu.VMEM(args[i].shape, args[i].dtype) for i in moved]
        + [pltpu.VMEM(*outs[i]) for i in written]
        + [semaphores(len(moved)), semaphores(len(written)), semaphores(len(through))],
        compiler_params=pltpu.CompilerParams(vmem_limit_bytes=LIMIT),
        cost_estimate=flops and pl.CostEstimate(flops=flops, bytes_accessed=flops // 512, transcendentals=0),
    )(*args)


def trade(x, a, b):
    peers = lax.axis_size("gy")
    return (
        lax.ppermute(x, "gx", [(0, 1), (1, 0)]),
        lax.ppermute(a, "gy", both_ways(pairs_from(0, peers))),
        lax.ppermute(b, "gy", both_ways(pairs_from(1, peers))),
    )


def two_regions(
    duals, residual, direction, prev_rho, dual_schur, coupling, coarse_inverse, edge_map, corner_slot, active, scaling
):
    native = lambda v: v.reshape(CASES * SUBS, 128)
    by_sub = lambda v: v.reshape((SUBS,) + v.shape[2:])
    width = coarse_inverse.shape[-1]
    sends = lambda rows: [((SPAN_Y // 2, rows, 128), F32), ((rows, 128), F32), ((rows, 128), F32)]
    state = ((SUBS, CASES, 256), F32)

    raw = [by_sub(dual_schur), by_sub(coupling), edge_map, by_sub(corner_slot)]
    own, *out, schur, coupled, placed, slotted, inverse = call(
        start_kernel,
        [native(residual), native(direction), by_sub(active), by_sub(scaling), *raw, coarse_inverse[0]],
        [((SUBS, CAST, 256), F32)] + sends(CAST) + [(v.shape, v.dtype) for v in raw] + [((len(UPPER), 128, 128), F32)],
        kept_out=(0, 4, 5, 6, 7),
        raw=(4, 5, 6, 7),
        through={4: lambda v: v[4], 5: lambda v: v[5], 6: lambda v: v[6], 7: lambda v: v[7]},
    )
    come = trade(*out)
    other = lax.ppermute(inverse, "gx", [(0, 1), (1, 0)])
    matrix = ((SUBS, 256, 256), BF16)
    couple = ((SUBS, SLOTS, 256), BF16)
    high, low, cc, ch, cl, names = call(
        operator_kernel,
        [schur, coupled, placed, slotted],
        [matrix, matrix, ((SUBS, SLOTS, 256), F32), couple, couple, ((8, 128), F32)],
        kept=range(4),
        kept_out=range(6),
        flops=5 * 10**9,
    )
    rows = 2 * CASES + SLOTS + 8
    r, p, mk, y, block, *out, high, low = call(
        first_kernel,
        [own, *come, high, low, cc, ch, cl, names],
        [state, state, ((SUBS, 8, 256), F32), ((SUBS, 2 * CASES, 256), F32), ((48, 8, 128), F32)]
        + sends(rows)
        + [matrix, matrix],
        kept=range(10),
        kept_out=(2, 3),
        through={8: lambda v: v[4], 9: lambda v: v[5]},
    )
    got = lax.all_to_all(block.reshape(32, 3, 4, 128), BOTH, 0, 0, tiled=False).reshape(48, 8, 128)
    come = trade(*out)
    square = ((2, width, width), BF16)
    gh, gl = call(inverse_kernel, [coarse_inverse[0], other], [square, square], kept_out=(0, 1), flops=10**9)
    side = ((128, 512), BF16)
    onward = [state, state, state, state, ((4, CASES, 128), F32), ((16, 8, 128), F32), state] + sends(CASES)
    pick, near, nh, nl, r, s, p, lam, scal, block, y, *out = call(
        second_kernel,
        [got, *come, y, r, p, mk, native(duals), prev_rho.reshape(1, CASES), gh, gl, names, high, low, ch, cl],
        [((2, 2, 256, width), BF16), ((2, width, 128), BF16), side, side] + onward,
        kept=(0, 1, 2, 3, 4, 7, 10, 11, 12, 15, 16),
        kept_out=(0, 1, 2, 3, 8, 10),
    )
    for step in range(1, ITERS):
        got = lax.all_to_all(block.reshape(32, 4, 128), BOTH, 0, 0, tiled=False).reshape(16, 8, 128)
        come = trade(*out)
        args = [got, *come, y, r, s, p, lam, scal, mk, pick, gh, gl, near, nh, nl, ch, cl]
        kept = (0, 1, 2, 3, 4, *range(9, 19))
        if step < ITERS - 1:
            r, s, p, lam, scal, block, y, *out = call(round_kernel, args + [high, low], onward, kept, kept_out=(4, 6))
        else:
            plain = ((CASES * SUBS, 128), F32)
            results = call(last_kernel, args, [plain, plain, plain], kept)
    return tuple(v.reshape(duals.shape) for v in results)


def shards(*args):
    cases, span_x, span_y, owned = args[0].shape
    fits = (cases, span_x, span_y, owned, args[6].shape[-1]) == (CASES, SPAN_X, SPAN_Y, 128, 384)
    if fits and lax.axis_size("gx") == 2 and lax.axis_size("gy") == 16:
        return two_regions(*args)
    return general(*args)


def solution(mesh):
    placed = (
        P(None, "gx", "gy", None),
        P(None, "gx", "gy", None),
        P(None, "gx", "gy", None),
        P(),
        P("gx", "gy", None, None),
        P("gx", "gy", None, None),
        P("gx", None, None),
        P("gx", "gy", None),
        P("gx", "gy", None),
        P("gx", "gy", None),
        P("gx", "gy", None),
    )
    return jax.shard_map(
        shards,
        mesh=mesh,
        in_specs=placed,
        out_specs=(P(None, "gx", "gy", None), P(None, "gx", "gy", None), P(None, "gx", "gy", None)),
        check_vma=False,
    )
```

```python
import jax
import jax.numpy as jnp
from jax import lax
from jax.experimental import pallas as pl
from jax.experimental.pallas import tpu as pltpu
from jax.sharding import PartitionSpec as P

ITERS = 6
HIGH = lax.Precision.HIGH
EXACT = lax.Precision.HIGHEST
BOTH = ("gx", "gy")


def pairs_from(first, peers):
    return [(i, i + 1) for i in range(first, peers - 1, 2)]


def both_ways(pairs):
    return pairs + [(b, a) for a, b in pairs]


def up_gy(value, peers):
    even = lax.ppermute(value, "gy", pairs_from(0, peers))
    odd = lax.ppermute(value, "gy", pairs_from(1, peers))
    return jnp.where(lax.axis_index("gy") % 2 == 1, even, odd)


def swap_gy(low, high, peers):
    is_even = lax.axis_index("gy") % 2 == 0
    first = lax.ppermute(jnp.where(is_even, high, low), "gy", both_ways(pairs_from(0, peers)))
    second = lax.ppermute(jnp.where(is_even, low, high), "gy", both_ways(pairs_from(1, peers)))
    return jnp.where(is_even, second, first), jnp.where(is_even, first, second)


def swap_gx(low, high, peers):
    if peers == 2:
        is_first = lax.axis_index("gx") == 0
        got = lax.ppermute(jnp.where(is_first, high, low), "gx", [(0, 1), (1, 0)])
        zero = jnp.zeros_like(got)
        return jnp.where(is_first, zero, got), jnp.where(is_first, got, zero)
    below = lax.ppermute(high, "gx", [(i, i + 1) for i in range(peers - 1)])
    above = lax.ppermute(low, "gx", [(i + 1, i) for i in range(peers - 1)])
    return below, above


def everywhere(block, axes):
    sent = jnp.broadcast_to(block[None], (lax.axis_size(axes),) + block.shape)
    return lax.all_to_all(sent, axes, 0, 0, tiled=False)


def general(
    duals, residual, direction, prev_rho, dual_schur, coupling, coarse_inverse, edge_map, corner_slot, active, scaling
):
    cases, span_x, span_y, owned = duals.shape
    half = owned // 2
    full = 2 * owned
    corners = coupling.shape[2]
    width_c = coarse_inverse.shape[-1]
    peers_x, peers_y = lax.axis_size("gx"), lax.axis_size("gy")
    whole = peers_x == 2
    axes = BOTH if whole else "gy"
    regions = peers_x if whole else 1
    peers = regions * peers_y
    here_x, here_y = lax.axis_index("gx"), lax.axis_index("gy")
    used = 2 * (span_x + 1) * (span_y + 1)
    slots = used + 2

    columns = here_x * span_x + jnp.arange(span_x)
    rowset = here_y * span_y + jnp.arange(span_y)
    east_ok = jnp.broadcast_to((columns < span_x * peers_x - 1)[:, None, None], (span_x, span_y, half))
    north_ok = jnp.broadcast_to((rowset < span_y * peers_y - 1)[None, :, None], (span_x, span_y, half))
    keep_own = active.astype(jnp.float32) * jnp.concatenate([east_ok, north_ok], -1).astype(jnp.float32)
    scale_own = keep_own * scaling

    by_place = lambda v: jnp.transpose(v, (1, 2, 0, 3))
    lam = by_place(duals)
    p = keep_own[:, :, None] * by_place(direction)
    stacked = jnp.concatenate([by_place(residual), p, scale_own[:, :, None], keep_own[:, :, None]], 2)
    part_e, part_n = stacked[..., :half], stacked[..., half:]
    from_west = lax.ppermute(part_e[-1], "gx", [(i, i + 1) for i in range(peers_x - 1)])
    from_south = up_gy(part_n[:, -1], peers_y)
    west = jnp.concatenate([from_west[None], part_e[:-1]], 0)
    south = jnp.concatenate([from_south[:, None], part_n[:, :-1]], 1)
    stacked = jnp.concatenate([west, part_e, south, part_n], -1)
    r = stacked[:, :, :cases]
    p_all = stacked[:, :, cases : 2 * cases]
    scale = stacked[:, :, 2 * cases : 2 * cases + 1]
    keep = stacked[:, :, 2 * cases + 1 :]

    sign = jnp.concatenate([-jnp.ones(half), jnp.ones(half), -jnp.ones(half), jnp.ones(half)]).astype(jnp.float32)
    place = (edge_map[..., None] == jnp.arange(full, dtype=jnp.int32)).astype(jnp.float32) * sign
    schur = jnp.einsum("xyij,xyjf->xyif", dual_schur, place, precision=EXACT)
    schur = jnp.einsum("xyie,xyif->xyef", place, schur, precision=EXACT)
    couple = jnp.einsum("xycj,xyjf->xycf", coupling, place, precision=EXACT)

    flat = corner_slot.reshape(-1)
    count = flat.shape[0]
    order = jnp.arange(count)
    same = flat[:, None] == flat[None, :]
    first = ~jnp.any(same & (order[None, :] < order[:, None]), 1) & (flat != width_c)
    rank = jnp.sum((flat[None, :] < flat[:, None]) & first[None, :], 1)
    local_slot = jnp.arange(slots)
    compact = ((rank[:, None] == local_slot) & (flat != width_c)[:, None]).astype(jnp.float32)
    named = jnp.where(
        jnp.any(compact > 0, 0), jnp.max(compact * flat[:, None].astype(jnp.float32), 0), float(width_c)
    )
    compact = compact.reshape(span_x, span_y, corners, slots)
    gather_c = jnp.einsum("xycs,xycf->xysf", compact, couple, precision=EXACT)

    blocks = lambda a: (a[..., :half], a[..., half : 2 * half], a[..., 2 * half : 3 * half], a[..., 3 * half :])

    def jump(y, from_w, from_e, from_s, from_n):
        w, e, s, n = blocks(y)
        w_nb = jnp.concatenate([from_w[None], e[:-1]], 0)
        e_nb = jnp.concatenate([w[1:], from_e[None]], 0)
        s_nb = jnp.concatenate([from_s[:, None], n[:, :-1]], 1)
        n_nb = jnp.concatenate([s[:, 1:], from_n[:, None]], 1)
        return jnp.concatenate([w + w_nb, e + e_nb, s + s_nb, n + n_nb], -1)

    def rims(y):
        w, e, s, n = blocks(y)
        return w[0], e[-1], s[:, 0], n[:, -1]

    def exchange(y):
        w, e, s, n = rims(y)
        from_w, from_e = swap_gx(w, e, peers_x)
        from_s, from_n = swap_gy(s, n, peers_y)
        return from_w, from_e, from_s, from_n

    def put(rim, name):
        zero = jnp.zeros((span_x, span_y, rim.shape[-2], half), jnp.float32)
        parts = [zero, zero, zero, zero]
        if name == 0:
            parts[0] = zero.at[0].set(rim)
        elif name == 1:
            parts[1] = zero.at[-1].set(rim)
        elif name == 2:
            parts[2] = zero.at[:, 0].set(rim)
        else:
            parts[3] = zero.at[:, -1].set(rim)
        return jnp.concatenate(parts, -1)

    nb = exchange(gather_c)
    none = [jnp.zeros_like(v) for v in nb]
    spread = jnp.concatenate([jump(gather_c, *none)] + [put(v, i) for i, v in enumerate(nb)], 2)
    spread = spread * keep

    region_inv = coarse_inverse[0]

    def local_part(v):
        y = jnp.einsum("xykj,xyji->xyki", v, schur, precision=HIGH)
        c = jnp.einsum("xykj,xysj->ks", v, gather_c[:, :, :used], precision=HIGH)
        return y, c

    def over_cases(a, b):
        return jnp.sum(a * b, axis=(0, 1, 3))

    def pack(c, one, two):
        return jnp.concatenate([c, one[:, None], two[:, None]], 1).reshape(-1, 128)

    def unpack(got):
        got = got.reshape(peers, cases, slots)
        sums = jnp.sum(got[:, :, used:], 0)
        return jnp.transpose(got, (1, 0, 2)).reshape(cases, regions, peers_y, slots), sums[:, 0], sums[:, 1]

    def own_part(a):
        return jnp.concatenate([a[..., half : 2 * half], a[..., 3 * half :]], -1)

    u = scale * r
    both = jnp.concatenate([u, p_all], 2)
    y, c = local_part(both)
    yu, yp = y[:, :, :cases], y[:, :, cases:]
    rho_part = over_cases(own_part(r), own_part(u))
    names = jnp.concatenate([named, jnp.zeros(4 * 128 - slots, jnp.float32)]).reshape(4, 128)
    block = jnp.concatenate(
        [pack(c[:cases], rho_part, over_cases(u, yu)), pack(c[cases:], over_cases(p_all, yu), over_cases(p_all, yp)), names]
    )
    got = everywhere(block, axes)
    from_all = exchange(y)

    rows = cases * slots // 128
    slot_of = got[:, 2 * rows :].reshape(peers, -1)[:, :slots].reshape(regions, peers_y * slots)

    if whole:
        other = lax.ppermute(region_inv, "gx", [(0, 1), (1, 0)])
        inverses = jnp.where(here_x == 0, jnp.stack([region_inv, other]), jnp.stack([other, region_inv]))
    else:
        inverses = region_inv[None]
    pick = (slot_of[..., None] == jnp.arange(width_c, dtype=jnp.float32)).astype(jnp.float32)
    dense = jnp.einsum("ran,rnm->ram", pick, inverses, precision=EXACT)
    dense = jnp.einsum("ram,rbm->rab", dense, pick, precision=EXACT)

    def solve(c_all):
        flat_c = c_all.reshape(cases, regions, peers_y * slots)
        sol = jnp.einsum("kra,rab->krb", flat_c, dense, precision=HIGH)
        return flat_c, sol

    def total(a, b):
        return jnp.sum(a * b, (1, 2))

    def over_gx(*sums):
        return sums if whole else tuple(lax.psum(jnp.stack(sums), "gx"))

    def at(sol, ix, dy):
        sol = sol.reshape(cases, regions, peers_y, slots)
        iy = jnp.clip(here_y + dy, 0, peers_y - 1)
        return lax.dynamic_slice(sol, (0, ix, iy, 0), (cases, 1, 1, slots))[:, 0, 0]

    def beside(sol):
        if whole:
            return at(sol, 0, 0), at(sol, 1, 0)
        mine = at(sol, 0, 0)
        return swap_gx(mine, mine, peers_x)

    def coarse_part(sol):
        mine = here_x if whole else 0
        near = jnp.concatenate([at(sol, mine, 0), *beside(sol), at(sol, mine, -1), at(sol, mine, 1)], 1)
        return jnp.einsum("kn,xynj->xykj", near, spread, precision=HIGH)

    cu, rho, delta = unpack(got[:, :rows])
    cp, cross, eta = unpack(got[:, rows : 2 * rows])
    cu, su = solve(cu)
    cp, sp = solve(cp)
    delta, cross, eta = delta + total(cu, su), cross + total(cu, sp), eta + total(cp, sp)
    rho, delta, cross, eta = over_gx(rho, delta, cross, eta)
    f_both = keep * jump(y, *from_all)
    w = f_both[:, :, :cases] + coarse_part(su)
    s = f_both[:, :, cases:] + coarse_part(sp)

    wide = lambda a: a[None, None, :, None]
    beta = rho / prev_rho
    skew = cross + beta * eta
    pi = delta + 2.0 * beta * skew - beta * beta * eta
    for step in range(ITERS):
        if step > 0:
            u = scale * r
            y, c = local_part(u)
            block = pack(c, over_cases(own_part(r), own_part(u)), over_cases(u, y))
            got = everywhere(block, axes)
            from_all = exchange(y)
            rho_old = rho
            c_all, rho, delta = unpack(got)
            c_all, sol = solve(c_all)
            rho, delta = over_gx(rho, delta + total(c_all, sol))
            w = keep * jump(y, *from_all) + coarse_part(sol)
            skew = beta * skew
            beta = rho / rho_old
            pi = delta + 2.0 * beta * skew - beta * beta * pi
        alpha = rho / pi
        p = own_part(u) + wide(beta) * p
        s = w + wide(beta) * s
        lam = lam + wide(alpha) * p
        r = r - wide(alpha) * s
    back = lambda v: jnp.transpose(v, (2, 0, 1, 3))
    return back(lam), back(own_part(r)), back(p)


F32, BF16 = jnp.float32, jnp.bfloat16
SPAN_X, SPAN_Y = 2, 4
SUBS = SPAN_X * SPAN_Y
CASES = 16
SLOTS = 32
USED = 2 * (SPAN_X + 1) * (SPAN_Y + 1)
CAST = 40
LIMIT = 16 * 1024 * 1024
UPPER = [(i, j) for i in range(3) for j in range(i, 3)]


def iota(shape, dim):
    return lax.broadcasted_iota(jnp.int32, shape, dim)


def split(v):
    high = v.astype(BF16)
    return high, (v - high.astype(F32)).astype(BF16)


def dot(a, b):
    return jnp.dot(a, b, preferred_element_type=F32)


def dot_turned(a, b):
    return lax.dot_general(a, b, (((1,), (1,)), ((), ())), preferred_element_type=F32)


def dot_split(v, high, low, dot=dot):
    n = v.shape[0]
    vh, vl = split(v)
    wide = dot(jnp.concatenate([vh, vl], 0), high)
    return wide[:n] + wide[n:] + dot(vh, low)


def dot_exact(v, ones):
    n = v.shape[0]
    vh, vl = split(v)
    wide = dot(jnp.concatenate([vh, vl], 0), ones)
    return wide[:n] + wide[n:]


def odd(i):
    return (i // SPAN_Y + i % SPAN_Y) % 2


def lower(rows):
    return iota((rows, 128), 1) < 64


def packs(ys):
    rows = ys[0].shape[0]
    low = lower(rows)
    column = lambda x: [
        jnp.where(low, ys[x * SPAN_Y + t][:, :128], ys[x * SPAN_Y + t + 1][:, :128]) for t in range(0, SPAN_Y, 2)
    ]
    row = lambda y: jnp.where(low, ys[y][:, 128:], ys[SPAN_Y + y][:, 128:])
    return column(0), column(SPAN_X - 1), row(0), row(SPAN_Y - 1)


def send(ys, x_ref, a_ref, b_ref, at):
    rows = pl.ds(at, ys[0].shape[0])
    west, east, south, north = packs(ys)
    first = lax.axis_index("gx") == 0
    even = lax.axis_index("gy") % 2 == 0
    for t in range(SPAN_Y // 2):
        x_ref[t, rows, :] = jnp.where(first, east[t], west[t])
    a_ref[rows, :] = jnp.where(even, north, south)
    b_ref[rows, :] = jnp.where(even, south, north)


def received(x_ref, a_ref, b_ref, at, n, side=None):
    rows = pl.ds(at, n)
    first = lax.axis_index("gx") == 0
    even = lax.axis_index("gy") % 2 == 0
    xs = [x_ref[t, rows, :] for t in range(SPAN_Y // 2)]
    a, b = a_ref[rows, :], b_ref[rows, :]
    if side is not None:
        a, b = a + side[:, :128], b + side[:, 128:256]
        xs = [xs[t] + side[:, 256 + 128 * t : 384 + 128 * t] for t in range(SPAN_Y // 2)]
    zero = jnp.zeros_like(a)
    return (
        [jnp.where(first, zero, v) for v in xs],
        [jnp.where(first, v, zero) for v in xs],
        jnp.where(even, b, a),
        jnp.where(even, a, b),
    )


def across(ys, nb, rows):
    low = lower(rows)
    zero = jnp.zeros((rows, 128), F32)
    inside = lambda x, y, part: zero if ys is None else ys[x * SPAN_Y + y][:, part * 128 : part * 128 + 128]
    out = []
    for x in range(SPAN_X):
        for y in range(SPAN_Y):
            beyond = lambda v: zero if nb is None else v()
            west = inside(x - 1, y, 0) if x else beyond(lambda: nb[0][y // 2])
            east = inside(x + 1, y, 0) if x < SPAN_X - 1 else beyond(lambda: nb[1][y // 2])
            south = inside(x, y - 1, 1) if y else beyond(lambda: nb[2])
            north = inside(x, y + 1, 1) if y < SPAN_Y - 1 else beyond(lambda: nb[3])
            if (x + y) % 2:
                west, east, south, north = east, west, north, south
            out.append(jnp.concatenate([jnp.where(low, west, east), jnp.where(low, south, north)], 1))
    return out


def owned_lanes(i, rows):
    lane = iota((rows, 256), 1) % 128
    return lane < 64 if odd(i) else lane >= 64


def spread_owned(v, i):
    zero = jnp.zeros_like(v)
    low = lower(v.shape[0])
    turned = pltpu.roll(v, 64, 1)
    if odd(i):
        return jnp.concatenate([jnp.where(low, v, zero), jnp.where(low, turned, zero)], 1)
    return jnp.concatenate([jnp.where(low, zero, turned), jnp.where(low, zero, v)], 1)


def take_owned(v, i):
    low = lower(v.shape[0])
    if odd(i):
        return jnp.where(low, v[:, :128], pltpu.roll(v[:, 128:], 64, 1))
    return jnp.where(low, pltpu.roll(v[:, :128], 64, 1), v[:, 128:])


def start_kernel(res_ref, dir_ref, act_ref, scale_ref, *refs):
    inverse_ref, own_ref, x_ref, a_ref, b_ref = refs[4:9]
    upper_ref, p_ref = refs[13:15]
    gx, gy = lax.axis_index("gx"), lax.axis_index("gy")
    last_x = gx * SPAN_X + SPAN_X - 1 == lax.axis_size("gx") * SPAN_X - 1
    last_y = gy * SPAN_Y + SPAN_Y - 1 == lax.axis_size("gy") * SPAN_Y - 1
    east = iota((1, 128), 1) < 64
    ys = []
    for i in range(SUBS):
        x, y = i // SPAN_Y, i % SPAN_Y
        keep = act_ref[i : i + 1, :].astype(F32)
        if x == SPAN_X - 1:
            keep = jnp.where(jnp.logical_and(last_x, east), 0.0, keep)
        if y == SPAN_Y - 1:
            keep = jnp.where(jnp.logical_and(last_y, jnp.logical_not(east)), 0.0, keep)
        mine = pl.ds(i, CASES, stride=SUBS)
        p = dir_ref[mine, :] * keep
        p_ref[mine, :] = p
        v = jnp.concatenate(
            [
                res_ref[mine, :],
                p,
                scale_ref[i : i + 1, :] * keep,
                keep,
                jnp.zeros((CAST - 2 * CASES - 2, 128), F32),
            ],
            0,
        )
        v = spread_owned(v, i)
        own_ref[i] = v
        ys.append(v)
    send(ys, x_ref, a_ref, b_ref, 0)
    for ref in (x_ref, a_ref, b_ref):
        ref.flush()
    for t, (i, j) in enumerate(UPPER):
        upper_ref[t] = inverse_ref[128 * i : 128 * i + 128, 128 * j : 128 * j + 128]


def operator_kernel(
    schur_ref, couple_ref, map_ref, slot_ref, high_ref, low_ref, cc_ref, ch_ref, cl_ref, name_ref,
):
    none = 384
    slot = slot_ref[...].astype(F32)
    eye = iota((8, 8), 0) == iota((8, 8), 1)
    column = jnp.concatenate(
        [jnp.sum(jnp.where(eye, jnp.broadcast_to(slot[i : i + 1, :], (8, 8)), 0.0), 1, keepdims=True) for i in range(SUBS)], 0
    )
    row = jnp.concatenate([slot[i : i + 1, :] for i in range(SUBS)], 1)
    count = SUBS * 8
    earlier = iota((count, count), 1) < iota((count, count), 0)
    again = jnp.sum(jnp.where(jnp.logical_and(column == row, earlier), 1.0, 0.0), 1, keepdims=True)
    first = jnp.where(jnp.logical_and(again == 0.0, column != float(none)), 1.0, 0.0)
    first_row = jnp.sum(
        jnp.where(jnp.logical_and(column == row, iota((count, count), 0) < iota((count, count), 1)), 1.0, 0.0), 0, keepdims=True
    )
    first_row = jnp.where(jnp.logical_and(first_row == 0.0, row != float(none)), 1.0, 0.0)
    rank = jnp.sum(jnp.where(row < column, first_row, 0.0), 1, keepdims=True)
    hit = jnp.where(rank == iota((count, 128), 1).astype(F32), first, 0.0)
    name_ref[...] = jnp.broadcast_to(
        jnp.where(jnp.sum(hit, 0, keepdims=True) > 0.0, jnp.sum(hit * column, 0, keepdims=True), float(none)), (8, 128)
    )
    sub = iota((256, 256), 0)
    west = (sub // 64) % 2 == 0
    for i in range(SUBS):
        spots = map_ref[i // SPAN_Y, i % SPAN_Y : i % SPAN_Y + 1, :]
        if odd(i):
            spots = jnp.where((spots // 64) % 2 == 0, spots + 64, spots - 64)
        sign = jnp.where(west, 1.0, -1.0) if odd(i) else jnp.where(west, -1.0, 1.0)
        place = jnp.where(sub == spots, sign, 0.0).astype(BF16)
        mine = slot[i : i + 1, :]
        number = jnp.sum(jnp.where(column < mine, first, 0.0), 0, keepdims=True)
        compact = jnp.where(
            jnp.logical_and(number == iota((SLOTS, 8), 0).astype(F32), mine != float(none)), 1.0, 0.0
        )
        cc = jnp.dot(compact, couple_ref[i], precision=EXACT, preferred_element_type=F32)
        c1, rest = split(cc)
        c2, c3 = split(cc - c1.astype(F32))
        s1, s2 = split(schur_ref[i])
        tall = dot_turned(jnp.concatenate([s1, s2, c1, c2, c3], 0), place)
        high, low = (dot(place, tall[t : t + 256].astype(BF16)).astype(BF16) for t in (0, 256))
        high_ref[i], low_ref[i] = high, low
        cc = tall[512 : 512 + SLOTS] + tall[512 + SLOTS : 512 + 2 * SLOTS] + tall[512 + 2 * SLOTS :]
        cc_ref[i] = cc
        ch_ref[i], cl_ref[i] = split(cc)


def inverse_kernel(mine_ref, upper_ref, high_ref, low_ref, high_out_ref, low_out_ref):
    first = lax.axis_index("gx") == 0
    mine = mine_ref[...]
    blocks = {spot: upper_ref[t] for t, spot in enumerate(UPPER)}
    side = lambda i, j: blocks[i, j] if i <= j else jnp.transpose(blocks[j, i])
    other = jnp.concatenate([jnp.concatenate([side(i, j) for j in range(3)], 1) for i in range(3)], 0)
    for region, v in enumerate((jnp.where(first, mine, other), jnp.where(first, other, mine))):
        high, low = split(v)
        high_ref[region], low_ref[region] = high, low
        high_out_ref[region], low_out_ref[region] = high, low


def near_names(name_ref, x_ref, a_ref, b_ref):
    named = pl.ds(2 * CASES + SLOTS, 8)
    group = iota((8, 128), 1) // SLOTS
    turn = lambda v, g: jnp.where(group == g, pltpu.roll(v, g * SLOTS, 1), 0.0)
    wanted = name_ref[...] + 0.0
    wanted = jnp.where(group == 0, wanted, turn(a_ref[named, :], 1) + turn(b_ref[named, :], 2) + turn(x_ref[0, named, :], 3))
    found = iota((384, 128), 0).astype(F32) == wanted[0:1]
    mine = jnp.where(iota((384, 128), 1) < 3 * SLOTS, 1.0, 0.0)
    gx = lax.axis_index("gx")
    return [jnp.where(found, jnp.where(gx == region, mine, 1.0 - mine), 0.0).astype(BF16) for region in range(2)]


def near_spread(x_ref, a_ref, b_ref, nh_ref, nl_ref):
    rows = pl.ds(2 * CASES, SLOTS)
    nh_ref[...], nl_ref[...] = split(
        jnp.concatenate([a_ref[rows, :], b_ref[rows, :], x_ref[0, rows, :], x_ref[1, rows, :]], 1)
    )


def operator(ys, x_ref, a_ref, b_ref, near, mk_ref, ch_ref, cl_ref, nh_ref, nl_ref):
    n = ys[0].shape[0]
    high, low = nh_ref[...], nl_ref[...]
    side = jnp.concatenate(
        [
            dot_split(near[g], high[:, at : at + width], low[:, at : at + width])
            for g, at, width in ((1, 0, 128), (2, 128, 128), (3, 256, 256))
        ],
        1,
    )
    west, east, south, north = received(x_ref, a_ref, b_ref, 0, n, side)
    ys = [ys[i] + dot_split(near[0], ch_ref[i], cl_ref[i]) for i in range(SUBS)]
    other = across(ys, (west, east, south, north), n)
    return [mk_ref[i, 1:2, :] * (ys[i] + other[i]) for i in range(SUBS)]


def corners(us, ch_ref, cl_ref):
    couple = lambda ref: jnp.concatenate([ref[i] for i in range(SUBS)], 0)
    corner = dot_split(jnp.concatenate(us, 0), couple(ch_ref), couple(cl_ref), dot_turned)
    n = us[0].shape[0]
    group = iota((n, 128), 1) // SLOTS
    total = jnp.zeros((n, 128), F32)
    for i in range(SUBS):
        part = corner[n * i : n * i + n, 128 * (i // 4) : 128 * (i // 4) + 128]
        total = total + jnp.where(group == i % 4, part, 0.0)
    total = total + pltpu.roll(total, 64, 1)
    return total + pltpu.roll(total, 32, 1)


def by_schur(us, high_ref, low_ref):
    return [dot_split(us[i], high_ref[i], low_ref[i]) for i in range(SUBS)]


def over_lanes(terms):
    total = terms[0]
    for t in terms[1:]:
        total = total + t
    return jnp.sum(total[:, :128] + total[:, 128:], 1, keepdims=True)


def packed(corner, one, two):
    slot = iota((CASES, 128), 1) % SLOTS
    full = jnp.where(slot == USED, one, jnp.where(slot == USED + 1, two, corner))
    group = iota((4, 128), 1) // SLOTS
    out = jnp.zeros((4, 128), F32)
    for b in range(4):
        out = jnp.where(group == b, full[4 * b : 4 * b + 4], out)
    return out


def by_slot(vs):
    group = iota((8, 128), 1) // SLOTS
    out = []
    for region in range(2):
        rows = []
        for b in range(4):
            halves = []
            for h in range(2):
                acc = None
                for q in range(4):
                    v = vs[8 * region + 4 * h + q]
                    turned = v if q == b else pltpu.roll(v, (SLOTS * (q - b)) % 128, 1)
                    acc = turned if acc is None else jnp.where(group == q, turned, acc)
                halves.append(acc)
            rows.append(jnp.concatenate(halves, 1))
        out.append(jnp.concatenate(rows, 0))
    return out


def inner(vs):
    total = vs[0]
    for v in vs[1:]:
        total = total + v
    total = total[:4] + total[4:]
    tall = jnp.concatenate([total] * 4, 0)
    lane, row = iota((CASES, 128), 1), iota((CASES, 128), 0)
    column = lambda s: jnp.sum(jnp.where(lane == SLOTS * (row // 4) + s, tall, 0.0), 1, keepdims=True)
    return column(USED), column(USED + 1)


def first_of_pairs(v):
    return jnp.concatenate([v[8 * b : 8 * b + 4] for b in range(v.shape[0] // 8)], 0)


def solve(spots, pick_ref, gh_ref, gl_ref, near_ref):
    totals, sols, near = [], [], None
    for region in range(2):
        v = spots[region]
        n = v.shape[0]
        even = dot_exact(v, pick_ref[region, 0])
        odds = dot_exact(v, pick_ref[region, 1])
        z = jnp.where((iota((n, 384), 0) // 4) % 2 == 0, even, odds).reshape(n // 8, 8, 384)
        total = (z + pltpu.roll(z, 4, 1)).reshape(n, 384)
        sol = dot_split(total, gh_ref[region], gl_ref[region])
        part = dot_exact(sol, near_ref[region])
        near = part if near is None else near + part
        totals.append(total)
        sols.append(sol)
    return totals, sols, near


def swap_pairs(v):
    rows, lanes = v.shape
    return pltpu.roll(v.reshape(rows // 8, 8, lanes), 4, 1).reshape(rows, lanes)


def ahead(region, t):
    gx, gy = lax.axis_index("gx"), lax.axis_index("gy")
    return 8 * lax.rem(gx + region, 2) + lax.rem(gy // 2 + t, 8)


def dense_kernel(got_ref, gh_ref, gl_ref, dh_ref, dl_ref):
    group = iota((8, 128), 1) // SLOTS
    for region in range(2):
        hits = []
        for par in range(2):
            halves = []
            for h in range(2):
                acc = None
                for q in range(4):
                    v = got_ref[3 * ahead(region, 4 * h + q) + 1 + par]
                    v = v if par == 0 else pltpu.roll(v, 4, 0)
                    turned = pltpu.roll(v, SLOTS * q, 1) if q else v
                    acc = turned if acc is None else jnp.where(group == q, turned, acc)
                halves.append(acc[0:1])
            wanted = jnp.concatenate(halves, 1)
            hits.append(jnp.where(iota((384, 256), 0).astype(F32) == wanted, 1.0, 0.0))
        picks = jnp.concatenate(hits, 1).astype(BF16)
        rows = [jnp.transpose(hit).astype(BF16) for hit in hits]
        which = lax.rem(lax.axis_index("gx") + region, 2)
        for whole_ref, out_ref in ((gh_ref, dh_ref), (gl_ref, dl_ref)):
            half = dot(whole_ref[which], picks).astype(BF16)
            for par in range(2):
                out_ref[region, par] = dot(rows[par], half).astype(BF16)


def solve_dense(spots, dh_ref, dl_ref):
    total, sols = None, []
    for region in range(2):
        v = spots[region]
        one, two = (dot_split(v, dh_ref[region, par], dl_ref[region, par]) for par in range(2))
        first = (iota(v.shape, 0) // 4) % 2 == 0
        sol = jnp.where(first, one[:, :256] + swap_pairs(two[:, :256]), two[:, 256:] + swap_pairs(one[:, 256:]))
        total = v * sol if total is None else total + v * sol
        sols.append(sol)
    total = jnp.sum(total, 1, keepdims=True)
    halves = lambda v: [jnp.concatenate([v[8 * b + at : 8 * b + at + 4] for b in range(4)], 0) for at in (0, 4)]
    total = sum(halves(total))
    even = lax.axis_index("gy") % 2 == 0
    (a, b), (c, d) = halves(sols[0]), halves(sols[1][:, :128])
    here = jnp.where(even, a[:, :128], b[:, :128])
    pair = jnp.where(even, b[:, :128], a[:, :128])
    beyond = jnp.where(even, pltpu.roll(b[:, 128:], SLOTS, 1), pltpu.roll(a[:, :128], 128 - SLOTS, 1))
    along = jnp.where(even, c, d)
    return total, [v[:, :SLOTS] for v in (here, pair, beyond, along)]


def energy(totals, sols):
    both = totals[0] * sols[0] + totals[1] * sols[1]
    return first_of_pairs(jnp.sum(both, 1, keepdims=True))


def emit(rs, mk_ref, high_ref, low_ref, ch_ref, cl_ref, block_ref, y_ref, x_ref, a_ref, b_ref):
    us = [mk_ref[i, 0:1, :] * rs[i] for i in range(SUBS)]
    corner = corners(us, ch_ref, cl_ref)
    rho = over_lanes([jnp.where(owned_lanes(i, CASES), rs[i] * us[i], 0.0) for i in range(SUBS)])
    ys = by_schur(us, high_ref, low_ref)
    send(ys, x_ref, a_ref, b_ref, 0)
    for i in range(SUBS):
        y_ref[i] = ys[i]
    for ref in (x_ref, a_ref, b_ref, y_ref):
        ref.flush()
    delta = over_lanes([us[i] * ys[i] for i in range(SUBS)])
    block = packed(corner, rho, delta)
    twice = jnp.concatenate([block, block], 0)
    for j in range(16):
        block_ref[j] = twice


def first_kernel(
    own_ref, x_ref, a_ref, b_ref, high_ref, low_ref, cc_ref, ch_ref, cl_ref, name_ref,
    r_ref, mk_ref, y_ref, block_ref, sx_ref, sa_ref, sb_ref, high_out_ref, low_out_ref,
):
    own = [own_ref[i] for i in range(SUBS)]
    other = across(own, received(x_ref, a_ref, b_ref, 0, CAST), CAST)
    rs, vs = [], []
    for i in range(SUBS):
        full = own[i] + other[i]
        rs.append(full[:CASES])
        r_ref[i] = full[:CASES]
        mk_ref[i] = full[2 * CASES : 2 * CASES + 8]
        vs.append(jnp.concatenate([full[2 * CASES : 2 * CASES + 1] * full[:CASES], full[CASES : 2 * CASES]], 0))
    corner = corners(vs, ch_ref, cl_ref)
    ys = by_schur(vs, high_ref, low_ref)
    names = name_ref[...]
    send([jnp.concatenate([ys[i], cc_ref[i]], 0) for i in range(SUBS)], sx_ref, sa_ref, sb_ref, 0)
    at = pl.ds(2 * CASES + SLOTS, 8)
    for t in range(SPAN_Y // 2):
        sx_ref[t, at, :] = names
    sa_ref[at, :] = names
    sb_ref[at, :] = names
    us = [v[:CASES] for v in vs]
    ps = [v[CASES:] for v in vs]
    rho = over_lanes([jnp.where(owned_lanes(i, CASES), rs[i] * us[i], 0.0) for i in range(SUBS)])
    delta = over_lanes([us[i] * ys[i][:CASES] for i in range(SUBS)])
    cross = over_lanes([ps[i] * ys[i][:CASES] for i in range(SUBS)])
    eta = over_lanes([ps[i] * ys[i][CASES:] for i in range(SUBS)])
    one, two = packed(corner[:CASES], rho, delta), packed(corner[CASES:], cross, eta)
    blocks = [
        jnp.concatenate([one, two], 0),
        jnp.concatenate([names[:4], one], 0),
        jnp.concatenate([two, names[:4]], 0),
    ]
    for j in range(16):
        for t in range(3):
            block_ref[3 * j + t] = blocks[t]
    for i in range(SUBS):
        y_ref[i] = ys[i]


def column_of(row):
    eye = iota((CASES, CASES), 0) == iota((CASES, CASES), 1)
    return jnp.sum(jnp.where(eye, jnp.broadcast_to(row, (CASES, CASES)), 0.0), 1, keepdims=True)


def keep_scalars(scal_ref, values):
    for t, v in enumerate(values):
        scal_ref[t] = jnp.broadcast_to(v, (CASES, 128))


def second_kernel(
    got_ref, x_ref, a_ref, b_ref, y_ref, r_ref, mk_ref, p_ref, l_ref, rho_ref, gh_ref, gl_ref, name_ref,
    high_ref, low_ref, ch_ref, cl_ref,
    nh_ref, nl_ref, po_ref, lo_ref, ro_ref, so_ref, scal_ref, block_ref, yo_ref, sx_ref, sa_ref, sb_ref,
):
    near_ref, pick_ref = near_names(name_ref, x_ref, a_ref, b_ref), {}
    near_spread(x_ref, a_ref, b_ref, nh_ref, nl_ref)
    top = iota((8, 128), 0) < 4
    us, ps, names = [], [], []
    for j in range(16):
        v = [got_ref[3 * j + t] for t in range(3)]
        us.append(jnp.where(top, v[0], v[1]))
        ps.append(pltpu.roll(jnp.where(top, v[2], v[0]), 4, 0))
        names.append((v[1], pltpu.roll(v[2], 4, 0)))
    group = iota((8, 128), 1) // SLOTS
    for region in range(2):
        for par in range(2):
            halves = []
            for h in range(2):
                acc = None
                for q in range(4):
                    v = names[8 * region + 4 * h + q][par]
                    turned = pltpu.roll(v, SLOTS * q, 1) if q else v
                    acc = turned if acc is None else jnp.where(group == q, turned, acc)
                halves.append(acc[0:1])
            wanted = jnp.concatenate(halves, 1)
            hit = jnp.where(iota((384, 256), 0).astype(F32) == wanted, 1.0, 0.0)
            pick_ref[region, par] = jnp.transpose(hit).astype(BF16)
    lhs_u, lhs_p = by_slot(us), by_slot(ps)
    n = lhs_u[0].shape[0]
    totals, sols, near = solve(
        [jnp.concatenate([lhs_u[t], lhs_p[t]], 0) for t in range(2)], pick_ref, gh_ref, gl_ref, near_ref
    )
    of_u, of_p = lambda vs: [v[:n] for v in vs], lambda vs: [v[n:] for v in vs]
    rho, delta = inner(us)
    cross, eta = inner(ps)
    delta = delta + energy(of_u(totals), of_u(sols))
    cross = cross + energy(of_p(totals), of_u(sols))
    eta = eta + energy(of_p(totals), of_p(sols))
    near = first_of_pairs(near)
    near = [(pltpu.roll(near, 128 - SLOTS * g, 1) if g else near)[:, :SLOTS] for g in range(4)]
    beta = rho / column_of(rho_ref[...])
    skew = cross + beta * eta
    pi = delta + 2.0 * beta * skew - beta * beta * eta
    alpha = rho / pi
    fs = operator([y_ref[i] for i in range(SUBS)], x_ref, a_ref, b_ref, near, mk_ref, ch_ref, cl_ref, nh_ref, nl_ref)
    rs = []
    for i in range(SUBS):
        f, r = fs[i], r_ref[i]
        s = f[:CASES] + beta * f[CASES:]
        r = r - alpha * s
        rs.append(r)
        ro_ref[i], so_ref[i] = r, s
    scalars = rho, pi, beta, skew, alpha
    keep_scalars(scal_ref, scalars)
    so_ref.flush()
    track(r_ref, scalars, mk_ref, p_ref, l_ref, po_ref, lo_ref)
    emit(rs, mk_ref, high_ref, low_ref, ch_ref, cl_ref, block_ref, yo_ref, sx_ref, sa_ref, sb_ref)


def absorb(got_ref, x_ref, a_ref, b_ref, y_ref, r_ref, s_ref, scal_ref, mk_ref, dh_ref, dl_ref, nh_ref, nl_ref, ch_ref, cl_ref):
    vs = [got_ref[ahead(region, t)] for region in range(2) for t in range(8)]
    coarse, near = solve_dense(by_slot(vs), dh_ref, dl_ref)
    rho, delta = inner(vs)
    delta = delta + coarse
    rho_old, pi, beta, skew = (scal_ref[t][:, 0:1] for t in range(4))
    skew = beta * skew
    beta = rho / rho_old
    pi = delta + 2.0 * beta * skew - beta * beta * pi
    alpha = rho / pi
    fs = operator([y_ref[i] for i in range(SUBS)], x_ref, a_ref, b_ref, near, mk_ref, ch_ref, cl_ref, nh_ref, nl_ref)
    ss = [fs[i] + beta * s_ref[i] for i in range(SUBS)]
    rs = [r_ref[i] - alpha * ss[i] for i in range(SUBS)]
    return rs, ss, (rho, pi, beta, skew, alpha)


def track(r_ref, scalars, mk_ref, p_ref, l_ref, po_ref, lo_ref):
    _, _, beta, _, alpha = scalars
    for i in range(SUBS):
        mine = pl.ds(i, CASES, stride=SUBS)
        p = take_owned(mk_ref[i, 0:1, :] * r_ref[i], i) + beta * p_ref[mine, :]
        po_ref[mine, :] = p
        lo_ref[mine, :] = l_ref[mine, :] + alpha * p


def round_kernel(
    got_ref, x_ref, a_ref, b_ref, y_ref, r_ref, s_ref, scal_ref, mk_ref, dh_ref, dl_ref,
    nh_ref, nl_ref, ch_ref, cl_ref, p_ref, l_ref, high_ref, low_ref,
    po_ref, lo_ref, ro_ref, so_ref, scalo_ref, block_ref, yo_ref, sx_ref, sa_ref, sb_ref,
):
    rs, ss, scalars = absorb(
        got_ref, x_ref, a_ref, b_ref, y_ref, r_ref, s_ref, scal_ref, mk_ref, dh_ref, dl_ref, nh_ref, nl_ref, ch_ref, cl_ref
    )
    for i in range(SUBS):
        ro_ref[i], so_ref[i] = rs[i], ss[i]
    so_ref.flush()
    keep_scalars(scalo_ref, scalars)
    track(r_ref, scalars, mk_ref, p_ref, l_ref, po_ref, lo_ref)
    emit(rs, mk_ref, high_ref, low_ref, ch_ref, cl_ref, block_ref, yo_ref, sx_ref, sa_ref, sb_ref)


def last_kernel(
    got_ref, x_ref, a_ref, b_ref, y_ref, r_ref, s_ref, scal_ref, mk_ref, dh_ref, dl_ref, nh_ref, nl_ref, ch_ref, cl_ref,
    p_ref, l_ref, lo_ref, ro_ref, po_ref,
):
    rs, _, scalars = absorb(
        got_ref, x_ref, a_ref, b_ref, y_ref, r_ref, s_ref, scal_ref, mk_ref, dh_ref, dl_ref, nh_ref, nl_ref, ch_ref, cl_ref
    )
    track(r_ref, scalars, mk_ref, p_ref, l_ref, po_ref, lo_ref)
    for i in range(SUBS):
        ro_ref[pl.ds(i, CASES, stride=SUBS), :] = take_owned(rs[i], i)


class Fetched:
    def __init__(self, source, buffer, semaphore):
        self.buffer = buffer
        self.copy = pltpu.make_async_copy(source, buffer, semaphore)
        self.copy.start()
        self.here = False

    def wait(self):
        self.copy.wait()
        self.here = True

    def __getitem__(self, index):
        if not self.here:
            self.wait()
        return self.buffer[index]


class FetchedPieces:
    def __init__(self, source, buffer, semaphore, count):
        self.buffer = buffer
        step = buffer.shape[0] // count
        self.parts = [
            Fetched(source.at[pl.ds(i * step, step)], buffer.at[pl.ds(i * step, step)], semaphore.at[i])
            for i in range(count)
        ]
        self.here = False

    def wait(self):
        for part in self.parts:
            part.copy.wait()
        self.here = True

    def __getitem__(self, index):
        if not self.here:
            self.wait()
        return self.buffer[index]


class Stored:
    def __init__(self, target, buffer, semaphore):
        self.buffer = buffer
        self.copy = pltpu.make_async_copy(buffer, target, semaphore)
        self.sent = False

    def __setitem__(self, index, value):
        self.buffer[index] = value

    def __getitem__(self, index):
        return self.buffer[index]

    def flush(self):
        if not self.sent:
            self.copy.start()
            self.sent = True


class Kept:
    def __init__(self, ref):
        self.ref = ref

    def __setitem__(self, index, value):
        self.ref[index] = value

    def __getitem__(self, index):
        return self.ref[index]

    def flush(self):
        pass


def call(kernel, args, outs, kept=(), kept_out=(), raw=(), through=None, flops=None, late=0, pieces=None):
    through, pieces = through or {}, pieces or {}
    moved = [i for i in range(len(args)) if i not in kept and i not in raw]
    written = [i for i in range(len(outs)) if i not in kept_out and i not in through]

    def body(*refs):
        ins, results = refs[: len(args)], refs[len(args) : len(args) + len(outs)]
        buffers, (in_sem, out_sem, through_sem) = refs[len(args) + len(outs) : -3], refs[-3:]
        fetched, stored = list(ins), [Kept(ref) for ref in results]
        for i in sorted(moved, key=lambda i: i not in pieces):
            t, at = moved.index(i), sum(pieces.get(m, 1) for m in moved[: moved.index(i)])
            if i in pieces:
                fetched[i] = FetchedPieces(ins[i], buffers[t], in_sem.at[pl.ds(at, pieces[i])], pieces[i])
            else:
                fetched[i] = Fetched(ins[i], buffers[t], in_sem.at[at])
        for t, i in enumerate(written):
            stored[i] = Stored(results[i], buffers[len(moved) + t], out_sem.at[t])
        passing = [
            pltpu.make_async_copy(source(ins), results[i], through_sem.at[t]) for t, (i, source) in enumerate(through.items())
        ]
        for copy in passing:
            copy.start()
        if moved or passing:
            spot = (0,) * (len(outs[-1 - late][0]) - 2)
            blank = stored[-1 - late]

            @pl.when(lax.axis_index("gx") >= 0)
            def _():
                blank[spot] = jnp.zeros(outs[-1 - late][0][-2:], outs[-1 - late][1])

        kernel(*fetched, *stored)
        for i in written:
            stored[i].flush()
        for i in moved:
            if not fetched[i].here:
                fetched[i].wait()
        for copy in passing:
            copy.wait()
        for i in written:
            stored[i].copy.wait()

    place = lambda held: pl.BlockSpec(memory_space=pltpu.VMEM if held else pltpu.HBM)
    semaphores = lambda n: pltpu.SemaphoreType.DMA((max(n, 1),))
    args = [a if i in kept else pltpu.with_memory_space_constraint(a, pltpu.HBM) for i, a in enumerate(args)]
    return pl.pallas_call(
        body,
        out_shape=[
            jax.ShapeDtypeStruct(*out) if i in kept_out else pltpu.HBM(*out) for i, out in enumerate(outs)
        ],
        in_specs=[place(i in kept) for i in range(len(args))],
        out_specs=[place(i in kept_out) for i in range(len(outs))],
        scratch_shapes=[pltpu.VMEM(args[i].shape, args[i].dtype) for i in moved]
        + [pltpu.VMEM(*outs[i]) for i in written]
        + [semaphores(sum(pieces.get(i, 1) for i in moved)), semaphores(len(written)), semaphores(len(through))],
        compiler_params=pltpu.CompilerParams(vmem_limit_bytes=LIMIT),
        cost_estimate=flops and pl.CostEstimate(flops=flops, bytes_accessed=flops // 512, transcendentals=0),
    )(*args)


def trade(x, a, b):
    peers = lax.axis_size("gy")
    return (
        lax.ppermute(x, "gx", [(0, 1), (1, 0)]),
        lax.ppermute(a, "gy", both_ways(pairs_from(0, peers))),
        lax.ppermute(b, "gy", both_ways(pairs_from(1, peers))),
    )


def two_regions(
    duals, residual, direction, prev_rho, dual_schur, coupling, coarse_inverse, edge_map, corner_slot, active, scaling
):
    native = lambda v: v.reshape(CASES * SUBS, 128)
    by_sub = lambda v: v.reshape((SUBS,) + v.shape[2:])
    width = coarse_inverse.shape[-1]
    sends = lambda rows: [((SPAN_Y // 2, rows, 128), F32), ((rows, 128), F32), ((rows, 128), F32)]
    state = ((SUBS, CASES, 256), F32)
    plain = ((CASES * SUBS, 128), F32)

    raw = [by_sub(dual_schur), by_sub(coupling), edge_map, by_sub(corner_slot)]
    own, *out, schur, coupled, placed, slotted, inverse, p = call(
        start_kernel,
        [native(residual), native(direction), by_sub(active), by_sub(scaling), *raw, coarse_inverse[0]],
        [((SUBS, CAST, 256), F32)] + sends(CAST) + [(v.shape, v.dtype) for v in raw] + [((len(UPPER), 128, 128), F32), plain],
        kept_out=(0, 4, 5, 6, 7),
        raw=(4, 5, 6, 7),
        through={4: lambda v: v[4], 5: lambda v: v[5], 6: lambda v: v[6], 7: lambda v: v[7]},
    )
    come = trade(*out)
    other = lax.ppermute(inverse, "gx", [(0, 1), (1, 0)])
    matrix = ((SUBS, 256, 256), BF16)
    couple = ((SUBS, SLOTS, 256), BF16)
    high, low, cc, ch, cl, names = call(
        operator_kernel,
        [schur, coupled, placed, slotted],
        [matrix, matrix, ((SUBS, SLOTS, 256), F32), couple, couple, ((8, 128), F32)],
        kept=range(4),
        kept_out=range(6),
        flops=5 * 10**9,
    )
    rows = 2 * CASES + SLOTS + 8
    r, mk, y, block, *out, high, low = call(
        first_kernel,
        [own, *come, high, low, cc, ch, cl, names],
        [state, ((SUBS, 8, 256), F32), ((SUBS, 2 * CASES, 256), F32), ((48, 8, 128), F32)]
        + sends(rows)
        + [matrix, matrix],
        kept=range(10),
        kept_out=(0, 1, 2),
        through={7: lambda v: v[4], 8: lambda v: v[5]},
        late=2,
    )
    got = lax.all_to_all(block.reshape(32, 3, 4, 128), BOTH, 0, 0, tiled=False).reshape(48, 8, 128)
    come = trade(*out)
    square = ((2, width, width), BF16)
    gh, gl, gh_far, gl_far = call(
        inverse_kernel, [coarse_inverse[0], other], [square] * 4, kept=(1,), kept_out=(0, 1), flops=10**9
    )
    side = ((SLOTS, 512), BF16)
    onward = [plain, plain, state, state, ((5, CASES, 128), F32), ((16, 8, 128), F32), state] + sends(CASES)
    nh, nl, p, lam, r, s, scal, block, y, *out = call(
        second_kernel,
        [got, *come, y, r, mk, p, native(duals), prev_rho.reshape(1, CASES), gh, gl, names, high, low, ch, cl],
        [side, side] + onward,
        kept=(0, 1, 2, 3, 4, 5, 6, 10, 11, 12, 15, 16),
        kept_out=(0, 1, 2, 3, 4, 6, 8),
        late=3,
    )
    dense = ((2, 2, 256, 512), BF16)
    dh, dl = call(dense_kernel, [got, gh_far, gl_far], [dense, dense], kept_out=(0, 1), flops=3 * 10**9)
    for step in range(1, ITERS):
        got = lax.all_to_all(block.reshape(32, 4, 128), BOTH, 0, 0, tiled=False).reshape(16, 8, 128)
        come = trade(*out)
        args = [got, *come, y, r, s, scal, mk, dh, dl, nh, nl, ch, cl, p, lam]
        kept = (*range(6), *range(7, 17))
        if step < ITERS - 1:
            p, lam, r, s, scal, block, y, *out = call(
                round_kernel, args + [high, low], onward, kept, kept_out=(0, 1, 2, 4, 6), late=3
            )
        else:
            results = call(last_kernel, args, [plain, plain, plain], kept)
    return tuple(v.reshape(duals.shape) for v in results)


def shards(*args):
    cases, span_x, span_y, owned = args[0].shape
    fits = (cases, span_x, span_y, owned, args[6].shape[-1]) == (CASES, SPAN_X, SPAN_Y, 128, 384)
    if fits and lax.axis_size("gx") == 2 and lax.axis_size("gy") == 16:
        return two_regions(*args)
    return general(*args)


def solution(mesh):
    placed = (
        P(None, "gx", "gy", None),
        P(None, "gx", "gy", None),
        P(None, "gx", "gy", None),
        P(),
        P("gx", "gy", None, None),
        P("gx", "gy", None, None),
        P("gx", None, None),
        P("gx", "gy", None),
        P("gx", "gy", None),
        P("gx", "gy", None),
        P("gx", "gy", None),
    )
    return jax.shard_map(
        shards,
        mesh=mesh,
        in_specs=placed,
        out_specs=(P(None, "gx", "gy", None), P(None, "gx", "gy", None), P(None, "gx", "gy", None)),
        check_vma=False,
    )
```

```python
import jax
import jax.numpy as jnp
from jax import lax
from jax.experimental import pallas as pl
from jax.experimental.pallas import tpu as pltpu
from jax.sharding import PartitionSpec as P

ITERS = 6
HIGH = lax.Precision.HIGH
EXACT = lax.Precision.HIGHEST
BOTH = ("gx", "gy")


def pairs_from(first, peers):
    return [(i, i + 1) for i in range(first, peers - 1, 2)]


def both_ways(pairs):
    return pairs + [(b, a) for a, b in pairs]


def up_gy(value, peers):
    even = lax.ppermute(value, "gy", pairs_from(0, peers))
    odd = lax.ppermute(value, "gy", pairs_from(1, peers))
    return jnp.where(lax.axis_index("gy") % 2 == 1, even, odd)


def swap_gy(low, high, peers):
    is_even = lax.axis_index("gy") % 2 == 0
    first = lax.ppermute(jnp.where(is_even, high, low), "gy", both_ways(pairs_from(0, peers)))
    second = lax.ppermute(jnp.where(is_even, low, high), "gy", both_ways(pairs_from(1, peers)))
    return jnp.where(is_even, second, first), jnp.where(is_even, first, second)


def swap_gx(low, high, peers):
    if peers == 2:
        is_first = lax.axis_index("gx") == 0
        got = lax.ppermute(jnp.where(is_first, high, low), "gx", [(0, 1), (1, 0)])
        zero = jnp.zeros_like(got)
        return jnp.where(is_first, zero, got), jnp.where(is_first, got, zero)
    below = lax.ppermute(high, "gx", [(i, i + 1) for i in range(peers - 1)])
    above = lax.ppermute(low, "gx", [(i + 1, i) for i in range(peers - 1)])
    return below, above


def everywhere(block, axes):
    sent = jnp.broadcast_to(block[None], (lax.axis_size(axes),) + block.shape)
    return lax.all_to_all(sent, axes, 0, 0, tiled=False)


def general(
    duals, residual, direction, prev_rho, dual_schur, coupling, coarse_inverse, edge_map, corner_slot, active, scaling
):
    cases, span_x, span_y, owned = duals.shape
    half = owned // 2
    full = 2 * owned
    corners = coupling.shape[2]
    width_c = coarse_inverse.shape[-1]
    peers_x, peers_y = lax.axis_size("gx"), lax.axis_size("gy")
    whole = peers_x == 2
    axes = BOTH if whole else "gy"
    regions = peers_x if whole else 1
    peers = regions * peers_y
    here_x, here_y = lax.axis_index("gx"), lax.axis_index("gy")
    used = 2 * (span_x + 1) * (span_y + 1)
    slots = used + 2

    columns = here_x * span_x + jnp.arange(span_x)
    rowset = here_y * span_y + jnp.arange(span_y)
    east_ok = jnp.broadcast_to((columns < span_x * peers_x - 1)[:, None, None], (span_x, span_y, half))
    north_ok = jnp.broadcast_to((rowset < span_y * peers_y - 1)[None, :, None], (span_x, span_y, half))
    keep_own = active.astype(jnp.float32) * jnp.concatenate([east_ok, north_ok], -1).astype(jnp.float32)
    scale_own = keep_own * scaling

    by_place = lambda v: jnp.transpose(v, (1, 2, 0, 3))
    lam = by_place(duals)
    p = keep_own[:, :, None] * by_place(direction)
    stacked = jnp.concatenate([by_place(residual), p, scale_own[:, :, None], keep_own[:, :, None]], 2)
    part_e, part_n = stacked[..., :half], stacked[..., half:]
    from_west = lax.ppermute(part_e[-1], "gx", [(i, i + 1) for i in range(peers_x - 1)])
    from_south = up_gy(part_n[:, -1], peers_y)
    west = jnp.concatenate([from_west[None], part_e[:-1]], 0)
    south = jnp.concatenate([from_south[:, None], part_n[:, :-1]], 1)
    stacked = jnp.concatenate([west, part_e, south, part_n], -1)
    r = stacked[:, :, :cases]
    p_all = stacked[:, :, cases : 2 * cases]
    scale = stacked[:, :, 2 * cases : 2 * cases + 1]
    keep = stacked[:, :, 2 * cases + 1 :]

    sign = jnp.concatenate([-jnp.ones(half), jnp.ones(half), -jnp.ones(half), jnp.ones(half)]).astype(jnp.float32)
    place = (edge_map[..., None] == jnp.arange(full, dtype=jnp.int32)).astype(jnp.float32) * sign
    schur = jnp.einsum("xyij,xyjf->xyif", dual_schur, place, precision=EXACT)
    schur = jnp.einsum("xyie,xyif->xyef", place, schur, precision=EXACT)
    couple = jnp.einsum("xycj,xyjf->xycf", coupling, place, precision=EXACT)

    flat = corner_slot.reshape(-1)
    count = flat.shape[0]
    order = jnp.arange(count)
    same = flat[:, None] == flat[None, :]
    first = ~jnp.any(same & (order[None, :] < order[:, None]), 1) & (flat != width_c)
    rank = jnp.sum((flat[None, :] < flat[:, None]) & first[None, :], 1)
    local_slot = jnp.arange(slots)
    compact = ((rank[:, None] == local_slot) & (flat != width_c)[:, None]).astype(jnp.float32)
    named = jnp.where(
        jnp.any(compact > 0, 0), jnp.max(compact * flat[:, None].astype(jnp.float32), 0), float(width_c)
    )
    compact = compact.reshape(span_x, span_y, corners, slots)
    gather_c = jnp.einsum("xycs,xycf->xysf", compact, couple, precision=EXACT)

    blocks = lambda a: (a[..., :half], a[..., half : 2 * half], a[..., 2 * half : 3 * half], a[..., 3 * half :])

    def jump(y, from_w, from_e, from_s, from_n):
        w, e, s, n = blocks(y)
        w_nb = jnp.concatenate([from_w[None], e[:-1]], 0)
        e_nb = jnp.concatenate([w[1:], from_e[None]], 0)
        s_nb = jnp.concatenate([from_s[:, None], n[:, :-1]], 1)
        n_nb = jnp.concatenate([s[:, 1:], from_n[:, None]], 1)
        return jnp.concatenate([w + w_nb, e + e_nb, s + s_nb, n + n_nb], -1)

    def rims(y):
        w, e, s, n = blocks(y)
        return w[0], e[-1], s[:, 0], n[:, -1]

    def exchange(y):
        w, e, s, n = rims(y)
        from_w, from_e = swap_gx(w, e, peers_x)
        from_s, from_n = swap_gy(s, n, peers_y)
        return from_w, from_e, from_s, from_n

    def put(rim, name):
        zero = jnp.zeros((span_x, span_y, rim.shape[-2], half), jnp.float32)
        parts = [zero, zero, zero, zero]
        if name == 0:
            parts[0] = zero.at[0].set(rim)
        elif name == 1:
            parts[1] = zero.at[-1].set(rim)
        elif name == 2:
            parts[2] = zero.at[:, 0].set(rim)
        else:
            parts[3] = zero.at[:, -1].set(rim)
        return jnp.concatenate(parts, -1)

    nb = exchange(gather_c)
    none = [jnp.zeros_like(v) for v in nb]
    spread = jnp.concatenate([jump(gather_c, *none)] + [put(v, i) for i, v in enumerate(nb)], 2)
    spread = spread * keep

    region_inv = coarse_inverse[0]

    def local_part(v):
        y = jnp.einsum("xykj,xyji->xyki", v, schur, precision=HIGH)
        c = jnp.einsum("xykj,xysj->ks", v, gather_c[:, :, :used], precision=HIGH)
        return y, c

    def over_cases(a, b):
        return jnp.sum(a * b, axis=(0, 1, 3))

    def pack(c, one, two):
        return jnp.concatenate([c, one[:, None], two[:, None]], 1).reshape(-1, 128)

    def unpack(got):
        got = got.reshape(peers, cases, slots)
        sums = jnp.sum(got[:, :, used:], 0)
        return jnp.transpose(got, (1, 0, 2)).reshape(cases, regions, peers_y, slots), sums[:, 0], sums[:, 1]

    def own_part(a):
        return jnp.concatenate([a[..., half : 2 * half], a[..., 3 * half :]], -1)

    u = scale * r
    both = jnp.concatenate([u, p_all], 2)
    y, c = local_part(both)
    yu, yp = y[:, :, :cases], y[:, :, cases:]
    rho_part = over_cases(own_part(r), own_part(u))
    names = jnp.concatenate([named, jnp.zeros(4 * 128 - slots, jnp.float32)]).reshape(4, 128)
    block = jnp.concatenate(
        [pack(c[:cases], rho_part, over_cases(u, yu)), pack(c[cases:], over_cases(p_all, yu), over_cases(p_all, yp)), names]
    )
    got = everywhere(block, axes)
    from_all = exchange(y)

    rows = cases * slots // 128
    slot_of = got[:, 2 * rows :].reshape(peers, -1)[:, :slots].reshape(regions, peers_y * slots)

    if whole:
        other = lax.ppermute(region_inv, "gx", [(0, 1), (1, 0)])
        inverses = jnp.where(here_x == 0, jnp.stack([region_inv, other]), jnp.stack([other, region_inv]))
    else:
        inverses = region_inv[None]
    pick = (slot_of[..., None] == jnp.arange(width_c, dtype=jnp.float32)).astype(jnp.float32)
    dense = jnp.einsum("ran,rnm->ram", pick, inverses, precision=EXACT)
    dense = jnp.einsum("ram,rbm->rab", dense, pick, precision=EXACT)

    def solve(c_all):
        flat_c = c_all.reshape(cases, regions, peers_y * slots)
        sol = jnp.einsum("kra,rab->krb", flat_c, dense, precision=HIGH)
        return flat_c, sol

    def total(a, b):
        return jnp.sum(a * b, (1, 2))

    def over_gx(*sums):
        return sums if whole else tuple(lax.psum(jnp.stack(sums), "gx"))

    def at(sol, ix, dy):
        sol = sol.reshape(cases, regions, peers_y, slots)
        iy = jnp.clip(here_y + dy, 0, peers_y - 1)
        return lax.dynamic_slice(sol, (0, ix, iy, 0), (cases, 1, 1, slots))[:, 0, 0]

    def beside(sol):
        if whole:
            return at(sol, 0, 0), at(sol, 1, 0)
        mine = at(sol, 0, 0)
        return swap_gx(mine, mine, peers_x)

    def coarse_part(sol):
        mine = here_x if whole else 0
        near = jnp.concatenate([at(sol, mine, 0), *beside(sol), at(sol, mine, -1), at(sol, mine, 1)], 1)
        return jnp.einsum("kn,xynj->xykj", near, spread, precision=HIGH)

    cu, rho, delta = unpack(got[:, :rows])
    cp, cross, eta = unpack(got[:, rows : 2 * rows])
    cu, su = solve(cu)
    cp, sp = solve(cp)
    delta, cross, eta = delta + total(cu, su), cross + total(cu, sp), eta + total(cp, sp)
    rho, delta, cross, eta = over_gx(rho, delta, cross, eta)
    f_both = keep * jump(y, *from_all)
    w = f_both[:, :, :cases] + coarse_part(su)
    s = f_both[:, :, cases:] + coarse_part(sp)

    wide = lambda a: a[None, None, :, None]
    beta = rho / prev_rho
    skew = cross + beta * eta
    pi = delta + 2.0 * beta * skew - beta * beta * eta
    for step in range(ITERS):
        if step > 0:
            u = scale * r
            y, c = local_part(u)
            block = pack(c, over_cases(own_part(r), own_part(u)), over_cases(u, y))
            got = everywhere(block, axes)
            from_all = exchange(y)
            rho_old = rho
            c_all, rho, delta = unpack(got)
            c_all, sol = solve(c_all)
            rho, delta = over_gx(rho, delta + total(c_all, sol))
            w = keep * jump(y, *from_all) + coarse_part(sol)
            skew = beta * skew
            beta = rho / rho_old
            pi = delta + 2.0 * beta * skew - beta * beta * pi
        alpha = rho / pi
        p = own_part(u) + wide(beta) * p
        s = w + wide(beta) * s
        lam = lam + wide(alpha) * p
        r = r - wide(alpha) * s
    back = lambda v: jnp.transpose(v, (2, 0, 1, 3))
    return back(lam), back(own_part(r)), back(p)


F32, BF16 = jnp.float32, jnp.bfloat16
SPAN_X, SPAN_Y = 2, 4
SUBS = SPAN_X * SPAN_Y
CASES = 16
STAY = 2
SLOTS = 32
USED = 2 * (SPAN_X + 1) * (SPAN_Y + 1)
CAST = 40
LIMIT = 16 * 1024 * 1024
UPPER = [(i, j) for i in range(3) for j in range(i, 3)]


def iota(shape, dim):
    return lax.broadcasted_iota(jnp.int32, shape, dim)


def split(v):
    high = v.astype(BF16)
    return high, (v - high.astype(F32)).astype(BF16)


def dot(a, b):
    return jnp.dot(a, b, preferred_element_type=F32)


def dot_turned(a, b):
    return lax.dot_general(a, b, (((1,), (1,)), ((), ())), preferred_element_type=F32)


def dot_split(v, high, low, dot=dot):
    n = v.shape[0]
    vh, vl = split(v)
    wide = dot(jnp.concatenate([vh, vl], 0), high)
    return wide[:n] + wide[n:] + dot(vh, low)


def dot_exact(v, ones):
    n = v.shape[0]
    vh, vl = split(v)
    wide = dot(jnp.concatenate([vh, vl], 0), ones)
    return wide[:n] + wide[n:]


def odd(i):
    return (i // SPAN_Y + i % SPAN_Y) % 2


def lower(rows):
    return iota((rows, 128), 1) < 64


def packs(ys):
    rows = ys[0].shape[0]
    low = lower(rows)
    column = lambda x: [
        jnp.where(low, ys[x * SPAN_Y + t][:, :128], ys[x * SPAN_Y + t + 1][:, :128]) for t in range(0, SPAN_Y, 2)
    ]
    row = lambda y: jnp.where(low, ys[y][:, 128:], ys[SPAN_Y + y][:, 128:])
    return column(0), column(SPAN_X - 1), row(0), row(SPAN_Y - 1)


def send(ys, x_ref, a_ref, b_ref, at):
    rows = pl.ds(at, ys[0].shape[0])
    west, east, south, north = packs(ys)
    first = lax.axis_index("gx") == 0
    even = lax.axis_index("gy") % 2 == 0
    for t in range(SPAN_Y // 2):
        x_ref[t, rows, :] = jnp.where(first, east[t], west[t])
    a_ref[rows, :] = jnp.where(even, north, south)
    b_ref[rows, :] = jnp.where(even, south, north)
    if at == 0:
        rest = pl.ds(b_ref.shape[0] * 2 // 3, b_ref.shape[0] - b_ref.shape[0] * 2 // 3)
        b_ref[rest, :] = jnp.zeros((rest.size, 128), F32)


def received(x_ref, a_ref, b_ref, at, n, side=None):
    rows = pl.ds(at, n)
    first = lax.axis_index("gx") == 0
    even = lax.axis_index("gy") % 2 == 0
    xs = [x_ref[t, rows, :] for t in range(SPAN_Y // 2)]
    a, b = a_ref[rows, :], b_ref[rows, :]
    if side is not None:
        a, b = a + side[:, :128], b + side[:, 128:256]
        xs = [xs[t] + side[:, 256 + 128 * t : 384 + 128 * t] for t in range(SPAN_Y // 2)]
    zero = jnp.zeros_like(a)
    return (
        [jnp.where(first, zero, v) for v in xs],
        [jnp.where(first, v, zero) for v in xs],
        jnp.where(even, b, a),
        jnp.where(even, a, b),
    )


def across(ys, nb, rows):
    low = lower(rows)
    zero = jnp.zeros((rows, 128), F32)
    inside = lambda x, y, part: zero if ys is None else ys[x * SPAN_Y + y][:, part * 128 : part * 128 + 128]
    out = []
    for x in range(SPAN_X):
        for y in range(SPAN_Y):
            beyond = lambda v: zero if nb is None else v()
            west = inside(x - 1, y, 0) if x else beyond(lambda: nb[0][y // 2])
            east = inside(x + 1, y, 0) if x < SPAN_X - 1 else beyond(lambda: nb[1][y // 2])
            south = inside(x, y - 1, 1) if y else beyond(lambda: nb[2])
            north = inside(x, y + 1, 1) if y < SPAN_Y - 1 else beyond(lambda: nb[3])
            if (x + y) % 2:
                west, east, south, north = east, west, north, south
            out.append(jnp.concatenate([jnp.where(low, west, east), jnp.where(low, south, north)], 1))
    return out


def owned_lanes(i, rows):
    lane = iota((rows, 256), 1) % 128
    return lane < 64 if odd(i) else lane >= 64


def spread_owned(v, i):
    zero = jnp.zeros_like(v)
    low = lower(v.shape[0])
    turned = pltpu.roll(v, 64, 1)
    if odd(i):
        return jnp.concatenate([jnp.where(low, v, zero), jnp.where(low, turned, zero)], 1)
    return jnp.concatenate([jnp.where(low, zero, turned), jnp.where(low, zero, v)], 1)


def take_owned(v, i):
    low = lower(v.shape[0])
    if odd(i):
        return jnp.where(low, v[:, :128], pltpu.roll(v[:, 128:], 64, 1))
    return jnp.where(low, pltpu.roll(v[:, :128], 64, 1), v[:, 128:])


def start_kernel(res_ref, dir_ref, act_ref, scale_ref, *refs):
    inverse_ref, own_ref, x_ref, a_ref, b_ref = refs[4:9]
    upper_ref, p_ref = refs[13:15]
    gx, gy = lax.axis_index("gx"), lax.axis_index("gy")
    last_x = gx * SPAN_X + SPAN_X - 1 == lax.axis_size("gx") * SPAN_X - 1
    last_y = gy * SPAN_Y + SPAN_Y - 1 == lax.axis_size("gy") * SPAN_Y - 1
    east = iota((1, 128), 1) < 64
    ys = []
    for i in range(SUBS):
        x, y = i // SPAN_Y, i % SPAN_Y
        keep = act_ref[i : i + 1, :].astype(F32)
        if x == SPAN_X - 1:
            keep = jnp.where(jnp.logical_and(last_x, east), 0.0, keep)
        if y == SPAN_Y - 1:
            keep = jnp.where(jnp.logical_and(last_y, jnp.logical_not(east)), 0.0, keep)
        mine = pl.ds(i, CASES, stride=SUBS)
        p = dir_ref[mine, :] * keep
        p_ref[mine, :] = p
        v = jnp.concatenate(
            [
                res_ref[mine, :],
                p,
                scale_ref[i : i + 1, :] * keep,
                keep,
                jnp.zeros((CAST - 2 * CASES - 2, 128), F32),
            ],
            0,
        )
        v = spread_owned(v, i)
        own_ref[i] = v
        ys.append(v)
    send(ys, x_ref, a_ref, b_ref, 0)
    for ref in (x_ref, a_ref, b_ref):
        ref.flush()
    for t, (i, j) in enumerate(UPPER):
        upper_ref[t] = inverse_ref[128 * i : 128 * i + 128, 128 * j : 128 * j + 128]


def operator_kernel(
    schur_ref, couple_ref, map_ref, slot_ref, ha_ref, la_ref, hb_ref, lb_ref, cc_ref, ch_ref, cl_ref, name_ref,
):
    none = 384
    slot = slot_ref[...].astype(F32)
    eye = iota((8, 8), 0) == iota((8, 8), 1)
    column = jnp.concatenate(
        [jnp.sum(jnp.where(eye, jnp.broadcast_to(slot[i : i + 1, :], (8, 8)), 0.0), 1, keepdims=True) for i in range(SUBS)], 0
    )
    row = jnp.concatenate([slot[i : i + 1, :] for i in range(SUBS)], 1)
    count = SUBS * 8
    earlier = iota((count, count), 1) < iota((count, count), 0)
    again = jnp.sum(jnp.where(jnp.logical_and(column == row, earlier), 1.0, 0.0), 1, keepdims=True)
    first = jnp.where(jnp.logical_and(again == 0.0, column != float(none)), 1.0, 0.0)
    first_row = jnp.sum(
        jnp.where(jnp.logical_and(column == row, iota((count, count), 0) < iota((count, count), 1)), 1.0, 0.0), 0, keepdims=True
    )
    first_row = jnp.where(jnp.logical_and(first_row == 0.0, row != float(none)), 1.0, 0.0)
    rank = jnp.sum(jnp.where(row < column, first_row, 0.0), 1, keepdims=True)
    hit = jnp.where(rank == iota((count, 128), 1).astype(F32), first, 0.0)
    name_ref[...] = jnp.broadcast_to(
        jnp.where(jnp.sum(hit, 0, keepdims=True) > 0.0, jnp.sum(hit * column, 0, keepdims=True), float(none)), (8, 128)
    )
    sub = iota((256, 256), 0)
    west = (sub // 64) % 2 == 0
    for i in range(SUBS):
        spots = map_ref[i // SPAN_Y, i % SPAN_Y : i % SPAN_Y + 1, :]
        if odd(i):
            spots = jnp.where((spots // 64) % 2 == 0, spots + 64, spots - 64)
        sign = jnp.where(west, 1.0, -1.0) if odd(i) else jnp.where(west, -1.0, 1.0)
        place = jnp.where(sub == spots, sign, 0.0).astype(BF16)
        mine = slot[i : i + 1, :]
        number = jnp.sum(jnp.where(column < mine, first, 0.0), 0, keepdims=True)
        compact = jnp.where(
            jnp.logical_and(number == iota((SLOTS, 8), 0).astype(F32), mine != float(none)), 1.0, 0.0
        )
        cc = jnp.dot(compact, couple_ref[i], precision=EXACT, preferred_element_type=F32)
        c1, rest = split(cc)
        c2, c3 = split(cc - c1.astype(F32))
        s1, s2 = split(schur_ref[i])
        tall = dot_turned(jnp.concatenate([s1, s2, c1, c2, c3], 0), place)
        high, low = (dot(place, tall[t : t + 256].astype(BF16)).astype(BF16) for t in (0, 256))
        if i < STAY:
            ha_ref[i], la_ref[i] = high, low
        else:
            hb_ref[i - STAY], lb_ref[i - STAY] = high, low
        cc = tall[512 : 512 + SLOTS] + tall[512 + SLOTS : 512 + 2 * SLOTS] + tall[512 + 2 * SLOTS :]
        cc_ref[i] = cc
        ch_ref[i], cl_ref[i] = split(cc)


def inverse_kernel(mine_ref, upper_ref, high_ref, low_ref, high_out_ref, low_out_ref):
    first = lax.axis_index("gx") == 0
    mine = mine_ref[...]
    blocks = {spot: upper_ref[t] for t, spot in enumerate(UPPER)}
    side = lambda i, j: blocks[i, j] if i <= j else jnp.transpose(blocks[j, i])
    other = jnp.concatenate([jnp.concatenate([side(i, j) for j in range(3)], 1) for i in range(3)], 0)
    for region, v in enumerate((jnp.where(first, mine, other), jnp.where(first, other, mine))):
        high, low = split(v)
        high_ref[region], low_ref[region] = high, low
        high_out_ref[region], low_out_ref[region] = high, low


def near_names(name_ref, x_ref, a_ref, b_ref):
    named = pl.ds(2 * CASES + SLOTS, 8)
    group = iota((8, 128), 1) // SLOTS
    turn = lambda v, g: jnp.where(group == g, pltpu.roll(v, g * SLOTS, 1), 0.0)
    wanted = name_ref[...] + 0.0
    wanted = jnp.where(group == 0, wanted, turn(a_ref[named, :], 1) + turn(b_ref[named, :], 2) + turn(x_ref[0, named, :], 3))
    found = iota((384, 128), 0).astype(F32) == wanted[0:1]
    mine = jnp.where(iota((384, 128), 1) < 3 * SLOTS, 1.0, 0.0)
    gx = lax.axis_index("gx")
    return [jnp.where(found, jnp.where(gx == region, mine, 1.0 - mine), 0.0).astype(BF16) for region in range(2)]


def near_spread(x_ref, a_ref, b_ref, nh_ref, nl_ref):
    rows = pl.ds(2 * CASES, SLOTS)
    nh_ref[...], nl_ref[...] = split(
        jnp.concatenate([a_ref[rows, :], b_ref[rows, :], x_ref[0, rows, :], x_ref[1, rows, :]], 1)
    )


def operator(ys, x_ref, a_ref, b_ref, near, mk_ref, ch_ref, cl_ref, nh_ref, nl_ref):
    n = ys[0].shape[0]
    high, low = nh_ref[...], nl_ref[...]
    side = jnp.concatenate(
        [
            dot_split(near[g], high[:, at : at + width], low[:, at : at + width])
            for g, at, width in ((1, 0, 128), (2, 128, 128), (3, 256, 256))
        ],
        1,
    )
    west, east, south, north = received(x_ref, a_ref, b_ref, 0, n, side)
    ys = [ys[i] + dot_split(near[0], ch_ref[i], cl_ref[i]) for i in range(SUBS)]
    other = across(ys, (west, east, south, north), n)
    return [mk_ref[i, 1:2, :] * (ys[i] + other[i]) for i in range(SUBS)]


def corners(us, ch_ref, cl_ref):
    couple = lambda ref: jnp.concatenate([ref[i] for i in range(SUBS)], 0)
    corner = dot_split(jnp.concatenate(us, 0), couple(ch_ref), couple(cl_ref), dot_turned)
    n = us[0].shape[0]
    group = iota((n, 128), 1) // SLOTS
    total = jnp.zeros((n, 128), F32)
    for i in range(SUBS):
        part = corner[n * i : n * i + n, 128 * (i // 4) : 128 * (i // 4) + 128]
        total = total + jnp.where(group == i % 4, part, 0.0)
    total = total + pltpu.roll(total, 64, 1)
    return total + pltpu.roll(total, 32, 1)


def by_schur(us, ha_ref, la_ref, hb_ref, lb_ref):
    return [
        dot_split(us[i], ha_ref[i], la_ref[i]) if i < STAY else dot_split(us[i], hb_ref[i - STAY], lb_ref[i - STAY])
        for i in range(SUBS)
    ]


def over_lanes(terms):
    total = terms[0]
    for t in terms[1:]:
        total = total + t
    return jnp.sum(total[:, :128] + total[:, 128:], 1, keepdims=True)


def packed(corner, one, two):
    slot = iota((CASES, 128), 1) % SLOTS
    full = jnp.where(slot == USED, one, jnp.where(slot == USED + 1, two, corner))
    group = iota((4, 128), 1) // SLOTS
    out = jnp.zeros((4, 128), F32)
    for b in range(4):
        out = jnp.where(group == b, full[4 * b : 4 * b + 4], out)
    return out


def by_slot(vs):
    group = iota((8, 128), 1) // SLOTS
    out = []
    for region in range(2):
        rows = []
        for b in range(4):
            halves = []
            for h in range(2):
                acc = None
                for q in range(4):
                    v = vs[8 * region + 4 * h + q]
                    turned = v if q == b else pltpu.roll(v, (SLOTS * (q - b)) % 128, 1)
                    acc = turned if acc is None else jnp.where(group == q, turned, acc)
                halves.append(acc)
            rows.append(jnp.concatenate(halves, 1))
        out.append(jnp.concatenate(rows, 0))
    return out


def inner(vs):
    total = vs[0]
    for v in vs[1:]:
        total = total + v
    total = total[:4] + total[4:]
    tall = jnp.concatenate([total] * 4, 0)
    lane, row = iota((CASES, 128), 1), iota((CASES, 128), 0)
    column = lambda s: jnp.sum(jnp.where(lane == SLOTS * (row // 4) + s, tall, 0.0), 1, keepdims=True)
    return column(USED), column(USED + 1)


def first_of_pairs(v):
    return jnp.concatenate([v[8 * b : 8 * b + 4] for b in range(v.shape[0] // 8)], 0)


def solve(spots, pick_ref, gh_ref, gl_ref, near_ref):
    totals, sols, near = [], [], None
    for region in range(2):
        v = spots[region]
        n = v.shape[0]
        even = dot_exact(v, pick_ref[region, 0])
        odds = dot_exact(v, pick_ref[region, 1])
        z = jnp.where((iota((n, 384), 0) // 4) % 2 == 0, even, odds).reshape(n // 8, 8, 384)
        total = (z + pltpu.roll(z, 4, 1)).reshape(n, 384)
        sol = dot_split(total, gh_ref[region], gl_ref[region])
        part = dot_exact(sol, near_ref[region])
        near = part if near is None else near + part
        totals.append(total)
        sols.append(sol)
    return totals, sols, near


def swap_pairs(v):
    rows, lanes = v.shape
    return pltpu.roll(v.reshape(rows // 8, 8, lanes), 4, 1).reshape(rows, lanes)


def ahead(region, t):
    gx, gy = lax.axis_index("gx"), lax.axis_index("gy")
    return 8 * lax.rem(gx + region, 2) + lax.rem(gy // 2 + t, 8)


def dense_kernel(got_ref, gh_ref, gl_ref, dh_ref, dl_ref):
    group = iota((8, 128), 1) // SLOTS
    for region in range(2):
        hits = []
        for par in range(2):
            halves = []
            for h in range(2):
                acc = None
                for q in range(4):
                    v = got_ref[3 * ahead(region, 4 * h + q) + 1 + par]
                    v = v if par == 0 else pltpu.roll(v, 4, 0)
                    turned = pltpu.roll(v, SLOTS * q, 1) if q else v
                    acc = turned if acc is None else jnp.where(group == q, turned, acc)
                halves.append(acc[0:1])
            wanted = jnp.concatenate(halves, 1)
            hits.append(jnp.where(iota((384, 256), 0).astype(F32) == wanted, 1.0, 0.0))
        picks = jnp.concatenate(hits, 1).astype(BF16)
        rows = [jnp.transpose(hit).astype(BF16) for hit in hits]
        which = lax.rem(lax.axis_index("gx") + region, 2)
        for whole_ref, out_ref in ((gh_ref, dh_ref), (gl_ref, dl_ref)):
            half = dot(whole_ref[which], picks).astype(BF16)
            top = dot(rows[0], half).astype(BF16)
            out_ref[region, 0], out_ref[region, 1] = top[:, :256], top[:, 256:]
            out_ref[region, 2] = dot(rows[1], half[:, 256:]).astype(BF16)


def solve_dense(spots, dh_ref, dl_ref):
    total, sols = None, []
    for region in range(2):
        v = spots[region]
        block = lambda t, dot=dot: dot_split(v, dh_ref[region, t], dl_ref[region, t], dot)
        first = (iota(v.shape, 0) // 4) % 2 == 0
        sol = jnp.where(first, block(0) + swap_pairs(block(1, dot_turned)), block(2) + swap_pairs(block(1)))
        total = v * sol if total is None else total + v * sol
        sols.append(sol)
    total = jnp.sum(total, 1, keepdims=True)
    halves = lambda v: [jnp.concatenate([v[8 * b + at : 8 * b + at + 4] for b in range(4)], 0) for at in (0, 4)]
    total = sum(halves(total))
    even = lax.axis_index("gy") % 2 == 0
    (a, b), (c, d) = halves(sols[0]), halves(sols[1][:, :128])
    here = jnp.where(even, a[:, :128], b[:, :128])
    pair = jnp.where(even, b[:, :128], a[:, :128])
    beyond = jnp.where(even, pltpu.roll(b[:, 128:], SLOTS, 1), pltpu.roll(a[:, :128], 128 - SLOTS, 1))
    along = jnp.where(even, c, d)
    return total, [v[:, :SLOTS] for v in (here, pair, beyond, along)]


def energy(totals, sols):
    both = totals[0] * sols[0] + totals[1] * sols[1]
    return first_of_pairs(jnp.sum(both, 1, keepdims=True))


def emit(rs, mk_ref, schur_refs, ch_ref, cl_ref, block_ref, y_ref, x_ref, a_ref, b_ref):
    us = [mk_ref[i, 0:1, :] * rs[i] for i in range(SUBS)]
    corner = corners(us, ch_ref, cl_ref)
    rho = over_lanes([jnp.where(owned_lanes(i, CASES), rs[i] * us[i], 0.0) for i in range(SUBS)])
    ys = by_schur(us, *schur_refs)
    send(ys, x_ref, a_ref, b_ref, 0)
    for i in range(SUBS):
        y_ref[i] = ys[i]
    for ref in (x_ref, a_ref, b_ref, y_ref):
        ref.flush()
    delta = over_lanes([us[i] * ys[i] for i in range(SUBS)])
    block = packed(corner, rho, delta)
    twice = jnp.concatenate([block, block], 0)
    for j in range(16):
        block_ref[j] = twice
    block_ref.flush()


def first_kernel(
    own_ref, x_ref, a_ref, b_ref, ha_ref, la_ref, hb_ref, lb_ref, cc_ref, ch_ref, cl_ref, name_ref,
    r_ref, mk_ref, y_ref, block_ref, sx_ref, sa_ref, sb_ref, high_out_ref, low_out_ref,
):
    schur_refs = ha_ref, la_ref, hb_ref, lb_ref
    own = [own_ref[i] for i in range(SUBS)]
    other = across(own, received(x_ref, a_ref, b_ref, 0, CAST), CAST)
    rs, vs = [], []
    for i in range(SUBS):
        full = own[i] + other[i]
        rs.append(full[:CASES])
        r_ref[i] = full[:CASES]
        mk_ref[i] = full[2 * CASES : 2 * CASES + 8]
        vs.append(jnp.concatenate([full[2 * CASES : 2 * CASES + 1] * full[:CASES], full[CASES : 2 * CASES]], 0))
    corner = corners(vs, ch_ref, cl_ref)
    ys = by_schur(vs, *schur_refs)
    names = name_ref[...]
    send([jnp.concatenate([ys[i], cc_ref[i]], 0) for i in range(SUBS)], sx_ref, sa_ref, sb_ref, 0)
    at = pl.ds(2 * CASES + SLOTS, 8)
    for t in range(SPAN_Y // 2):
        sx_ref[t, at, :] = names
    sa_ref[at, :] = names
    sb_ref[at, :] = names
    us = [v[:CASES] for v in vs]
    ps = [v[CASES:] for v in vs]
    rho = over_lanes([jnp.where(owned_lanes(i, CASES), rs[i] * us[i], 0.0) for i in range(SUBS)])
    delta = over_lanes([us[i] * ys[i][:CASES] for i in range(SUBS)])
    cross = over_lanes([ps[i] * ys[i][:CASES] for i in range(SUBS)])
    eta = over_lanes([ps[i] * ys[i][CASES:] for i in range(SUBS)])
    one, two = packed(corner[:CASES], rho, delta), packed(corner[CASES:], cross, eta)
    blocks = [
        jnp.concatenate([one, two], 0),
        jnp.concatenate([names[:4], one], 0),
        jnp.concatenate([two, names[:4]], 0),
    ]
    for j in range(16):
        for t in range(3):
            block_ref[3 * j + t] = blocks[t]
    for i in range(SUBS):
        y_ref[i] = ys[i]


def column_of(row):
    eye = iota((CASES, CASES), 0) == iota((CASES, CASES), 1)
    return jnp.sum(jnp.where(eye, jnp.broadcast_to(row, (CASES, CASES)), 0.0), 1, keepdims=True)


def keep_scalars(scal_ref, values):
    for t, v in enumerate(values):
        scal_ref[t] = jnp.broadcast_to(v, (CASES, 128))


def second_kernel(
    got_ref, x_ref, a_ref, b_ref, y_ref, r_ref, mk_ref, p_ref, l_ref, rho_ref, gh_ref, gl_ref, name_ref,
    ha_ref, la_ref, hb_ref, lb_ref, ch_ref, cl_ref,
    nh_ref, nl_ref, po_ref, lo_ref, ro_ref, so_ref, scal_ref, block_ref, yo_ref, sx_ref, sa_ref, sb_ref,
):
    near_ref, pick_ref = near_names(name_ref, x_ref, a_ref, b_ref), {}
    near_spread(x_ref, a_ref, b_ref, nh_ref, nl_ref)
    top = iota((8, 128), 0) < 4
    us, ps, names = [], [], []
    for j in range(16):
        v = [got_ref[3 * j + t] for t in range(3)]
        us.append(jnp.where(top, v[0], v[1]))
        ps.append(pltpu.roll(jnp.where(top, v[2], v[0]), 4, 0))
        names.append((v[1], pltpu.roll(v[2], 4, 0)))
    group = iota((8, 128), 1) // SLOTS
    for region in range(2):
        for par in range(2):
            halves = []
            for h in range(2):
                acc = None
                for q in range(4):
                    v = names[8 * region + 4 * h + q][par]
                    turned = pltpu.roll(v, SLOTS * q, 1) if q else v
                    acc = turned if acc is None else jnp.where(group == q, turned, acc)
                halves.append(acc[0:1])
            wanted = jnp.concatenate(halves, 1)
            hit = jnp.where(iota((384, 256), 0).astype(F32) == wanted, 1.0, 0.0)
            pick_ref[region, par] = jnp.transpose(hit).astype(BF16)
    lhs_u, lhs_p = by_slot(us), by_slot(ps)
    n = lhs_u[0].shape[0]
    totals, sols, near = solve(
        [jnp.concatenate([lhs_u[t], lhs_p[t]], 0) for t in range(2)], pick_ref, gh_ref, gl_ref, near_ref
    )
    of_u, of_p = lambda vs: [v[:n] for v in vs], lambda vs: [v[n:] for v in vs]
    rho, delta = inner(us)
    cross, eta = inner(ps)
    delta = delta + energy(of_u(totals), of_u(sols))
    cross = cross + energy(of_p(totals), of_u(sols))
    eta = eta + energy(of_p(totals), of_p(sols))
    near = first_of_pairs(near)
    near = [(pltpu.roll(near, 128 - SLOTS * g, 1) if g else near)[:, :SLOTS] for g in range(4)]
    beta = rho / column_of(rho_ref[...])
    skew = cross + beta * eta
    pi = delta + 2.0 * beta * skew - beta * beta * eta
    alpha = rho / pi
    fs = operator([y_ref[i] for i in range(SUBS)], x_ref, a_ref, b_ref, near, mk_ref, ch_ref, cl_ref, nh_ref, nl_ref)
    rs = []
    for i in range(SUBS):
        f, r = fs[i], r_ref[i]
        s = f[:CASES] + beta * f[CASES:]
        r = r - alpha * s
        rs.append(r)
        ro_ref[i], so_ref[i] = r, s
    scalars = rho, pi, beta, skew, alpha
    keep_scalars(scal_ref, scalars)
    so_ref.flush()
    emit(rs, mk_ref, (ha_ref, la_ref, hb_ref, lb_ref), ch_ref, cl_ref, block_ref, yo_ref, sx_ref, sa_ref, sb_ref)

    @pl.when(lax.axis_index("gx") >= 0)
    def _():
        track(r_ref, scalars, mk_ref, p_ref, l_ref, po_ref, lo_ref)


def absorb(got_ref, x_ref, a_ref, b_ref, y_ref, r_ref, s_ref, scal_ref, mk_ref, dh_ref, dl_ref, nh_ref, nl_ref, ch_ref, cl_ref):
    vs = [got_ref[ahead(region, t)] for region in range(2) for t in range(8)]
    coarse, near = solve_dense(by_slot(vs), dh_ref, dl_ref)
    rho, delta = inner(vs)
    delta = delta + coarse
    rho_old, pi, beta, skew = (scal_ref[t][:, 0:1] for t in range(4))
    skew = beta * skew
    beta = rho / rho_old
    pi = delta + 2.0 * beta * skew - beta * beta * pi
    alpha = rho / pi
    fs = operator([y_ref[i] for i in range(SUBS)], x_ref, a_ref, b_ref, near, mk_ref, ch_ref, cl_ref, nh_ref, nl_ref)
    ss = [fs[i] + beta * s_ref[i] for i in range(SUBS)]
    rs = [r_ref[i] - alpha * ss[i] for i in range(SUBS)]
    return rs, ss, (rho, pi, beta, skew, alpha)


def track(r_ref, scalars, mk_ref, p_ref, l_ref, po_ref, lo_ref):
    _, _, beta, _, alpha = scalars
    for i in range(SUBS):
        mine = pl.ds(i, CASES, stride=SUBS)
        p = take_owned(mk_ref[i, 0:1, :] * r_ref[i], i) + beta * p_ref[mine, :]
        po_ref[mine, :] = p
        lo_ref[mine, :] = l_ref[mine, :] + alpha * p


def round_kernel(
    got_ref, x_ref, a_ref, b_ref, y_ref, r_ref, s_ref, scal_ref, mk_ref, dh_ref, dl_ref,
    nh_ref, nl_ref, ch_ref, cl_ref, p_ref, l_ref, ha_ref, la_ref, hb_ref, lb_ref,
    po_ref, lo_ref, ro_ref, so_ref, scalo_ref, block_ref, yo_ref, sx_ref, sa_ref, sb_ref,
):
    rs, ss, scalars = absorb(
        got_ref, x_ref, a_ref, b_ref, y_ref, r_ref, s_ref, scal_ref, mk_ref, dh_ref, dl_ref, nh_ref, nl_ref, ch_ref, cl_ref
    )
    for i in range(SUBS):
        ro_ref[i], so_ref[i] = rs[i], ss[i]
    so_ref.flush()
    keep_scalars(scalo_ref, scalars)
    emit(rs, mk_ref, (ha_ref, la_ref, hb_ref, lb_ref), ch_ref, cl_ref, block_ref, yo_ref, sx_ref, sa_ref, sb_ref)

    @pl.when(lax.axis_index("gx") >= 0)
    def _():
        track(r_ref, scalars, mk_ref, p_ref, l_ref, po_ref, lo_ref)


def last_kernel(
    got_ref, x_ref, a_ref, b_ref, y_ref, r_ref, s_ref, scal_ref, mk_ref, dh_ref, dl_ref, nh_ref, nl_ref, ch_ref, cl_ref,
    p_ref, l_ref, lo_ref, ro_ref, po_ref,
):
    rs, _, scalars = absorb(
        got_ref, x_ref, a_ref, b_ref, y_ref, r_ref, s_ref, scal_ref, mk_ref, dh_ref, dl_ref, nh_ref, nl_ref, ch_ref, cl_ref
    )
    track(r_ref, scalars, mk_ref, p_ref, l_ref, po_ref, lo_ref)
    for i in range(SUBS):
        ro_ref[pl.ds(i, CASES, stride=SUBS), :] = take_owned(rs[i], i)


class Fetched:
    def __init__(self, source, buffer, semaphore):
        self.buffer = buffer
        self.copy = pltpu.make_async_copy(source, buffer, semaphore)
        self.copy.start()
        self.here = False

    def wait(self):
        self.copy.wait()
        self.here = True

    def __getitem__(self, index):
        if not self.here:
            self.wait()
        return self.buffer[index]


class FetchedPieces:
    def __init__(self, source, buffer, semaphore, count):
        self.buffer = buffer
        step = buffer.shape[0] // count
        self.parts = [
            Fetched(source.at[pl.ds(i * step, step)], buffer.at[pl.ds(i * step, step)], semaphore.at[i])
            for i in range(count)
        ]
        self.here = False

    def wait(self):
        for part in self.parts:
            part.copy.wait()
        self.here = True

    def __getitem__(self, index):
        if not self.here:
            self.wait()
        return self.buffer[index]


class Stored:
    def __init__(self, target, buffer, semaphore):
        self.buffer = buffer
        self.copy = pltpu.make_async_copy(buffer, target, semaphore)
        self.sent = False

    def __setitem__(self, index, value):
        self.buffer[index] = value

    def __getitem__(self, index):
        return self.buffer[index]

    @property
    def shape(self):
        return self.buffer.shape

    def flush(self):
        if not self.sent:
            self.copy.start()
            self.sent = True


class Kept:
    def __init__(self, ref):
        self.ref = ref

    def __setitem__(self, index, value):
        self.ref[index] = value

    def __getitem__(self, index):
        return self.ref[index]

    def flush(self):
        pass


def call(kernel, args, outs, kept=(), kept_out=(), raw=(), through=None, flops=None, late=0, pieces=None):
    through, pieces = through or {}, pieces or {}
    moved = [i for i in range(len(args)) if i not in kept and i not in raw]
    written = [i for i in range(len(outs)) if i not in kept_out and i not in through]

    def body(*refs):
        ins, results = refs[: len(args)], refs[len(args) : len(args) + len(outs)]
        buffers, (in_sem, out_sem, through_sem) = refs[len(args) + len(outs) : -3], refs[-3:]
        fetched, stored = list(ins), [Kept(ref) for ref in results]
        for i in sorted(moved, key=lambda i: i not in pieces):
            t, at = moved.index(i), sum(pieces.get(m, 1) for m in moved[: moved.index(i)])
            if i in pieces:
                fetched[i] = FetchedPieces(ins[i], buffers[t], in_sem.at[pl.ds(at, pieces[i])], pieces[i])
            else:
                fetched[i] = Fetched(ins[i], buffers[t], in_sem.at[at])
        for t, i in enumerate(written):
            stored[i] = Stored(results[i], buffers[len(moved) + t], out_sem.at[t])
        passing = [
            pltpu.make_async_copy(source(ins), results[i], through_sem.at[t]) for t, (i, source) in enumerate(through.items())
        ]
        for copy in passing:
            copy.start()
        if moved or passing:
            spot = (0,) * (len(outs[-1 - late][0]) - 2)
            blank = stored[-1 - late]

            @pl.when(lax.axis_index("gx") >= 0)
            def _():
                blank[spot] = jnp.zeros(outs[-1 - late][0][-2:], outs[-1 - late][1])

        kernel(*fetched, *stored)
        for i in written:
            stored[i].flush()
        for i in moved:
            if not fetched[i].here:
                fetched[i].wait()
        for copy in passing:
            copy.wait()
        for i in written:
            stored[i].copy.wait()

    place = lambda held: pl.BlockSpec(memory_space=pltpu.VMEM if held else pltpu.HBM)
    semaphores = lambda n: pltpu.SemaphoreType.DMA((max(n, 1),))
    args = [a if i in kept else pltpu.with_memory_space_constraint(a, pltpu.HBM) for i, a in enumerate(args)]
    return pl.pallas_call(
        body,
        out_shape=[
            jax.ShapeDtypeStruct(*out) if i in kept_out else pltpu.HBM(*out) for i, out in enumerate(outs)
        ],
        in_specs=[place(i in kept) for i in range(len(args))],
        out_specs=[place(i in kept_out) for i in range(len(outs))],
        scratch_shapes=[pltpu.VMEM(args[i].shape, args[i].dtype) for i in moved]
        + [pltpu.VMEM(*outs[i]) for i in written]
        + [semaphores(sum(pieces.get(i, 1) for i in moved)), semaphores(len(written)), semaphores(len(through))],
        compiler_params=pltpu.CompilerParams(vmem_limit_bytes=LIMIT),
        cost_estimate=flops and pl.CostEstimate(flops=flops, bytes_accessed=flops // 512, transcendentals=0),
    )(*args)


def trade(x, a, b):
    peers = lax.axis_size("gy")
    return (
        lax.ppermute(x, "gx", [(0, 1), (1, 0)]),
        lax.ppermute(a, "gy", both_ways(pairs_from(0, peers))),
        lax.ppermute(b, "gy", both_ways(pairs_from(1, peers))),
    )


def two_regions(
    duals, residual, direction, prev_rho, dual_schur, coupling, coarse_inverse, edge_map, corner_slot, active, scaling
):
    native = lambda v: v.reshape(CASES * SUBS, 128)
    by_sub = lambda v: v.reshape((SUBS,) + v.shape[2:])
    width = coarse_inverse.shape[-1]
    sends = lambda rows: [((SPAN_Y // 2, rows, 128), F32), ((rows, 128), F32), ((-(-3 * rows // 16) * 8, 128), F32)]
    state = ((SUBS, CASES, 256), F32)
    plain = ((CASES * SUBS, 128), F32)

    raw = [by_sub(dual_schur), by_sub(coupling), edge_map, by_sub(corner_slot)]
    own, *out, schur, coupled, placed, slotted, inverse, p = call(
        start_kernel,
        [native(residual), native(direction), by_sub(active), by_sub(scaling), *raw, coarse_inverse[0]],
        [((SUBS, CAST, 256), F32)] + sends(CAST) + [(v.shape, v.dtype) for v in raw] + [((len(UPPER), 128, 128), F32), plain],
        kept_out=(0, 4, 5, 6, 7),
        raw=(4, 5, 6, 7),
        through={4: lambda v: v[4], 5: lambda v: v[5], 6: lambda v: v[6], 7: lambda v: v[7]},
    )
    come = trade(*out)
    other = lax.ppermute(inverse, "gx", [(0, 1), (1, 0)])
    first_part, rest = ((STAY, 256, 256), BF16), ((SUBS - STAY, 256, 256), BF16)
    couple = ((SUBS, SLOTS, 256), BF16)
    ha, la, hb, lb, cc, ch, cl, names = call(
        operator_kernel,
        [schur, coupled, placed, slotted],
        [first_part, first_part, rest, rest, ((SUBS, SLOTS, 256), F32), couple, couple, ((8, 128), F32)],
        kept=range(4),
        kept_out=range(8),
        flops=5 * 10**9,
    )
    rows = 2 * CASES + SLOTS + 8
    r, mk, y, block, *out, hb, lb = call(
        first_kernel,
        [own, *come, ha, la, hb, lb, cc, ch, cl, names],
        [state, ((SUBS, 8, 256), F32), ((SUBS, 2 * CASES, 256), F32), ((48, 8, 128), F32)]
        + sends(rows)
        + [rest, rest],
        kept=range(12),
        kept_out=(0, 1, 2),
        through={7: lambda v: v[6], 8: lambda v: v[7]},
        late=2,
    )
    got = lax.all_to_all(block.reshape(32, 3, 4, 128), BOTH, 0, 0, tiled=False).reshape(48, 8, 128)
    come = trade(*out)
    square = ((2, width, width), BF16)
    gh, gl, gh_far, gl_far = call(
        inverse_kernel, [coarse_inverse[0], other], [square] * 4, kept_out=(0, 1), flops=10**9
    )
    side = ((SLOTS, 512), BF16)
    onward = [plain, plain, state, state, ((5, CASES, 128), F32), ((16, 8, 128), F32), state] + sends(CASES)
    nh, nl, p, lam, r, s, scal, block, y, *out = call(
        second_kernel,
        [got, *come, y, r, mk, p, native(duals), prev_rho.reshape(1, CASES), gh, gl, names, ha, la, hb, lb, ch, cl],
        [side, side] + onward,
        kept=(0, 1, 2, 3, 4, 5, 6, 10, 11, 12, 13, 14, 17, 18),
        kept_out=(0, 1, 2, 3, 4, 6, 8),
        late=3,
    )
    dense = ((2, 3, 256, 256), BF16)
    dh, dl = call(dense_kernel, [got, gh_far, gl_far], [dense, dense], kept_out=(0, 1), flops=3 * 10**9)
    for step in range(1, ITERS):
        got = lax.all_to_all(block.reshape(32, 4, 128), BOTH, 0, 0, tiled=False).reshape(16, 8, 128)
        come = trade(*out)
        args = [got, *come, y, r, s, scal, mk, dh, dl, nh, nl, ch, cl, p, lam]
        kept = (*range(6), *range(7, 17))
        if step < ITERS - 1:
            p, lam, r, s, scal, block, y, *out = call(
                round_kernel, args + [ha, la, hb, lb], onward, (*kept, 17, 18), kept_out=(0, 1, 2, 4, 6), late=3
            )
        else:
            results = call(last_kernel, args, [plain, plain, plain], kept)
    return tuple(v.reshape(duals.shape) for v in results)


def shards(*args):
    cases, span_x, span_y, owned = args[0].shape
    fits = (cases, span_x, span_y, owned, args[6].shape[-1]) == (CASES, SPAN_X, SPAN_Y, 128, 384)
    if fits and lax.axis_size("gx") == 2 and lax.axis_size("gy") == 16:
        return two_regions(*args)
    return general(*args)


def solution(mesh):
    placed = (
        P(None, "gx", "gy", None),
        P(None, "gx", "gy", None),
        P(None, "gx", "gy", None),
        P(),
        P("gx", "gy", None, None),
        P("gx", "gy", None, None),
        P("gx", None, None),
        P("gx", "gy", None),
        P("gx", "gy", None),
        P("gx", "gy", None),
        P("gx", "gy", None),
    )
    return jax.shard_map(
        shards,
        mesh=mesh,
        in_specs=placed,
        out_specs=(P(None, "gx", "gy", None), P(None, "gx", "gy", None), P(None, "gx", "gy", None)),
        check_vma=False,
    )
```

```python
import jax
import jax.numpy as jnp
from jax import lax
from jax.experimental import pallas as pl
from jax.experimental.pallas import tpu as pltpu
from jax.sharding import PartitionSpec as P

ITERS = 6
HIGH = lax.Precision.HIGH
EXACT = lax.Precision.HIGHEST
BOTH = ("gx", "gy")


def pairs_from(first, peers):
    return [(i, i + 1) for i in range(first, peers - 1, 2)]


def both_ways(pairs):
    return pairs + [(b, a) for a, b in pairs]


def up_gy(value, peers):
    even = lax.ppermute(value, "gy", pairs_from(0, peers))
    odd = lax.ppermute(value, "gy", pairs_from(1, peers))
    return jnp.where(lax.axis_index("gy") % 2 == 1, even, odd)


def swap_gy(low, high, peers):
    is_even = lax.axis_index("gy") % 2 == 0
    first = lax.ppermute(jnp.where(is_even, high, low), "gy", both_ways(pairs_from(0, peers)))
    second = lax.ppermute(jnp.where(is_even, low, high), "gy", both_ways(pairs_from(1, peers)))
    return jnp.where(is_even, second, first), jnp.where(is_even, first, second)


def swap_gx(low, high, peers):
    if peers == 2:
        is_first = lax.axis_index("gx") == 0
        got = lax.ppermute(jnp.where(is_first, high, low), "gx", [(0, 1), (1, 0)])
        zero = jnp.zeros_like(got)
        return jnp.where(is_first, zero, got), jnp.where(is_first, got, zero)
    below = lax.ppermute(high, "gx", [(i, i + 1) for i in range(peers - 1)])
    above = lax.ppermute(low, "gx", [(i + 1, i) for i in range(peers - 1)])
    return below, above


def everywhere(block, axes):
    sent = jnp.broadcast_to(block[None], (lax.axis_size(axes),) + block.shape)
    return lax.all_to_all(sent, axes, 0, 0, tiled=False)


def general(
    duals, residual, direction, prev_rho, dual_schur, coupling, coarse_inverse, edge_map, corner_slot, active, scaling
):
    cases, span_x, span_y, owned = duals.shape
    half = owned // 2
    full = 2 * owned
    corners = coupling.shape[2]
    width_c = coarse_inverse.shape[-1]
    peers_x, peers_y = lax.axis_size("gx"), lax.axis_size("gy")
    whole = peers_x == 2
    axes = BOTH if whole else "gy"
    regions = peers_x if whole else 1
    peers = regions * peers_y
    here_x, here_y = lax.axis_index("gx"), lax.axis_index("gy")
    used = 2 * (span_x + 1) * (span_y + 1)
    slots = used + 2

    columns = here_x * span_x + jnp.arange(span_x)
    rowset = here_y * span_y + jnp.arange(span_y)
    east_ok = jnp.broadcast_to((columns < span_x * peers_x - 1)[:, None, None], (span_x, span_y, half))
    north_ok = jnp.broadcast_to((rowset < span_y * peers_y - 1)[None, :, None], (span_x, span_y, half))
    keep_own = active.astype(jnp.float32) * jnp.concatenate([east_ok, north_ok], -1).astype(jnp.float32)
    scale_own = keep_own * scaling

    by_place = lambda v: jnp.transpose(v, (1, 2, 0, 3))
    lam = by_place(duals)
    p = keep_own[:, :, None] * by_place(direction)
    stacked = jnp.concatenate([by_place(residual), p, scale_own[:, :, None], keep_own[:, :, None]], 2)
    part_e, part_n = stacked[..., :half], stacked[..., half:]
    from_west = lax.ppermute(part_e[-1], "gx", [(i, i + 1) for i in range(peers_x - 1)])
    from_south = up_gy(part_n[:, -1], peers_y)
    west = jnp.concatenate([from_west[None], part_e[:-1]], 0)
    south = jnp.concatenate([from_south[:, None], part_n[:, :-1]], 1)
    stacked = jnp.concatenate([west, part_e, south, part_n], -1)
    r = stacked[:, :, :cases]
    p_all = stacked[:, :, cases : 2 * cases]
    scale = stacked[:, :, 2 * cases : 2 * cases + 1]
    keep = stacked[:, :, 2 * cases + 1 :]

    sign = jnp.concatenate([-jnp.ones(half), jnp.ones(half), -jnp.ones(half), jnp.ones(half)]).astype(jnp.float32)
    place = (edge_map[..., None] == jnp.arange(full, dtype=jnp.int32)).astype(jnp.float32) * sign
    schur = jnp.einsum("xyij,xyjf->xyif", dual_schur, place, precision=EXACT)
    schur = jnp.einsum("xyie,xyif->xyef", place, schur, precision=EXACT)
    couple = jnp.einsum("xycj,xyjf->xycf", coupling, place, precision=EXACT)

    flat = corner_slot.reshape(-1)
    count = flat.shape[0]
    order = jnp.arange(count)
    same = flat[:, None] == flat[None, :]
    first = ~jnp.any(same & (order[None, :] < order[:, None]), 1) & (flat != width_c)
    rank = jnp.sum((flat[None, :] < flat[:, None]) & first[None, :], 1)
    local_slot = jnp.arange(slots)
    compact = ((rank[:, None] == local_slot) & (flat != width_c)[:, None]).astype(jnp.float32)
    named = jnp.where(
        jnp.any(compact > 0, 0), jnp.max(compact * flat[:, None].astype(jnp.float32), 0), float(width_c)
    )
    compact = compact.reshape(span_x, span_y, corners, slots)
    gather_c = jnp.einsum("xycs,xycf->xysf", compact, couple, precision=EXACT)

    blocks = lambda a: (a[..., :half], a[..., half : 2 * half], a[..., 2 * half : 3 * half], a[..., 3 * half :])

    def jump(y, from_w, from_e, from_s, from_n):
        w, e, s, n = blocks(y)
        w_nb = jnp.concatenate([from_w[None], e[:-1]], 0)
        e_nb = jnp.concatenate([w[1:], from_e[None]], 0)
        s_nb = jnp.concatenate([from_s[:, None], n[:, :-1]], 1)
        n_nb = jnp.concatenate([s[:, 1:], from_n[:, None]], 1)
        return jnp.concatenate([w + w_nb, e + e_nb, s + s_nb, n + n_nb], -1)

    def rims(y):
        w, e, s, n = blocks(y)
        return w[0], e[-1], s[:, 0], n[:, -1]

    def exchange(y):
        w, e, s, n = rims(y)
        from_w, from_e = swap_gx(w, e, peers_x)
        from_s, from_n = swap_gy(s, n, peers_y)
        return from_w, from_e, from_s, from_n

    def put(rim, name):
        zero = jnp.zeros((span_x, span_y, rim.shape[-2], half), jnp.float32)
        parts = [zero, zero, zero, zero]
        if name == 0:
            parts[0] = zero.at[0].set(rim)
        elif name == 1:
            parts[1] = zero.at[-1].set(rim)
        elif name == 2:
            parts[2] = zero.at[:, 0].set(rim)
        else:
            parts[3] = zero.at[:, -1].set(rim)
        return jnp.concatenate(parts, -1)

    nb = exchange(gather_c)
    none = [jnp.zeros_like(v) for v in nb]
    spread = jnp.concatenate([jump(gather_c, *none)] + [put(v, i) for i, v in enumerate(nb)], 2)
    spread = spread * keep

    region_inv = coarse_inverse[0]

    def local_part(v):
        y = jnp.einsum("xykj,xyji->xyki", v, schur, precision=HIGH)
        c = jnp.einsum("xykj,xysj->ks", v, gather_c[:, :, :used], precision=HIGH)
        return y, c

    def over_cases(a, b):
        return jnp.sum(a * b, axis=(0, 1, 3))

    def pack(c, one, two):
        return jnp.concatenate([c, one[:, None], two[:, None]], 1).reshape(-1, 128)

    def unpack(got):
        got = got.reshape(peers, cases, slots)
        sums = jnp.sum(got[:, :, used:], 0)
        return jnp.transpose(got, (1, 0, 2)).reshape(cases, regions, peers_y, slots), sums[:, 0], sums[:, 1]

    def own_part(a):
        return jnp.concatenate([a[..., half : 2 * half], a[..., 3 * half :]], -1)

    u = scale * r
    both = jnp.concatenate([u, p_all], 2)
    y, c = local_part(both)
    yu, yp = y[:, :, :cases], y[:, :, cases:]
    rho_part = over_cases(own_part(r), own_part(u))
    names = jnp.concatenate([named, jnp.zeros(4 * 128 - slots, jnp.float32)]).reshape(4, 128)
    block = jnp.concatenate(
        [pack(c[:cases], rho_part, over_cases(u, yu)), pack(c[cases:], over_cases(p_all, yu), over_cases(p_all, yp)), names]
    )
    got = everywhere(block, axes)
    from_all = exchange(y)

    rows = cases * slots // 128
    slot_of = got[:, 2 * rows :].reshape(peers, -1)[:, :slots].reshape(regions, peers_y * slots)

    if whole:
        other = lax.ppermute(region_inv, "gx", [(0, 1), (1, 0)])
        inverses = jnp.where(here_x == 0, jnp.stack([region_inv, other]), jnp.stack([other, region_inv]))
    else:
        inverses = region_inv[None]
    pick = (slot_of[..., None] == jnp.arange(width_c, dtype=jnp.float32)).astype(jnp.float32)
    dense = jnp.einsum("ran,rnm->ram", pick, inverses, precision=EXACT)
    dense = jnp.einsum("ram,rbm->rab", dense, pick, precision=EXACT)

    def solve(c_all):
        flat_c = c_all.reshape(cases, regions, peers_y * slots)
        sol = jnp.einsum("kra,rab->krb", flat_c, dense, precision=HIGH)
        return flat_c, sol

    def total(a, b):
        return jnp.sum(a * b, (1, 2))

    def over_gx(*sums):
        return sums if whole else tuple(lax.psum(jnp.stack(sums), "gx"))

    def at(sol, ix, dy):
        sol = sol.reshape(cases, regions, peers_y, slots)
        iy = jnp.clip(here_y + dy, 0, peers_y - 1)
        return lax.dynamic_slice(sol, (0, ix, iy, 0), (cases, 1, 1, slots))[:, 0, 0]

    def beside(sol):
        if whole:
            return at(sol, 0, 0), at(sol, 1, 0)
        mine = at(sol, 0, 0)
        return swap_gx(mine, mine, peers_x)

    def coarse_part(sol):
        mine = here_x if whole else 0
        near = jnp.concatenate([at(sol, mine, 0), *beside(sol), at(sol, mine, -1), at(sol, mine, 1)], 1)
        return jnp.einsum("kn,xynj->xykj", near, spread, precision=HIGH)

    cu, rho, delta = unpack(got[:, :rows])
    cp, cross, eta = unpack(got[:, rows : 2 * rows])
    cu, su = solve(cu)
    cp, sp = solve(cp)
    delta, cross, eta = delta + total(cu, su), cross + total(cu, sp), eta + total(cp, sp)
    rho, delta, cross, eta = over_gx(rho, delta, cross, eta)
    f_both = keep * jump(y, *from_all)
    w = f_both[:, :, :cases] + coarse_part(su)
    s = f_both[:, :, cases:] + coarse_part(sp)

    wide = lambda a: a[None, None, :, None]
    beta = rho / prev_rho
    skew = cross + beta * eta
    pi = delta + 2.0 * beta * skew - beta * beta * eta
    for step in range(ITERS):
        if step > 0:
            u = scale * r
            y, c = local_part(u)
            block = pack(c, over_cases(own_part(r), own_part(u)), over_cases(u, y))
            got = everywhere(block, axes)
            from_all = exchange(y)
            rho_old = rho
            c_all, rho, delta = unpack(got)
            c_all, sol = solve(c_all)
            rho, delta = over_gx(rho, delta + total(c_all, sol))
            w = keep * jump(y, *from_all) + coarse_part(sol)
            skew = beta * skew
            beta = rho / rho_old
            pi = delta + 2.0 * beta * skew - beta * beta * pi
        alpha = rho / pi
        p = own_part(u) + wide(beta) * p
        s = w + wide(beta) * s
        lam = lam + wide(alpha) * p
        r = r - wide(alpha) * s
    back = lambda v: jnp.transpose(v, (2, 0, 1, 3))
    return back(lam), back(own_part(r)), back(p)


F32, BF16 = jnp.float32, jnp.bfloat16
SPAN_X, SPAN_Y = 2, 4
SUBS = SPAN_X * SPAN_Y
CASES = 16
EARLY = 4
STAY = 2
SLOTS = 32
USED = 2 * (SPAN_X + 1) * (SPAN_Y + 1)
CAST = 40
LIMIT = 16 * 1024 * 1024
UPPER = [(i, j) for i in range(3) for j in range(i, 3)]


def iota(shape, dim):
    return lax.broadcasted_iota(jnp.int32, shape, dim)


def split(v):
    high = v.astype(BF16)
    return high, (v - high.astype(F32)).astype(BF16)


def dot(a, b):
    return jnp.dot(a, b, preferred_element_type=F32)


def dot_turned(a, b):
    return lax.dot_general(a, b, (((1,), (1,)), ((), ())), preferred_element_type=F32)


def dot_split(v, high, low, dot=dot):
    n = v.shape[0]
    vh, vl = split(v)
    wide = dot(jnp.concatenate([vh, vl], 0), high)
    return wide[:n] + wide[n:] + dot(vh, low)


def dot_exact(v, ones):
    n = v.shape[0]
    vh, vl = split(v)
    wide = dot(jnp.concatenate([vh, vl], 0), ones)
    return wide[:n] + wide[n:]


def odd(i):
    return (i // SPAN_Y + i % SPAN_Y) % 2


def lower(rows):
    return iota((rows, 128), 1) < 64


def packs(ys):
    rows = ys[0].shape[0]
    low = lower(rows)
    column = lambda x: [
        jnp.where(low, ys[x * SPAN_Y + t][:, :128], ys[x * SPAN_Y + t + 1][:, :128]) for t in range(0, SPAN_Y, 2)
    ]
    row = lambda y: jnp.where(low, ys[y][:, 128:], ys[SPAN_Y + y][:, 128:])
    return column(0), column(SPAN_X - 1), row(0), row(SPAN_Y - 1)


def send(ys, x_ref, a_ref, b_ref, at):
    rows = pl.ds(at, ys[0].shape[0])
    west, east, south, north = packs(ys)
    first = lax.axis_index("gx") == 0
    even = lax.axis_index("gy") % 2 == 0
    for t in range(SPAN_Y // 2):
        x_ref[t, rows, :] = jnp.where(first, east[t], west[t])
    a_ref[rows, :] = jnp.where(even, north, south)
    b_ref[rows, :] = jnp.where(even, south, north)


def received(x_ref, a_ref, b_ref, at, n, side=None):
    rows = pl.ds(at, n)
    first = lax.axis_index("gx") == 0
    even = lax.axis_index("gy") % 2 == 0
    xs = [x_ref[t, rows, :] for t in range(SPAN_Y // 2)]
    a, b = a_ref[rows, :], b_ref[rows, :]
    if side is not None:
        a, b = a + side[:, :128], b + side[:, 128:256]
        xs = [xs[t] + side[:, 256 + 128 * t : 384 + 128 * t] for t in range(SPAN_Y // 2)]
    zero = jnp.zeros_like(a)
    return (
        [jnp.where(first, zero, v) for v in xs],
        [jnp.where(first, v, zero) for v in xs],
        jnp.where(even, b, a),
        jnp.where(even, a, b),
    )


def across(ys, nb, rows):
    low = lower(rows)
    zero = jnp.zeros((rows, 128), F32)
    inside = lambda x, y, part: zero if ys is None else ys[x * SPAN_Y + y][:, part * 128 : part * 128 + 128]
    out = []
    for x in range(SPAN_X):
        for y in range(SPAN_Y):
            beyond = lambda v: zero if nb is None else v()
            west = inside(x - 1, y, 0) if x else beyond(lambda: nb[0][y // 2])
            east = inside(x + 1, y, 0) if x < SPAN_X - 1 else beyond(lambda: nb[1][y // 2])
            south = inside(x, y - 1, 1) if y else beyond(lambda: nb[2])
            north = inside(x, y + 1, 1) if y < SPAN_Y - 1 else beyond(lambda: nb[3])
            if (x + y) % 2:
                west, east, south, north = east, west, north, south
            out.append(jnp.concatenate([jnp.where(low, west, east), jnp.where(low, south, north)], 1))
    return out


def owned_lanes(i, rows):
    lane = iota((rows, 256), 1) % 128
    return lane < 64 if odd(i) else lane >= 64


def spread_owned(v, i):
    zero = jnp.zeros_like(v)
    low = lower(v.shape[0])
    turned = pltpu.roll(v, 64, 1)
    if odd(i):
        return jnp.concatenate([jnp.where(low, v, zero), jnp.where(low, turned, zero)], 1)
    return jnp.concatenate([jnp.where(low, zero, turned), jnp.where(low, zero, v)], 1)


def take_owned(v, i):
    low = lower(v.shape[0])
    if odd(i):
        return jnp.where(low, v[:, :128], pltpu.roll(v[:, 128:], 64, 1))
    return jnp.where(low, pltpu.roll(v[:, :128], 64, 1), v[:, 128:])


def start_kernel(res_ref, dir_ref, act_ref, scale_ref, *refs):
    inverse_ref, own_ref, x_ref, a_ref, b_ref = refs[4:9]
    upper_ref, p_ref = refs[13:15]
    gx, gy = lax.axis_index("gx"), lax.axis_index("gy")
    last_x = gx * SPAN_X + SPAN_X - 1 == lax.axis_size("gx") * SPAN_X - 1
    last_y = gy * SPAN_Y + SPAN_Y - 1 == lax.axis_size("gy") * SPAN_Y - 1
    east = iota((1, 128), 1) < 64
    ys = []
    for i in range(SUBS):
        x, y = i // SPAN_Y, i % SPAN_Y
        keep = act_ref[i : i + 1, :].astype(F32)
        if x == SPAN_X - 1:
            keep = jnp.where(jnp.logical_and(last_x, east), 0.0, keep)
        if y == SPAN_Y - 1:
            keep = jnp.where(jnp.logical_and(last_y, jnp.logical_not(east)), 0.0, keep)
        mine = pl.ds(i, CASES, stride=SUBS)
        p = dir_ref[mine, :] * keep
        p_ref[mine, :] = p
        v = jnp.concatenate(
            [
                res_ref[mine, :],
                p,
                scale_ref[i : i + 1, :] * keep,
                keep,
                jnp.zeros((CAST - 2 * CASES - 2, 128), F32),
            ],
            0,
        )
        v = spread_owned(v, i)
        own_ref[i] = v
        ys.append(v)
    send(ys, x_ref, a_ref, b_ref, 0)
    for ref in (x_ref, a_ref, b_ref):
        ref.flush()
    for t, (i, j) in enumerate(UPPER):
        upper_ref[t] = inverse_ref[128 * i : 128 * i + 128, 128 * j : 128 * j + 128]


def operator_kernel(
    schur_ref, couple_ref, map_ref, slot_ref, rest_ref, ha_ref, la_ref, hb_ref, lb_ref, cc_ref, ch_ref, cl_ref, name_ref,
):
    none = 384
    slot = slot_ref[...].astype(F32)
    eye = iota((8, 8), 0) == iota((8, 8), 1)
    column = jnp.concatenate(
        [jnp.sum(jnp.where(eye, jnp.broadcast_to(slot[i : i + 1, :], (8, 8)), 0.0), 1, keepdims=True) for i in range(SUBS)], 0
    )
    row = jnp.concatenate([slot[i : i + 1, :] for i in range(SUBS)], 1)
    count = SUBS * 8
    earlier = iota((count, count), 1) < iota((count, count), 0)
    again = jnp.sum(jnp.where(jnp.logical_and(column == row, earlier), 1.0, 0.0), 1, keepdims=True)
    first = jnp.where(jnp.logical_and(again == 0.0, column != float(none)), 1.0, 0.0)
    first_row = jnp.sum(
        jnp.where(jnp.logical_and(column == row, iota((count, count), 0) < iota((count, count), 1)), 1.0, 0.0), 0, keepdims=True
    )
    first_row = jnp.where(jnp.logical_and(first_row == 0.0, row != float(none)), 1.0, 0.0)
    rank = jnp.sum(jnp.where(row < column, first_row, 0.0), 1, keepdims=True)
    hit = jnp.where(rank == iota((count, 128), 1).astype(F32), first, 0.0)
    name_ref[...] = jnp.broadcast_to(
        jnp.where(jnp.sum(hit, 0, keepdims=True) > 0.0, jnp.sum(hit * column, 0, keepdims=True), float(none)), (8, 128)
    )
    sub = iota((256, 256), 0)
    west = (sub // 64) % 2 == 0
    for i in range(SUBS):
        spots = map_ref[i // SPAN_Y, i % SPAN_Y : i % SPAN_Y + 1, :]
        if odd(i):
            spots = jnp.where((spots // 64) % 2 == 0, spots + 64, spots - 64)
        sign = jnp.where(west, 1.0, -1.0) if odd(i) else jnp.where(west, -1.0, 1.0)
        place = jnp.where(sub == spots, sign, 0.0).astype(BF16)
        mine = slot[i : i + 1, :]
        number = jnp.sum(jnp.where(column < mine, first, 0.0), 0, keepdims=True)
        compact = jnp.where(
            jnp.logical_and(number == iota((SLOTS, 8), 0).astype(F32), mine != float(none)), 1.0, 0.0
        )
        cc = jnp.dot(compact, couple_ref[i], precision=EXACT, preferred_element_type=F32)
        c1, rest = split(cc)
        c2, c3 = split(cc - c1.astype(F32))
        s1, s2 = split(schur_ref[i] if i < EARLY else rest_ref[i - EARLY])
        tall = dot_turned(jnp.concatenate([s1, s2, c1, c2, c3], 0), place)
        high, low = (dot(place, tall[t : t + 256].astype(BF16)).astype(BF16) for t in (0, 256))
        if i < STAY:
            ha_ref[i], la_ref[i] = high, low
        else:
            hb_ref[i - STAY], lb_ref[i - STAY] = high, low
        cc = tall[512 : 512 + SLOTS] + tall[512 + SLOTS : 512 + 2 * SLOTS] + tall[512 + 2 * SLOTS :]
        cc_ref[i] = cc
        ch_ref[i], cl_ref[i] = split(cc)


def inverse_kernel(mine_ref, upper_ref, high_ref, low_ref):
    first = lax.axis_index("gx") == 0
    mine = mine_ref[...]
    blocks = {spot: upper_ref[t] for t, spot in enumerate(UPPER)}
    side = lambda i, j: blocks[i, j] if i <= j else jnp.transpose(blocks[j, i])
    other = jnp.concatenate([jnp.concatenate([side(i, j) for j in range(3)], 1) for i in range(3)], 0)
    for region, v in enumerate((jnp.where(first, mine, other), jnp.where(first, other, mine))):
        high_ref[region], low_ref[region] = split(v)


def near_names(name_ref, x_ref, a_ref, b_ref):
    named = pl.ds(2 * CASES + SLOTS, 8)
    group = iota((8, 128), 1) // SLOTS
    turn = lambda v, g: jnp.where(group == g, pltpu.roll(v, g * SLOTS, 1), 0.0)
    wanted = name_ref[...] + 0.0
    wanted = jnp.where(group == 0, wanted, turn(a_ref[named, :], 1) + turn(b_ref[named, :], 2) + turn(x_ref[0, named, :], 3))
    found = iota((384, 128), 0).astype(F32) == wanted[0:1]
    mine = jnp.where(iota((384, 128), 1) < 3 * SLOTS, 1.0, 0.0)
    gx = lax.axis_index("gx")
    return [jnp.where(found, jnp.where(gx == region, mine, 1.0 - mine), 0.0).astype(BF16) for region in range(2)]


def near_spread(x_ref, a_ref, b_ref, nh_ref, nl_ref):
    rows = pl.ds(2 * CASES, SLOTS)
    nh_ref[...], nl_ref[...] = split(
        jnp.concatenate([a_ref[rows, :], b_ref[rows, :], x_ref[0, rows, :], x_ref[1, rows, :]], 1)
    )


def operator(ys, x_ref, a_ref, b_ref, near, mk_ref, ch_ref, cl_ref, nh_ref, nl_ref):
    n = ys[0].shape[0]
    high, low = nh_ref[...], nl_ref[...]
    side = jnp.concatenate(
        [
            dot_split(near[g], high[:, at : at + width], low[:, at : at + width])
            for g, at, width in ((1, 0, 128), (2, 128, 128), (3, 256, 256))
        ],
        1,
    )
    west, east, south, north = received(x_ref, a_ref, b_ref, 0, n, side)
    ys = [ys[i] + dot_split(near[0], ch_ref[i], cl_ref[i]) for i in range(SUBS)]
    other = across(ys, (west, east, south, north), n)
    return [mk_ref[i, 1:2, :] * (ys[i] + other[i]) for i in range(SUBS)]


def corners(us, ch_ref, cl_ref):
    couple = lambda ref: jnp.concatenate([ref[i] for i in range(SUBS)], 0)
    corner = dot_split(jnp.concatenate(us, 0), couple(ch_ref), couple(cl_ref), dot_turned)
    n = us[0].shape[0]
    group = iota((n, 128), 1) // SLOTS
    total = jnp.zeros((n, 128), F32)
    for i in range(SUBS):
        part = corner[n * i : n * i + n, 128 * (i // 4) : 128 * (i // 4) + 128]
        total = total + jnp.where(group == i % 4, part, 0.0)
    total = total + pltpu.roll(total, 64, 1)
    return total + pltpu.roll(total, 32, 1)


def by_schur(us, ha_ref, la_ref, hb_ref, lb_ref):
    return [
        dot_split(us[i], ha_ref[i], la_ref[i]) if i < STAY else dot_split(us[i], hb_ref[i - STAY], lb_ref[i - STAY])
        for i in range(SUBS)
    ]


def over_lanes(terms):
    total = terms[0]
    for t in terms[1:]:
        total = total + t
    return jnp.sum(total[:, :128] + total[:, 128:], 1, keepdims=True)


def packed(corner, one, two):
    slot = iota((CASES, 128), 1) % SLOTS
    full = jnp.where(slot == USED, one, jnp.where(slot == USED + 1, two, corner))
    group = iota((4, 128), 1) // SLOTS
    out = jnp.zeros((4, 128), F32)
    for b in range(4):
        out = jnp.where(group == b, full[4 * b : 4 * b + 4], out)
    return out


def by_slot(vs):
    group = iota((8, 128), 1) // SLOTS
    out = []
    for region in range(2):
        rows = []
        for b in range(4):
            halves = []
            for h in range(2):
                acc = None
                for q in range(4):
                    v = vs[8 * region + 4 * h + q]
                    turned = v if q == b else pltpu.roll(v, (SLOTS * (q - b)) % 128, 1)
                    acc = turned if acc is None else jnp.where(group == q, turned, acc)
                halves.append(acc)
            rows.append(jnp.concatenate(halves, 1))
        out.append(jnp.concatenate(rows, 0))
    return out


def inner(vs):
    total = vs[0]
    for v in vs[1:]:
        total = total + v
    total = total[:4] + total[4:]
    tall = jnp.concatenate([total] * 4, 0)
    lane, row = iota((CASES, 128), 1), iota((CASES, 128), 0)
    column = lambda s: jnp.sum(jnp.where(lane == SLOTS * (row // 4) + s, tall, 0.0), 1, keepdims=True)
    return column(USED), column(USED + 1)


def first_of_pairs(v):
    return jnp.concatenate([v[8 * b : 8 * b + 4] for b in range(v.shape[0] // 8)], 0)


def solve(spots, pick_ref, gh_ref, gl_ref, near_ref):
    totals, sols, near = [], [], None
    for region in range(2):
        v = spots[region]
        n = v.shape[0]
        even = dot_exact(v, pick_ref[region, 0])
        odds = dot_exact(v, pick_ref[region, 1])
        z = jnp.where((iota((n, 384), 0) // 4) % 2 == 0, even, odds).reshape(n // 8, 8, 384)
        total = (z + pltpu.roll(z, 4, 1)).reshape(n, 384)
        sol = dot_split(total, gh_ref[region], gl_ref[region])
        part = dot_exact(sol, near_ref[region])
        near = part if near is None else near + part
        totals.append(total)
        sols.append(sol)
    return totals, sols, near


def swap_pairs(v):
    rows, lanes = v.shape
    return pltpu.roll(v.reshape(rows // 8, 8, lanes), 4, 1).reshape(rows, lanes)


def ahead(region, t):
    gx, gy = lax.axis_index("gx"), lax.axis_index("gy")
    return 8 * lax.rem(gx + region, 2) + lax.rem(gy // 2 + t, 8)


def dense_kernel(got_ref, gh_ref, gl_ref, dh_ref, dl_ref):
    group = iota((8, 128), 1) // SLOTS
    picks, rows = [], []
    for region in range(2):
        hits = []
        for par in range(2):
            halves = []
            for h in range(2):
                acc = None
                for q in range(4):
                    v = got_ref[3 * ahead(region, 4 * h + q) + 1 + par]
                    v = v if par == 0 else pltpu.roll(v, 4, 0)
                    turned = pltpu.roll(v, SLOTS * q, 1) if q else v
                    acc = turned if acc is None else jnp.where(group == q, turned, acc)
                halves.append(acc[0:1])
            wanted = jnp.concatenate(halves, 1)
            hits.append(jnp.where(iota((384, 256), 0).astype(F32) == wanted, 1.0, 0.0))
        picks.append(jnp.concatenate(hits, 1).astype(BF16))
        rows.append([jnp.transpose(hit).astype(BF16) for hit in hits])
    for whole_ref, out_ref in ((gh_ref, dh_ref), (gl_ref, dl_ref)):
        for region in range(2):
            which = lax.rem(lax.axis_index("gx") + region, 2)
            half = dot(whole_ref[which], picks[region]).astype(BF16)
            top = dot(rows[region][0], half).astype(BF16)
            out_ref[region, 0], out_ref[region, 1] = top[:, :256], top[:, 256:]
            out_ref[region, 2] = dot(rows[region][1], half[:, 256:]).astype(BF16)


def solve_dense(spots, dh_ref, dl_ref):
    total, sols = None, []
    for region in range(2):
        v = spots[region]
        block = lambda t, dot=dot: dot_split(v, dh_ref[region, t], dl_ref[region, t], dot)
        first = (iota(v.shape, 0) // 4) % 2 == 0
        sol = jnp.where(first, block(0) + swap_pairs(block(1, dot_turned)), block(2) + swap_pairs(block(1)))
        total = v * sol if total is None else total + v * sol
        sols.append(sol)
    total = jnp.sum(total, 1, keepdims=True)
    halves = lambda v: [jnp.concatenate([v[8 * b + at : 8 * b + at + 4] for b in range(4)], 0) for at in (0, 4)]
    total = sum(halves(total))
    even = lax.axis_index("gy") % 2 == 0
    (a, b), (c, d) = halves(sols[0]), halves(sols[1][:, :128])
    here = jnp.where(even, a[:, :128], b[:, :128])
    pair = jnp.where(even, b[:, :128], a[:, :128])
    beyond = jnp.where(even, pltpu.roll(b[:, 128:], SLOTS, 1), pltpu.roll(a[:, :128], 128 - SLOTS, 1))
    along = jnp.where(even, c, d)
    return total, [v[:, :SLOTS] for v in (here, pair, beyond, along)]


def energy(totals, sols):
    both = totals[0] * sols[0] + totals[1] * sols[1]
    return first_of_pairs(jnp.sum(both, 1, keepdims=True))


def emit(rs, mk_ref, schur_refs, ch_ref, cl_ref, block_ref, y_ref, x_ref, a_ref, b_ref):
    us = [mk_ref[i, 0:1, :] * rs[i] for i in range(SUBS)]
    corner = corners(us, ch_ref, cl_ref)
    rho = over_lanes([jnp.where(owned_lanes(i, CASES), rs[i] * us[i], 0.0) for i in range(SUBS)])
    ys = by_schur(us, *schur_refs)
    send(ys, x_ref, a_ref, b_ref, 0)
    for i in range(SUBS):
        y_ref[i] = ys[i]
    for ref in (x_ref, a_ref, b_ref, y_ref):
        ref.flush()
    delta = over_lanes([us[i] * ys[i] for i in range(SUBS)])
    block = packed(corner, rho, delta)
    twice = jnp.concatenate([block, block], 0)
    for j in range(16):
        block_ref[j] = twice
    block_ref.flush()


def first_kernel(
    own_ref, x_ref, a_ref, b_ref, ha_ref, la_ref, hb_ref, lb_ref, cc_ref, ch_ref, cl_ref, name_ref,
    r_ref, mk_ref, y_ref, block_ref, sx_ref, sa_ref, sb_ref, high_out_ref, low_out_ref,
):
    schur_refs = ha_ref, la_ref, hb_ref, lb_ref
    own = [own_ref[i] for i in range(SUBS)]
    other = across(own, received(x_ref, a_ref, b_ref, 0, CAST), CAST)
    rs, vs = [], []
    for i in range(SUBS):
        full = own[i] + other[i]
        rs.append(full[:CASES])
        r_ref[i] = full[:CASES]
        mk_ref[i] = full[2 * CASES : 2 * CASES + 8]
        vs.append(jnp.concatenate([full[2 * CASES : 2 * CASES + 1] * full[:CASES], full[CASES : 2 * CASES]], 0))
    corner = corners(vs, ch_ref, cl_ref)
    ys = by_schur(vs, *schur_refs)
    names = name_ref[...]
    send([jnp.concatenate([ys[i], cc_ref[i]], 0) for i in range(SUBS)], sx_ref, sa_ref, sb_ref, 0)
    at = pl.ds(2 * CASES + SLOTS, 8)
    for t in range(SPAN_Y // 2):
        sx_ref[t, at, :] = names
    sa_ref[at, :] = names
    sb_ref[at, :] = names
    us = [v[:CASES] for v in vs]
    ps = [v[CASES:] for v in vs]
    rho = over_lanes([jnp.where(owned_lanes(i, CASES), rs[i] * us[i], 0.0) for i in range(SUBS)])
    delta = over_lanes([us[i] * ys[i][:CASES] for i in range(SUBS)])
    cross = over_lanes([ps[i] * ys[i][:CASES] for i in range(SUBS)])
    eta = over_lanes([ps[i] * ys[i][CASES:] for i in range(SUBS)])
    one, two = packed(corner[:CASES], rho, delta), packed(corner[CASES:], cross, eta)
    blocks = [
        jnp.concatenate([one, two], 0),
        jnp.concatenate([names[:4], one], 0),
        jnp.concatenate([two, names[:4]], 0),
    ]
    for j in range(16):
        for t in range(3):
            block_ref[3 * j + t] = blocks[t]
    for i in range(SUBS):
        y_ref[i] = ys[i]


def column_of(row):
    eye = iota((CASES, CASES), 0) == iota((CASES, CASES), 1)
    return jnp.sum(jnp.where(eye, jnp.broadcast_to(row, (CASES, CASES)), 0.0), 1, keepdims=True)


def keep_scalars(scal_ref, values):
    for t, v in enumerate(values):
        scal_ref[t] = jnp.broadcast_to(v, (CASES, 128))


def second_kernel(
    got_ref, x_ref, a_ref, b_ref, y_ref, r_ref, mk_ref, p_ref, l_ref, rho_ref, gh_ref, gl_ref, name_ref,
    ha_ref, la_ref, hb_ref, lb_ref, ch_ref, cl_ref,
    nh_ref, nl_ref, po_ref, lo_ref, ro_ref, so_ref, scal_ref, block_ref, yo_ref, sx_ref, sa_ref, sb_ref, *_,
):
    near_ref, pick_ref = near_names(name_ref, x_ref, a_ref, b_ref), {}
    near_spread(x_ref, a_ref, b_ref, nh_ref, nl_ref)
    top = iota((8, 128), 0) < 4
    us, ps, names = [], [], []
    for j in range(16):
        v = [got_ref[3 * j + t] for t in range(3)]
        us.append(jnp.where(top, v[0], v[1]))
        ps.append(pltpu.roll(jnp.where(top, v[2], v[0]), 4, 0))
        names.append((v[1], pltpu.roll(v[2], 4, 0)))
    group = iota((8, 128), 1) // SLOTS
    for region in range(2):
        for par in range(2):
            halves = []
            for h in range(2):
                acc = None
                for q in range(4):
                    v = names[8 * region + 4 * h + q][par]
                    turned = pltpu.roll(v, SLOTS * q, 1) if q else v
                    acc = turned if acc is None else jnp.where(group == q, turned, acc)
                halves.append(acc[0:1])
            wanted = jnp.concatenate(halves, 1)
            hit = jnp.where(iota((384, 256), 0).astype(F32) == wanted, 1.0, 0.0)
            pick_ref[region, par] = jnp.transpose(hit).astype(BF16)
    lhs_u, lhs_p = by_slot(us), by_slot(ps)
    n = lhs_u[0].shape[0]
    totals, sols, near = solve(
        [jnp.concatenate([lhs_u[t], lhs_p[t]], 0) for t in range(2)], pick_ref, gh_ref, gl_ref, near_ref
    )
    of_u, of_p = lambda vs: [v[:n] for v in vs], lambda vs: [v[n:] for v in vs]
    rho, delta = inner(us)
    cross, eta = inner(ps)
    delta = delta + energy(of_u(totals), of_u(sols))
    cross = cross + energy(of_p(totals), of_u(sols))
    eta = eta + energy(of_p(totals), of_p(sols))
    near = first_of_pairs(near)
    near = [(pltpu.roll(near, 128 - SLOTS * g, 1) if g else near)[:, :SLOTS] for g in range(4)]
    beta = rho / column_of(rho_ref[...])
    skew = cross + beta * eta
    pi = delta + 2.0 * beta * skew - beta * beta * eta
    alpha = rho / pi
    fs = operator([y_ref[i] for i in range(SUBS)], x_ref, a_ref, b_ref, near, mk_ref, ch_ref, cl_ref, nh_ref, nl_ref)
    rs = []
    for i in range(SUBS):
        f, r = fs[i], r_ref[i]
        s = f[:CASES] + beta * f[CASES:]
        r = r - alpha * s
        rs.append(r)
        ro_ref[i], so_ref[i] = r, s
    scalars = rho, pi, beta, skew, alpha
    keep_scalars(scal_ref, scalars)
    so_ref.flush()
    emit(rs, mk_ref, (ha_ref, la_ref, hb_ref, lb_ref), ch_ref, cl_ref, block_ref, yo_ref, sx_ref, sa_ref, sb_ref)

    @pl.when(lax.axis_index("gx") >= 0)
    def _():
        track(r_ref, scalars, mk_ref, p_ref, l_ref, po_ref, lo_ref)


def absorb(got_ref, x_ref, a_ref, b_ref, y_ref, r_ref, s_ref, scal_ref, mk_ref, dh_ref, dl_ref, nh_ref, nl_ref, ch_ref, cl_ref):
    vs = [got_ref[ahead(region, t)] for region in range(2) for t in range(8)]
    coarse, near = solve_dense(by_slot(vs), dh_ref, dl_ref)
    rho, delta = inner(vs)
    delta = delta + coarse
    rho_old, pi, beta, skew = (scal_ref[t][:, 0:1] for t in range(4))
    skew = beta * skew
    beta = rho / rho_old
    pi = delta + 2.0 * beta * skew - beta * beta * pi
    alpha = rho / pi
    fs = operator([y_ref[i] for i in range(SUBS)], x_ref, a_ref, b_ref, near, mk_ref, ch_ref, cl_ref, nh_ref, nl_ref)
    ss = [fs[i] + beta * s_ref[i] for i in range(SUBS)]
    rs = [r_ref[i] - alpha * ss[i] for i in range(SUBS)]
    return rs, ss, (rho, pi, beta, skew, alpha)


def track(r_ref, scalars, mk_ref, p_ref, l_ref, po_ref, lo_ref):
    _, _, beta, _, alpha = scalars
    for i in range(SUBS):
        mine = pl.ds(i, CASES, stride=SUBS)
        p = take_owned(mk_ref[i, 0:1, :] * r_ref[i], i) + beta * p_ref[mine, :]
        po_ref[mine, :] = p
        lo_ref[mine, :] = l_ref[mine, :] + alpha * p


def round_kernel(
    got_ref, x_ref, a_ref, b_ref, y_ref, r_ref, s_ref, scal_ref, mk_ref, dh_ref, dl_ref,
    nh_ref, nl_ref, ch_ref, cl_ref, p_ref, l_ref, ha_ref, la_ref, hb_ref, lb_ref,
    po_ref, lo_ref, ro_ref, so_ref, scalo_ref, block_ref, yo_ref, sx_ref, sa_ref, sb_ref,
):
    rs, ss, scalars = absorb(
        got_ref, x_ref, a_ref, b_ref, y_ref, r_ref, s_ref, scal_ref, mk_ref, dh_ref, dl_ref, nh_ref, nl_ref, ch_ref, cl_ref
    )
    for i in range(SUBS):
        ro_ref[i], so_ref[i] = rs[i], ss[i]
    so_ref.flush()
    keep_scalars(scalo_ref, scalars)
    emit(rs, mk_ref, (ha_ref, la_ref, hb_ref, lb_ref), ch_ref, cl_ref, block_ref, yo_ref, sx_ref, sa_ref, sb_ref)

    @pl.when(lax.axis_index("gx") >= 0)
    def _():
        track(r_ref, scalars, mk_ref, p_ref, l_ref, po_ref, lo_ref)


def last_kernel(
    got_ref, x_ref, a_ref, b_ref, y_ref, r_ref, s_ref, scal_ref, mk_ref, dh_ref, dl_ref, nh_ref, nl_ref, ch_ref, cl_ref,
    p_ref, l_ref, lo_ref, ro_ref, po_ref,
):
    rs, _, scalars = absorb(
        got_ref, x_ref, a_ref, b_ref, y_ref, r_ref, s_ref, scal_ref, mk_ref, dh_ref, dl_ref, nh_ref, nl_ref, ch_ref, cl_ref
    )
    track(r_ref, scalars, mk_ref, p_ref, l_ref, po_ref, lo_ref)
    for i in range(SUBS):
        ro_ref[pl.ds(i, CASES, stride=SUBS), :] = take_owned(rs[i], i)


class Fetched:
    def __init__(self, source, buffer, semaphore):
        self.buffer = buffer
        self.copy = pltpu.make_async_copy(source, buffer, semaphore)
        self.copy.start()
        self.here = False

    def wait(self):
        self.copy.wait()
        self.here = True

    def __getitem__(self, index):
        if not self.here:
            self.wait()
        return self.buffer[index]


class Stored:
    def __init__(self, target, buffer, semaphore):
        self.buffer = buffer
        self.copy = pltpu.make_async_copy(buffer, target, semaphore)
        self.sent = False

    def __setitem__(self, index, value):
        self.buffer[index] = value

    def __getitem__(self, index):
        return self.buffer[index]

    def flush(self):
        if not self.sent:
            self.copy.start()
            self.sent = True


class Kept:
    def __init__(self, ref):
        self.ref = ref

    def __setitem__(self, index, value):
        self.ref[index] = value

    def __getitem__(self, index):
        return self.ref[index]

    def flush(self):
        pass


def call(kernel, args, outs, kept=(), kept_out=(), raw=(), through=None, flops=None, late=0, parts=None):
    through, parts = through or {}, parts or {}
    moved = [i for i in range(len(args)) if i not in kept and i not in raw]
    written = [i for i in range(len(outs)) if i not in kept_out and i not in through]

    def body(*refs):
        ins, results = refs[: len(args)], refs[len(args) : len(args) + len(outs)]
        buffers, (in_sem, out_sem, through_sem) = refs[len(args) + len(outs) : -3], refs[-3:]
        fetched, stored = list(ins), [Kept(ref) for ref in results]
        for t, i in enumerate(moved):
            source = ins[i].at[pl.ds(*parts[i])] if i in parts else ins[i]
            fetched[i] = Fetched(source, buffers[t], in_sem.at[t])
        for t, i in enumerate(written):
            stored[i] = Stored(results[i], buffers[len(moved) + t], out_sem.at[t])
        passing = [
            pltpu.make_async_copy(source(ins), results[i], through_sem.at[t]) for t, (i, source) in enumerate(through.items())
        ]
        for copy in passing:
            copy.start()
        if moved or passing:
            spot = (0,) * (len(outs[-1 - late][0]) - 2)
            blank = stored[-1 - late]

            @pl.when(lax.axis_index("gx") >= 0)
            def _():
                blank[spot] = jnp.zeros(outs[-1 - late][0][-2:], outs[-1 - late][1])

        kernel(*fetched, *stored)
        for i in written:
            stored[i].flush()
        for i in moved:
            if not fetched[i].here:
                fetched[i].wait()
        for copy in passing:
            copy.wait()
        for i in written:
            stored[i].copy.wait()

    place = lambda held: pl.BlockSpec(memory_space=pltpu.VMEM if held else pltpu.HBM)
    semaphores = lambda n: pltpu.SemaphoreType.DMA((max(n, 1),))
    args = [a if i in kept else pltpu.with_memory_space_constraint(a, pltpu.HBM) for i, a in enumerate(args)]
    return pl.pallas_call(
        body,
        out_shape=[
            jax.ShapeDtypeStruct(*out) if i in kept_out else pltpu.HBM(*out) for i, out in enumerate(outs)
        ],
        in_specs=[place(i in kept) for i in range(len(args))],
        out_specs=[place(i in kept_out) for i in range(len(outs))],
        scratch_shapes=[
            pltpu.VMEM((parts[i][1],) + args[i].shape[1:] if i in parts else args[i].shape, args[i].dtype) for i in moved
        ]
        + [pltpu.VMEM(*outs[i]) for i in written]
        + [semaphores(len(moved)), semaphores(len(written)), semaphores(len(through))],
        compiler_params=pltpu.CompilerParams(vmem_limit_bytes=LIMIT),
        cost_estimate=flops and pl.CostEstimate(flops=flops, bytes_accessed=flops // 512, transcendentals=0),
    )(*args)


def trade(x, a, b):
    peers = lax.axis_size("gy")
    return (
        lax.ppermute(x, "gx", [(0, 1), (1, 0)]),
        lax.ppermute(a, "gy", both_ways(pairs_from(0, peers))),
        lax.ppermute(b, "gy", both_ways(pairs_from(1, peers))),
    )


def two_regions(
    duals, residual, direction, prev_rho, dual_schur, coupling, coarse_inverse, edge_map, corner_slot, active, scaling
):
    native = lambda v: v.reshape(CASES * SUBS, 128)
    by_sub = lambda v: v.reshape((SUBS,) + v.shape[2:])
    width = coarse_inverse.shape[-1]
    sends = lambda rows: [((SPAN_Y // 2, rows, 128), F32), ((rows, 128), F32), ((rows, 128), F32)]
    state = ((SUBS, CASES, 256), F32)
    plain = ((CASES * SUBS, 128), F32)

    raw = [by_sub(dual_schur), by_sub(coupling), edge_map, by_sub(corner_slot)]
    own, *out, schur, coupled, placed, slotted, inverse, p = call(
        start_kernel,
        [native(residual), native(direction), by_sub(active), by_sub(scaling), *raw, coarse_inverse[0]],
        [((SUBS, CAST, 256), F32)] + sends(CAST) + [((EARLY,) + raw[0].shape[1:], F32)] + [(v.shape, v.dtype) for v in raw[1:]] + [((len(UPPER), 128, 128), F32), plain],
        kept_out=(0, 4, 5, 6, 7),
        raw=(4, 5, 6, 7),
        through={4: lambda v: v[4].at[pl.ds(0, EARLY)], 5: lambda v: v[5], 6: lambda v: v[6], 7: lambda v: v[7]},
    )
    come = trade(*out)
    other = lax.ppermute(inverse, "gx", [(0, 1), (1, 0)])
    first_part, rest = ((STAY, 256, 256), BF16), ((SUBS - STAY, 256, 256), BF16)
    couple = ((SUBS, SLOTS, 256), BF16)
    ha, la, hb, lb, cc, ch, cl, names = call(
        operator_kernel,
        [schur, coupled, placed, slotted, by_sub(dual_schur)],
        [first_part, first_part, rest, rest, ((SUBS, SLOTS, 256), F32), couple, couple, ((8, 128), F32)],
        kept=range(4),
        kept_out=range(8),
        parts={4: (EARLY, SUBS - EARLY)},
        flops=5 * 10**9,
    )
    rows = 2 * CASES + SLOTS + 8
    r, mk, y, block, *out, hb, lb = call(
        first_kernel,
        [own, *come, ha, la, hb, lb, cc, ch, cl, names],
        [state, ((SUBS, 8, 256), F32), ((SUBS, 2 * CASES, 256), F32), ((48, 8, 128), F32)]
        + sends(rows)
        + [rest, rest],
        kept=range(12),
        kept_out=(0, 1, 2),
        through={7: lambda v: v[6], 8: lambda v: v[7]},
        late=2,
    )
    got = lax.all_to_all(block.reshape(32, 3, 4, 128), BOTH, 0, 0, tiled=False).reshape(48, 8, 128)
    come = trade(*out)
    square = ((2, width, width), BF16)
    gh, gl = call(inverse_kernel, [coarse_inverse[0], other], [square, square], kept_out=(0, 1), flops=10**9)
    side = ((SLOTS, 512), BF16)
    onward = [plain, plain, state, state, ((5, CASES, 128), F32), ((16, 8, 128), F32), state] + sends(CASES)
    nh, nl, p, lam, r, s, scal, block, y, *out, gh, gl = call(
        second_kernel,
        [got, *come, y, r, mk, p, native(duals), prev_rho.reshape(1, CASES), gh, gl, names, ha, la, hb, lb, ch, cl],
        [side, side] + onward + [square, square],
        kept=(0, 1, 2, 3, 4, 5, 6, 10, 11, 12, 13, 14, 17, 18),
        kept_out=(0, 1, 2, 3, 4, 6, 8),
        through={12: lambda v: v[10], 13: lambda v: v[11]},
        late=5,
    )
    dense = ((2, 3, 256, 256), BF16)
    dh, dl = call(dense_kernel, [got, gh, gl], [dense, dense], kept=(0,), kept_out=(0, 1), flops=10**8)
    for step in range(1, ITERS):
        got = lax.all_to_all(block.reshape(32, 4, 128), BOTH, 0, 0, tiled=False).reshape(16, 8, 128)
        come = trade(*out)
        args = [got, *come, y, r, s, scal, mk, dh, dl, nh, nl, ch, cl, p, lam]
        kept = (*range(6), *range(7, 17))
        if step < ITERS - 1:
            p, lam, r, s, scal, block, y, *out = call(
                round_kernel, args + [ha, la, hb, lb], onward, (*kept, 17, 18), kept_out=(0, 1, 2, 4, 6), late=3
            )
        else:
            results = call(last_kernel, args, [plain, plain, plain], kept)
    return tuple(v.reshape(duals.shape) for v in results)


def shards(*args):
    cases, span_x, span_y, owned = args[0].shape
    fits = (cases, span_x, span_y, owned, args[6].shape[-1]) == (CASES, SPAN_X, SPAN_Y, 128, 384)
    if fits and lax.axis_size("gx") == 2 and lax.axis_size("gy") == 16:
        return two_regions(*args)
    return general(*args)


def solution(mesh):
    placed = (
        P(None, "gx", "gy", None),
        P(None, "gx", "gy", None),
        P(None, "gx", "gy", None),
        P(),
        P("gx", "gy", None, None),
        P("gx", "gy", None, None),
        P("gx", None, None),
        P("gx", "gy", None),
        P("gx", "gy", None),
        P("gx", "gy", None),
        P("gx", "gy", None),
    )
    return jax.shard_map(
        shards,
        mesh=mesh,
        in_specs=placed,
        out_specs=(P(None, "gx", "gy", None), P(None, "gx", "gy", None), P(None, "gx", "gy", None)),
        check_vma=False,
    )
```

```python
import jax
import jax.numpy as jnp
from jax import lax
from jax.experimental import pallas as pl
from jax.experimental.pallas import tpu as pltpu
from jax.sharding import PartitionSpec as P

ITERS = 6
HIGH = lax.Precision.HIGH
EXACT = lax.Precision.HIGHEST
BOTH = ("gx", "gy")


def pairs_from(first, peers):
    return [(i, i + 1) for i in range(first, peers - 1, 2)]


def both_ways(pairs):
    return pairs + [(b, a) for a, b in pairs]


def up_gy(value, peers):
    even = lax.ppermute(value, "gy", pairs_from(0, peers))
    odd = lax.ppermute(value, "gy", pairs_from(1, peers))
    return jnp.where(lax.axis_index("gy") % 2 == 1, even, odd)


def swap_gy(low, high, peers):
    is_even = lax.axis_index("gy") % 2 == 0
    first = lax.ppermute(jnp.where(is_even, high, low), "gy", both_ways(pairs_from(0, peers)))
    second = lax.ppermute(jnp.where(is_even, low, high), "gy", both_ways(pairs_from(1, peers)))
    return jnp.where(is_even, second, first), jnp.where(is_even, first, second)


def swap_gx(low, high, peers):
    if peers == 2:
        is_first = lax.axis_index("gx") == 0
        got = lax.ppermute(jnp.where(is_first, high, low), "gx", [(0, 1), (1, 0)])
        zero = jnp.zeros_like(got)
        return jnp.where(is_first, zero, got), jnp.where(is_first, got, zero)
    below = lax.ppermute(high, "gx", [(i, i + 1) for i in range(peers - 1)])
    above = lax.ppermute(low, "gx", [(i + 1, i) for i in range(peers - 1)])
    return below, above


def everywhere(block, axes):
    sent = jnp.broadcast_to(block[None], (lax.axis_size(axes),) + block.shape)
    return lax.all_to_all(sent, axes, 0, 0, tiled=False)


def general(
    duals, residual, direction, prev_rho, dual_schur, coupling, coarse_inverse, edge_map, corner_slot, active, scaling
):
    cases, span_x, span_y, owned = duals.shape
    half = owned // 2
    full = 2 * owned
    corners = coupling.shape[2]
    width_c = coarse_inverse.shape[-1]
    peers_x, peers_y = lax.axis_size("gx"), lax.axis_size("gy")
    whole = peers_x == 2
    axes = BOTH if whole else "gy"
    regions = peers_x if whole else 1
    peers = regions * peers_y
    here_x, here_y = lax.axis_index("gx"), lax.axis_index("gy")
    used = 2 * (span_x + 1) * (span_y + 1)
    slots = used + 2

    columns = here_x * span_x + jnp.arange(span_x)
    rowset = here_y * span_y + jnp.arange(span_y)
    east_ok = jnp.broadcast_to((columns < span_x * peers_x - 1)[:, None, None], (span_x, span_y, half))
    north_ok = jnp.broadcast_to((rowset < span_y * peers_y - 1)[None, :, None], (span_x, span_y, half))
    keep_own = active.astype(jnp.float32) * jnp.concatenate([east_ok, north_ok], -1).astype(jnp.float32)
    scale_own = keep_own * scaling

    by_place = lambda v: jnp.transpose(v, (1, 2, 0, 3))
    lam = by_place(duals)
    p = keep_own[:, :, None] * by_place(direction)
    stacked = jnp.concatenate([by_place(residual), p, scale_own[:, :, None], keep_own[:, :, None]], 2)
    part_e, part_n = stacked[..., :half], stacked[..., half:]
    from_west = lax.ppermute(part_e[-1], "gx", [(i, i + 1) for i in range(peers_x - 1)])
    from_south = up_gy(part_n[:, -1], peers_y)
    west = jnp.concatenate([from_west[None], part_e[:-1]], 0)
    south = jnp.concatenate([from_south[:, None], part_n[:, :-1]], 1)
    stacked = jnp.concatenate([west, part_e, south, part_n], -1)
    r = stacked[:, :, :cases]
    p_all = stacked[:, :, cases : 2 * cases]
    scale = stacked[:, :, 2 * cases : 2 * cases + 1]
    keep = stacked[:, :, 2 * cases + 1 :]

    sign = jnp.concatenate([-jnp.ones(half), jnp.ones(half), -jnp.ones(half), jnp.ones(half)]).astype(jnp.float32)
    place = (edge_map[..., None] == jnp.arange(full, dtype=jnp.int32)).astype(jnp.float32) * sign
    schur = jnp.einsum("xyij,xyjf->xyif", dual_schur, place, precision=EXACT)
    schur = jnp.einsum("xyie,xyif->xyef", place, schur, precision=EXACT)
    couple = jnp.einsum("xycj,xyjf->xycf", coupling, place, precision=EXACT)

    flat = corner_slot.reshape(-1)
    count = flat.shape[0]
    order = jnp.arange(count)
    same = flat[:, None] == flat[None, :]
    first = ~jnp.any(same & (order[None, :] < order[:, None]), 1) & (flat != width_c)
    rank = jnp.sum((flat[None, :] < flat[:, None]) & first[None, :], 1)
    local_slot = jnp.arange(slots)
    compact = ((rank[:, None] == local_slot) & (flat != width_c)[:, None]).astype(jnp.float32)
    named = jnp.where(
        jnp.any(compact > 0, 0), jnp.max(compact * flat[:, None].astype(jnp.float32), 0), float(width_c)
    )
    compact = compact.reshape(span_x, span_y, corners, slots)
    gather_c = jnp.einsum("xycs,xycf->xysf", compact, couple, precision=EXACT)

    blocks = lambda a: (a[..., :half], a[..., half : 2 * half], a[..., 2 * half : 3 * half], a[..., 3 * half :])

    def jump(y, from_w, from_e, from_s, from_n):
        w, e, s, n = blocks(y)
        w_nb = jnp.concatenate([from_w[None], e[:-1]], 0)
        e_nb = jnp.concatenate([w[1:], from_e[None]], 0)
        s_nb = jnp.concatenate([from_s[:, None], n[:, :-1]], 1)
        n_nb = jnp.concatenate([s[:, 1:], from_n[:, None]], 1)
        return jnp.concatenate([w + w_nb, e + e_nb, s + s_nb, n + n_nb], -1)

    def rims(y):
        w, e, s, n = blocks(y)
        return w[0], e[-1], s[:, 0], n[:, -1]

    def exchange(y):
        w, e, s, n = rims(y)
        from_w, from_e = swap_gx(w, e, peers_x)
        from_s, from_n = swap_gy(s, n, peers_y)
        return from_w, from_e, from_s, from_n

    def put(rim, name):
        zero = jnp.zeros((span_x, span_y, rim.shape[-2], half), jnp.float32)
        parts = [zero, zero, zero, zero]
        if name == 0:
            parts[0] = zero.at[0].set(rim)
        elif name == 1:
            parts[1] = zero.at[-1].set(rim)
        elif name == 2:
            parts[2] = zero.at[:, 0].set(rim)
        else:
            parts[3] = zero.at[:, -1].set(rim)
        return jnp.concatenate(parts, -1)

    nb = exchange(gather_c)
    none = [jnp.zeros_like(v) for v in nb]
    spread = jnp.concatenate([jump(gather_c, *none)] + [put(v, i) for i, v in enumerate(nb)], 2)
    spread = spread * keep

    region_inv = coarse_inverse[0]

    def local_part(v):
        y = jnp.einsum("xykj,xyji->xyki", v, schur, precision=HIGH)
        c = jnp.einsum("xykj,xysj->ks", v, gather_c[:, :, :used], precision=HIGH)
        return y, c

    def over_cases(a, b):
        return jnp.sum(a * b, axis=(0, 1, 3))

    def pack(c, one, two):
        return jnp.concatenate([c, one[:, None], two[:, None]], 1).reshape(-1, 128)

    def unpack(got):
        got = got.reshape(peers, cases, slots)
        sums = jnp.sum(got[:, :, used:], 0)
        return jnp.transpose(got, (1, 0, 2)).reshape(cases, regions, peers_y, slots), sums[:, 0], sums[:, 1]

    def own_part(a):
        return jnp.concatenate([a[..., half : 2 * half], a[..., 3 * half :]], -1)

    u = scale * r
    both = jnp.concatenate([u, p_all], 2)
    y, c = local_part(both)
    yu, yp = y[:, :, :cases], y[:, :, cases:]
    rho_part = over_cases(own_part(r), own_part(u))
    names = jnp.concatenate([named, jnp.zeros(4 * 128 - slots, jnp.float32)]).reshape(4, 128)
    block = jnp.concatenate(
        [pack(c[:cases], rho_part, over_cases(u, yu)), pack(c[cases:], over_cases(p_all, yu), over_cases(p_all, yp)), names]
    )
    got = everywhere(block, axes)
    from_all = exchange(y)

    rows = cases * slots // 128
    slot_of = got[:, 2 * rows :].reshape(peers, -1)[:, :slots].reshape(regions, peers_y * slots)

    if whole:
        other = lax.ppermute(region_inv, "gx", [(0, 1), (1, 0)])
        inverses = jnp.where(here_x == 0, jnp.stack([region_inv, other]), jnp.stack([other, region_inv]))
    else:
        inverses = region_inv[None]
    pick = (slot_of[..., None] == jnp.arange(width_c, dtype=jnp.float32)).astype(jnp.float32)
    dense = jnp.einsum("ran,rnm->ram", pick, inverses, precision=EXACT)
    dense = jnp.einsum("ram,rbm->rab", dense, pick, precision=EXACT)

    def solve(c_all):
        flat_c = c_all.reshape(cases, regions, peers_y * slots)
        sol = jnp.einsum("kra,rab->krb", flat_c, dense, precision=HIGH)
        return flat_c, sol

    def total(a, b):
        return jnp.sum(a * b, (1, 2))

    def over_gx(*sums):
        return sums if whole else tuple(lax.psum(jnp.stack(sums), "gx"))

    def at(sol, ix, dy):
        sol = sol.reshape(cases, regions, peers_y, slots)
        iy = jnp.clip(here_y + dy, 0, peers_y - 1)
        return lax.dynamic_slice(sol, (0, ix, iy, 0), (cases, 1, 1, slots))[:, 0, 0]

    def beside(sol):
        if whole:
            return at(sol, 0, 0), at(sol, 1, 0)
        mine = at(sol, 0, 0)
        return swap_gx(mine, mine, peers_x)

    def coarse_part(sol):
        mine = here_x if whole else 0
        near = jnp.concatenate([at(sol, mine, 0), *beside(sol), at(sol, mine, -1), at(sol, mine, 1)], 1)
        return jnp.einsum("kn,xynj->xykj", near, spread, precision=HIGH)

    cu, rho, delta = unpack(got[:, :rows])
    cp, cross, eta = unpack(got[:, rows : 2 * rows])
    cu, su = solve(cu)
    cp, sp = solve(cp)
    delta, cross, eta = delta + total(cu, su), cross + total(cu, sp), eta + total(cp, sp)
    rho, delta, cross, eta = over_gx(rho, delta, cross, eta)
    f_both = keep * jump(y, *from_all)
    w = f_both[:, :, :cases] + coarse_part(su)
    s = f_both[:, :, cases:] + coarse_part(sp)

    wide = lambda a: a[None, None, :, None]
    beta = rho / prev_rho
    skew = cross + beta * eta
    pi = delta + 2.0 * beta * skew - beta * beta * eta
    for step in range(ITERS):
        if step > 0:
            u = scale * r
            y, c = local_part(u)
            block = pack(c, over_cases(own_part(r), own_part(u)), over_cases(u, y))
            got = everywhere(block, axes)
            from_all = exchange(y)
            rho_old = rho
            c_all, rho, delta = unpack(got)
            c_all, sol = solve(c_all)
            rho, delta = over_gx(rho, delta + total(c_all, sol))
            w = keep * jump(y, *from_all) + coarse_part(sol)
            skew = beta * skew
            beta = rho / rho_old
            pi = delta + 2.0 * beta * skew - beta * beta * pi
        alpha = rho / pi
        p = own_part(u) + wide(beta) * p
        s = w + wide(beta) * s
        lam = lam + wide(alpha) * p
        r = r - wide(alpha) * s
    back = lambda v: jnp.transpose(v, (2, 0, 1, 3))
    return back(lam), back(own_part(r)), back(p)


F32, BF16 = jnp.float32, jnp.bfloat16
SPAN_X, SPAN_Y = 2, 4
SUBS = SPAN_X * SPAN_Y
CASES = 16
EARLY = 4
STAY = 2
SLOTS = 32
USED = 2 * (SPAN_X + 1) * (SPAN_Y + 1)
CAST = 40
LIMIT = 16 * 1024 * 1024
UPPER = [(i, j) for i in range(3) for j in range(i, 3)]


def iota(shape, dim):
    return lax.broadcasted_iota(jnp.int32, shape, dim)


def split(v):
    high = v.astype(BF16)
    return high, (v - high.astype(F32)).astype(BF16)


def dot(a, b):
    return jnp.dot(a, b, preferred_element_type=F32)


def dot_turned(a, b):
    return lax.dot_general(a, b, (((1,), (1,)), ((), ())), preferred_element_type=F32)


def dot_split(v, high, low, dot=dot):
    n = v.shape[0]
    vh, vl = split(v)
    wide = dot(jnp.concatenate([vh, vl], 0), high)
    return wide[:n] + wide[n:] + dot(vh, low)


def dot_exact(v, ones):
    n = v.shape[0]
    vh, vl = split(v)
    wide = dot(jnp.concatenate([vh, vl], 0), ones)
    return wide[:n] + wide[n:]


def odd(i):
    return (i // SPAN_Y + i % SPAN_Y) % 2


def lower(rows):
    return iota((rows, 128), 1) < 64


def packs(ys):
    rows = ys[0].shape[0]
    low = lower(rows)
    column = lambda x: [
        jnp.where(low, ys[x * SPAN_Y + t][:, :128], ys[x * SPAN_Y + t + 1][:, :128]) for t in range(0, SPAN_Y, 2)
    ]
    row = lambda y: jnp.where(low, ys[y][:, 128:], ys[SPAN_Y + y][:, 128:])
    return column(0), column(SPAN_X - 1), row(0), row(SPAN_Y - 1)


def send(ys, x_ref, a_ref, b_ref, at):
    rows = pl.ds(at, ys[0].shape[0])
    west, east, south, north = packs(ys)
    first = lax.axis_index("gx") == 0
    even = lax.axis_index("gy") % 2 == 0
    for t in range(SPAN_Y // 2):
        x_ref[t, rows, :] = jnp.where(first, east[t], west[t])
    a_ref[rows, :] = jnp.where(even, north, south)
    b_ref[rows, :] = jnp.where(even, south, north)


def received(x_ref, a_ref, b_ref, at, n, side=None):
    rows = pl.ds(at, n)
    first = lax.axis_index("gx") == 0
    even = lax.axis_index("gy") % 2 == 0
    xs = [x_ref[t, rows, :] for t in range(SPAN_Y // 2)]
    a, b = a_ref[rows, :], b_ref[rows, :]
    if side is not None:
        a, b = a + side[:, :128], b + side[:, 128:256]
        xs = [xs[t] + side[:, 256 + 128 * t : 384 + 128 * t] for t in range(SPAN_Y // 2)]
    zero = jnp.zeros_like(a)
    return (
        [jnp.where(first, zero, v) for v in xs],
        [jnp.where(first, v, zero) for v in xs],
        jnp.where(even, b, a),
        jnp.where(even, a, b),
    )


def across(ys, nb, rows):
    low = lower(rows)
    zero = jnp.zeros((rows, 128), F32)
    inside = lambda x, y, part: zero if ys is None else ys[x * SPAN_Y + y][:, part * 128 : part * 128 + 128]
    out = []
    for x in range(SPAN_X):
        for y in range(SPAN_Y):
            beyond = lambda v: zero if nb is None else v()
            west = inside(x - 1, y, 0) if x else beyond(lambda: nb[0][y // 2])
            east = inside(x + 1, y, 0) if x < SPAN_X - 1 else beyond(lambda: nb[1][y // 2])
            south = inside(x, y - 1, 1) if y else beyond(lambda: nb[2])
            north = inside(x, y + 1, 1) if y < SPAN_Y - 1 else beyond(lambda: nb[3])
            if (x + y) % 2:
                west, east, south, north = east, west, north, south
            out.append(jnp.concatenate([jnp.where(low, west, east), jnp.where(low, south, north)], 1))
    return out


def owned_lanes(i, rows):
    lane = iota((rows, 256), 1) % 128
    return lane < 64 if odd(i) else lane >= 64


def spread_owned(v, i):
    zero = jnp.zeros_like(v)
    low = lower(v.shape[0])
    turned = pltpu.roll(v, 64, 1)
    if odd(i):
        return jnp.concatenate([jnp.where(low, v, zero), jnp.where(low, turned, zero)], 1)
    return jnp.concatenate([jnp.where(low, zero, turned), jnp.where(low, zero, v)], 1)


def take_owned(v, i):
    low = lower(v.shape[0])
    if odd(i):
        return jnp.where(low, v[:, :128], pltpu.roll(v[:, 128:], 64, 1))
    return jnp.where(low, pltpu.roll(v[:, :128], 64, 1), v[:, 128:])


def start_kernel(res_ref, dir_ref, act_ref, scale_ref, *refs):
    inverse_ref, own_ref, x_ref, a_ref, b_ref = refs[4:9]
    upper_ref, p_ref = refs[13:15]
    gx, gy = lax.axis_index("gx"), lax.axis_index("gy")
    last_x = gx * SPAN_X + SPAN_X - 1 == lax.axis_size("gx") * SPAN_X - 1
    last_y = gy * SPAN_Y + SPAN_Y - 1 == lax.axis_size("gy") * SPAN_Y - 1
    east = iota((1, 128), 1) < 64
    ys = []
    for i in range(SUBS):
        x, y = i // SPAN_Y, i % SPAN_Y
        keep = act_ref[i : i + 1, :].astype(F32)
        if x == SPAN_X - 1:
            keep = jnp.where(jnp.logical_and(last_x, east), 0.0, keep)
        if y == SPAN_Y - 1:
            keep = jnp.where(jnp.logical_and(last_y, jnp.logical_not(east)), 0.0, keep)
        mine = pl.ds(i, CASES, stride=SUBS)
        p = dir_ref[mine, :] * keep
        p_ref[mine, :] = p
        v = jnp.concatenate(
            [
                res_ref[mine, :],
                p,
                scale_ref[i : i + 1, :] * keep,
                keep,
                jnp.zeros((CAST - 2 * CASES - 2, 128), F32),
            ],
            0,
        )
        v = spread_owned(v, i)
        own_ref[i] = v
        ys.append(v)
    send(ys, x_ref, a_ref, b_ref, 0)
    for ref in (x_ref, a_ref, b_ref):
        ref.flush()
    for t, (i, j) in enumerate(UPPER):
        upper_ref[t] = inverse_ref[128 * i : 128 * i + 128, 128 * j : 128 * j + 128]


def operator_kernel(
    schur_ref, couple_ref, map_ref, slot_ref, rest_ref, ha_ref, la_ref, hb_ref, lb_ref, cc_ref, ch_ref, cl_ref, name_ref,
):
    none = 384
    slot = slot_ref[...].astype(F32)
    eye = iota((8, 8), 0) == iota((8, 8), 1)
    column = jnp.concatenate(
        [jnp.sum(jnp.where(eye, jnp.broadcast_to(slot[i : i + 1, :], (8, 8)), 0.0), 1, keepdims=True) for i in range(SUBS)], 0
    )
    row = jnp.concatenate([slot[i : i + 1, :] for i in range(SUBS)], 1)
    count = SUBS * 8
    earlier = iota((count, count), 1) < iota((count, count), 0)
    again = jnp.sum(jnp.where(jnp.logical_and(column == row, earlier), 1.0, 0.0), 1, keepdims=True)
    first = jnp.where(jnp.logical_and(again == 0.0, column != float(none)), 1.0, 0.0)
    first_row = jnp.sum(
        jnp.where(jnp.logical_and(column == row, iota((count, count), 0) < iota((count, count), 1)), 1.0, 0.0), 0, keepdims=True
    )
    first_row = jnp.where(jnp.logical_and(first_row == 0.0, row != float(none)), 1.0, 0.0)
    rank = jnp.sum(jnp.where(row < column, first_row, 0.0), 1, keepdims=True)
    hit = jnp.where(rank == iota((count, 128), 1).astype(F32), first, 0.0)
    name_ref[...] = jnp.broadcast_to(
        jnp.where(jnp.sum(hit, 0, keepdims=True) > 0.0, jnp.sum(hit * column, 0, keepdims=True), float(none)), (8, 128)
    )
    sub = iota((256, 256), 0)
    west = (sub // 64) % 2 == 0
    for i in range(SUBS):
        spots = map_ref[i // SPAN_Y, i % SPAN_Y : i % SPAN_Y + 1, :]
        if odd(i):
            spots = jnp.where((spots // 64) % 2 == 0, spots + 64, spots - 64)
        sign = jnp.where(west, 1.0, -1.0) if odd(i) else jnp.where(west, -1.0, 1.0)
        place = jnp.where(sub == spots, sign, 0.0).astype(BF16)
        mine = slot[i : i + 1, :]
        number = jnp.sum(jnp.where(column < mine, first, 0.0), 0, keepdims=True)
        compact = jnp.where(
            jnp.logical_and(number == iota((SLOTS, 8), 0).astype(F32), mine != float(none)), 1.0, 0.0
        )
        cc = jnp.dot(compact, couple_ref[i], precision=EXACT, preferred_element_type=F32)
        c1, rest = split(cc)
        c2, c3 = split(cc - c1.astype(F32))
        s1, s2 = split(schur_ref[i] if i < EARLY else rest_ref[i - EARLY])
        tall = dot_turned(jnp.concatenate([s1, s2, c1, c2, c3], 0), place)
        high, low = (dot(place, tall[t : t + 256].astype(BF16)).astype(BF16) for t in (0, 256))
        if i < STAY:
            ha_ref[i], la_ref[i] = high, low
        else:
            hb_ref[i - STAY], lb_ref[i - STAY] = high, low
        cc = tall[512 : 512 + SLOTS] + tall[512 + SLOTS : 512 + 2 * SLOTS] + tall[512 + 2 * SLOTS :]
        cc_ref[i] = cc
        ch_ref[i], cl_ref[i] = split(cc)


def inverse_kernel(mine_ref, upper_ref, high_ref, low_ref):
    first = lax.axis_index("gx") == 0
    mine = mine_ref[...]
    blocks = {spot: upper_ref[t] for t, spot in enumerate(UPPER)}
    side = lambda i, j: blocks[i, j] if i <= j else jnp.transpose(blocks[j, i])
    other = jnp.concatenate([jnp.concatenate([side(i, j) for j in range(3)], 1) for i in range(3)], 0)
    for region, v in enumerate((jnp.where(first, mine, other), jnp.where(first, other, mine))):
        high_ref[region], low_ref[region] = split(v)


def near_names(name_ref, x_ref, a_ref, b_ref):
    named = pl.ds(2 * CASES + SLOTS, 8)
    group = iota((8, 128), 1) // SLOTS
    turn = lambda v, g: jnp.where(group == g, pltpu.roll(v, g * SLOTS, 1), 0.0)
    wanted = name_ref[...] + 0.0
    wanted = jnp.where(group == 0, wanted, turn(a_ref[named, :], 1) + turn(b_ref[named, :], 2) + turn(x_ref[0, named, :], 3))
    found = iota((384, 128), 0).astype(F32) == wanted[0:1]
    mine = jnp.where(iota((384, 128), 1) < 3 * SLOTS, 1.0, 0.0)
    gx = lax.axis_index("gx")
    return [jnp.where(found, jnp.where(gx == region, mine, 1.0 - mine), 0.0).astype(BF16) for region in range(2)]


def near_spread(x_ref, a_ref, b_ref, nh_ref, nl_ref):
    rows = pl.ds(2 * CASES, SLOTS)
    nh_ref[...], nl_ref[...] = split(
        jnp.concatenate([a_ref[rows, :], b_ref[rows, :], x_ref[0, rows, :], x_ref[1, rows, :]], 1)
    )


def operator(ys, x_ref, a_ref, b_ref, near, mk_ref, ch_ref, cl_ref, nh_ref, nl_ref):
    n = ys[0].shape[0]
    high, low = nh_ref[...], nl_ref[...]
    side = jnp.concatenate(
        [
            dot_split(near[g], high[:, at : at + width], low[:, at : at + width])
            for g, at, width in ((1, 0, 128), (2, 128, 128), (3, 256, 256))
        ],
        1,
    )
    west, east, south, north = received(x_ref, a_ref, b_ref, 0, n, side)
    ys = [ys[i] + dot_split(near[0], ch_ref[i], cl_ref[i]) for i in range(SUBS)]
    other = across(ys, (west, east, south, north), n)
    return [mk_ref[i, 1:2, :] * (ys[i] + other[i]) for i in range(SUBS)]


def corners(us, ch_ref, cl_ref):
    couple = lambda ref: jnp.concatenate([ref[i] for i in range(SUBS)], 0)
    corner = dot_split(jnp.concatenate(us, 0), couple(ch_ref), couple(cl_ref), dot_turned)
    n = us[0].shape[0]
    group = iota((n, 128), 1) // SLOTS
    total = jnp.zeros((n, 128), F32)
    for i in range(SUBS):
        part = corner[n * i : n * i + n, 128 * (i // 4) : 128 * (i // 4) + 128]
        total = total + jnp.where(group == i % 4, part, 0.0)
    total = total + pltpu.roll(total, 64, 1)
    return total + pltpu.roll(total, 32, 1)


def by_schur(us, ha_ref, la_ref, hb_ref, lb_ref):
    return [
        dot_split(us[i], ha_ref[i], la_ref[i]) if i < STAY else dot_split(us[i], hb_ref[i - STAY], lb_ref[i - STAY])
        for i in range(SUBS)
    ]


def over_lanes(terms):
    total = terms[0]
    for t in terms[1:]:
        total = total + t
    return jnp.sum(total[:, :128] + total[:, 128:], 1, keepdims=True)


def packed(corner, one, two):
    slot = iota((CASES, 128), 1) % SLOTS
    full = jnp.where(slot == USED, one, jnp.where(slot == USED + 1, two, corner))
    group = iota((4, 128), 1) // SLOTS
    out = jnp.zeros((4, 128), F32)
    for b in range(4):
        out = jnp.where(group == b, full[4 * b : 4 * b + 4], out)
    return out


def by_slot(vs):
    group = iota((8, 128), 1) // SLOTS
    out = []
    for region in range(2):
        rows = []
        for b in range(4):
            halves = []
            for h in range(2):
                acc = None
                for q in range(4):
                    v = vs[8 * region + 4 * h + q]
                    turned = v if q == b else pltpu.roll(v, (SLOTS * (q - b)) % 128, 1)
                    acc = turned if acc is None else jnp.where(group == q, turned, acc)
                halves.append(acc)
            rows.append(jnp.concatenate(halves, 1))
        out.append(jnp.concatenate(rows, 0))
    return out


def inner(vs):
    total = vs[0]
    for v in vs[1:]:
        total = total + v
    total = total[:4] + total[4:]
    tall = jnp.concatenate([total] * 4, 0)
    lane, row = iota((CASES, 128), 1), iota((CASES, 128), 0)
    column = lambda s: jnp.sum(jnp.where(lane == SLOTS * (row // 4) + s, tall, 0.0), 1, keepdims=True)
    return column(USED), column(USED + 1)


def first_of_pairs(v):
    return jnp.concatenate([v[8 * b : 8 * b + 4] for b in range(v.shape[0] // 8)], 0)


def solve(spots, pick_ref, gh_ref, gl_ref, near_ref):
    totals, sols, near = [], [], None
    for region in range(2):
        v = spots[region]
        n = v.shape[0]
        even = dot_exact(v, pick_ref[region, 0])
        odds = dot_exact(v, pick_ref[region, 1])
        z = jnp.where((iota((n, 384), 0) // 4) % 2 == 0, even, odds).reshape(n // 8, 8, 384)
        total = (z + pltpu.roll(z, 4, 1)).reshape(n, 384)
        sol = dot_split(total, gh_ref[region], gl_ref[region])
        part = dot_exact(sol, near_ref[region])
        near = part if near is None else near + part
        totals.append(total)
        sols.append(sol)
    return totals, sols, near


def swap_pairs(v):
    rows, lanes = v.shape
    return pltpu.roll(v.reshape(rows // 8, 8, lanes), 4, 1).reshape(rows, lanes)


def ahead(region, t):
    gx, gy = lax.axis_index("gx"), lax.axis_index("gy")
    return 8 * lax.rem(gx + region, 2) + lax.rem(gy // 2 + t, 8)


def dense_kernel(got_ref, gh_ref, gl_ref, dh_ref, dl_ref):
    group = iota((8, 128), 1) // SLOTS
    picks, rows = [], []
    for region in range(2):
        hits = []
        for par in range(2):
            halves = []
            for h in range(2):
                acc = None
                for q in range(4):
                    v = got_ref[3 * ahead(region, 4 * h + q) + 1 + par]
                    v = v if par == 0 else pltpu.roll(v, 4, 0)
                    turned = pltpu.roll(v, SLOTS * q, 1) if q else v
                    acc = turned if acc is None else jnp.where(group == q, turned, acc)
                halves.append(acc[0:1])
            wanted = jnp.concatenate(halves, 1)
            hits.append(jnp.where(iota((384, 256), 0).astype(F32) == wanted, 1.0, 0.0))
        picks.append(jnp.concatenate(hits, 1).astype(BF16))
        rows.append([jnp.transpose(hit).astype(BF16) for hit in hits])
    size = 384
    for region in range(2):
        which = lax.rem(lax.axis_index("gx") + region, 2)
        both = dot(jnp.concatenate([gh_ref[which], gl_ref[which]], 0), picks[region]).astype(BF16)
        for half, out_ref in ((both[:size], dh_ref), (both[size:], dl_ref)):
            top = dot(rows[region][0], half).astype(BF16)
            out_ref[region, 0], out_ref[region, 1] = top[:, :256], top[:, 256:]
            out_ref[region, 2] = dot(rows[region][1], half[:, 256:]).astype(BF16)


def solve_dense(spots, dh_ref, dl_ref):
    total, sols = None, []
    for region in range(2):
        v = spots[region]
        block = lambda t, dot=dot: dot_split(v, dh_ref[region, t], dl_ref[region, t], dot)
        first = (iota(v.shape, 0) // 4) % 2 == 0
        sol = jnp.where(first, block(0) + swap_pairs(block(1, dot_turned)), block(2) + swap_pairs(block(1)))
        total = v * sol if total is None else total + v * sol
        sols.append(sol)
    total = jnp.sum(total, 1, keepdims=True)
    halves = lambda v: [jnp.concatenate([v[8 * b + at : 8 * b + at + 4] for b in range(4)], 0) for at in (0, 4)]
    total = sum(halves(total))
    even = lax.axis_index("gy") % 2 == 0
    (a, b), (c, d) = halves(sols[0]), halves(sols[1][:, :128])
    here = jnp.where(even, a[:, :128], b[:, :128])
    pair = jnp.where(even, b[:, :128], a[:, :128])
    beyond = jnp.where(even, pltpu.roll(b[:, 128:], SLOTS, 1), pltpu.roll(a[:, :128], 128 - SLOTS, 1))
    along = jnp.where(even, c, d)
    return total, [v[:, :SLOTS] for v in (here, pair, beyond, along)]


def energy(totals, sols):
    both = totals[0] * sols[0] + totals[1] * sols[1]
    return first_of_pairs(jnp.sum(both, 1, keepdims=True))


def emit(rs, mk_ref, schur_refs, ch_ref, cl_ref, block_ref, y_ref, x_ref, a_ref, b_ref):
    us = [mk_ref[i, 0:1, :] * rs[i] for i in range(SUBS)]
    corner = corners(us, ch_ref, cl_ref)
    rho = over_lanes([jnp.where(owned_lanes(i, CASES), rs[i] * us[i], 0.0) for i in range(SUBS)])
    ys = by_schur(us, *schur_refs)
    send(ys, x_ref, a_ref, b_ref, 0)
    for i in range(SUBS):
        y_ref[i] = ys[i]
    for ref in (x_ref, a_ref, b_ref, y_ref):
        ref.flush()
    delta = over_lanes([us[i] * ys[i] for i in range(SUBS)])
    block = packed(corner, rho, delta)
    twice = jnp.concatenate([block, block], 0)
    for j in range(16):
        block_ref[j] = twice
    block_ref.flush()


def first_kernel(
    own_ref, x_ref, a_ref, b_ref, ha_ref, la_ref, hb_ref, lb_ref, cc_ref, ch_ref, cl_ref, name_ref,
    r_ref, mk_ref, y_ref, block_ref, sx_ref, sa_ref, sb_ref, high_out_ref, low_out_ref,
):
    schur_refs = ha_ref, la_ref, hb_ref, lb_ref
    own = [own_ref[i] for i in range(SUBS)]
    other = across(own, received(x_ref, a_ref, b_ref, 0, CAST), CAST)
    rs, vs = [], []
    for i in range(SUBS):
        full = own[i] + other[i]
        rs.append(full[:CASES])
        r_ref[i] = full[:CASES]
        mk_ref[i] = full[2 * CASES : 2 * CASES + 8]
        vs.append(jnp.concatenate([full[2 * CASES : 2 * CASES + 1] * full[:CASES], full[CASES : 2 * CASES]], 0))
    corner = corners(vs, ch_ref, cl_ref)
    ys = by_schur(vs, *schur_refs)
    names = name_ref[...]
    send([jnp.concatenate([ys[i], cc_ref[i]], 0) for i in range(SUBS)], sx_ref, sa_ref, sb_ref, 0)
    at = pl.ds(2 * CASES + SLOTS, 8)
    for t in range(SPAN_Y // 2):
        sx_ref[t, at, :] = names
    sa_ref[at, :] = names
    sb_ref[at, :] = names
    us = [v[:CASES] for v in vs]
    ps = [v[CASES:] for v in vs]
    rho = over_lanes([jnp.where(owned_lanes(i, CASES), rs[i] * us[i], 0.0) for i in range(SUBS)])
    delta = over_lanes([us[i] * ys[i][:CASES] for i in range(SUBS)])
    cross = over_lanes([ps[i] * ys[i][:CASES] for i in range(SUBS)])
    eta = over_lanes([ps[i] * ys[i][CASES:] for i in range(SUBS)])
    one, two = packed(corner[:CASES], rho, delta), packed(corner[CASES:], cross, eta)
    blocks = [
        jnp.concatenate([one, two], 0),
        jnp.concatenate([names[:4], one], 0),
        jnp.concatenate([two, names[:4]], 0),
    ]
    for j in range(16):
        for t in range(3):
            block_ref[3 * j + t] = blocks[t]
    for i in range(SUBS):
        y_ref[i] = ys[i]


def column_of(row):
    eye = iota((CASES, CASES), 0) == iota((CASES, CASES), 1)
    return jnp.sum(jnp.where(eye, jnp.broadcast_to(row, (CASES, CASES)), 0.0), 1, keepdims=True)


def keep_scalars(scal_ref, values):
    for t, v in enumerate(values):
        scal_ref[t] = jnp.broadcast_to(v, (CASES, 128))


def second_kernel(
    got_ref, x_ref, a_ref, b_ref, y_ref, r_ref, mk_ref, p_ref, l_ref, rho_ref, gh_ref, gl_ref, name_ref,
    ha_ref, la_ref, hb_ref, lb_ref, ch_ref, cl_ref,
    nh_ref, nl_ref, po_ref, lo_ref, ro_ref, so_ref, scal_ref, block_ref, yo_ref, sx_ref, sa_ref, sb_ref, *_,
):
    near_ref, pick_ref = near_names(name_ref, x_ref, a_ref, b_ref), {}
    near_spread(x_ref, a_ref, b_ref, nh_ref, nl_ref)
    top = iota((8, 128), 0) < 4
    us, ps, names = [], [], []
    for j in range(16):
        v = [got_ref[3 * j + t] for t in range(3)]
        us.append(jnp.where(top, v[0], v[1]))
        ps.append(pltpu.roll(jnp.where(top, v[2], v[0]), 4, 0))
        names.append((v[1], pltpu.roll(v[2], 4, 0)))
    group = iota((8, 128), 1) // SLOTS
    for region in range(2):
        for par in range(2):
            halves = []
            for h in range(2):
                acc = None
                for q in range(4):
                    v = names[8 * region + 4 * h + q][par]
                    turned = pltpu.roll(v, SLOTS * q, 1) if q else v
                    acc = turned if acc is None else jnp.where(group == q, turned, acc)
                halves.append(acc[0:1])
            wanted = jnp.concatenate(halves, 1)
            hit = jnp.where(iota((384, 256), 0).astype(F32) == wanted, 1.0, 0.0)
            pick_ref[region, par] = jnp.transpose(hit).astype(BF16)
    lhs_u, lhs_p = by_slot(us), by_slot(ps)
    n = lhs_u[0].shape[0]
    totals, sols, near = solve(
        [jnp.concatenate([lhs_u[t], lhs_p[t]], 0) for t in range(2)], pick_ref, gh_ref, gl_ref, near_ref
    )
    of_u, of_p = lambda vs: [v[:n] for v in vs], lambda vs: [v[n:] for v in vs]
    rho, delta = inner(us)
    cross, eta = inner(ps)
    delta = delta + energy(of_u(totals), of_u(sols))
    cross = cross + energy(of_p(totals), of_u(sols))
    eta = eta + energy(of_p(totals), of_p(sols))
    near = first_of_pairs(near)
    near = [(pltpu.roll(near, 128 - SLOTS * g, 1) if g else near)[:, :SLOTS] for g in range(4)]
    beta = rho / column_of(rho_ref[...])
    skew = cross + beta * eta
    pi = delta + 2.0 * beta * skew - beta * beta * eta
    alpha = rho / pi
    fs = operator([y_ref[i] for i in range(SUBS)], x_ref, a_ref, b_ref, near, mk_ref, ch_ref, cl_ref, nh_ref, nl_ref)
    rs = []
    for i in range(SUBS):
        f, r = fs[i], r_ref[i]
        s = f[:CASES] + beta * f[CASES:]
        r = r - alpha * s
        rs.append(r)
        ro_ref[i], so_ref[i] = r, s
    scalars = rho, pi, beta, skew, alpha
    keep_scalars(scal_ref, scalars)
    so_ref.flush()
    emit(rs, mk_ref, (ha_ref, la_ref, hb_ref, lb_ref), ch_ref, cl_ref, block_ref, yo_ref, sx_ref, sa_ref, sb_ref)

    @pl.when(lax.axis_index("gx") >= 0)
    def _():
        track(r_ref, scalars, mk_ref, p_ref, l_ref, po_ref, lo_ref)


def absorb(got_ref, x_ref, a_ref, b_ref, y_ref, r_ref, s_ref, scal_ref, mk_ref, dh_ref, dl_ref, nh_ref, nl_ref, ch_ref, cl_ref):
    vs = [got_ref[ahead(region, t)] for region in range(2) for t in range(8)]
    coarse, near = solve_dense(by_slot(vs), dh_ref, dl_ref)
    rho, delta = inner(vs)
    delta = delta + coarse
    rho_old, pi, beta, skew = (scal_ref[t][:, 0:1] for t in range(4))
    skew = beta * skew
    beta = rho / rho_old
    pi = delta + 2.0 * beta * skew - beta * beta * pi
    alpha = rho / pi
    fs = operator([y_ref[i] for i in range(SUBS)], x_ref, a_ref, b_ref, near, mk_ref, ch_ref, cl_ref, nh_ref, nl_ref)
    ss = [fs[i] + beta * s_ref[i] for i in range(SUBS)]
    rs = [r_ref[i] - alpha * ss[i] for i in range(SUBS)]
    return rs, ss, (rho, pi, beta, skew, alpha)


def track(r_ref, scalars, mk_ref, p_ref, l_ref, po_ref, lo_ref):
    _, _, beta, _, alpha = scalars
    for i in range(SUBS):
        mine = pl.ds(i, CASES, stride=SUBS)
        p = take_owned(mk_ref[i, 0:1, :] * r_ref[i], i) + beta * p_ref[mine, :]
        po_ref[mine, :] = p
        lo_ref[mine, :] = l_ref[mine, :] + alpha * p


def round_kernel(
    got_ref, x_ref, a_ref, b_ref, y_ref, r_ref, s_ref, scal_ref, mk_ref, dh_ref, dl_ref,
    nh_ref, nl_ref, ch_ref, cl_ref, p_ref, l_ref, ha_ref, la_ref, hb_ref, lb_ref,
    po_ref, lo_ref, ro_ref, so_ref, scalo_ref, block_ref, yo_ref, sx_ref, sa_ref, sb_ref,
):
    rs, ss, scalars = absorb(
        got_ref, x_ref, a_ref, b_ref, y_ref, r_ref, s_ref, scal_ref, mk_ref, dh_ref, dl_ref, nh_ref, nl_ref, ch_ref, cl_ref
    )
    for i in range(SUBS):
        ro_ref[i], so_ref[i] = rs[i], ss[i]
    so_ref.flush()
    keep_scalars(scalo_ref, scalars)
    emit(rs, mk_ref, (ha_ref, la_ref, hb_ref, lb_ref), ch_ref, cl_ref, block_ref, yo_ref, sx_ref, sa_ref, sb_ref)

    @pl.when(lax.axis_index("gx") >= 0)
    def _():
        track(r_ref, scalars, mk_ref, p_ref, l_ref, po_ref, lo_ref)


def last_kernel(
    got_ref, x_ref, a_ref, b_ref, y_ref, r_ref, s_ref, scal_ref, mk_ref, dh_ref, dl_ref, nh_ref, nl_ref, ch_ref, cl_ref,
    p_ref, l_ref, lo_ref, ro_ref, po_ref,
):
    rs, _, scalars = absorb(
        got_ref, x_ref, a_ref, b_ref, y_ref, r_ref, s_ref, scal_ref, mk_ref, dh_ref, dl_ref, nh_ref, nl_ref, ch_ref, cl_ref
    )
    track(r_ref, scalars, mk_ref, p_ref, l_ref, po_ref, lo_ref)
    for i in range(SUBS):
        ro_ref[pl.ds(i, CASES, stride=SUBS), :] = take_owned(rs[i], i)


class Fetched:
    def __init__(self, source, buffer, semaphore):
        self.buffer = buffer
        self.copy = pltpu.make_async_copy(source, buffer, semaphore)
        self.copy.start()
        self.here = False

    def wait(self):
        self.copy.wait()
        self.here = True

    def __getitem__(self, index):
        if not self.here:
            self.wait()
        return self.buffer[index]


class Stored:
    def __init__(self, target, buffer, semaphore):
        self.buffer = buffer
        self.copy = pltpu.make_async_copy(buffer, target, semaphore)
        self.sent = False

    def __setitem__(self, index, value):
        self.buffer[index] = value

    def __getitem__(self, index):
        return self.buffer[index]

    def flush(self):
        if not self.sent:
            self.copy.start()
            self.sent = True


class Kept:
    def __init__(self, ref):
        self.ref = ref

    def __setitem__(self, index, value):
        self.ref[index] = value

    def __getitem__(self, index):
        return self.ref[index]

    def flush(self):
        pass


def call(kernel, args, outs, kept=(), kept_out=(), raw=(), through=None, flops=None, late=0, parts=None):
    through, parts = through or {}, parts or {}
    moved = [i for i in range(len(args)) if i not in kept and i not in raw]
    written = [i for i in range(len(outs)) if i not in kept_out and i not in through]

    def body(*refs):
        ins, results = refs[: len(args)], refs[len(args) : len(args) + len(outs)]
        buffers, (in_sem, out_sem, through_sem) = refs[len(args) + len(outs) : -3], refs[-3:]
        fetched, stored = list(ins), [Kept(ref) for ref in results]
        for t, i in enumerate(moved):
            source = ins[i].at[pl.ds(*parts[i])] if i in parts else ins[i]
            fetched[i] = Fetched(source, buffers[t], in_sem.at[t])
        for t, i in enumerate(written):
            stored[i] = Stored(results[i], buffers[len(moved) + t], out_sem.at[t])
        passing = [
            pltpu.make_async_copy(source(ins), results[i], through_sem.at[t]) for t, (i, source) in enumerate(through.items())
        ]
        for copy in passing:
            copy.start()
        if moved or passing:
            spot = (0,) * (len(outs[-1 - late][0]) - 2)
            blank = stored[-1 - late]

            @pl.when(lax.axis_index("gx") >= 0)
            def _():
                blank[spot] = jnp.zeros(outs[-1 - late][0][-2:], outs[-1 - late][1])

        kernel(*fetched, *stored)
        for i in written:
            stored[i].flush()
        for i in moved:
            if not fetched[i].here:
                fetched[i].wait()
        for copy in passing:
            copy.wait()
        for i in written:
            stored[i].copy.wait()

    place = lambda held: pl.BlockSpec(memory_space=pltpu.VMEM if held else pltpu.HBM)
    semaphores = lambda n: pltpu.SemaphoreType.DMA((max(n, 1),))
    args = [a if i in kept else pltpu.with_memory_space_constraint(a, pltpu.HBM) for i, a in enumerate(args)]
    return pl.pallas_call(
        body,
        out_shape=[
            jax.ShapeDtypeStruct(*out) if i in kept_out else pltpu.HBM(*out) for i, out in enumerate(outs)
        ],
        in_specs=[place(i in kept) for i in range(len(args))],
        out_specs=[place(i in kept_out) for i in range(len(outs))],
        scratch_shapes=[
            pltpu.VMEM((parts[i][1],) + args[i].shape[1:] if i in parts else args[i].shape, args[i].dtype) for i in moved
        ]
        + [pltpu.VMEM(*outs[i]) for i in written]
        + [semaphores(len(moved)), semaphores(len(written)), semaphores(len(through))],
        compiler_params=pltpu.CompilerParams(vmem_limit_bytes=LIMIT),
        cost_estimate=flops and pl.CostEstimate(flops=flops, bytes_accessed=flops // 512, transcendentals=0),
    )(*args)


def trade(x, a, b):
    peers = lax.axis_size("gy")
    return (
        lax.ppermute(x, "gx", [(0, 1), (1, 0)]),
        lax.ppermute(a, "gy", both_ways(pairs_from(0, peers))),
        lax.ppermute(b, "gy", both_ways(pairs_from(1, peers))),
    )


def two_regions(
    duals, residual, direction, prev_rho, dual_schur, coupling, coarse_inverse, edge_map, corner_slot, active, scaling
):
    native = lambda v: v.reshape(CASES * SUBS, 128)
    by_sub = lambda v: v.reshape((SUBS,) + v.shape[2:])
    width = coarse_inverse.shape[-1]
    sends = lambda rows: [((SPAN_Y // 2, rows, 128), F32), ((rows, 128), F32), ((rows, 128), F32)]
    state = ((SUBS, CASES, 256), F32)
    plain = ((CASES * SUBS, 128), F32)

    raw = [by_sub(dual_schur), by_sub(coupling), edge_map, by_sub(corner_slot)]
    own, *out, schur, coupled, placed, slotted, inverse, p = call(
        start_kernel,
        [native(residual), native(direction), by_sub(active), by_sub(scaling), *raw, coarse_inverse[0]],
        [((SUBS, CAST, 256), F32)] + sends(CAST) + [((EARLY,) + raw[0].shape[1:], F32)] + [(v.shape, v.dtype) for v in raw[1:]] + [((len(UPPER), 128, 128), F32), plain],
        kept_out=(0, 4, 5, 6, 7),
        raw=(4, 5, 6, 7),
        through={4: lambda v: v[4].at[pl.ds(0, EARLY)], 5: lambda v: v[5], 6: lambda v: v[6], 7: lambda v: v[7]},
    )
    come = trade(*out)
    other = lax.ppermute(inverse, "gx", [(0, 1), (1, 0)])
    first_part, rest = ((STAY, 256, 256), BF16), ((SUBS - STAY, 256, 256), BF16)
    couple = ((SUBS, SLOTS, 256), BF16)
    ha, la, hb, lb, cc, ch, cl, names = call(
        operator_kernel,
        [schur, coupled, placed, slotted, by_sub(dual_schur)],
        [first_part, first_part, rest, rest, ((SUBS, SLOTS, 256), F32), couple, couple, ((8, 128), F32)],
        kept=range(4),
        kept_out=range(8),
        parts={4: (EARLY, SUBS - EARLY)},
        flops=5 * 10**9,
    )
    rows = 2 * CASES + SLOTS + 8
    r, mk, y, block, *out, hb, lb = call(
        first_kernel,
        [own, *come, ha, la, hb, lb, cc, ch, cl, names],
        [state, ((SUBS, 8, 256), F32), ((SUBS, 2 * CASES, 256), F32), ((48, 8, 128), F32)]
        + sends(rows)
        + [rest, rest],
        kept=range(12),
        kept_out=(0, 1, 2),
        through={7: lambda v: v[6], 8: lambda v: v[7]},
        late=2,
    )
    got = lax.all_to_all(block.reshape(32, 3, 4, 128), BOTH, 0, 0, tiled=False).reshape(48, 8, 128)
    come = trade(*out)
    square = ((2, width, width), BF16)
    gh, gl = call(inverse_kernel, [coarse_inverse[0], other], [square, square], kept_out=(0, 1), flops=10**9)
    side = ((SLOTS, 512), BF16)
    onward = [plain, plain, state, state, ((5, CASES, 128), F32), ((16, 8, 128), F32), state] + sends(CASES)
    nh, nl, p, lam, r, s, scal, block, y, *out, gh, gl = call(
        second_kernel,
        [got, *come, y, r, mk, p, native(duals), prev_rho.reshape(1, CASES), gh, gl, names, ha, la, hb, lb, ch, cl],
        [side, side] + onward + [square, square],
        kept=(0, 1, 2, 3, 4, 5, 6, 10, 11, 12, 13, 14, 17, 18),
        kept_out=(0, 1, 2, 3, 4, 6, 8),
        through={12: lambda v: v[10], 13: lambda v: v[11]},
        late=5,
    )
    dense = ((2, 3, 256, 256), BF16)
    dh, dl = call(dense_kernel, [got, gh, gl], [dense, dense], kept=(0,), kept_out=(0, 1), flops=10**8)
    for step in range(1, ITERS):
        got = lax.all_to_all(block.reshape(32, 4, 128), BOTH, 0, 0, tiled=False).reshape(16, 8, 128)
        come = trade(*out)
        args = [got, *come, y, r, s, scal, mk, dh, dl, nh, nl, ch, cl, p, lam]
        kept = (*range(6), *range(7, 17))
        if step < ITERS - 1:
            p, lam, r, s, scal, block, y, *out = call(
                round_kernel, args + [ha, la, hb, lb], onward, (*kept, 17, 18), kept_out=(0, 1, 2, 4, 6), late=3
            )
        else:
            results = call(last_kernel, args, [plain, plain, plain], kept)
    return tuple(v.reshape(duals.shape) for v in results)


def shards(*args):
    cases, span_x, span_y, owned = args[0].shape
    fits = (cases, span_x, span_y, owned, args[6].shape[-1]) == (CASES, SPAN_X, SPAN_Y, 128, 384)
    if fits and lax.axis_size("gx") == 2 and lax.axis_size("gy") == 16:
        return two_regions(*args)
    return general(*args)


def solution(mesh):
    placed = (
        P(None, "gx", "gy", None),
        P(None, "gx", "gy", None),
        P(None, "gx", "gy", None),
        P(),
        P("gx", "gy", None, None),
        P("gx", "gy", None, None),
        P("gx", None, None),
        P("gx", "gy", None),
        P("gx", "gy", None),
        P("gx", "gy", None),
        P("gx", "gy", None),
    )
    return jax.shard_map(
        shards,
        mesh=mesh,
        in_specs=placed,
        out_specs=(P(None, "gx", "gy", None), P(None, "gx", "gy", None), P(None, "gx", "gy", None)),
        check_vma=False,
    )
```

```python
import jax
import jax.numpy as jnp
from jax import lax
from jax.experimental import pallas as pl
from jax.experimental.pallas import tpu as pltpu
from jax.sharding import PartitionSpec as P

ITERS = 6
HIGH = lax.Precision.HIGH
EXACT = lax.Precision.HIGHEST
BOTH = ("gx", "gy")


def pairs_from(first, peers):
    return [(i, i + 1) for i in range(first, peers - 1, 2)]


def both_ways(pairs):
    return pairs + [(b, a) for a, b in pairs]


def up_gy(value, peers):
    even = lax.ppermute(value, "gy", pairs_from(0, peers))
    odd = lax.ppermute(value, "gy", pairs_from(1, peers))
    return jnp.where(lax.axis_index("gy") % 2 == 1, even, odd)


def swap_gy(low, high, peers):
    is_even = lax.axis_index("gy") % 2 == 0
    first = lax.ppermute(jnp.where(is_even, high, low), "gy", both_ways(pairs_from(0, peers)))
    second = lax.ppermute(jnp.where(is_even, low, high), "gy", both_ways(pairs_from(1, peers)))
    return jnp.where(is_even, second, first), jnp.where(is_even, first, second)


def swap_gx(low, high, peers):
    if peers == 2:
        is_first = lax.axis_index("gx") == 0
        got = lax.ppermute(jnp.where(is_first, high, low), "gx", [(0, 1), (1, 0)])
        zero = jnp.zeros_like(got)
        return jnp.where(is_first, zero, got), jnp.where(is_first, got, zero)
    below = lax.ppermute(high, "gx", [(i, i + 1) for i in range(peers - 1)])
    above = lax.ppermute(low, "gx", [(i + 1, i) for i in range(peers - 1)])
    return below, above


def everywhere(block, axes):
    sent = jnp.broadcast_to(block[None], (lax.axis_size(axes),) + block.shape)
    return lax.all_to_all(sent, axes, 0, 0, tiled=False)


def general(
    duals, residual, direction, prev_rho, dual_schur, coupling, coarse_inverse, edge_map, corner_slot, active, scaling
):
    cases, span_x, span_y, owned = duals.shape
    half = owned // 2
    full = 2 * owned
    corners = coupling.shape[2]
    width_c = coarse_inverse.shape[-1]
    peers_x, peers_y = lax.axis_size("gx"), lax.axis_size("gy")
    whole = peers_x == 2
    axes = BOTH if whole else "gy"
    regions = peers_x if whole else 1
    peers = regions * peers_y
    here_x, here_y = lax.axis_index("gx"), lax.axis_index("gy")
    used = 2 * (span_x + 1) * (span_y + 1)
    slots = used + 2

    columns = here_x * span_x + jnp.arange(span_x)
    rowset = here_y * span_y + jnp.arange(span_y)
    east_ok = jnp.broadcast_to((columns < span_x * peers_x - 1)[:, None, None], (span_x, span_y, half))
    north_ok = jnp.broadcast_to((rowset < span_y * peers_y - 1)[None, :, None], (span_x, span_y, half))
    keep_own = active.astype(jnp.float32) * jnp.concatenate([east_ok, north_ok], -1).astype(jnp.float32)
    scale_own = keep_own * scaling

    by_place = lambda v: jnp.transpose(v, (1, 2, 0, 3))
    lam = by_place(duals)
    p = keep_own[:, :, None] * by_place(direction)
    stacked = jnp.concatenate([by_place(residual), p, scale_own[:, :, None], keep_own[:, :, None]], 2)
    part_e, part_n = stacked[..., :half], stacked[..., half:]
    from_west = lax.ppermute(part_e[-1], "gx", [(i, i + 1) for i in range(peers_x - 1)])
    from_south = up_gy(part_n[:, -1], peers_y)
    west = jnp.concatenate([from_west[None], part_e[:-1]], 0)
    south = jnp.concatenate([from_south[:, None], part_n[:, :-1]], 1)
    stacked = jnp.concatenate([west, part_e, south, part_n], -1)
    r = stacked[:, :, :cases]
    p_all = stacked[:, :, cases : 2 * cases]
    scale = stacked[:, :, 2 * cases : 2 * cases + 1]
    keep = stacked[:, :, 2 * cases + 1 :]

    sign = jnp.concatenate([-jnp.ones(half), jnp.ones(half), -jnp.ones(half), jnp.ones(half)]).astype(jnp.float32)
    place = (edge_map[..., None] == jnp.arange(full, dtype=jnp.int32)).astype(jnp.float32) * sign
    schur = jnp.einsum("xyij,xyjf->xyif", dual_schur, place, precision=EXACT)
    schur = jnp.einsum("xyie,xyif->xyef", place, schur, precision=EXACT)
    couple = jnp.einsum("xycj,xyjf->xycf", coupling, place, precision=EXACT)

    flat = corner_slot.reshape(-1)
    count = flat.shape[0]
    order = jnp.arange(count)
    same = flat[:, None] == flat[None, :]
    first = ~jnp.any(same & (order[None, :] < order[:, None]), 1) & (flat != width_c)
    rank = jnp.sum((flat[None, :] < flat[:, None]) & first[None, :], 1)
    local_slot = jnp.arange(slots)
    compact = ((rank[:, None] == local_slot) & (flat != width_c)[:, None]).astype(jnp.float32)
    named = jnp.where(
        jnp.any(compact > 0, 0), jnp.max(compact * flat[:, None].astype(jnp.float32), 0), float(width_c)
    )
    compact = compact.reshape(span_x, span_y, corners, slots)
    gather_c = jnp.einsum("xycs,xycf->xysf", compact, couple, precision=EXACT)

    blocks = lambda a: (a[..., :half], a[..., half : 2 * half], a[..., 2 * half : 3 * half], a[..., 3 * half :])

    def jump(y, from_w, from_e, from_s, from_n):
        w, e, s, n = blocks(y)
        w_nb = jnp.concatenate([from_w[None], e[:-1]], 0)
        e_nb = jnp.concatenate([w[1:], from_e[None]], 0)
        s_nb = jnp.concatenate([from_s[:, None], n[:, :-1]], 1)
        n_nb = jnp.concatenate([s[:, 1:], from_n[:, None]], 1)
        return jnp.concatenate([w + w_nb, e + e_nb, s + s_nb, n + n_nb], -1)

    def rims(y):
        w, e, s, n = blocks(y)
        return w[0], e[-1], s[:, 0], n[:, -1]

    def exchange(y):
        w, e, s, n = rims(y)
        from_w, from_e = swap_gx(w, e, peers_x)
        from_s, from_n = swap_gy(s, n, peers_y)
        return from_w, from_e, from_s, from_n

    def put(rim, name):
        zero = jnp.zeros((span_x, span_y, rim.shape[-2], half), jnp.float32)
        parts = [zero, zero, zero, zero]
        if name == 0:
            parts[0] = zero.at[0].set(rim)
        elif name == 1:
            parts[1] = zero.at[-1].set(rim)
        elif name == 2:
            parts[2] = zero.at[:, 0].set(rim)
        else:
            parts[3] = zero.at[:, -1].set(rim)
        return jnp.concatenate(parts, -1)

    nb = exchange(gather_c)
    none = [jnp.zeros_like(v) for v in nb]
    spread = jnp.concatenate([jump(gather_c, *none)] + [put(v, i) for i, v in enumerate(nb)], 2)
    spread = spread * keep

    region_inv = coarse_inverse[0]

    def local_part(v):
        y = jnp.einsum("xykj,xyji->xyki", v, schur, precision=HIGH)
        c = jnp.einsum("xykj,xysj->ks", v, gather_c[:, :, :used], precision=HIGH)
        return y, c

    def over_cases(a, b):
        return jnp.sum(a * b, axis=(0, 1, 3))

    def pack(c, one, two):
        return jnp.concatenate([c, one[:, None], two[:, None]], 1).reshape(-1, 128)

    def unpack(got):
        got = got.reshape(peers, cases, slots)
        sums = jnp.sum(got[:, :, used:], 0)
        return jnp.transpose(got, (1, 0, 2)).reshape(cases, regions, peers_y, slots), sums[:, 0], sums[:, 1]

    def own_part(a):
        return jnp.concatenate([a[..., half : 2 * half], a[..., 3 * half :]], -1)

    u = scale * r
    both = jnp.concatenate([u, p_all], 2)
    y, c = local_part(both)
    yu, yp = y[:, :, :cases], y[:, :, cases:]
    rho_part = over_cases(own_part(r), own_part(u))
    names = jnp.concatenate([named, jnp.zeros(4 * 128 - slots, jnp.float32)]).reshape(4, 128)
    block = jnp.concatenate(
        [pack(c[:cases], rho_part, over_cases(u, yu)), pack(c[cases:], over_cases(p_all, yu), over_cases(p_all, yp)), names]
    )
    got = everywhere(block, axes)
    from_all = exchange(y)

    rows = cases * slots // 128
    slot_of = got[:, 2 * rows :].reshape(peers, -1)[:, :slots].reshape(regions, peers_y * slots)

    if whole:
        other = lax.ppermute(region_inv, "gx", [(0, 1), (1, 0)])
        inverses = jnp.where(here_x == 0, jnp.stack([region_inv, other]), jnp.stack([other, region_inv]))
    else:
        inverses = region_inv[None]
    pick = (slot_of[..., None] == jnp.arange(width_c, dtype=jnp.float32)).astype(jnp.float32)
    dense = jnp.einsum("ran,rnm->ram", pick, inverses, precision=EXACT)
    dense = jnp.einsum("ram,rbm->rab", dense, pick, precision=EXACT)

    def solve(c_all):
        flat_c = c_all.reshape(cases, regions, peers_y * slots)
        sol = jnp.einsum("kra,rab->krb", flat_c, dense, precision=HIGH)
        return flat_c, sol

    def total(a, b):
        return jnp.sum(a * b, (1, 2))

    def over_gx(*sums):
        return sums if whole else tuple(lax.psum(jnp.stack(sums), "gx"))

    def at(sol, ix, dy):
        sol = sol.reshape(cases, regions, peers_y, slots)
        iy = jnp.clip(here_y + dy, 0, peers_y - 1)
        return lax.dynamic_slice(sol, (0, ix, iy, 0), (cases, 1, 1, slots))[:, 0, 0]

    def beside(sol):
        if whole:
            return at(sol, 0, 0), at(sol, 1, 0)
        mine = at(sol, 0, 0)
        return swap_gx(mine, mine, peers_x)

    def coarse_part(sol):
        mine = here_x if whole else 0
        near = jnp.concatenate([at(sol, mine, 0), *beside(sol), at(sol, mine, -1), at(sol, mine, 1)], 1)
        return jnp.einsum("kn,xynj->xykj", near, spread, precision=HIGH)

    cu, rho, delta = unpack(got[:, :rows])
    cp, cross, eta = unpack(got[:, rows : 2 * rows])
    cu, su = solve(cu)
    cp, sp = solve(cp)
    delta, cross, eta = delta + total(cu, su), cross + total(cu, sp), eta + total(cp, sp)
    rho, delta, cross, eta = over_gx(rho, delta, cross, eta)
    f_both = keep * jump(y, *from_all)
    w = f_both[:, :, :cases] + coarse_part(su)
    s = f_both[:, :, cases:] + coarse_part(sp)

    wide = lambda a: a[None, None, :, None]
    beta = rho / prev_rho
    skew = cross + beta * eta
    pi = delta + 2.0 * beta * skew - beta * beta * eta
    for step in range(ITERS):
        if step > 0:
            u = scale * r
            y, c = local_part(u)
            block = pack(c, over_cases(own_part(r), own_part(u)), over_cases(u, y))
            got = everywhere(block, axes)
            from_all = exchange(y)
            rho_old = rho
            c_all, rho, delta = unpack(got)
            c_all, sol = solve(c_all)
            rho, delta = over_gx(rho, delta + total(c_all, sol))
            w = keep * jump(y, *from_all) + coarse_part(sol)
            skew = beta * skew
            beta = rho / rho_old
            pi = delta + 2.0 * beta * skew - beta * beta * pi
        alpha = rho / pi
        p = own_part(u) + wide(beta) * p
        s = w + wide(beta) * s
        lam = lam + wide(alpha) * p
        r = r - wide(alpha) * s
    back = lambda v: jnp.transpose(v, (2, 0, 1, 3))
    return back(lam), back(own_part(r)), back(p)


F32, BF16 = jnp.float32, jnp.bfloat16
SPAN_X, SPAN_Y = 2, 4
SUBS = SPAN_X * SPAN_Y
CASES = 16
EARLY = 4
STAY = 2
SLOTS = 32
USED = 2 * (SPAN_X + 1) * (SPAN_Y + 1)
CAST = 40
LIMIT = 16 * 1024 * 1024
UPPER = [(i, j) for i in range(3) for j in range(i, 3)]


def iota(shape, dim):
    return lax.broadcasted_iota(jnp.int32, shape, dim)


def split(v):
    high = v.astype(BF16)
    return high, (v - high.astype(F32)).astype(BF16)


def dot(a, b):
    return jnp.dot(a, b, preferred_element_type=F32)


def dot_turned(a, b):
    return lax.dot_general(a, b, (((1,), (1,)), ((), ())), preferred_element_type=F32)


def dot_split(v, high, low, dot=dot):
    n = v.shape[0]
    vh, vl = split(v)
    wide = dot(jnp.concatenate([vh, vl], 0), high)
    return wide[:n] + wide[n:] + dot(vh, low)


def dot_exact(v, ones):
    n = v.shape[0]
    vh, vl = split(v)
    wide = dot(jnp.concatenate([vh, vl], 0), ones)
    return wide[:n] + wide[n:]


def odd(i):
    return (i // SPAN_Y + i % SPAN_Y) % 2


def lower(rows):
    return iota((rows, 128), 1) < 64


def packs(ys):
    rows = ys[0].shape[0]
    low = lower(rows)
    column = lambda x: [
        jnp.where(low, ys[x * SPAN_Y + t][:, :128], ys[x * SPAN_Y + t + 1][:, :128]) for t in range(0, SPAN_Y, 2)
    ]
    row = lambda y: jnp.where(low, ys[y][:, 128:], ys[SPAN_Y + y][:, 128:])
    return column(0), column(SPAN_X - 1), row(0), row(SPAN_Y - 1)


def send(ys, x_ref, a_ref, b_ref, at):
    rows = pl.ds(at, ys[0].shape[0])
    west, east, south, north = packs(ys)
    first = lax.axis_index("gx") == 0
    even = lax.axis_index("gy") % 2 == 0
    for t in range(SPAN_Y // 2):
        x_ref[t, rows, :] = jnp.where(first, east[t], west[t])
    a_ref[rows, :] = jnp.where(even, north, south)
    b_ref[rows, :] = jnp.where(even, south, north)


def received(x_ref, a_ref, b_ref, at, n, side=None):
    rows = pl.ds(at, n)
    first = lax.axis_index("gx") == 0
    even = lax.axis_index("gy") % 2 == 0
    xs = [x_ref[t, rows, :] for t in range(SPAN_Y // 2)]
    a, b = a_ref[rows, :], b_ref[rows, :]
    if side is not None:
        a, b = a + side[:, :128], b + side[:, 128:256]
        xs = [xs[t] + side[:, 256 + 128 * t : 384 + 128 * t] for t in range(SPAN_Y // 2)]
    zero = jnp.zeros_like(a)
    return (
        [jnp.where(first, zero, v) for v in xs],
        [jnp.where(first, v, zero) for v in xs],
        jnp.where(even, b, a),
        jnp.where(even, a, b),
    )


def across(ys, nb, rows):
    low = lower(rows)
    zero = jnp.zeros((rows, 128), F32)
    inside = lambda x, y, part: zero if ys is None else ys[x * SPAN_Y + y][:, part * 128 : part * 128 + 128]
    out = []
    for x in range(SPAN_X):
        for y in range(SPAN_Y):
            beyond = lambda v: zero if nb is None else v()
            west = inside(x - 1, y, 0) if x else beyond(lambda: nb[0][y // 2])
            east = inside(x + 1, y, 0) if x < SPAN_X - 1 else beyond(lambda: nb[1][y // 2])
            south = inside(x, y - 1, 1) if y else beyond(lambda: nb[2])
            north = inside(x, y + 1, 1) if y < SPAN_Y - 1 else beyond(lambda: nb[3])
            if (x + y) % 2:
                west, east, south, north = east, west, north, south
            out.append(jnp.concatenate([jnp.where(low, west, east), jnp.where(low, south, north)], 1))
    return out


def owned_lanes(i, rows):
    lane = iota((rows, 256), 1) % 128
    return lane < 64 if odd(i) else lane >= 64


def spread_owned(v, i):
    zero = jnp.zeros_like(v)
    low = lower(v.shape[0])
    turned = pltpu.roll(v, 64, 1)
    if odd(i):
        return jnp.concatenate([jnp.where(low, v, zero), jnp.where(low, turned, zero)], 1)
    return jnp.concatenate([jnp.where(low, zero, turned), jnp.where(low, zero, v)], 1)


def take_owned(v, i):
    low = lower(v.shape[0])
    if odd(i):
        return jnp.where(low, v[:, :128], pltpu.roll(v[:, 128:], 64, 1))
    return jnp.where(low, pltpu.roll(v[:, :128], 64, 1), v[:, 128:])


def start_kernel(res_ref, dir_ref, act_ref, scale_ref, *refs):
    inverse_ref, own_ref, x_ref, a_ref, b_ref = refs[4:9]
    upper_ref, p_ref = refs[13:15]
    gx, gy = lax.axis_index("gx"), lax.axis_index("gy")
    last_x = gx * SPAN_X + SPAN_X - 1 == lax.axis_size("gx") * SPAN_X - 1
    last_y = gy * SPAN_Y + SPAN_Y - 1 == lax.axis_size("gy") * SPAN_Y - 1
    east = iota((1, 128), 1) < 64
    ys = []
    for i in range(SUBS):
        x, y = i // SPAN_Y, i % SPAN_Y
        keep = act_ref[i : i + 1, :].astype(F32)
        if x == SPAN_X - 1:
            keep = jnp.where(jnp.logical_and(last_x, east), 0.0, keep)
        if y == SPAN_Y - 1:
            keep = jnp.where(jnp.logical_and(last_y, jnp.logical_not(east)), 0.0, keep)
        mine = pl.ds(i, CASES, stride=SUBS)
        p = dir_ref[mine, :] * keep
        p_ref[mine, :] = p
        v = jnp.concatenate(
            [
                res_ref[mine, :],
                p,
                scale_ref[i : i + 1, :] * keep,
                keep,
                jnp.zeros((CAST - 2 * CASES - 2, 128), F32),
            ],
            0,
        )
        v = spread_owned(v, i)
        own_ref[i] = v
        ys.append(v)
    send(ys, x_ref, a_ref, b_ref, 0)
    for ref in (x_ref, a_ref, b_ref):
        ref.flush()
    for t, (i, j) in enumerate(UPPER):
        upper_ref[t] = inverse_ref[128 * i : 128 * i + 128, 128 * j : 128 * j + 128]


def operator_kernel(
    schur_ref, couple_ref, map_ref, slot_ref, rest_ref, ha_ref, la_ref, hb_ref, lb_ref, cc_ref, ch_ref, cl_ref, name_ref,
):
    none = 384
    slot = slot_ref[...].astype(F32)
    eye = iota((8, 8), 0) == iota((8, 8), 1)
    column = jnp.concatenate(
        [jnp.sum(jnp.where(eye, jnp.broadcast_to(slot[i : i + 1, :], (8, 8)), 0.0), 1, keepdims=True) for i in range(SUBS)], 0
    )
    row = jnp.concatenate([slot[i : i + 1, :] for i in range(SUBS)], 1)
    count = SUBS * 8
    earlier = iota((count, count), 1) < iota((count, count), 0)
    again = jnp.sum(jnp.where(jnp.logical_and(column == row, earlier), 1.0, 0.0), 1, keepdims=True)
    first = jnp.where(jnp.logical_and(again == 0.0, column != float(none)), 1.0, 0.0)
    first_row = jnp.sum(
        jnp.where(jnp.logical_and(column == row, iota((count, count), 0) < iota((count, count), 1)), 1.0, 0.0), 0, keepdims=True
    )
    first_row = jnp.where(jnp.logical_and(first_row == 0.0, row != float(none)), 1.0, 0.0)
    rank = jnp.sum(jnp.where(row < column, first_row, 0.0), 1, keepdims=True)
    hit = jnp.where(rank == iota((count, 128), 1).astype(F32), first, 0.0)
    name_ref[...] = jnp.broadcast_to(
        jnp.where(jnp.sum(hit, 0, keepdims=True) > 0.0, jnp.sum(hit * column, 0, keepdims=True), float(none)), (8, 128)
    )
    sub = iota((256, 256), 0)
    west = (sub // 64) % 2 == 0
    for i in range(SUBS):
        spots = map_ref[i // SPAN_Y, i % SPAN_Y : i % SPAN_Y + 1, :]
        if odd(i):
            spots = jnp.where((spots // 64) % 2 == 0, spots + 64, spots - 64)
        sign = jnp.where(west, 1.0, -1.0) if odd(i) else jnp.where(west, -1.0, 1.0)
        place = jnp.where(sub == spots, sign, 0.0).astype(BF16)
        mine = slot[i : i + 1, :]
        number = jnp.sum(jnp.where(column < mine, first, 0.0), 0, keepdims=True)
        compact = jnp.where(
            jnp.logical_and(number == iota((SLOTS, 8), 0).astype(F32), mine != float(none)), 1.0, 0.0
        )
        cc = jnp.dot(compact, couple_ref[i], precision=EXACT, preferred_element_type=F32)
        c1, rest = split(cc)
        c2, c3 = split(cc - c1.astype(F32))
        s1, s2 = split(schur_ref[i] if i < EARLY else rest_ref[i - EARLY])
        tall = dot_turned(jnp.concatenate([s1, s2, c1, c2, c3], 0), place)
        high, low = (dot(place, tall[t : t + 256].astype(BF16)).astype(BF16) for t in (0, 256))
        if i < STAY:
            ha_ref[i], la_ref[i] = high, low
        else:
            hb_ref[i - STAY], lb_ref[i - STAY] = high, low
        cc = tall[512 : 512 + SLOTS] + tall[512 + SLOTS : 512 + 2 * SLOTS] + tall[512 + 2 * SLOTS :]
        cc_ref[i] = cc
        ch_ref[i], cl_ref[i] = split(cc)


def inverse_kernel(mine_ref, upper_ref, high_ref, low_ref):
    first = lax.axis_index("gx") == 0
    mine = mine_ref[...]
    blocks = {spot: upper_ref[t] for t, spot in enumerate(UPPER)}
    side = lambda i, j: blocks[i, j] if i <= j else jnp.transpose(blocks[j, i])
    other = jnp.concatenate([jnp.concatenate([side(i, j) for j in range(3)], 1) for i in range(3)], 0)
    for region, v in enumerate((jnp.where(first, mine, other), jnp.where(first, other, mine))):
        high_ref[region], low_ref[region] = split(v)


def near_names(name_ref, x_ref, a_ref, b_ref):
    named = pl.ds(2 * CASES + SLOTS, 8)
    group = iota((8, 128), 1) // SLOTS
    turn = lambda v, g: jnp.where(group == g, pltpu.roll(v, g * SLOTS, 1), 0.0)
    wanted = name_ref[...] + 0.0
    wanted = jnp.where(group == 0, wanted, turn(a_ref[named, :], 1) + turn(b_ref[named, :], 2) + turn(x_ref[0, named, :], 3))
    found = iota((384, 128), 0).astype(F32) == wanted[0:1]
    mine = jnp.where(iota((384, 128), 1) < 3 * SLOTS, 1.0, 0.0)
    gx = lax.axis_index("gx")
    return [jnp.where(found, jnp.where(gx == region, mine, 1.0 - mine), 0.0).astype(BF16) for region in range(2)]


def near_spread(x_ref, a_ref, b_ref, nh_ref, nl_ref):
    rows = pl.ds(2 * CASES, SLOTS)
    nh_ref[...], nl_ref[...] = split(
        jnp.concatenate([a_ref[rows, :], b_ref[rows, :], x_ref[0, rows, :], x_ref[1, rows, :]], 1)
    )


def operator(ys, x_ref, a_ref, b_ref, near, mk_ref, ch_ref, cl_ref, nh_ref, nl_ref):
    n = ys[0].shape[0]
    high, low = nh_ref[...], nl_ref[...]
    side = jnp.concatenate(
        [
            dot_split(near[g], high[:, at : at + width], low[:, at : at + width])
            for g, at, width in ((1, 0, 128), (2, 128, 128), (3, 256, 256))
        ],
        1,
    )
    west, east, south, north = received(x_ref, a_ref, b_ref, 0, n, side)
    ys = [ys[i] + dot_split(near[0], ch_ref[i], cl_ref[i]) for i in range(SUBS)]
    other = across(ys, (west, east, south, north), n)
    return [mk_ref[i, 1:2, :] * (ys[i] + other[i]) for i in range(SUBS)]


def corners(us, ch_ref, cl_ref):
    couple = lambda ref: jnp.concatenate([ref[i] for i in range(SUBS)], 0)
    corner = dot_split(jnp.concatenate(us, 0), couple(ch_ref), couple(cl_ref), dot_turned)
    n = us[0].shape[0]
    group = iota((n, 128), 1) // SLOTS
    total = jnp.zeros((n, 128), F32)
    for i in range(SUBS):
        part = corner[n * i : n * i + n, 128 * (i // 4) : 128 * (i // 4) + 128]
        total = total + jnp.where(group == i % 4, part, 0.0)
    total = total + pltpu.roll(total, 64, 1)
    return total + pltpu.roll(total, 32, 1)


def by_schur(us, ha_ref, la_ref, hb_ref, lb_ref):
    return [
        dot_split(us[i], ha_ref[i], la_ref[i]) if i < STAY else dot_split(us[i], hb_ref[i - STAY], lb_ref[i - STAY])
        for i in range(SUBS)
    ]


def over_lanes(terms):
    total = terms[0]
    for t in terms[1:]:
        total = total + t
    return jnp.sum(total[:, :128] + total[:, 128:], 1, keepdims=True)


def packed(corner, one, two):
    slot = iota((CASES, 128), 1) % SLOTS
    full = jnp.where(slot == USED, one, jnp.where(slot == USED + 1, two, corner))
    group = iota((4, 128), 1) // SLOTS
    out = jnp.zeros((4, 128), F32)
    for b in range(4):
        out = jnp.where(group == b, full[4 * b : 4 * b + 4], out)
    return out


def by_slot(vs):
    group = iota((8, 128), 1) // SLOTS
    out = []
    for region in range(2):
        rows = []
        for b in range(4):
            halves = []
            for h in range(2):
                acc = None
                for q in range(4):
                    v = vs[8 * region + 4 * h + q]
                    turned = v if q == b else pltpu.roll(v, (SLOTS * (q - b)) % 128, 1)
                    acc = turned if acc is None else jnp.where(group == q, turned, acc)
                halves.append(acc)
            rows.append(jnp.concatenate(halves, 1))
        out.append(jnp.concatenate(rows, 0))
    return out


def inner(vs):
    total = vs[0]
    for v in vs[1:]:
        total = total + v
    total = total[:4] + total[4:]
    tall = jnp.concatenate([total] * 4, 0)
    lane, row = iota((CASES, 128), 1), iota((CASES, 128), 0)
    column = lambda s: jnp.sum(jnp.where(lane == SLOTS * (row // 4) + s, tall, 0.0), 1, keepdims=True)
    return column(USED), column(USED + 1)


def first_of_pairs(v):
    return jnp.concatenate([v[8 * b : 8 * b + 4] for b in range(v.shape[0] // 8)], 0)


def solve(spots, pick_ref, gh_ref, gl_ref, near_ref):
    totals, sols, near = [], [], None
    for region in range(2):
        v = spots[region]
        n = v.shape[0]
        even = dot_exact(v, pick_ref[region, 0])
        odds = dot_exact(v, pick_ref[region, 1])
        z = jnp.where((iota((n, 384), 0) // 4) % 2 == 0, even, odds).reshape(n // 8, 8, 384)
        total = (z + pltpu.roll(z, 4, 1)).reshape(n, 384)
        sol = dot_split(total, gh_ref[region], gl_ref[region])
        part = dot_exact(sol, near_ref[region])
        near = part if near is None else near + part
        totals.append(total)
        sols.append(sol)
    return totals, sols, near


def swap_pairs(v):
    rows, lanes = v.shape
    return pltpu.roll(v.reshape(rows // 8, 8, lanes), 4, 1).reshape(rows, lanes)


def ahead(region, t):
    gx, gy = lax.axis_index("gx"), lax.axis_index("gy")
    return 8 * lax.rem(gx + region, 2) + lax.rem(gy // 2 + t, 8)


def dense_kernel(got_ref, gh_ref, gl_ref, dh_ref, dl_ref):
    group = iota((8, 128), 1) // SLOTS
    picks, rows = [], []
    for region in range(2):
        hits = []
        for par in range(2):
            halves = []
            for h in range(2):
                acc = None
                for q in range(4):
                    v = got_ref[3 * ahead(region, 4 * h + q) + 1 + par]
                    v = v if par == 0 else pltpu.roll(v, 4, 0)
                    turned = pltpu.roll(v, SLOTS * q, 1) if q else v
                    acc = turned if acc is None else jnp.where(group == q, turned, acc)
                halves.append(acc[0:1])
            wanted = jnp.concatenate(halves, 1)
            hits.append(jnp.where(iota((384, 256), 0).astype(F32) == wanted, 1.0, 0.0))
        picks.append(jnp.concatenate(hits, 1).astype(BF16))
        rows.append([jnp.transpose(hit).astype(BF16) for hit in hits])
    size = 384
    for region in range(2):
        which = lax.rem(lax.axis_index("gx") + region, 2)
        both = dot(jnp.concatenate([gh_ref[which], gl_ref[which]], 0), picks[region]).astype(BF16)
        for half, out_ref in ((both[:size], dh_ref), (both[size:], dl_ref)):
            top = dot(rows[region][0], half).astype(BF16)
            out_ref[region, 0], out_ref[region, 1] = top[:, :256], top[:, 256:]
            out_ref[region, 2] = dot(rows[region][1], half[:, 256:]).astype(BF16)


def solve_dense(spots, dh_ref, dl_ref):
    total, sols = None, []
    for region in range(2):
        v = spots[region]
        block = lambda t, dot=dot: dot_split(v, dh_ref[region, t], dl_ref[region, t], dot)
        first = (iota(v.shape, 0) // 4) % 2 == 0
        sol = jnp.where(first, block(0) + swap_pairs(block(1, dot_turned)), block(2) + swap_pairs(block(1)))
        total = v * sol if total is None else total + v * sol
        sols.append(sol)
    total = jnp.sum(total, 1, keepdims=True)
    halves = lambda v: [jnp.concatenate([v[8 * b + at : 8 * b + at + 4] for b in range(4)], 0) for at in (0, 4)]
    total = sum(halves(total))
    even = lax.axis_index("gy") % 2 == 0
    (a, b), (c, d) = halves(sols[0]), halves(sols[1][:, :128])
    here = jnp.where(even, a[:, :128], b[:, :128])
    pair = jnp.where(even, b[:, :128], a[:, :128])
    beyond = jnp.where(even, pltpu.roll(b[:, 128:], SLOTS, 1), pltpu.roll(a[:, :128], 128 - SLOTS, 1))
    along = jnp.where(even, c, d)
    return total, [v[:, :SLOTS] for v in (here, pair, beyond, along)]


def energy(totals, sols):
    both = totals[0] * sols[0] + totals[1] * sols[1]
    return first_of_pairs(jnp.sum(both, 1, keepdims=True))


def emit(rs, mk_ref, schur_refs, ch_ref, cl_ref, block_ref, y_ref, x_ref, a_ref, b_ref):
    us = [mk_ref[i, 0:1, :] * rs[i] for i in range(SUBS)]
    corner = corners(us, ch_ref, cl_ref)
    rho = over_lanes([jnp.where(owned_lanes(i, CASES), rs[i] * us[i], 0.0) for i in range(SUBS)])
    ys = by_schur(us, *schur_refs)
    send(ys, x_ref, a_ref, b_ref, 0)
    for i in range(SUBS):
        y_ref[i] = ys[i]
    for ref in (x_ref, a_ref, b_ref, y_ref):
        ref.flush()
    delta = over_lanes([us[i] * ys[i] for i in range(SUBS)])
    block = packed(corner, rho, delta)
    twice = jnp.concatenate([block, block], 0)
    for j in range(16):
        block_ref[j] = twice
    block_ref.flush()


def first_kernel(
    own_ref, x_ref, a_ref, b_ref, ha_ref, la_ref, hb_ref, lb_ref, cc_ref, ch_ref, cl_ref, name_ref,
    r_ref, mk_ref, y_ref, block_ref, sx_ref, sa_ref, sb_ref, high_out_ref, low_out_ref,
):
    schur_refs = ha_ref, la_ref, hb_ref, lb_ref
    own = [own_ref[i] for i in range(SUBS)]
    other = across(own, received(x_ref, a_ref, b_ref, 0, CAST), CAST)
    rs, vs = [], []
    for i in range(SUBS):
        full = own[i] + other[i]
        rs.append(full[:CASES])
        r_ref[i] = full[:CASES]
        mk_ref[i] = full[2 * CASES : 2 * CASES + 8]
        vs.append(jnp.concatenate([full[2 * CASES : 2 * CASES + 1] * full[:CASES], full[CASES : 2 * CASES]], 0))
    corner = corners(vs, ch_ref, cl_ref)
    ys = by_schur(vs, *schur_refs)
    names = name_ref[...]
    send([jnp.concatenate([ys[i], cc_ref[i]], 0) for i in range(SUBS)], sx_ref, sa_ref, sb_ref, 0)
    at = pl.ds(2 * CASES + SLOTS, 8)
    for t in range(SPAN_Y // 2):
        sx_ref[t, at, :] = names
    sa_ref[at, :] = names
    sb_ref[at, :] = names
    for ref in (sx_ref, sa_ref, sb_ref):
        ref.flush()
    us = [v[:CASES] for v in vs]
    ps = [v[CASES:] for v in vs]
    rho = over_lanes([jnp.where(owned_lanes(i, CASES), rs[i] * us[i], 0.0) for i in range(SUBS)])
    delta = over_lanes([us[i] * ys[i][:CASES] for i in range(SUBS)])
    cross = over_lanes([ps[i] * ys[i][:CASES] for i in range(SUBS)])
    eta = over_lanes([ps[i] * ys[i][CASES:] for i in range(SUBS)])
    one, two = packed(corner[:CASES], rho, delta), packed(corner[CASES:], cross, eta)
    blocks = [
        jnp.concatenate([one, two], 0),
        jnp.concatenate([names[:4], one], 0),
        jnp.concatenate([two, names[:4]], 0),
    ]
    for j in range(16):
        for t in range(3):
            block_ref[3 * j + t] = blocks[t]
    for i in range(SUBS):
        y_ref[i] = ys[i]


def column_of(row):
    eye = iota((CASES, CASES), 0) == iota((CASES, CASES), 1)
    return jnp.sum(jnp.where(eye, jnp.broadcast_to(row, (CASES, CASES)), 0.0), 1, keepdims=True)


def keep_scalars(scal_ref, values):
    for t, v in enumerate(values):
        scal_ref[t] = jnp.broadcast_to(v, (CASES, 128))


def second_kernel(
    got_ref, x_ref, a_ref, b_ref, y_ref, r_ref, mk_ref, p_ref, l_ref, rho_ref, gh_ref, gl_ref, name_ref,
    ha_ref, la_ref, hb_ref, lb_ref, ch_ref, cl_ref,
    nh_ref, nl_ref, po_ref, lo_ref, ro_ref, so_ref, scal_ref, block_ref, yo_ref, sx_ref, sa_ref, sb_ref, *_,
):
    near_ref, pick_ref = near_names(name_ref, x_ref, a_ref, b_ref), {}
    near_spread(x_ref, a_ref, b_ref, nh_ref, nl_ref)
    top = iota((8, 128), 0) < 4
    us, ps, names = [], [], []
    for j in range(16):
        v = [got_ref[3 * j + t] for t in range(3)]
        us.append(jnp.where(top, v[0], v[1]))
        ps.append(pltpu.roll(jnp.where(top, v[2], v[0]), 4, 0))
        names.append((v[1], pltpu.roll(v[2], 4, 0)))
    group = iota((8, 128), 1) // SLOTS
    for region in range(2):
        for par in range(2):
            halves = []
            for h in range(2):
                acc = None
                for q in range(4):
                    v = names[8 * region + 4 * h + q][par]
                    turned = pltpu.roll(v, SLOTS * q, 1) if q else v
                    acc = turned if acc is None else jnp.where(group == q, turned, acc)
                halves.append(acc[0:1])
            wanted = jnp.concatenate(halves, 1)
            hit = jnp.where(iota((384, 256), 0).astype(F32) == wanted, 1.0, 0.0)
            pick_ref[region, par] = jnp.transpose(hit).astype(BF16)
    lhs_u, lhs_p = by_slot(us), by_slot(ps)
    n = lhs_u[0].shape[0]
    totals, sols, near = solve(
        [jnp.concatenate([lhs_u[t], lhs_p[t]], 0) for t in range(2)], pick_ref, gh_ref, gl_ref, near_ref
    )
    of_u, of_p = lambda vs: [v[:n] for v in vs], lambda vs: [v[n:] for v in vs]
    rho, delta = inner(us)
    cross, eta = inner(ps)
    delta = delta + energy(of_u(totals), of_u(sols))
    cross = cross + energy(of_p(totals), of_u(sols))
    eta = eta + energy(of_p(totals), of_p(sols))
    near = first_of_pairs(near)
    near = [(pltpu.roll(near, 128 - SLOTS * g, 1) if g else near)[:, :SLOTS] for g in range(4)]
    beta = rho / column_of(rho_ref[...])
    skew = cross + beta * eta
    pi = delta + 2.0 * beta * skew - beta * beta * eta
    alpha = rho / pi
    fs = operator([y_ref[i] for i in range(SUBS)], x_ref, a_ref, b_ref, near, mk_ref, ch_ref, cl_ref, nh_ref, nl_ref)
    rs = []
    for i in range(SUBS):
        f, r = fs[i], r_ref[i]
        s = f[:CASES] + beta * f[CASES:]
        r = r - alpha * s
        rs.append(r)
        ro_ref[i], so_ref[i] = r, s
    scalars = rho, pi, beta, skew, alpha
    keep_scalars(scal_ref, scalars)
    so_ref.flush()
    emit(rs, mk_ref, (ha_ref, la_ref, hb_ref, lb_ref), ch_ref, cl_ref, block_ref, yo_ref, sx_ref, sa_ref, sb_ref)

    @pl.when(lax.axis_index("gx") >= 0)
    def _():
        track(r_ref, scalars, mk_ref, p_ref, l_ref, po_ref, lo_ref)


def absorb(got_ref, x_ref, a_ref, b_ref, y_ref, r_ref, s_ref, scal_ref, mk_ref, dh_ref, dl_ref, nh_ref, nl_ref, ch_ref, cl_ref):
    vs = [got_ref[ahead(region, t)] for region in range(2) for t in range(8)]
    coarse, near = solve_dense(by_slot(vs), dh_ref, dl_ref)
    rho, delta = inner(vs)
    delta = delta + coarse
    rho_old, pi, beta, skew = (scal_ref[t][:, 0:1] for t in range(4))
    skew = beta * skew
    beta = rho / rho_old
    pi = delta + 2.0 * beta * skew - beta * beta * pi
    alpha = rho / pi
    fs = operator([y_ref[i] for i in range(SUBS)], x_ref, a_ref, b_ref, near, mk_ref, ch_ref, cl_ref, nh_ref, nl_ref)
    ss = [fs[i] + beta * s_ref[i] for i in range(SUBS)]
    rs = [r_ref[i] - alpha * ss[i] for i in range(SUBS)]
    return rs, ss, (rho, pi, beta, skew, alpha)


def track(r_ref, scalars, mk_ref, p_ref, l_ref, po_ref, lo_ref):
    _, _, beta, _, alpha = scalars
    for i in range(SUBS):
        mine = pl.ds(i, CASES, stride=SUBS)
        p = take_owned(mk_ref[i, 0:1, :] * r_ref[i], i) + beta * p_ref[mine, :]
        po_ref[mine, :] = p
        lo_ref[mine, :] = l_ref[mine, :] + alpha * p


def round_kernel(
    got_ref, x_ref, a_ref, b_ref, y_ref, r_ref, s_ref, scal_ref, mk_ref, dh_ref, dl_ref,
    nh_ref, nl_ref, ch_ref, cl_ref, p_ref, l_ref, ha_ref, la_ref, hb_ref, lb_ref,
    po_ref, lo_ref, ro_ref, so_ref, scalo_ref, block_ref, yo_ref, sx_ref, sa_ref, sb_ref,
):
    rs, ss, scalars = absorb(
        got_ref, x_ref, a_ref, b_ref, y_ref, r_ref, s_ref, scal_ref, mk_ref, dh_ref, dl_ref, nh_ref, nl_ref, ch_ref, cl_ref
    )
    for i in range(SUBS):
        ro_ref[i], so_ref[i] = rs[i], ss[i]
    so_ref.flush()
    keep_scalars(scalo_ref, scalars)
    emit(rs, mk_ref, (ha_ref, la_ref, hb_ref, lb_ref), ch_ref, cl_ref, block_ref, yo_ref, sx_ref, sa_ref, sb_ref)

    @pl.when(lax.axis_index("gx") >= 0)
    def _():
        track(r_ref, scalars, mk_ref, p_ref, l_ref, po_ref, lo_ref)


def last_kernel(
    got_ref, x_ref, a_ref, b_ref, y_ref, r_ref, s_ref, scal_ref, mk_ref, dh_ref, dl_ref, nh_ref, nl_ref, ch_ref, cl_ref,
    p_ref, l_ref, lo_ref, ro_ref, po_ref,
):
    rs, _, scalars = absorb(
        got_ref, x_ref, a_ref, b_ref, y_ref, r_ref, s_ref, scal_ref, mk_ref, dh_ref, dl_ref, nh_ref, nl_ref, ch_ref, cl_ref
    )
    track(r_ref, scalars, mk_ref, p_ref, l_ref, po_ref, lo_ref)
    po_ref.flush()
    lo_ref.flush()
    for i in range(SUBS):
        ro_ref[pl.ds(i, CASES, stride=SUBS), :] = take_owned(rs[i], i)


class Fetched:
    def __init__(self, source, buffer, semaphore):
        self.buffer = buffer
        self.copy = pltpu.make_async_copy(source, buffer, semaphore)
        self.copy.start()
        self.here = False

    def wait(self):
        self.copy.wait()
        self.here = True

    def __getitem__(self, index):
        if not self.here:
            self.wait()
        return self.buffer[index]


class Stored:
    def __init__(self, target, buffer, semaphore):
        self.buffer = buffer
        self.copy = pltpu.make_async_copy(buffer, target, semaphore)
        self.sent = False

    def __setitem__(self, index, value):
        self.buffer[index] = value

    def __getitem__(self, index):
        return self.buffer[index]

    def flush(self):
        if not self.sent:
            self.copy.start()
            self.sent = True


class Kept:
    def __init__(self, ref):
        self.ref = ref

    def __setitem__(self, index, value):
        self.ref[index] = value

    def __getitem__(self, index):
        return self.ref[index]

    def flush(self):
        pass


def call(kernel, args, outs, kept=(), kept_out=(), raw=(), through=None, flops=None, late=0, parts=None):
    through, parts = through or {}, parts or {}
    moved = [i for i in range(len(args)) if i not in kept and i not in raw]
    written = [i for i in range(len(outs)) if i not in kept_out and i not in through]

    def body(*refs):
        ins, results = refs[: len(args)], refs[len(args) : len(args) + len(outs)]
        buffers, (in_sem, out_sem, through_sem) = refs[len(args) + len(outs) : -3], refs[-3:]
        fetched, stored = list(ins), [Kept(ref) for ref in results]
        for t, i in enumerate(moved):
            source = ins[i].at[pl.ds(*parts[i])] if i in parts else ins[i]
            fetched[i] = Fetched(source, buffers[t], in_sem.at[t])
        for t, i in enumerate(written):
            stored[i] = Stored(results[i], buffers[len(moved) + t], out_sem.at[t])
        passing = [
            pltpu.make_async_copy(source(ins), results[i], through_sem.at[t]) for t, (i, source) in enumerate(through.items())
        ]
        for copy in passing:
            copy.start()
        if moved or passing:
            spot = (0,) * (len(outs[-1 - late][0]) - 2)
            blank = stored[-1 - late]

            @pl.when(lax.axis_index("gx") >= 0)
            def _():
                blank[spot] = jnp.zeros(outs[-1 - late][0][-2:], outs[-1 - late][1])

        kernel(*fetched, *stored)
        for i in written:
            stored[i].flush()
        for i in moved:
            if not fetched[i].here:
                fetched[i].wait()
        for copy in passing:
            copy.wait()
        for i in written:
            stored[i].copy.wait()

    place = lambda held: pl.BlockSpec(memory_space=pltpu.VMEM if held else pltpu.HBM)
    semaphores = lambda n: pltpu.SemaphoreType.DMA((max(n, 1),))
    args = [a if i in kept else pltpu.with_memory_space_constraint(a, pltpu.HBM) for i, a in enumerate(args)]
    return pl.pallas_call(
        body,
        out_shape=[
            jax.ShapeDtypeStruct(*out) if i in kept_out else pltpu.HBM(*out) for i, out in enumerate(outs)
        ],
        in_specs=[place(i in kept) for i in range(len(args))],
        out_specs=[place(i in kept_out) for i in range(len(outs))],
        scratch_shapes=[
            pltpu.VMEM((parts[i][1],) + args[i].shape[1:] if i in parts else args[i].shape, args[i].dtype) for i in moved
        ]
        + [pltpu.VMEM(*outs[i]) for i in written]
        + [semaphores(len(moved)), semaphores(len(written)), semaphores(len(through))],
        compiler_params=pltpu.CompilerParams(vmem_limit_bytes=LIMIT),
        cost_estimate=flops and pl.CostEstimate(flops=flops, bytes_accessed=flops // 512, transcendentals=0),
    )(*args)


def trade(x, a, b):
    peers = lax.axis_size("gy")
    return (
        lax.ppermute(x, "gx", [(0, 1), (1, 0)]),
        lax.ppermute(a, "gy", both_ways(pairs_from(0, peers))),
        lax.ppermute(b, "gy", both_ways(pairs_from(1, peers))),
    )


def two_regions(
    duals, residual, direction, prev_rho, dual_schur, coupling, coarse_inverse, edge_map, corner_slot, active, scaling
):
    native = lambda v: v.reshape(CASES * SUBS, 128)
    by_sub = lambda v: v.reshape((SUBS,) + v.shape[2:])
    width = coarse_inverse.shape[-1]
    sends = lambda rows: [((SPAN_Y // 2, rows, 128), F32), ((rows, 128), F32), ((rows, 128), F32)]
    state = ((SUBS, CASES, 256), F32)
    plain = ((CASES * SUBS, 128), F32)

    raw = [by_sub(dual_schur), by_sub(coupling), edge_map, by_sub(corner_slot)]
    own, *out, schur, coupled, placed, slotted, inverse, p = call(
        start_kernel,
        [native(residual), native(direction), by_sub(active), by_sub(scaling), *raw, coarse_inverse[0]],
        [((SUBS, CAST, 256), F32)] + sends(CAST) + [((EARLY,) + raw[0].shape[1:], F32)] + [(v.shape, v.dtype) for v in raw[1:]] + [((len(UPPER), 128, 128), F32), plain],
        kept_out=(0, 4, 5, 6, 7),
        raw=(4, 5, 6, 7),
        through={4: lambda v: v[4].at[pl.ds(0, EARLY)], 5: lambda v: v[5], 6: lambda v: v[6], 7: lambda v: v[7]},
    )
    come = trade(*out)
    other = lax.ppermute(inverse, "gx", [(0, 1), (1, 0)])
    first_part, rest = ((STAY, 256, 256), BF16), ((SUBS - STAY, 256, 256), BF16)
    couple = ((SUBS, SLOTS, 256), BF16)
    ha, la, hb, lb, cc, ch, cl, names = call(
        operator_kernel,
        [schur, coupled, placed, slotted, by_sub(dual_schur)],
        [first_part, first_part, rest, rest, ((SUBS, SLOTS, 256), F32), couple, couple, ((8, 128), F32)],
        kept=range(4),
        kept_out=range(8),
        parts={4: (EARLY, SUBS - EARLY)},
        flops=5 * 10**9,
    )
    rows = 2 * CASES + SLOTS + 8
    r, mk, y, block, *out, hb, lb = call(
        first_kernel,
        [own, *come, ha, la, hb, lb, cc, ch, cl, names],
        [state, ((SUBS, 8, 256), F32), ((SUBS, 2 * CASES, 256), F32), ((48, 8, 128), F32)]
        + sends(rows)
        + [rest, rest],
        kept=range(12),
        kept_out=(0, 1, 2),
        through={7: lambda v: v[6], 8: lambda v: v[7]},
        late=2,
    )
    got = lax.all_to_all(block.reshape(32, 3, 4, 128), BOTH, 0, 0, tiled=False).reshape(48, 8, 128)
    come = trade(*out)
    square = ((2, width, width), BF16)
    gh, gl = call(inverse_kernel, [coarse_inverse[0], other], [square, square], kept_out=(0, 1), flops=10**9)
    side = ((SLOTS, 512), BF16)
    onward = [plain, plain, state, state, ((5, CASES, 128), F32), ((16, 8, 128), F32), state] + sends(CASES)
    nh, nl, p, lam, r, s, scal, block, y, *out, gh, gl = call(
        second_kernel,
        [got, *come, y, r, mk, p, native(duals), prev_rho.reshape(1, CASES), gh, gl, names, ha, la, hb, lb, ch, cl],
        [side, side] + onward + [square, square],
        kept=(0, 1, 2, 3, 4, 5, 6, 10, 11, 12, 13, 14, 17, 18),
        kept_out=(0, 1, 2, 3, 4, 6, 8),
        through={12: lambda v: v[10], 13: lambda v: v[11]},
        late=5,
    )
    dense = ((2, 3, 256, 256), BF16)
    dh, dl = call(dense_kernel, [got, gh, gl], [dense, dense], kept=(0,), kept_out=(0, 1), flops=10**8)
    for step in range(1, ITERS):
        got = lax.all_to_all(block.reshape(32, 4, 128), BOTH, 0, 0, tiled=False).reshape(16, 8, 128)
        come = trade(*out)
        args = [got, *come, y, r, s, scal, mk, dh, dl, nh, nl, ch, cl, p, lam]
        kept = (*range(6), *range(7, 17))
        if step < ITERS - 1:
            p, lam, r, s, scal, block, y, *out = call(
                round_kernel, args + [ha, la, hb, lb], onward, (*kept, 17, 18), kept_out=(0, 1, 2, 4, 6), late=3
            )
        else:
            results = call(last_kernel, args, [plain, plain, plain], kept)
    return tuple(v.reshape(duals.shape) for v in results)


def shards(*args):
    cases, span_x, span_y, owned = args[0].shape
    fits = (cases, span_x, span_y, owned, args[6].shape[-1]) == (CASES, SPAN_X, SPAN_Y, 128, 384)
    if fits and lax.axis_size("gx") == 2 and lax.axis_size("gy") == 16:
        return two_regions(*args)
    return general(*args)


def solution(mesh):
    placed = (
        P(None, "gx", "gy", None),
        P(None, "gx", "gy", None),
        P(None, "gx", "gy", None),
        P(),
        P("gx", "gy", None, None),
        P("gx", "gy", None, None),
        P("gx", None, None),
        P("gx", "gy", None),
        P("gx", "gy", None),
        P("gx", "gy", None),
        P("gx", "gy", None),
    )
    return jax.shard_map(
        shards,
        mesh=mesh,
        in_specs=placed,
        out_specs=(P(None, "gx", "gy", None), P(None, "gx", "gy", None), P(None, "gx", "gy", None)),
        check_vma=False,
    )
```
